32 devices in a mesh: head: 4 (over y, x), ctx: 8 (over z, core).
Axes of the slice: x: 2, y: 2, z: 4, core: 2. Of those that a mesh axis runs over, the one named last changes fastest.
Arguments:
- queries: bfloat16 [8, 512, 8192], P('ctx', 'head'), may hold values from -6 to 6
- keys: bfloat16 [8, 512, 8192], P('ctx', 'head'), may hold values from -6 to 6
- values: bfloat16 [8, 512, 8192], P('ctx', 'head'), may hold values from -6 to 6
- gate: bfloat16 [8, 512, 8192], P('ctx', 'head'), may hold values from -6 to 6
- log_decay: float32 [8, 64, 512], P('ctx', 'head'), may hold values from -1 to 0, as said below
- norm_gain: bfloat16 [8192], P('head'), may hold values from 0.099609375 to 1.8984375
Outputs:
- attended: bfloat16 [8, 512, 8192], P('ctx', 'head')
The draws below stay inside these ranges and needn't reach their ends.
Inputs may be any that keep to these rules, and one draw needn't show every extreme that they name: `log_decay`: every entry is negative.
All inputs are finite; a program needn't handle non-finite values.
Results may differ from the reference program's by a relative error of at most 0.0048.
Values may be sent and summed in bfloat16 or wider, within the bound.
No kernel may reach another device: no remote copies, remote signals or barrier semaphores. Data moves between devices by JAX's collectives and lax.ppermute only.
A program may use at most 192 MiB of HBM per device.

```python
import math
import jax
import jax.numpy as jnp
from jax import lax

HEAD_COUNT = 64
DH = 128
HD = 8192
BLOCK_GROUPS = 8
BLOCK_LENGTH = 512
SEQUENCE_TOKENS = 4096


def draw_log_decay(key, part):
    key = jax.random.fold_in(key, 7)
    token_flows = jax.random.split(key, 5)
    fast_share = 0.5
    fast_heads = jax.random.uniform(token_flows[0], (HEAD_COUNT,)) < fast_share
    slow_rate = math.log(2.0) / (2.0 * SEQUENCE_TOKENS)
    base_rate = jnp.where(fast_heads, 1.0 / 40.0, slow_rate)
    block_factor = jnp.exp(jax.random.uniform(token_flows[1], (BLOCK_GROUPS, HEAD_COUNT, 1), minval=math.log(0.5), maxval=math.log(2.0)))
    roughness = jax.random.uniform(token_flows[2], (BLOCK_GROUPS, HEAD_COUNT, BLOCK_LENGTH), minval=0.5, maxval=1.5)
    decay_rate = base_rate[None, :, None] * block_factor * roughness
    block_runs = jax.random.uniform(token_flows[3], (BLOCK_GROUPS, HEAD_COUNT, BLOCK_LENGTH)) < 2.0 / SEQUENCE_TOKENS
    retained_fraction = jax.random.uniform(token_flows[4], (BLOCK_GROUPS, HEAD_COUNT, BLOCK_LENGTH), minval=0.5, maxval=0.8)
    return (jnp.where(block_runs, jnp.log(retained_fraction), 0.0) - decay_rate).astype(jnp.float32)


def levels(stream_key, dims, cuts, least, largest):
    gain = 1.0
    for dim, shards_of in cuts:
        steps = jax.random.uniform(jax.random.fold_in(jax.random.fold_in(stream_key, 6), dim), (shards_of,), jnp.float32, least / len(cuts), largest / len(cuts))
        gain = gain * jnp.repeat(jnp.exp(steps), dims[dim] // shards_of).reshape((-1,) + (1,) * (len(dims) - 1 - dim))
    return gain


def gaussian(own_key, dims, width, limit, pieces=(), held_as=jnp.bfloat16):
    result = jax.random.normal(own_key, dims, jnp.float32) * width
    if len(pieces) > 0:
        result = levels(own_key, dims, pieces, -0.22, 0.18) * result
    return jnp.clip(result, min=-limit, max=limit).astype(held_as)


def setup_inputs(seed: int = 0) -> dict:
    key_of = jax.random.split(jax.random.key(seed), 7)
    queries = gaussian(key_of[0], (BLOCK_GROUPS, BLOCK_LENGTH, HD), 1.0, 6.0, ((0, 8), (1, 4)))
    keys = gaussian(key_of[1], (BLOCK_GROUPS, BLOCK_LENGTH, HD), 1.0, 6.0, ((0, 8), (1, 4)))
    values = gaussian(key_of[2], (BLOCK_GROUPS, BLOCK_LENGTH, HD), 1.0, 6.0, ((0, 8), (1, 4)))
    gate = gaussian(key_of[3], (BLOCK_GROUPS, BLOCK_LENGTH, HD), 1.5, 6.0, ((0, 8), (1, 4)))
    log_decay = draw_log_decay(jax.random.fold_in(key_of[6], 71), 0)
    norm_gain = jnp.clip(1.0 + 0.18 * jax.random.normal(key_of[5], (HD,), jnp.float32), 0.099609375, 1.8984375).astype(jnp.bfloat16)
    return dict(queries=queries, keys=keys, values=values, gate=gate, log_decay=log_decay, norm_gain=norm_gain)


def reference(queries, keys, values, gate, log_decay, norm_gain):
    position = jnp.arange(BLOCK_LENGTH)
    causal_mask = position[:, None] >= position[None, :]
    gain_wide = norm_gain.astype(jnp.float32)

    def group_step(carry_state, inputs):
        query_group, key_group, value_group, gate_group, decay_group = inputs
        query_heads = query_group.reshape(BLOCK_LENGTH, HEAD_COUNT, DH).astype(jnp.float32)
        key_heads = key_group.reshape(BLOCK_LENGTH, HEAD_COUNT, DH).astype(jnp.float32)
        value_heads = value_group.reshape(BLOCK_LENGTH, HEAD_COUNT, DH).astype(jnp.float32)
        cumulative = jnp.cumsum(decay_group, axis=-1)
        group_total = cumulative[:, -1]
        scores = jnp.einsum('thd,shd->hts', query_heads, key_heads)
        log_gap = cumulative[:, :, None] - cumulative[:, None, :]
        weights = (scores * jnp.exp(jnp.where(causal_mask[None], log_gap, -jnp.inf))).astype(jnp.bfloat16)
        inside_part = jnp.einsum('hts,shd->thd', weights.astype(jnp.float32), value_heads)
        carried_part = jnp.einsum('thd,hde->the', query_heads, carry_state, precision=lax.Precision.HIGHEST)
        mixed = inside_part + carried_part * jnp.exp(cumulative).T[:, :, None]
        inv_rms = lax.rsqrt(lax.optimization_barrier(jnp.mean(mixed * mixed, axis=-1, keepdims=True)) + 1e-06)
        normed = (mixed * inv_rms).reshape(BLOCK_LENGTH, HEAD_COUNT * DH) * gain_wide * jax.nn.sigmoid(gate_group.astype(jnp.float32))
        decayed_keys = (key_heads * jnp.exp(group_total[None, :] - cumulative.T)[:, :, None]).astype(jnp.bfloat16)
        block_state = jnp.einsum('thd,the->hde', decayed_keys.astype(jnp.float32), value_heads)
        next_state = jnp.exp(group_total)[:, None, None] * carry_state + block_state
        return (next_state, normed.astype(jnp.bfloat16))
    empty_state = jnp.zeros((HEAD_COUNT, DH, DH), jnp.float32)
    _, outputs = lax.scan(group_step, empty_state, (queries, keys, values, gate, log_decay))
    return outputs
```

```python
import functools

import jax
import jax.numpy as jnp
from jax import lax
from jax.experimental import pallas as pl
from jax.experimental.pallas import tpu as pltpu
from jax.sharding import PartitionSpec as P

GROUPS = 1
VMEM_LIMIT = 48 * 1024 * 1024
NN = (((1,), (0,)), ((), ()))
NT = (((1,), (1,)), ((), ()))
TN = (((0,), (0,)), ((), ()))


def dot(a, b, dims, precision=None):
    return lax.dot_general(a, b, dims, precision=precision, preferred_element_type=jnp.float32)


def exact_dot(a, b, dims):
    return dot(a, b, dims, lax.Precision.HIGHEST)


def triangle(length, keep):
    rows = lax.broadcasted_iota(jnp.int32, (length, length), 0)
    columns = lax.broadcasted_iota(jnp.int32, (length, length), 1)
    return jnp.where(keep(rows, columns), 1.0, 0.0).astype(jnp.float32)


def params():
    return pltpu.CompilerParams(vmem_limit_bytes=VMEM_LIMIT)


def state_kernel(heads, dim, keys_ref, values_ref, small_ref, state_ref):
    decay = small_ref[0, 0]
    length = decay.shape[1]
    later = exact_dot(triangle(length, lambda s, u: u > s), decay, NT)
    weight = jnp.exp(later)
    for head in range(heads):
        columns = slice(head * dim, (head + 1) * dim)
        decayed = keys_ref[0, :, columns].astype(jnp.float32) * weight[:, head : head + 1]
        high = decayed.astype(jnp.bfloat16)
        low = (decayed - high.astype(jnp.float32)).astype(jnp.bfloat16)
        value = values_ref[0, :, columns]
        state = dot(high, value, TN) + dot(low, value, TN)
        state_ref[0, head] = state.astype(jnp.bfloat16)


def inside_kernel(heads, dim, queries_ref, keys_ref, values_ref, small_ref, inside_ref):
    decay = small_ref[0, 0]
    length = decay.shape[1]
    down = exact_dot(triangle(length, lambda t, u: u <= t), decay, NT)
    across = exact_dot(decay, triangle(length, lambda u, s: u <= s), NN)
    rows = lax.broadcasted_iota(jnp.int32, (length, length), 0)
    causal = rows >= lax.broadcasted_iota(jnp.int32, (length, length), 1)
    for head in range(heads):
        columns = slice(head * dim, (head + 1) * dim)
        scores = dot(queries_ref[0, :, columns], keys_ref[0, :, columns], NT)
        gap = down[:, head : head + 1] - across[head : head + 1, :]
        weights = scores * jnp.exp(jnp.where(causal, gap, -jnp.inf))
        inside_ref[:, columns] = dot(weights.astype(jnp.bfloat16), values_ref[0, :, columns], NN)


def total_kernel(first, heads, pieces, rows, weight_ref, decay_ref, state_ref, total_ref):
    parts, _, dim, _ = state_ref.shape
    for head in range(heads):
        place = first + head
        total = weight_ref[place * parts] * state_ref[0, head].astype(jnp.float32)
        for part in range(1, parts):
            total += weight_ref[place * parts + part] * state_ref[part, head].astype(jnp.float32)
        start = head * dim
        if rows >= dim:
            total_ref[start // rows, start % rows : start % rows + dim, :] = total
        else:
            for cut in range(dim // rows):
                total_ref[start // rows + cut, :rows, :] = total[cut * rows : (cut + 1) * rows]
    for piece in range(pieces):
        for turn in range(max(1, rows // dim)):
            place = first + (piece * rows) // dim + turn
            total_ref[piece, rows + turn : rows + turn + 1, :] = jnp.full(
                (1, total_ref.shape[2]), decay_ref[place], jnp.float32
            )


def scan_kernel(rows, dim, total_ref, carried_ref):
    height = min(rows, dim)
    for turn in range(rows // height):
        span = slice(turn * height, (turn + 1) * height)
        state = jnp.zeros((height, total_ref.shape[2]), jnp.float32)
        for block in range(total_ref.shape[0]):
            carried_ref[block, span, :] = state
            decay = total_ref[block, rows + turn : rows + turn + 1, :]
            state = decay * state + total_ref[block, span, :]


def prefix_kernel(first, heads, weight_ref, state_ref, carried_ref, prefix_ref):
    parts = state_ref.shape[0]
    for head in range(heads):
        place = (first + head) * parts * (parts + 1)
        states = [state_ref[part, head].astype(jnp.float32) for part in range(parts - 1)]
        carried = carried_ref[head]
        for part in range(parts):
            base = place + part * (parts + 1)
            prefix = weight_ref[base + parts] * carried
            for earlier in range(part):
                prefix += weight_ref[base + earlier] * states[earlier]
            prefix_ref[part, head] = prefix.astype(jnp.bfloat16)


def output_kernel(
    heads, dim, queries_ref, prefix_ref, inside_ref, gate_ref, decay_ref, gain_ref, *rest
):
    out_ref = rest[-1]
    decay = decay_ref[0, 0]
    length = decay.shape[1]
    down = jnp.exp(exact_dot(triangle(length, lambda t, u: u <= t), decay, NT))
    for head in range(heads):
        columns = slice(head * dim, (head + 1) * dim)
        carried_part = dot(queries_ref[0, :, columns], prefix_ref[0, head], NN)
        mixed = inside_ref[:, columns] + carried_part * down[:, head : head + 1]
        inv_rms = lax.rsqrt(jnp.mean(mixed * mixed, axis=-1, keepdims=True) + 1e-06)
        gate = jax.nn.sigmoid(gate_ref[0, :, columns].astype(jnp.float32))
        normed = mixed * inv_rms * gain_ref[0, 0, head : head + 1, :] * gate
        out_ref[0, :, columns] = normed.astype(jnp.bfloat16)


def on_device(parts, blocks, queries, keys, values, gate, log_decay, norm_gain):
    _, length, width = queries.shape
    owned = log_decay.shape[1]
    dim = width // (owned * parts)
    groups = GROUPS
    heads = owned // groups
    span = heads * dim
    rows = span // blocks
    turns = max(1, rows // dim)
    pad = -(-turns // 8) * 8

    decay = log_decay[0].reshape(owned, parts, length)
    gain = jnp.broadcast_to(norm_gain.astype(jnp.float32).reshape(1, owned, dim), (parts, owned, dim))
    small = lax.all_to_all(
        jnp.stack([decay.transpose(1, 0, 2), gain], axis=1), "head", 0, 0, tiled=True
    )

    part_total = decay.sum(axis=-1)
    zero = jnp.zeros((owned,), jnp.float32)
    total_weight = jnp.stack(
        [jnp.exp(part_total[:, part + 1 :].sum(axis=-1)) for part in range(parts)], axis=-1
    ).reshape(-1)
    block_decay = jnp.exp(part_total.sum(axis=-1))
    prefix_weight = jnp.stack(
        [
            jnp.exp(part_total[:, earlier + 1 : part].sum(axis=-1)) if earlier < part else zero
            for part in range(parts)
            for earlier in range(parts)
        ]
        + [jnp.exp(part_total[:, :part].sum(axis=-1)) for part in range(parts)],
        axis=-1,
    )
    prefix_weight = jnp.concatenate(
        [
            prefix_weight[:, : parts * parts].reshape(owned, parts, parts),
            prefix_weight[:, parts * parts :].reshape(owned, parts, 1),
        ],
        axis=-1,
    ).reshape(-1)

    smem = pl.BlockSpec(memory_space=pltpu.SMEM)
    vmem = pl.BlockSpec(memory_space=pltpu.VMEM)

    def features(group):
        return pl.BlockSpec((1, length, span), lambda o: (0, 0, o * groups + group))

    def heads_of(group, which):
        return pl.BlockSpec((1, 1, heads, length), lambda o: (o, which, group, 0))

    states_spec = pl.BlockSpec((1, heads, dim, dim), lambda o: (o, 0, 0, 0))
    states_type = jax.ShapeDtypeStruct((parts, heads, dim, dim), jnp.bfloat16)

    sent = [
        pl.pallas_call(
            functools.partial(state_kernel, heads, dim),
            grid=(parts,),
            in_specs=[features(group), features(group), heads_of(group, 0)],
            out_specs=states_spec,
            out_shape=states_type,
            compiler_params=params(),
            name=f"state{group}",
        )(keys, values, small)
        for group in range(groups)
    ]
    held = [lax.all_to_all(state, "head", 0, 0, tiled=True) for state in sent]

    wide = owned * dim // 2
    inside = pl.pallas_call(
        functools.partial(inside_kernel, owned // 2, dim),
        grid=(parts * 2,),
        in_specs=[pl.BlockSpec((1, length, wide), lambda o: (0, 0, o))] * 3
        + [pl.BlockSpec((1, 1, owned // 2, length), lambda o: (o // 2, 0, o % 2, 0))],
        out_specs=pl.BlockSpec((length, wide), lambda o: (0, o)),
        out_shape=jax.ShapeDtypeStruct((length, width), jnp.float32),
        compiler_params=params(),
        name="inside",
    )(queries, keys, values, small)

    prefixes = []
    for group in range(groups):
        total = pl.pallas_call(
            functools.partial(total_kernel, group * heads, heads, blocks, rows),
            in_specs=[smem, smem, vmem],
            out_specs=vmem,
            out_shape=jax.ShapeDtypeStruct((blocks, rows + pad, dim), jnp.float32),
            compiler_params=params(),
            name=f"total{group}",
        )(total_weight, block_decay, held[group])
        totals = lax.all_to_all(total, "ctx", 0, 0, tiled=True)
        carried = pl.pallas_call(
            functools.partial(scan_kernel, rows, dim),
            in_specs=[vmem],
            out_specs=vmem,
            out_shape=jax.ShapeDtypeStruct((blocks, rows, dim), jnp.float32),
            compiler_params=params(),
            name=f"scan{group}",
        )(totals)
        carried = lax.all_to_all(carried, "ctx", 0, 0, tiled=True).reshape(heads, dim, dim)
        prefix = pl.pallas_call(
            functools.partial(prefix_kernel, group * heads, heads),
            in_specs=[smem, vmem, vmem],
            out_specs=vmem,
            out_shape=states_type,
            compiler_params=params(),
            name=f"prefix{group}",
        )(prefix_weight, held[group], carried)
        prefixes.append(lax.all_to_all(prefix, "head", 0, 0, tiled=True))

    out = ()
    for group in range(groups):
        out = (
            pl.pallas_call(
                functools.partial(output_kernel, heads, dim),
                grid=(parts,),
                in_specs=[
                    features(group),
                    states_spec,
                    pl.BlockSpec((length, span), lambda o, group=group: (0, o * groups + group)),
                    features(group),
                    heads_of(group, 0),
                    heads_of(group, 1),
                ]
                + [pl.BlockSpec(memory_space=pl.ANY)] * len(out),
                out_specs=features(group),
                out_shape=jax.ShapeDtypeStruct((1, length, width), jnp.bfloat16),
                input_output_aliases={6: 0} if out else {},
                compiler_params=params(),
                name=f"output{group}",
            )(queries, prefixes[group], inside, gate, small, small, *out),
        )
    return out[0]


def solution(mesh):
    return jax.shard_map(
        functools.partial(on_device, mesh.shape["head"], mesh.shape["ctx"]),
        mesh=mesh,
        in_specs=(
            P("ctx", "head", None),
            P("ctx", "head", None),
            P("ctx", "head", None),
            P("ctx", "head", None),
            P("ctx", "head", None),
            P("head"),
        ),
        out_specs=P("ctx", "head", None),
        check_vma=False,
    )
```

```python
import functools

import jax
import jax.numpy as jnp
from jax import lax
from jax.experimental import pallas as pl
from jax.experimental.pallas import tpu as pltpu
from jax.sharding import Mesh
from jax.sharding import PartitionSpec as P

GROUPS = 2
EXTRA = 16
VMEM_LIMIT = 48 * 1024 * 1024
NN = (((1,), (0,)), ((), ()))
NT = (((1,), (1,)), ((), ()))
TN = (((0,), (0,)), ((), ()))


def dot(a, b, dims, precision=None):
    return lax.dot_general(a, b, dims, precision=precision, preferred_element_type=jnp.float32)


def exact_dot(a, b, dims):
    return dot(a, b, dims, lax.Precision.HIGHEST)


def triangle(length, keep):
    rows = lax.broadcasted_iota(jnp.int32, (length, length), 0)
    columns = lax.broadcasted_iota(jnp.int32, (length, length), 1)
    return jnp.where(keep(rows, columns), 1.0, 0.0).astype(jnp.float32)


def params():
    return pltpu.CompilerParams(vmem_limit_bytes=VMEM_LIMIT)


def split(value):
    first = value.astype(jnp.bfloat16)
    left = value - first.astype(jnp.float32)
    second = left.astype(jnp.bfloat16)
    return first, second, (left - second.astype(jnp.float32)).astype(jnp.bfloat16)


def join(rows, head):
    wide = rows.astype(jnp.float32)
    return wide[3 * head : 3 * head + 1] + (
        wide[3 * head + 1 : 3 * head + 2] + wide[3 * head + 2 : 3 * head + 3]
    )


def decay_rows(totals):
    parts = [part for total in totals for part in split(total)]
    blank = jnp.zeros((EXTRA - len(parts), totals[0].shape[1]), jnp.bfloat16)
    return jnp.concatenate(parts + [blank], axis=0)


def state_kernel(heads, dim, keys_ref, values_ref, small_ref, state_ref):
    decay = small_ref[0, 0]
    owners, owned = state_ref.shape[0], heads // state_ref.shape[0]
    length = decay.shape[1]
    later = exact_dot(triangle(length, lambda s, u: u > s), decay, NT)
    weight = jnp.exp(later)
    whole = jnp.broadcast_to(jnp.sum(decay, axis=1, keepdims=True), (heads, dim))
    for owner in range(owners):
        for place in range(owned):
            head = owner * owned + place
            columns = slice(head * dim, (head + 1) * dim)
            decayed = keys_ref[0, :, columns].astype(jnp.float32) * weight[:, head : head + 1]
            high = decayed.astype(jnp.bfloat16)
            low = (decayed - high.astype(jnp.float32)).astype(jnp.bfloat16)
            both = dot(values_ref[0, :, columns], jnp.concatenate([high, low], axis=1), TN)
            state = both[:, :dim] + both[:, dim:]
            state_ref[owner, place * dim : (place + 1) * dim, :] = state.astype(jnp.bfloat16)
        state_ref[owner, owned * dim :, :] = decay_rows(
            [whole[owner * owned + place : owner * owned + place + 1] for place in range(owned)]
        )


def inside_kernel(heads, dim, queries_ref, keys_ref, values_ref, small_ref, inside_ref):
    decay = small_ref[0, 0]
    length = decay.shape[1]
    down = exact_dot(triangle(length, lambda t, u: u <= t), decay, NT)
    across = exact_dot(decay, triangle(length, lambda u, s: u <= s), NN)
    rows = lax.broadcasted_iota(jnp.int32, (length, length), 0)
    causal = rows >= lax.broadcasted_iota(jnp.int32, (length, length), 1)
    for head in range(heads):
        columns = slice(head * dim, (head + 1) * dim)
        scores = dot(queries_ref[0, :, columns], keys_ref[0, :, columns], NT)
        gap = down[:, head : head + 1] - across[head : head + 1, :]
        weights = scores * jnp.exp(jnp.where(causal, gap, -jnp.inf))
        inside_ref[:, columns] = dot(weights.astype(jnp.bfloat16), values_ref[0, :, columns], NN)


def total_kernel(heads, dim, state_ref, total_ref):
    parts = state_ref.shape[0]
    extra = [state_ref[part, heads * dim :, :] for part in range(parts)]
    sums = []
    for head in range(heads):
        span = slice(head * dim, (head + 1) * dim)
        after = jnp.zeros((1, dim), jnp.float32)
        total = state_ref[parts - 1, span, :].astype(jnp.float32)
        for part in range(parts - 2, -1, -1):
            after += join(extra[part + 1], head)
            total += jnp.exp(after) * state_ref[part, span, :].astype(jnp.float32)
        total_ref[span, :] = total.astype(jnp.bfloat16)
        sums.append(after + join(extra[0], head))
    total_ref[heads * dim :, :] = decay_rows(sums)


def prefix_kernel(heads, dim, state_ref, *rest):
    total_refs, prefix_ref = rest[:-1], rest[-1]
    parts = state_ref.shape[0]
    extra = [state_ref[part, heads * dim :, :] for part in range(parts)]
    more = [total_ref[heads * dim :, :] for total_ref in total_refs]
    for head in range(heads):
        span = slice(head * dim, (head + 1) * dim)
        prefix = jnp.zeros((dim, dim), jnp.float32)
        after = jnp.zeros((1, dim), jnp.float32)
        for turn, total_ref in enumerate(total_refs):
            prefix += jnp.exp(after) * total_ref[span, :].astype(jnp.float32)
            after += join(more[turn], head)
        for part in range(parts):
            prefix_ref[part, span, :] = prefix.astype(jnp.bfloat16)
            if part < parts - 1:
                prefix = jnp.exp(join(extra[part], head)) * prefix
                prefix += state_ref[part, span, :].astype(jnp.float32)


def output_kernel(
    heads, dim, queries_ref, prefix_ref, inside_ref, gate_ref, decay_ref, gain_ref, *rest
):
    out_ref = rest[-1]
    decay = decay_ref[0, 0]
    owned = heads // prefix_ref.shape[0]
    length = decay.shape[1]
    down = jnp.exp(exact_dot(triangle(length, lambda t, u: u <= t), decay, NT))
    for head in range(heads):
        columns = slice(head * dim, (head + 1) * dim)
        start = head % owned * dim
        prefix = prefix_ref[head // owned, start : start + dim, :]
        carried_part = dot(queries_ref[0, :, columns], prefix, NT)
        mixed = inside_ref[:, columns] + carried_part * down[:, head : head + 1]
        inv_rms = lax.rsqrt(jnp.mean(mixed * mixed, axis=-1, keepdims=True) + 1e-06)
        gate = jax.nn.sigmoid(gate_ref[0, :, columns].astype(jnp.float32))
        normed = mixed * inv_rms * gain_ref[0, 0, head : head + 1, :] * gate
        out_ref[0, :, columns] = normed.astype(jnp.bfloat16)


def on_device(parts, planes, queries, keys, values, gate, log_decay, norm_gain):
    _, length, width = queries.shape
    local = log_decay.shape[1]
    dim = width // (local * parts)
    owners = 2 * parts
    owned = local * parts // (owners * GROUPS)
    rows = owned * dim + EXTRA
    plane = ("core", "head")

    decay = log_decay[0].reshape(local, parts, length).transpose(1, 0, 2)
    gain = norm_gain.astype(jnp.float32).reshape(1, local, dim)
    small = lax.all_to_all(
        jnp.stack([decay, jnp.broadcast_to(gain, (parts, local, dim))], axis=1),
        "head",
        0,
        0,
        tiled=True,
    )

    step = 8
    steps = local * parts // step
    per_group = steps // GROUPS
    per_local = local // step
    vmem = pl.BlockSpec(memory_space=pltpu.VMEM)

    def features(group):
        return pl.BlockSpec((1, length, step * dim), lambda b: (0, 0, group * per_group + b))

    def heads_of(group, which):
        def place(b):
            at = group * per_group + b
            return at // per_local, which, at % per_local, 0

        return pl.BlockSpec((1, 1, step, length), place)

    held = []
    for group in range(GROUPS):
        state = pl.pallas_call(
            functools.partial(state_kernel, step, dim),
            grid=(per_group,),
            in_specs=[features(group), features(group), heads_of(group, 0)],
            out_specs=pl.BlockSpec((step // owned, rows, dim), lambda b: (b, 0, 0)),
            out_shape=jax.ShapeDtypeStruct((owners, rows, dim), jnp.bfloat16),
            compiler_params=params(),
            name=f"state{group}",
        )(keys, values, small)
        held.append(lax.all_to_all(state, plane, 0, 0, tiled=True))

    prefixes = []
    for group in range(GROUPS):
        total = pl.pallas_call(
            functools.partial(total_kernel, owned, dim),
            in_specs=[vmem],
            out_specs=vmem,
            out_shape=jax.ShapeDtypeStruct((rows, dim), jnp.bfloat16),
            compiler_params=params(),
            name=f"total{group}",
        )(held[group])
        totals = [
            lax.ppermute(total, "z", [(at, at + far) for at in range(planes - far)])
            for far in range(1, planes)
        ]
        prefix = pl.pallas_call(
            functools.partial(prefix_kernel, owned, dim),
            in_specs=[vmem] * planes,
            out_specs=vmem,
            out_shape=jax.ShapeDtypeStruct((owners, owned * dim, dim), jnp.bfloat16),
            compiler_params=params(),
            name=f"prefix{group}",
        )(held[group], *totals)
        prefixes.append(lax.all_to_all(prefix, plane, 0, 0, tiled=True))

    inside = pl.pallas_call(
        functools.partial(inside_kernel, step, dim),
        grid=(steps,),
        in_specs=[features(0)] * 3 + [heads_of(0, 0)],
        out_specs=pl.BlockSpec((length, step * dim), lambda b: (0, b)),
        out_shape=jax.ShapeDtypeStruct((length, width), jnp.float32),
        compiler_params=params(),
        name="inside",
    )(queries, keys, values, small)

    out = ()
    for group in range(GROUPS):
        out = (
            pl.pallas_call(
                functools.partial(output_kernel, step, dim),
                grid=(per_group,),
                in_specs=[
                    features(group),
                    pl.BlockSpec((step // owned, owned * dim, dim), lambda b: (b, 0, 0)),
                    pl.BlockSpec(
                        (length, step * dim), lambda b, group=group: (0, group * per_group + b)
                    ),
                    features(group),
                    heads_of(group, 0),
                    heads_of(group, 1),
                ]
                + [pl.BlockSpec(memory_space=pl.ANY)] * len(out),
                out_specs=features(group),
                out_shape=jax.ShapeDtypeStruct((1, length, width), jnp.bfloat16),
                input_output_aliases={6: 0} if out else {},
                compiler_params=params(),
                name=f"output{group}",
            )(queries, prefixes[group], inside, gate, small, small, *out),
        )
    return out[0]


def solution(mesh):
    parts, blocks = mesh.shape["head"], mesh.shape["ctx"]
    names = mesh.axis_names
    at = names.index("ctx")
    shape = mesh.devices.shape[:at] + (blocks // 2, 2) + mesh.devices.shape[at + 1 :]
    finer = Mesh(mesh.devices.reshape(shape), names[:at] + ("z", "core") + names[at + 1 :])
    tokens = P(("z", "core"), "head", None)
    return jax.shard_map(
        functools.partial(on_device, parts, blocks // 2),
        mesh=finer,
        in_specs=(tokens,) * 5 + (P("head"),),
        out_specs=tokens,
        check_vma=False,
    )
```

```python
import functools

import jax
import jax.numpy as jnp
from jax import lax
from jax.experimental import pallas as pl
from jax.experimental.pallas import tpu as pltpu
from jax.sharding import Mesh
from jax.sharding import PartitionSpec as P

GROUPS = 2
EXTRA = 16
VMEM_LIMIT = 48 * 1024 * 1024
NN = (((1,), (0,)), ((), ()))
NT = (((1,), (1,)), ((), ()))
TN = (((0,), (0,)), ((), ()))


def dot(a, b, dims, precision=None):
    return lax.dot_general(a, b, dims, precision=precision, preferred_element_type=jnp.float32)


def exact_dot(a, b, dims):
    return dot(a, b, dims, lax.Precision.HIGHEST)


def triangle(length, keep):
    rows = lax.broadcasted_iota(jnp.int32, (length, length), 0)
    columns = lax.broadcasted_iota(jnp.int32, (length, length), 1)
    return jnp.where(keep(rows, columns), 1.0, 0.0).astype(jnp.float32)


def params():
    return pltpu.CompilerParams(vmem_limit_bytes=VMEM_LIMIT)


def cost(microseconds):
    return pl.CostEstimate(flops=int(microseconds * 1e9), transcendentals=0, bytes_accessed=0)


def in_hbm(*arrays):
    return tuple(pltpu.with_memory_space_constraint(array, pltpu.HBM) for array in arrays)


def split(value):
    first = value.astype(jnp.bfloat16)
    left = value - first.astype(jnp.float32)
    second = left.astype(jnp.bfloat16)
    return first, second, (left - second.astype(jnp.float32)).astype(jnp.bfloat16)


def join(rows, head):
    wide = rows.astype(jnp.float32)
    return wide[3 * head : 3 * head + 1] + (
        wide[3 * head + 1 : 3 * head + 2] + wide[3 * head + 2 : 3 * head + 3]
    )


def decay_rows(totals):
    parts = [part for total in totals for part in split(total)]
    blank = jnp.zeros((EXTRA - len(parts), totals[0].shape[1]), jnp.bfloat16)
    return jnp.concatenate(parts + [blank], axis=0)


def spread(me, stacked_ref, slots):
    for slot, slot_ref in enumerate(slots):
        slot_ref[...] = stacked_ref[me ^ slot]


def gather(me, stacked_ref, slots):
    for slot, slot_ref in enumerate(slots):
        stacked_ref[me ^ slot] = slot_ref[...]


def state_kernel(heads, dim, me_ref, keys_ref, values_ref, small_ref, *rest):
    slots, state_ref = rest[:-1], rest[-1]
    decay = small_ref[0, 0]
    owned = (state_ref.shape[1] - EXTRA) // dim
    owners = heads // owned
    first = pl.program_id(0) * owners
    length = decay.shape[1]
    later = exact_dot(triangle(length, lambda s, u: u > s), decay, NT)
    weight = jnp.exp(later)
    whole = jnp.broadcast_to(jnp.sum(decay, axis=1, keepdims=True), (heads, dim))
    for owner in range(owners):
        for place in range(owned):
            head = owner * owned + place
            columns = slice(head * dim, (head + 1) * dim)
            decayed = keys_ref[0, :, columns].astype(jnp.float32) * weight[:, head : head + 1]
            high = decayed.astype(jnp.bfloat16)
            low = (decayed - high.astype(jnp.float32)).astype(jnp.bfloat16)
            both = dot(values_ref[0, :, columns], jnp.concatenate([high, low], axis=1), TN)
            state = both[:, :dim] + both[:, dim:]
            span = slice(place * dim, (place + 1) * dim)
            state_ref[first + owner, span, :] = state.astype(jnp.bfloat16)
        state_ref[first + owner, owned * dim :, :] = decay_rows(
            [whole[owner * owned + place : owner * owned + place + 1] for place in range(owned)]
        )

    @pl.when(pl.program_id(0) == pl.num_programs(0) - 1)
    def _():
        spread(me_ref[0], state_ref, slots)


def inside_kernel(heads, dim, queries_ref, keys_ref, values_ref, small_ref, inside_ref):
    decay = small_ref[0, 0]
    length = decay.shape[1]
    down = exact_dot(triangle(length, lambda t, u: u <= t), decay, NT)
    across = exact_dot(decay, triangle(length, lambda u, s: u <= s), NN)
    rows = lax.broadcasted_iota(jnp.int32, (length, length), 0)
    causal = rows >= lax.broadcasted_iota(jnp.int32, (length, length), 1)
    for head in range(heads):
        columns = slice(head * dim, (head + 1) * dim)
        scores = dot(queries_ref[0, :, columns], keys_ref[0, :, columns], NT)
        gap = down[:, head : head + 1] - across[head : head + 1, :]
        weights = scores * jnp.exp(jnp.where(causal, gap, -jnp.inf))
        inside_ref[:, columns] = dot(weights.astype(jnp.bfloat16), values_ref[0, :, columns], NN)


def total_kernel(heads, dim, me_ref, *rest):
    slots, total_ref, state_ref = rest[:-2], rest[-2], rest[-1]
    parts = state_ref.shape[0]
    gather(me_ref[0], state_ref, slots)
    extra = [state_ref[part, heads * dim :, :] for part in range(parts)]
    sums = []
    for head in range(heads):
        span = slice(head * dim, (head + 1) * dim)
        after = jnp.zeros((1, dim), jnp.float32)
        total = state_ref[parts - 1, span, :].astype(jnp.float32)
        for part in range(parts - 2, -1, -1):
            after += join(extra[part + 1], head)
            total += jnp.exp(after) * state_ref[part, span, :].astype(jnp.float32)
        total_ref[span, :] = total.astype(jnp.bfloat16)
        sums.append(after + join(extra[0], head))
    total_ref[heads * dim :, :] = decay_rows(sums)


def prefix_kernel(heads, dim, parts, me_ref, *rest):
    state_ref, prefix_ref = rest[-2:]
    slots, total_refs, results = rest[:parts], rest[parts : -2 - parts], rest[-2 - parts : -2]
    gather(me_ref[0], state_ref, slots)
    extra = [state_ref[part, heads * dim :, :] for part in range(parts)]
    more = [total_ref[heads * dim :, :] for total_ref in total_refs]
    for head in range(heads):
        span = slice(head * dim, (head + 1) * dim)
        prefix = jnp.zeros((dim, dim), jnp.float32)
        after = jnp.zeros((1, dim), jnp.float32)
        for turn, total_ref in enumerate(total_refs):
            prefix += jnp.exp(after) * total_ref[span, :].astype(jnp.float32)
            after += join(more[turn], head)
        for part in range(parts):
            prefix_ref[part, span, :] = prefix.astype(jnp.bfloat16)
            if part < parts - 1:
                prefix = jnp.exp(join(extra[part], head)) * prefix
                prefix += state_ref[part, span, :].astype(jnp.float32)
    spread(me_ref[0], prefix_ref, results)


def output_kernel(
    heads, dim, parts, me_ref, queries_ref, inside_ref, gate_ref, decay_ref, gain_ref, *rest
):
    slots, out_ref, prefix_ref = rest[:parts], rest[-2], rest[-1]

    @pl.when(pl.program_id(0) == 0)
    def _():
        gather(me_ref[0], prefix_ref, slots)

    decay = decay_ref[0, 0]
    owned = prefix_ref.shape[1] // dim
    first = pl.program_id(0) * (heads // owned)
    length = decay.shape[1]
    down = jnp.exp(exact_dot(triangle(length, lambda t, u: u <= t), decay, NT))
    for head in range(heads):
        columns = slice(head * dim, (head + 1) * dim)
        start = head % owned * dim
        prefix = prefix_ref[first + head // owned, start : start + dim, :]
        carried_part = dot(queries_ref[0, :, columns], prefix, NT)
        mixed = inside_ref[:, columns] + carried_part * down[:, head : head + 1]
        inv_rms = lax.rsqrt(jnp.mean(mixed * mixed, axis=-1, keepdims=True) + 1e-06)
        gate = jax.nn.sigmoid(gate_ref[0, :, columns].astype(jnp.float32))
        normed = mixed * inv_rms * gain_ref[0, 0, head : head + 1, :] * gate
        out_ref[0, :, columns] = normed.astype(jnp.bfloat16)


def on_device(parts, planes, queries, keys, values, gate, log_decay, norm_gain):
    _, length, width = queries.shape
    local = log_decay.shape[1]
    dim = width // (local * parts)
    owners = 2 * parts
    owned = local * parts // (owners * GROUPS)
    rows = owned * dim + EXTRA
    plane = ("core", "head")

    decay = log_decay[0].reshape(local, parts, length).transpose(1, 0, 2)
    gain = norm_gain.astype(jnp.float32).reshape(1, local, dim)
    small = lax.all_to_all(
        jnp.stack([decay, jnp.broadcast_to(gain, (parts, local, dim))], axis=1),
        "head",
        0,
        0,
        tiled=True,
    )

    step = 8
    steps = local * parts // step
    per_group = steps // GROUPS
    per_local = local // step
    vmem = pl.BlockSpec(memory_space=pltpu.VMEM)

    def features(group):
        return pl.BlockSpec((1, length, step * dim), lambda b: (0, 0, group * per_group + b))

    def heads_of(group, which):
        def place(b):
            at = group * per_group + b
            return at // per_local, which, at % per_local, 0

        return pl.BlockSpec((1, 1, step, length), place)

    smem = pl.BlockSpec(memory_space=pltpu.SMEM)
    me = lax.axis_index(plane).astype(jnp.int32).reshape(1)
    order = sorted(range(1, owners), key=lambda slot: -bin(slot % parts).count("1"))

    def by_mesh(at):
        return at % parts * 2 + at // parts

    def exchange(slots):
        arrived = list(slots)
        for slot in order:
            pairs = [(by_mesh(at), by_mesh(at ^ slot)) for at in range(owners)]
            arrived[slot] = lax.ppermute(slots[slot], ("head", "core"), pairs)
        return arrived

    def full(shape):
        return pl.BlockSpec(shape, lambda b: (0,) * len(shape))

    queries, keys, values, gate = in_hbm(queries, keys, values, gate)
    held = []
    for group in range(GROUPS):
        state = pl.pallas_call(
            functools.partial(state_kernel, step, dim),
            grid=(per_group,),
            in_specs=[smem, features(group), features(group), heads_of(group, 0)],
            out_specs=[full((rows, dim))] * owners,
            out_shape=[jax.ShapeDtypeStruct((rows, dim), jnp.bfloat16)] * owners,
            scratch_shapes=[pltpu.VMEM((owners, rows, dim), jnp.bfloat16)],
            compiler_params=params(),
            cost_estimate=cost(6 // GROUPS),
            name=f"state{group}",
        )(me, keys, values, small)
        held.append(exchange(state))

    inside = pl.pallas_call(
        functools.partial(inside_kernel, step, dim),
        grid=(steps,),
        in_specs=[features(0)] * 3 + [heads_of(0, 0)],
        out_specs=pl.BlockSpec((length, step * dim), lambda b: (0, b)),
        out_shape=jax.ShapeDtypeStruct((length, width), jnp.float32),
        compiler_params=params(),
        cost_estimate=cost(14),
        name="inside",
    )(queries, keys, values, small)

    prefixes = []
    for group in range(GROUPS):
        total = pl.pallas_call(
            functools.partial(total_kernel, owned, dim),
            in_specs=[smem] + [vmem] * owners,
            out_specs=vmem,
            out_shape=jax.ShapeDtypeStruct((rows, dim), jnp.bfloat16),
            scratch_shapes=[pltpu.VMEM((owners, rows, dim), jnp.bfloat16)],
            compiler_params=params(),
            cost_estimate=cost(1),
            name=f"total{group}",
        )(me, *held[group])
        totals = [
            lax.ppermute(total, "z", [(at, at + far) for at in range(planes - far)])
            for far in range(1, planes)
        ]
        prefix = pl.pallas_call(
            functools.partial(prefix_kernel, owned, dim, owners),
            in_specs=[smem] + [vmem] * (owners + planes - 1),
            out_specs=[vmem] * owners,
            out_shape=[jax.ShapeDtypeStruct((owned * dim, dim), jnp.bfloat16)] * owners,
            scratch_shapes=[
                pltpu.VMEM((owners, rows, dim), jnp.bfloat16),
                pltpu.VMEM((owners, owned * dim, dim), jnp.bfloat16),
            ],
            compiler_params=params(),
            cost_estimate=cost(1),
            name=f"prefix{group}",
        )(me, *held[group], *totals)
        prefixes.append(exchange(prefix))

    out = ()
    for group in range(GROUPS):
        out = (
            pl.pallas_call(
                functools.partial(output_kernel, step, dim, owners),
                grid=(per_group,),
                in_specs=[
                    smem,
                    features(group),
                    pl.BlockSpec(
                        (length, step * dim), lambda b, group=group: (0, group * per_group + b)
                    ),
                    features(group),
                    heads_of(group, 0),
                    heads_of(group, 1),
                ]
                + [full((owned * dim, dim))] * owners
                + [pl.BlockSpec(memory_space=pl.ANY)] * len(out),
                out_specs=features(group),
                out_shape=jax.ShapeDtypeStruct((1, length, width), jnp.bfloat16),
                scratch_shapes=[pltpu.VMEM((owners, owned * dim, dim), jnp.bfloat16)],
                input_output_aliases={6 + owners: 0} if out else {},
                compiler_params=params(),
                cost_estimate=cost(10 // GROUPS),
                name=f"output{group}",
            )(me, queries, inside, gate, small, small, *prefixes[group], *out),
        )
    return out[0]


def solution(mesh):
    parts, blocks = mesh.shape["head"], mesh.shape["ctx"]
    names = mesh.axis_names
    at = names.index("ctx")
    shape = mesh.devices.shape[:at] + (blocks // 2, 2) + mesh.devices.shape[at + 1 :]
    finer = Mesh(mesh.devices.reshape(shape), names[:at] + ("z", "core") + names[at + 1 :])
    tokens = P(("z", "core"), "head", None)
    return jax.shard_map(
        functools.partial(on_device, parts, blocks // 2),
        mesh=finer,
        in_specs=(tokens,) * 5 + (P("head"),),
        out_specs=tokens,
        check_vma=False,
    )
```

```python
import functools

import jax
import jax.numpy as jnp
from jax import lax
from jax.experimental import pallas as pl
from jax.experimental.pallas import tpu as pltpu
from jax.sharding import Mesh
from jax.sharding import PartitionSpec as P

GROUPS = 2
EXTRA = 16
VMEM_LIMIT = 24 * 1024 * 1024
NN = (((1,), (0,)), ((), ()))
NT = (((1,), (1,)), ((), ()))
TN = (((0,), (0,)), ((), ()))


def dot(a, b, dims, precision=None):
    return lax.dot_general(a, b, dims, precision=precision, preferred_element_type=jnp.float32)


def exact_dot(a, b, dims):
    return dot(a, b, dims, lax.Precision.HIGHEST)


def triangle(length, keep):
    rows = lax.broadcasted_iota(jnp.int32, (length, length), 0)
    columns = lax.broadcasted_iota(jnp.int32, (length, length), 1)
    return jnp.where(keep(rows, columns), 1.0, 0.0).astype(jnp.float32)


def params():
    return pltpu.CompilerParams(vmem_limit_bytes=VMEM_LIMIT)


def cost(microseconds):
    return pl.CostEstimate(flops=int(microseconds * 1e9), transcendentals=0, bytes_accessed=0)


def in_hbm(*arrays):
    return tuple(pltpu.with_memory_space_constraint(array, pltpu.HBM) for array in arrays)


def split(value):
    first = value.astype(jnp.bfloat16)
    left = value - first.astype(jnp.float32)
    second = left.astype(jnp.bfloat16)
    return first, second, (left - second.astype(jnp.float32)).astype(jnp.bfloat16)


def join(rows, head):
    wide = rows.astype(jnp.float32)
    return wide[3 * head : 3 * head + 1] + (
        wide[3 * head + 1 : 3 * head + 2] + wide[3 * head + 2 : 3 * head + 3]
    )


def decay_rows(totals):
    parts = [part for total in totals for part in split(total)]
    blank = jnp.zeros((EXTRA - len(parts), totals[0].shape[1]), jnp.bfloat16)
    return jnp.concatenate(parts + [blank], axis=0)


def spread(me, stacked_ref, slots):
    for slot, slot_ref in enumerate(slots):
        slot_ref[...] = stacked_ref[me ^ slot]


def gather(me, stacked_ref, slots):
    for slot, slot_ref in enumerate(slots):
        stacked_ref[me ^ slot] = slot_ref[...]


def state_kernel(heads, dim, parts, me_ref, keys_ref, values_ref, small_ref, *rest):
    slots, state_ref = rest[-1 - parts : -1], rest[-1]
    decay = small_ref[0]
    owned = (state_ref.shape[1] - EXTRA) // dim
    owners = heads // owned
    first = pl.program_id(0) * owners
    length = decay.shape[1]
    later = exact_dot(triangle(length, lambda s, u: u > s), decay, NT)
    weight = jnp.exp(later)
    whole = jnp.broadcast_to(jnp.sum(decay, axis=1, keepdims=True), (heads, dim))
    for owner in range(owners):
        for place in range(owned):
            head = owner * owned + place
            columns = slice(head * dim, (head + 1) * dim)
            decayed = keys_ref[0, :, columns].astype(jnp.float32) * weight[:, head : head + 1]
            high = decayed.astype(jnp.bfloat16)
            low = (decayed - high.astype(jnp.float32)).astype(jnp.bfloat16)
            both = dot(values_ref[0, :, columns], jnp.concatenate([high, low], axis=1), TN)
            state = both[:, :dim] + both[:, dim:]
            span = slice(place * dim, (place + 1) * dim)
            state_ref[first + owner, span, :] = state.astype(jnp.bfloat16)
        state_ref[first + owner, owned * dim :, :] = decay_rows(
            [whole[owner * owned + place : owner * owned + place + 1] for place in range(owned)]
        )

    @pl.when(pl.program_id(0) == pl.num_programs(0) - 1)
    def _():
        spread(me_ref[0], state_ref, slots)


def inside_kernel(heads, dim, queries_ref, keys_ref, values_ref, small_ref, *rest):
    inside_ref, done_ref = rest[-2:]
    decay = small_ref[0]
    length = decay.shape[1]
    down = exact_dot(triangle(length, lambda t, u: u <= t), decay, NT)
    across = exact_dot(decay, triangle(length, lambda u, s: u <= s), NN)
    rows = lax.broadcasted_iota(jnp.int32, (length, length), 0)
    causal = rows >= lax.broadcasted_iota(jnp.int32, (length, length), 1)
    columns = [slice(head * dim, (head + 1) * dim) for head in range(heads)]
    scores = [dot(queries_ref[0, :, c], keys_ref[0, :, c], NT) for c in columns]
    weights = []
    for head in range(heads):
        gap = down[:, head : head + 1] - across[head : head + 1, :]
        weight = scores[head] * jnp.exp(jnp.where(causal, gap, -jnp.inf))
        weights.append(weight.astype(jnp.bfloat16))
    for head, c in enumerate(columns):
        inside_ref[:, c] = dot(weights[head], values_ref[0, :, c], NN)
    done_ref[...] = jnp.zeros_like(done_ref)


def total_kernel(heads, dim, me_ref, *rest):
    total_ref, state_ref = rest[-2:]
    parts = state_ref.shape[0]
    slots = rest[:parts]
    gather(me_ref[0], state_ref, slots)
    extra = [state_ref[part, heads * dim :, :] for part in range(parts)]
    sums = []
    for head in range(heads):
        span = slice(head * dim, (head + 1) * dim)
        after = jnp.zeros((1, dim), jnp.float32)
        total = state_ref[parts - 1, span, :].astype(jnp.float32)
        for part in range(parts - 2, -1, -1):
            after += join(extra[part + 1], head)
            total += jnp.exp(after) * state_ref[part, span, :].astype(jnp.float32)
        total_ref[span, :] = total.astype(jnp.bfloat16)
        sums.append(after + join(extra[0], head))
    total_ref[heads * dim :, :] = decay_rows(sums)


def prefix_kernel(heads, dim, parts, me_ref, totals_ref, *rest):
    state_ref, prefix_ref = rest[-2:]
    slots, results = rest[:parts], rest[-2 - parts : -2]
    gather(me_ref[0], state_ref, slots)
    planes = totals_ref.shape[0]
    extra = [state_ref[part, heads * dim :, :] for part in range(parts)]
    more = [totals_ref[plane, heads * dim :, :] for plane in range(planes)]
    earlier = [jnp.where(plane < me_ref[1], 1.0, 0.0) for plane in range(planes)]
    for head in range(heads):
        span = slice(head * dim, (head + 1) * dim)
        prefix = jnp.zeros((dim, dim), jnp.float32)
        after = jnp.zeros((1, dim), jnp.float32)
        for plane in range(planes - 2, -1, -1):
            factor = earlier[plane] * jnp.exp(after)
            prefix += factor * totals_ref[plane, span, :].astype(jnp.float32)
            after += earlier[plane] * join(more[plane], head)
        for part in range(parts):
            prefix_ref[part, span, :] = prefix.astype(jnp.bfloat16)
            if part < parts - 1:
                prefix = jnp.exp(join(extra[part], head)) * prefix
                prefix += state_ref[part, span, :].astype(jnp.float32)
    spread(me_ref[0], prefix_ref, results)


def output_kernel(
    heads, dim, parts, me_ref, queries_ref, inside_ref, gate_ref, decay_ref, gain_ref, *rest
):
    slots, out_ref, prefix_ref = rest[:parts], rest[-2], rest[-1]

    @pl.when(pl.program_id(0) == 0)
    def _():
        gather(me_ref[0], prefix_ref, slots)

    decay = decay_ref[0]
    owned = prefix_ref.shape[1] // dim
    first = pl.program_id(0) * (heads // owned)
    length = decay.shape[1]
    down = jnp.exp(exact_dot(triangle(length, lambda t, u: u <= t), decay, NT))
    for head in range(heads):
        columns = slice(head * dim, (head + 1) * dim)
        start = head % owned * dim
        prefix = prefix_ref[first + head // owned, start : start + dim, :]
        carried_part = dot(queries_ref[0, :, columns], prefix, NT)
        mixed = inside_ref[:, columns] + carried_part * down[:, head : head + 1]
        inv_rms = lax.rsqrt(jnp.mean(mixed * mixed, axis=-1, keepdims=True) + 1e-06)
        gate = jax.nn.sigmoid(gate_ref[0, :, columns].astype(jnp.float32))
        normed = mixed * inv_rms * gain_ref[head : head + 1, :].astype(jnp.float32) * gate
        out_ref[0, :, columns] = normed.astype(jnp.bfloat16)


def on_device(parts, planes, queries, keys, values, gate, log_decay, norm_gain):
    _, length, width = queries.shape
    local = log_decay.shape[1]
    dim = width // (local * parts)
    owners = 2 * parts
    owned = local * parts // (owners * GROUPS)
    rows = owned * dim + EXTRA
    plane = ("core", "head")

    decay = log_decay[0].reshape(local, parts, length).transpose(1, 0, 2)
    small = lax.all_to_all(decay, "head", 0, 0, tiled=True)
    gain = lax.all_gather(norm_gain.reshape(local, dim), "head", tiled=True)

    step = 8
    steps = local * parts // step
    per_group = steps // GROUPS
    per_local = local // step
    vmem = pl.BlockSpec(memory_space=pltpu.VMEM)

    def features(group):
        return pl.BlockSpec((1, length, step * dim), lambda b: (0, 0, group * per_group + b))

    def heads_of(group):
        def place(b):
            at = group * per_group + b
            return at // per_local, at % per_local, 0

        return pl.BlockSpec((1, step, length), place)

    smem = pl.BlockSpec(memory_space=pltpu.SMEM)
    me = jnp.stack([lax.axis_index(plane), lax.axis_index("z")]).astype(jnp.int32)
    order = sorted(range(1, owners), key=lambda slot: -bin(slot % parts).count("1"))

    def by_mesh(at):
        return at % parts * 2 + at // parts

    def exchange(slots):
        arrived = list(slots)
        for slot in order:
            pairs = [(by_mesh(at), by_mesh(at ^ slot)) for at in range(owners)]
            arrived[slot] = lax.ppermute(slots[slot], ("head", "core"), pairs)
        return arrived

    def full(shape):
        return pl.BlockSpec(shape, lambda b: (0,) * len(shape))

    queries, keys, values, gate = in_hbm(queries, keys, values, gate)
    hbm = pl.BlockSpec(memory_space=pl.ANY)
    before = ()

    held = []
    for group in range(GROUPS):
        state = pl.pallas_call(
            functools.partial(state_kernel, step, dim, owners),
            grid=(per_group,),
            in_specs=[smem, features(group), features(group), heads_of(group)]
            + [hbm] * len(before),
            out_specs=[full((rows, dim))] * owners,
            out_shape=[jax.ShapeDtypeStruct((rows, dim), jnp.bfloat16)] * owners,
            scratch_shapes=[pltpu.VMEM((owners, rows, dim), jnp.bfloat16)],
            compiler_params=params(),
            cost_estimate=cost(6 // GROUPS),
            name=f"state{group}",
        )(me, keys, values, small, *before)
        before = state[:1]
        held.append(exchange(state))

    pieces = 2 * GROUPS
    per_piece = steps // pieces
    token = jax.ShapeDtypeStruct((8, 128), jnp.float32)

    def inside_part(at, inside, before):
        def place(b):
            return (at * per_piece + b) // per_local, (at * per_piece + b) % per_local, 0

        def block(b):
            return 0, at * per_piece + b

        *inside, made = pl.pallas_call(
            functools.partial(inside_kernel, step, dim),
            grid=(per_piece,),
            in_specs=[pl.BlockSpec((1, length, step * dim), lambda b: (0,) + block(b))] * 3
            + [pl.BlockSpec((1, step, length), place)]
            + [hbm] * (len(inside) + len(before)),
            out_specs=[pl.BlockSpec((length, step * dim), block), full(token.shape)],
            out_shape=[jax.ShapeDtypeStruct((length, width), jnp.float32), token],
            input_output_aliases={4: 0} if inside else {},
            compiler_params=params(),
            cost_estimate=cost(14 // pieces),
            name=f"inside{at}",
        )(queries, keys, values, small, *inside, *before)
        return inside, made

    inside = ()
    gathered = []
    for group in range(GROUPS):
        inside, made = inside_part(group, inside, before)
        total = pl.pallas_call(
            functools.partial(total_kernel, owned, dim),
            in_specs=[smem] + [vmem] * owners + [hbm],
            out_specs=vmem,
            out_shape=jax.ShapeDtypeStruct((rows, dim), jnp.bfloat16),
            scratch_shapes=[pltpu.VMEM((owners, rows, dim), jnp.bfloat16)],
            compiler_params=params(),
            cost_estimate=cost(1),
            name=f"total{group}",
        )(me, *held[group], made)
        before = (total,)
        gathered.append(lax.all_gather(total, "z"))

    prefixes = []
    for group in range(GROUPS):
        inside, made = inside_part(GROUPS + group, inside, before)
        prefix = pl.pallas_call(
            functools.partial(prefix_kernel, owned, dim, owners),
            in_specs=[smem] + [vmem] * (owners + 1) + [hbm],
            out_specs=[vmem] * owners,
            out_shape=[jax.ShapeDtypeStruct((owned * dim, dim), jnp.bfloat16)] * owners,
            scratch_shapes=[
                pltpu.VMEM((owners, rows, dim), jnp.bfloat16),
                pltpu.VMEM((owners, owned * dim, dim), jnp.bfloat16),
            ],
            compiler_params=params(),
            cost_estimate=cost(1),
            name=f"prefix{group}",
        )(me, gathered[group], *held[group], made)
        before = prefix[:1]
        prefixes.append(exchange(prefix))

    out = ()
    for group in range(GROUPS):
        out = (
            pl.pallas_call(
                functools.partial(output_kernel, step, dim, owners),
                grid=(per_group,),
                in_specs=[
                    smem,
                    features(group),
                    pl.BlockSpec(
                        (length, step * dim), lambda b, group=group: (0, group * per_group + b)
                    ),
                    features(group),
                    heads_of(group),
                    pl.BlockSpec((step, dim), lambda b, group=group: (group * per_group + b, 0)),
                ]
                + [full((owned * dim, dim))] * owners
                + [hbm] * len(out or before),
                out_specs=features(group),
                out_shape=jax.ShapeDtypeStruct((1, length, width), jnp.bfloat16),
                scratch_shapes=[pltpu.VMEM((owners, owned * dim, dim), jnp.bfloat16)],
                input_output_aliases={6 + owners: 0} if out else {},
                compiler_params=params(),
                cost_estimate=cost(10 // GROUPS),
                name=f"output{group}",
            )(me, queries, *inside, gate, small, gain, *prefixes[group], *(out or before)),
        )
    return out[0]


def solution(mesh):
    parts, blocks = mesh.shape["head"], mesh.shape["ctx"]
    names = mesh.axis_names
    at = names.index("ctx")
    shape = mesh.devices.shape[:at] + (blocks // 2, 2) + mesh.devices.shape[at + 1 :]
    finer = Mesh(mesh.devices.reshape(shape), names[:at] + ("z", "core") + names[at + 1 :])
    tokens = P(("z", "core"), "head", None)
    return jax.shard_map(
        functools.partial(on_device, parts, blocks // 2),
        mesh=finer,
        in_specs=(tokens,) * 5 + (P("head"),),
        out_specs=tokens,
        check_vma=False,
    )
```

```python
import functools

import jax
import jax.numpy as jnp
from jax import lax
from jax.experimental import pallas as pl
from jax.experimental.pallas import tpu as pltpu
from jax.sharding import Mesh
from jax.sharding import PartitionSpec as P

GROUPS = 2
STEP = 8
EXTRA = 16
VMEM_LIMIT = 24 * 1024 * 1024
NN = (((1,), (0,)), ((), ()))
NT = (((1,), (1,)), ((), ()))
TN = (((0,), (0,)), ((), ()))


def dot(a, b, dims, precision=None):
    return lax.dot_general(a, b, dims, precision=precision, preferred_element_type=jnp.float32)


def exact_dot(a, b, dims):
    return dot(a, b, dims, lax.Precision.HIGHEST)


def triangle(length, keep):
    rows = lax.broadcasted_iota(jnp.int32, (length, length), 0)
    columns = lax.broadcasted_iota(jnp.int32, (length, length), 1)
    return jnp.where(keep(rows, columns), 1.0, 0.0).astype(jnp.float32)


def split(value):
    first = value.astype(jnp.bfloat16)
    left = value - first.astype(jnp.float32)
    second = left.astype(jnp.bfloat16)
    return first, second, (left - second.astype(jnp.float32)).astype(jnp.bfloat16)


def join(rows, head):
    wide = rows.astype(jnp.float32)
    return wide[3 * head : 3 * head + 1] + (
        wide[3 * head + 1 : 3 * head + 2] + wide[3 * head + 2 : 3 * head + 3]
    )


def decay_rows(totals):
    parts = [part for total in totals for part in split(total)]
    blank = jnp.zeros((EXTRA - len(parts), totals[0].shape[1]), jnp.bfloat16)
    return jnp.concatenate(parts + [blank], axis=0)


def pack_kernel(parts, decay_ref, packed_ref):
    length = packed_ref.shape[2]
    for place in range(packed_ref.shape[0]):
        start = place % parts * length
        packed_ref[place] = decay_ref[0, :, start : start + length]


def state_kernel(dim, owned, me_ref, *refs):
    keys, values, decays = refs[0:2], refs[2:4], refs[4:6]
    stacked_ref = refs[-1]
    parts = stacked_ref.shape[0]
    slots = refs[-1 - parts : -1]
    owners = STEP // owned
    first = pl.program_id(0) * owners
    part, core = me_ref[1], me_ref[2]
    for source in range(2):
        block = core if source == 0 else 1 - core
        decay = decays[source][0]
        length = decay.shape[1]
        weight = jnp.exp(exact_dot(triangle(length, lambda s, u: u > s), decay, NT))
        whole = jnp.broadcast_to(jnp.sum(decay, axis=1, keepdims=True), (STEP, dim))
        both = []
        for head in range(STEP):
            columns = slice(head * dim, (head + 1) * dim)
            decayed = keys[source][0, :, columns].astype(jnp.float32) * weight[:, head : head + 1]
            high = decayed.astype(jnp.bfloat16)
            low = (decayed - high.astype(jnp.float32)).astype(jnp.bfloat16)
            both.append(
                dot(values[source][0, :, columns], jnp.concatenate([high, low], axis=1), TN)
            )
        for head in range(STEP):
            owner, place = divmod(head, owned)
            state = both[head][:, :dim] + both[head][:, dim:]
            span = slice(place * dim, (place + 1) * dim)
            stacked_ref[first + owner, block, span, :] = state.astype(jnp.bfloat16)
        for owner in range(owners):
            stacked_ref[first + owner, block, owned * dim :, :] = decay_rows(
                [whole[head : head + 1] for head in range(owner * owned, (owner + 1) * owned)]
            )

    @pl.when(pl.program_id(0) == pl.num_programs(0) - 1)
    def _():
        for slot, slot_ref in enumerate(slots):
            slot_ref[...] = stacked_ref[part ^ slot]


def inside_kernel(dim, me_ref, queries_ref, keys_ref, values_ref, decay_ref, *rest):
    inside_ref, done_ref = rest[-2:]
    decay = decay_ref[0]
    length = decay.shape[1]
    down = exact_dot(triangle(length, lambda t, u: u <= t), decay, NT)
    across = exact_dot(decay, triangle(length, lambda u, s: u <= s), NN)
    rows = lax.broadcasted_iota(jnp.int32, (length, length), 0)
    causal = rows >= lax.broadcasted_iota(jnp.int32, (length, length), 1)
    columns = [slice(head * dim, (head + 1) * dim) for head in range(STEP)]
    scores = [dot(queries_ref[0, :, c], keys_ref[0, :, c], NT) for c in columns]
    weights = []
    for head in range(STEP):
        gap = down[:, head : head + 1] - across[head : head + 1, :]
        weight = scores[head] * jnp.exp(jnp.where(causal, gap, -jnp.inf))
        weights.append(weight.astype(jnp.bfloat16))
    for head, c in enumerate(columns):
        inside_ref[:, c] = dot(weights[head], values_ref[0, :, c], NN)
    done_ref[...] = jnp.zeros_like(done_ref)


def gather_states(part, slots, stacked_ref):
    parts = len(slots)
    for slot, slot_ref in enumerate(slots):
        for block in range(2):
            stacked_ref[block * parts + (part ^ slot)] = slot_ref[block]


def total_kernel(dim, owned, parts, me_ref, *refs):
    total_ref, stacked_ref = refs[-2:]
    gather_states(me_ref[1], refs[:parts], stacked_ref)
    count = 2 * parts
    extra = [stacked_ref[at, owned * dim :, :] for at in range(count)]
    sums = []
    for head in range(owned):
        span = slice(head * dim, (head + 1) * dim)
        after = jnp.zeros((1, dim), jnp.float32)
        total = stacked_ref[count - 1, span, :].astype(jnp.float32)
        for at in range(count - 2, -1, -1):
            after += join(extra[at + 1], head)
            total += jnp.exp(after) * stacked_ref[at, span, :].astype(jnp.float32)
        total_ref[span, :] = total.astype(jnp.bfloat16)
        sums.append(after + join(extra[0], head))
    total_ref[owned * dim :, :] = decay_rows(sums)


def prefix_kernel(dim, owned, parts, planes, me_ref, gain_ref, *refs):
    stacked_ref, prefix_ref = refs[-2:]
    slots, totals = refs[:parts], refs[parts : parts + planes - 1]
    count = 2 * parts
    results = refs[-2 - count : -2]
    gather_states(me_ref[1], slots, stacked_ref)
    extra = [stacked_ref[at, owned * dim :, :] for at in range(count)]
    more = [total_ref[owned * dim :, :] for total_ref in totals]
    for head in range(owned):
        span = slice(head * dim, (head + 1) * dim)
        prefix = jnp.zeros((dim, dim), jnp.float32)
        after = jnp.zeros((1, dim), jnp.float32)
        for turn, total_ref in enumerate(totals):
            prefix += jnp.exp(after) * total_ref[span, :].astype(jnp.float32)
            after += join(more[turn], head)
        for at in range(count):
            prefix_ref[at, span, :] = prefix.astype(jnp.bfloat16)
            if at < count - 1:
                prefix = jnp.exp(join(extra[at], head)) * prefix
                prefix += stacked_ref[at, span, :].astype(jnp.float32)
    for slot, result_ref in enumerate(results):
        result_ref[: owned * dim, :] = prefix_ref[me_ref[0] ^ slot]
        result_ref[owned * dim :, :] = gain_ref[...]


def output_kernel(
    dim, owned, count, local, place, me_ref, queries_ref, inside_ref, gate_ref, decay_ref, *refs
):
    slots, out_ref, stacked_ref = refs[:count], refs[-2], refs[-1]
    turn = pl.program_id(0)

    @pl.when(turn == 0)
    def _():
        for slot, slot_ref in enumerate(slots):
            stacked_ref[me_ref[0] ^ slot] = slot_ref[...]

    decay = decay_ref[0]
    length = decay.shape[1]
    first = turn * (STEP // owned)
    at = place(turn)
    gains = stacked_ref[at // (local // STEP), owned * dim :, :].astype(jnp.float32)
    gain = gains[:STEP]
    for other in range(1, local // STEP):
        here = at % (local // STEP) == other
        gain = jnp.where(here, gains[other * STEP : (other + 1) * STEP], gain)
    down = jnp.exp(exact_dot(triangle(length, lambda t, u: u <= t), decay, NT))
    columns = [slice(head * dim, (head + 1) * dim) for head in range(STEP)]
    carried = []
    for head, c in enumerate(columns):
        start = head % owned * dim
        prefix = stacked_ref[first + head // owned, start : start + dim, :]
        carried.append(dot(queries_ref[0, :, c], prefix, NT))
    for head, c in enumerate(columns):
        mixed = inside_ref[:, c] + carried[head] * down[:, head : head + 1]
        inv_rms = lax.rsqrt(jnp.mean(mixed * mixed, axis=-1, keepdims=True) + 1e-06)
        gate = jax.nn.sigmoid(gate_ref[0, :, c].astype(jnp.float32))
        normed = mixed * inv_rms * gain[head : head + 1, :] * gate
        out_ref[0, :, c] = normed.astype(jnp.bfloat16)


def kernel_call(body, name, grid, in_specs, out_specs, out_shape, scratch=(), aliases={}, cost=1):
    return pl.pallas_call(
        body,
        grid_spec=pltpu.PrefetchScalarGridSpec(
            num_scalar_prefetch=1,
            grid=grid,
            in_specs=in_specs,
            out_specs=out_specs,
            scratch_shapes=scratch,
        ),
        out_shape=out_shape,
        input_output_aliases=aliases,
        compiler_params=pltpu.CompilerParams(vmem_limit_bytes=VMEM_LIMIT),
        cost_estimate=pl.CostEstimate(
            flops=int(cost * 1e9), transcendentals=0, bytes_accessed=0
        ),
        name=name,
    )


def on_device(parts, planes, queries, keys, values, gate, log_decay, norm_gain):
    _, length, width = queries.shape
    local = log_decay.shape[1]
    dim = width // (local * parts)
    count = 2 * parts
    half = local * parts // 2
    owned = half // (GROUPS * parts)
    rows = owned * dim + EXTRA
    per_half, per_group, per_local = half // STEP, half // GROUPS // STEP, local // STEP
    core, part = lax.axis_index("core"), lax.axis_index("head")
    me = jnp.stack([core * parts + part, part, core]).astype(jnp.int32)
    swap = [(0, 1), (1, 0)]

    values_other = lax.ppermute(values, "core", swap)
    keys_other = lax.ppermute(keys, "core", swap)
    packed = pl.pallas_call(
        functools.partial(pack_kernel, parts),
        out_shape=jax.ShapeDtypeStruct((count, local, length), jnp.float32),
        name="pack",
    )(log_decay)
    decay = lax.all_to_all(packed, ("core", "head"), 0, 0, tiled=True)
    gain = norm_gain.reshape(local, dim)

    queries, keys, values, gate = (
        pltpu.with_memory_space_constraint(array, pltpu.HBM)
        for array in (queries, keys, values, gate)
    )

    vmem = pl.BlockSpec(memory_space=pltpu.VMEM)
    hbm = pl.BlockSpec(memory_space=pl.ANY)

    def full(shape):
        return pl.BlockSpec(shape, lambda b, me: (0,) * len(shape))

    def features(place):
        return pl.BlockSpec((1, length, STEP * dim), lambda b, me: (0, 0, place(b, me)))

    def decays(place, other=False):
        def block(b, me):
            at = place(b, me)
            which = 1 - me[2] if other else me[2]
            return which * parts + at // per_local, at % per_local, 0

        return pl.BlockSpec((1, STEP, length), block)

    def exchange(slots, axes, number):
        arrived = list(slots)
        for slot in sorted(range(1, len(slots)), key=lambda s: -bin(s % parts).count("1")):
            pairs = [(number(at), number(at ^ slot)) for at in range(len(slots))]
            arrived[slot] = lax.ppermute(slots[slot], axes, pairs)
        return arrived

    before = ()
    held = []
    for group in range(GROUPS):

        def mine(b, me, group=group):
            return me[2] * per_half + group * per_group + b

        state_type = jax.ShapeDtypeStruct((2, rows, dim), jnp.bfloat16)
        state = kernel_call(
            functools.partial(state_kernel, dim, owned),
            f"state{group}",
            (per_group,),
            [features(mine)] * 4
            + [decays(mine), decays(mine, other=True)]
            + [hbm] * len(before),
            [full(state_type.shape)] * parts,
            [state_type] * parts,
            [pltpu.VMEM((parts,) + state_type.shape, jnp.bfloat16)],
            cost=4,
        )(me, keys, keys_other, values, values_other, decay, decay, *before)
        before = state[:1]
        held.append(exchange(state, "head", lambda at: at))

    pieces = 2 * GROUPS
    per_piece = 2 * per_half // pieces
    token = jax.ShapeDtypeStruct((8, 128), jnp.float32)

    def inside_part(at, inside, before):
        def place(b, me):
            return at * per_piece + b

        *inside, made = kernel_call(
            functools.partial(inside_kernel, dim),
            f"inside{at}",
            (per_piece,),
            [features(place)] * 3 + [decays(place)] + [hbm] * (len(inside) + len(before)),
            [
                pl.BlockSpec((length, STEP * dim), lambda b, me: (0, place(b, me))),
                full(token.shape),
            ],
            [jax.ShapeDtypeStruct((length, width), jnp.float32), token],
            aliases={5: 0} if inside else {},
            cost=3,
        )(me, queries, keys, values, decay, *inside, *before)
        return inside, made

    inside = ()
    arrived = []
    stacked = pltpu.VMEM((count, rows, dim), jnp.bfloat16)
    for group in range(GROUPS):
        inside, made = inside_part(group, inside, before)
        total = kernel_call(
            functools.partial(total_kernel, dim, owned, parts),
            f"total{group}",
            (),
            [vmem] * parts + [hbm],
            vmem,
            jax.ShapeDtypeStruct((rows, dim), jnp.bfloat16),
            [stacked],
        )(me, *held[group], made)
        before = (total,)
        arrived.append(
            [
                lax.ppermute(total, "z", [(at, at + far) for at in range(planes - far)])
                for far in range(1, planes)
            ]
        )

    prefixes = []
    prefix_type = jax.ShapeDtypeStruct((owned * dim + local, dim), jnp.bfloat16)
    for group in range(GROUPS):
        inside, made = inside_part(GROUPS + group, inside, before)
        prefix = kernel_call(
            functools.partial(prefix_kernel, dim, owned, parts, planes),
            f"prefix{group}",
            (),
            [vmem] * (parts + planes) + [hbm],
            [vmem] * count,
            [prefix_type] * count,
            [stacked, pltpu.VMEM((count, owned * dim, dim), jnp.bfloat16)],
        )(me, gain, *held[group], *arrived[group], made)
        before = prefix[:1]
        prefixes.append(
            exchange(prefix, ("head", "core"), lambda at: at % parts * 2 + at // parts)
        )

    out = ()
    for group in range(GROUPS):

        def place(b, me=None, group=group):
            return b // per_group * per_half + group * per_group + b % per_group

        out = (
            kernel_call(
                functools.partial(output_kernel, dim, owned, count, local, place),
                f"output{group}",
                (2 * per_group,),
                [
                    features(place),
                    pl.BlockSpec(
                        (length, STEP * dim), lambda b, me, place=place: (0, place(b))
                    ),
                    features(place),
                    decays(place),
                ]
                + [full(prefix_type.shape)] * count
                + [hbm] * len(out or before),
                features(place),
                jax.ShapeDtypeStruct((1, length, width), jnp.bfloat16),
                [pltpu.VMEM((count,) + prefix_type.shape, jnp.bfloat16)],
                aliases={5 + count: 0} if out else {},
                cost=5,
            )(me, queries, *inside, gate, decay, *prefixes[group], *(out or before)),
        )
    return out[0]


def solution(mesh):
    parts, blocks = mesh.shape["head"], mesh.shape["ctx"]
    names = mesh.axis_names
    at = names.index("ctx")
    shape = mesh.devices.shape[:at] + (blocks // 2, 2) + mesh.devices.shape[at + 1 :]
    finer = Mesh(mesh.devices.reshape(shape), names[:at] + ("z", "core") + names[at + 1 :])
    tokens = P(("z", "core"), "head", None)
    return jax.shard_map(
        functools.partial(on_device, parts, blocks // 2),
        mesh=finer,
        in_specs=(tokens,) * 5 + (P("head"),),
        out_specs=tokens,
        check_vma=False,
    )
```

```python
import functools

import jax
import jax.numpy as jnp
from jax import lax
from jax.experimental import pallas as pl
from jax.experimental.pallas import tpu as pltpu
from jax.sharding import Mesh
from jax.sharding import PartitionSpec as P

GROUPS = 2
STEP = 8
EXTRA = 16
VMEM_LIMIT = 24 * 1024 * 1024
NN = (((1,), (0,)), ((), ()))
NT = (((1,), (1,)), ((), ()))
TN = (((0,), (0,)), ((), ()))


def dot(a, b, dims, precision=None):
    return lax.dot_general(a, b, dims, precision=precision, preferred_element_type=jnp.float32)


def exact_dot(a, b, dims):
    return dot(a, b, dims, lax.Precision.HIGHEST)


def triangle(length, keep):
    rows = lax.broadcasted_iota(jnp.int32, (length, length), 0)
    columns = lax.broadcasted_iota(jnp.int32, (length, length), 1)
    return jnp.where(keep(rows, columns), 1.0, 0.0).astype(jnp.float32)


def split(value):
    first = value.astype(jnp.bfloat16)
    left = value - first.astype(jnp.float32)
    second = left.astype(jnp.bfloat16)
    return first, second, (left - second.astype(jnp.float32)).astype(jnp.bfloat16)


def join(rows, head):
    wide = rows.astype(jnp.float32)
    return wide[3 * head : 3 * head + 1] + (
        wide[3 * head + 1 : 3 * head + 2] + wide[3 * head + 2 : 3 * head + 3]
    )


def decay_rows(totals):
    parts = [part for total in totals for part in split(total)]
    blank = jnp.zeros((EXTRA - len(parts), totals[0].shape[1]), jnp.bfloat16)
    return jnp.concatenate(parts + [blank], axis=0)


def pack_kernel(me_ref, mine_ref, other_ref, *slots):
    length = slots[0].shape[2]
    for slot, slot_ref in enumerate(slots):
        span = pl.ds(pl.multiple_of((me_ref[0] ^ slot) * length, length), length)
        slot_ref[0] = mine_ref[0, :, span]
        slot_ref[1] = other_ref[0, :, span]


def state_kernel(dim, owned, parts, place, me_ref, *refs):
    keys, values, sources = refs[0:2], refs[2:4], refs[4 : 4 + parts]
    decay_ref, stacked_ref = refs[-2:]
    slots = refs[-2 - parts : -2]
    owners = STEP // owned
    turn = pl.program_id(0)
    part, core = me_ref[0], me_ref[1]

    @pl.when(turn == 0)
    def _():
        for slot, source_ref in enumerate(sources):
            for source in range(2):
                decay_ref[source * parts + (part ^ slot)] = source_ref[source]

    at = place(turn, me_ref)
    per_local, length = decay_ref.shape[1] // STEP, decay_ref.shape[2]
    rows = pl.ds(pl.multiple_of(at % per_local * STEP, STEP), STEP)
    for source in range(2):
        block = core if source == 0 else 1 - core
        decay = decay_ref[source * parts + at // per_local, rows, :]
        weight = jnp.exp(exact_dot(decay, triangle(length, lambda u, s: u > s), NN))
        whole = jnp.broadcast_to(jnp.sum(decay, axis=1, keepdims=True), (STEP, dim))
        both = []
        for head in range(STEP):
            columns = slice(head * dim, (head + 1) * dim)
            turned = keys[source][0, :, columns].T
            decayed = turned.astype(jnp.float32) * weight[head : head + 1, :]
            high = decayed.astype(jnp.bfloat16)
            low = (decayed - high.astype(jnp.float32)).astype(jnp.bfloat16)
            both.append(
                dot(jnp.concatenate([high, low], axis=0), values[source][0, :, columns], NN)
            )
        for head in range(STEP):
            owner, spot = divmod(head, owned)
            state = both[head][:dim] + both[head][dim:]
            span = slice(spot * dim, (spot + 1) * dim)
            stacked_ref[turn * owners + owner, block, span, :] = state.astype(jnp.bfloat16)
        for owner in range(owners):
            stacked_ref[turn * owners + owner, block, owned * dim :, :] = decay_rows(
                [whole[head : head + 1] for head in range(owner * owned, (owner + 1) * owned)]
            )

    @pl.when(turn == pl.num_programs(0) - 1)
    def _():
        for slot, slot_ref in enumerate(slots):
            slot_ref[...] = stacked_ref[part ^ slot]


def inside_kernel(dim, me_ref, queries_ref, keys_ref, values_ref, decay_ref, *rest):
    inside_ref, done_ref = rest[-2:]
    decay = decay_ref[0]
    length = decay.shape[1]
    down = exact_dot(triangle(length, lambda t, u: u <= t), decay, NT)
    across = exact_dot(decay, triangle(length, lambda u, s: u <= s), NN)
    rows = lax.broadcasted_iota(jnp.int32, (length, length), 0)
    causal = rows >= lax.broadcasted_iota(jnp.int32, (length, length), 1)
    columns = [slice(head * dim, (head + 1) * dim) for head in range(STEP)]
    scores = [dot(queries_ref[0, :, c], keys_ref[0, :, c], NT) for c in columns]
    weights = []
    for head in range(STEP):
        gap = down[:, head : head + 1] - across[head : head + 1, :]
        weight = scores[head] * jnp.exp(jnp.where(causal, gap, -jnp.inf))
        weights.append(weight.astype(jnp.bfloat16))
    for head, c in enumerate(columns):
        inside_ref[:, c] = dot(weights[head], values_ref[0, :, c], NN)
    done_ref[...] = jnp.zeros_like(done_ref)


def gather_states(part, slots, stacked_ref):
    parts = len(slots)
    for slot, slot_ref in enumerate(slots):
        for block in range(2):
            stacked_ref[block * parts + (part ^ slot)] = slot_ref[block]


def total_kernel(dim, owned, parts, me_ref, *refs):
    total_ref, stacked_ref = refs[-2:]
    gather_states(me_ref[0], refs[:parts], stacked_ref)
    count = 2 * parts
    extra = [stacked_ref[at, owned * dim :, :] for at in range(count)]
    sums = []
    for head in range(owned):
        span = slice(head * dim, (head + 1) * dim)
        after = jnp.zeros((1, dim), jnp.float32)
        total = stacked_ref[count - 1, span, :].astype(jnp.float32)
        for at in range(count - 2, -1, -1):
            after += join(extra[at + 1], head)
            total += jnp.exp(after) * stacked_ref[at, span, :].astype(jnp.float32)
        total_ref[span, :] = total.astype(jnp.bfloat16)
        sums.append(after + join(extra[0], head))
    total_ref[owned * dim :, :] = decay_rows(sums)


def widen_kernel(dim, owned, me_ref, later_ref, earlier_ref, *refs):
    out_ref = refs[-1]
    later, earlier = later_ref[owned * dim :, :], earlier_ref[owned * dim :, :]
    sums = []
    for head in range(owned):
        span = slice(head * dim, (head + 1) * dim)
        after = join(later, head)
        total = later_ref[span, :].astype(jnp.float32)
        total += jnp.exp(after) * earlier_ref[span, :].astype(jnp.float32)
        out_ref[span, :] = total.astype(jnp.bfloat16)
        sums.append(after + join(earlier, head))
    out_ref[owned * dim :, :] = decay_rows(sums)


def prefix_kernel(dim, owned, parts, stretches, me_ref, gain_ref, *refs):
    stacked_ref, prefix_ref = refs[-2:]
    slots, totals = refs[:parts], refs[parts : parts + stretches]
    count = 2 * parts
    results = refs[-2 - parts : -2]
    gather_states(me_ref[0], slots, stacked_ref)
    extra = [stacked_ref[at, owned * dim :, :] for at in range(count)]
    more = [total_ref[owned * dim :, :] for total_ref in totals]
    for head in range(owned):
        span = slice(head * dim, (head + 1) * dim)
        prefix = jnp.zeros((dim, dim), jnp.float32)
        after = jnp.zeros((1, dim), jnp.float32)
        for turn, total_ref in enumerate(totals):
            prefix += jnp.exp(after) * total_ref[span, :].astype(jnp.float32)
            after += join(more[turn], head)
        for at in range(count):
            prefix_ref[at, span, :] = prefix.astype(jnp.bfloat16)
            if at < count - 1:
                prefix = jnp.exp(join(extra[at], head)) * prefix
                prefix += stacked_ref[at, span, :].astype(jnp.float32)
    size = owned * dim
    for slot, result_ref in enumerate(results):
        for block in range(2):
            result_ref[block * size : (block + 1) * size, :] = prefix_ref[
                block * parts + (me_ref[0] ^ slot)
            ]
        result_ref[2 * size :, :] = gain_ref[...]


def merge_kernel(parts, me_ref, *refs):
    slots, (mine_ref, other_ref, gain_ref) = refs[:parts], refs[-3:]
    size = mine_ref.shape[1]
    local = gain_ref.shape[0] // parts
    for slot, slot_ref in enumerate(slots):
        owner = me_ref[0] ^ slot
        mine = pl.multiple_of(me_ref[1] * size, size)
        other = pl.multiple_of((1 - me_ref[1]) * size, size)
        mine_ref[owner] = slot_ref[pl.ds(mine, size), :]
        other_ref[owner] = slot_ref[pl.ds(other, size), :]
        gain_ref[pl.ds(pl.multiple_of(owner * local, local), local), :] = slot_ref[
            2 * size :, :
        ].astype(jnp.float32)


def output_kernel(
    dim, owned, me_ref, queries_ref, inside_ref, gate_ref, decay_ref, gain_ref, prefix_ref, *refs
):
    out_ref, done_ref = refs[-2:]
    decay = decay_ref[0]
    length = decay.shape[1]
    down = jnp.exp(exact_dot(triangle(length, lambda t, u: u <= t), decay, NT))
    average = jnp.full((dim, dim), 1.0 / dim, jnp.bfloat16)
    columns = [slice(head * dim, (head + 1) * dim) for head in range(STEP)]
    carried = []
    for head, c in enumerate(columns):
        start = head % owned * dim
        prefix = prefix_ref[head // owned, start : start + dim, :]
        carried.append(dot(queries_ref[0, :, c], prefix, NN))
    mixed, means = [], []
    for head, c in enumerate(columns):
        mixed.append(inside_ref[:, c] + carried[head] * down[:, head : head + 1])
        means.append(dot((mixed[head] * mixed[head]).astype(jnp.bfloat16), average, NN))
    for head, c in enumerate(columns):
        half_gain = 0.5 * gain_ref[head : head + 1, :]
        turned = jnp.tanh(0.5 * gate_ref[0, :, c].astype(jnp.float32))
        normed = mixed[head] * lax.rsqrt(means[head] + 1e-06) * (half_gain + half_gain * turned)
        out_ref[0, :, c] = normed.astype(jnp.bfloat16)
    done_ref[...] = jnp.zeros_like(done_ref)


def kernel_call(body, name, grid, in_specs, out_specs, out_shape, scratch=(), aliases={}, cost=1):
    return pl.pallas_call(
        body,
        grid_spec=pltpu.PrefetchScalarGridSpec(
            num_scalar_prefetch=1,
            grid=grid,
            in_specs=in_specs,
            out_specs=out_specs,
            scratch_shapes=scratch,
        ),
        out_shape=out_shape,
        input_output_aliases=aliases,
        compiler_params=pltpu.CompilerParams(vmem_limit_bytes=VMEM_LIMIT),
        cost_estimate=pl.CostEstimate(
            flops=int(cost * 1e9), transcendentals=0, bytes_accessed=0
        ),
        name=name,
    )


def on_device(parts, planes, queries, keys, values, gate, log_decay, norm_gain):
    _, length, width = queries.shape
    local = log_decay.shape[1]
    dim = width // (local * parts)
    count = 2 * parts
    half = local * parts // 2
    owned = half // (GROUPS * parts)
    rows = owned * dim + EXTRA
    per_half, per_group, per_local = half // STEP, half // GROUPS // STEP, local // STEP
    me = jnp.stack([lax.axis_index("head"), lax.axis_index("core")]).astype(jnp.int32)
    swap = [(0, 1), (1, 0)]

    log_decay_other = lax.ppermute(log_decay, "core", swap)
    values_other = lax.ppermute(values, "core", swap)
    keys_other = lax.ppermute(keys, "core", swap)
    gain = norm_gain.reshape(local, dim)

    queries, keys, values, gate = (
        pltpu.with_memory_space_constraint(array, pltpu.HBM)
        for array in (queries, keys, values, gate)
    )

    vmem = pl.BlockSpec(memory_space=pltpu.VMEM)
    hbm = pl.BlockSpec(memory_space=pl.ANY)

    def full(shape):
        return pl.BlockSpec(shape, lambda b, me: (0,) * len(shape))

    def features(place):
        return pl.BlockSpec((1, length, STEP * dim), lambda b, me: (0, 0, place(b, me)))

    def decays(place):
        def block(b, me):
            at = place(b, me)
            return at // per_local, at % per_local, 0

        return pl.BlockSpec((1, STEP, length), block)

    def exchange(slots):
        arrived = list(slots)
        for slot in sorted(range(1, parts), key=lambda s: -bin(s).count("1")):
            pairs = [(at, at ^ slot) for at in range(parts)]
            arrived[slot] = lax.ppermute(slots[slot], "head", pairs)
        return arrived

    packed = kernel_call(
        pack_kernel,
        "pack",
        (),
        [vmem, vmem],
        [vmem] * parts,
        [jax.ShapeDtypeStruct((2, local, length), jnp.float32)] * parts,
    )(me, log_decay, log_decay_other)
    packed = exchange(packed)

    before = ()
    held = []
    state_type = jax.ShapeDtypeStruct((2, rows, dim), jnp.bfloat16)
    decay_type = jax.ShapeDtypeStruct((count, local, length), jnp.float32)
    for group in range(GROUPS):

        def mine(b, me, group=group):
            return me[1] * per_half + group * per_group + b

        *state, decay = kernel_call(
            functools.partial(state_kernel, dim, owned, parts, mine),
            f"state{group}",
            (per_group,),
            [features(mine)] * 4 + [full((2, local, length))] * parts + [hbm] * len(before),
            [full(state_type.shape)] * parts + [full(decay_type.shape)],
            [state_type] * parts + [decay_type],
            [pltpu.VMEM((parts,) + state_type.shape, jnp.bfloat16)],
            cost=4,
        )(me, keys, keys_other, values, values_other, *packed, *before)
        before = tuple(state[:1])
        held.append(exchange(state))

    pieces = 2 * GROUPS
    per_piece = 2 * per_half // pieces
    token = jax.ShapeDtypeStruct((8, 128), jnp.float32)

    def inside_part(at, inside, before):
        def place(b, me):
            return at * per_piece + b

        *inside, made = kernel_call(
            functools.partial(inside_kernel, dim),
            f"inside{at}",
            (per_piece,),
            [features(place)] * 3 + [decays(place)] + [hbm] * (len(inside) + len(before)),
            [
                pl.BlockSpec((length, STEP * dim), lambda b, me: (0, place(b, me))),
                full(token.shape),
            ],
            [jax.ShapeDtypeStruct((length, width), jnp.float32), token],
            aliases={5: 0} if inside else {},
            cost=3,
        )(me, queries, keys, values, decay, *inside, *before)
        return inside, made

    inside = ()
    arrived = []
    stacked = pltpu.VMEM((count, rows, dim), jnp.bfloat16)
    total_type = jax.ShapeDtypeStruct((rows, dim), jnp.bfloat16)

    def upward(total, far):
        return lax.ppermute(total, "z", [(at, at + far) for at in range(planes - far)])

    for group in range(GROUPS):
        inside, made = inside_part(group, inside, before)
        total = kernel_call(
            functools.partial(total_kernel, dim, owned, parts),
            f"total{group}",
            (),
            [vmem] * parts + [hbm],
            vmem,
            total_type,
            [stacked],
        )(me, *held[group], made)
        stretches, far = [upward(total, 1)], 1
        while 2 * far < planes:
            total = kernel_call(
                functools.partial(widen_kernel, dim, owned),
                f"widen{group}_{far}",
                (),
                [vmem] * 2,
                vmem,
                total_type,
            )(me, total, stretches[-1])
            far *= 2
            stretches.append(upward(total, far))
        before = (total,)
        arrived.append(stretches)

    prefixes = []
    size = owned * dim
    prefix_type = jax.ShapeDtypeStruct((2 * size + local, dim), jnp.bfloat16)
    for group in range(GROUPS):
        inside, made = inside_part(GROUPS + group, inside, before)
        prefix = kernel_call(
            functools.partial(prefix_kernel, dim, owned, parts, len(arrived[group])),
            f"prefix{group}",
            (),
            [vmem] * (1 + parts + len(arrived[group])) + [hbm],
            [vmem] * parts,
            [prefix_type] * parts,
            [stacked, pltpu.VMEM((count, size, dim), jnp.bfloat16)],
        )(me, gain, *held[group], *arrived[group], made)
        before = tuple(prefix[:1])
        prefixes.append(exchange(prefix))

    def merge(group, before):
        part_type = jax.ShapeDtypeStruct((parts, size, dim), jnp.bfloat16)
        return kernel_call(
            functools.partial(merge_kernel, parts),
            f"merge{group}",
            (),
            [vmem] * parts + [hbm] * len(before),
            [vmem] * 3,
            [part_type, part_type, jax.ShapeDtypeStruct((parts * local, dim), jnp.float32)],
        )(me, *prefixes[group], *before)

    def output(group, other, prefix, gains, out, before):
        def place(b, me):
            which = 1 - me[1] if other else me[1]
            return which * per_half + group * per_group + b

        *out, made = kernel_call(
            functools.partial(output_kernel, dim, owned),
            f"output{group}_{other}",
            (per_group,),
            [
                features(place),
                pl.BlockSpec((length, STEP * dim), lambda b, me: (0, place(b, me))),
                features(place),
                decays(place),
                pl.BlockSpec((STEP, dim), lambda b, me: (place(b, me), 0)),
                pl.BlockSpec((STEP // owned, size, dim), lambda b, me: (b, 0, 0)),
            ]
            + [hbm] * (len(out) + len(before)),
            [features(place), full(token.shape)],
            [jax.ShapeDtypeStruct((1, length, width), jnp.bfloat16), token],
            aliases={7: 0} if out else {},
            cost=3,
        )(me, queries, *inside, gate, decay, gains, prefix, *out, *before)
        return out, (made,)

    out, late = (), None
    for group in range(GROUPS):
        mine, other, gains = merge(group, before)
        other = lax.ppermute(other, "core", swap)
        if late is not None:
            out, before = output(group - 1, 1, *late, out, (gains,))
        out, before = output(group, 0, mine, gains, out, before if late is not None else ())
        late = (other, gains)
    out, _ = output(GROUPS - 1, 1, *late, out, before)
    return out[0]


def solution(mesh):
    parts, blocks = mesh.shape["head"], mesh.shape["ctx"]
    names = mesh.axis_names
    at = names.index("ctx")
    shape = mesh.devices.shape[:at] + (blocks // 2, 2) + mesh.devices.shape[at + 1 :]
    finer = Mesh(mesh.devices.reshape(shape), names[:at] + ("z", "core") + names[at + 1 :])
    tokens = P(("z", "core"), "head", None)
    return jax.shard_map(
        functools.partial(on_device, parts, blocks // 2),
        mesh=finer,
        in_specs=(tokens,) * 5 + (P("head"),),
        out_specs=tokens,
        check_vma=False,
    )
```

```python
import functools

import jax
import jax.numpy as jnp
from jax import lax
from jax.experimental import pallas as pl
from jax.experimental.pallas import tpu as pltpu
from jax.sharding import Mesh
from jax.sharding import PartitionSpec as P

GROUPS = 2
STEP = 8
EXTRA = 16
VMEM_LIMIT = 24 * 1024 * 1024
NN = (((1,), (0,)), ((), ()))
NT = (((1,), (1,)), ((), ()))
TN = (((0,), (0,)), ((), ()))


def dot(a, b, dims, precision=None):
    return lax.dot_general(a, b, dims, precision=precision, preferred_element_type=jnp.float32)


def exact_dot(a, b, dims):
    return dot(a, b, dims, lax.Precision.HIGHEST)


def triangle(length, keep):
    rows = lax.broadcasted_iota(jnp.int32, (length, length), 0)
    columns = lax.broadcasted_iota(jnp.int32, (length, length), 1)
    return jnp.where(keep(rows, columns), 1.0, 0.0).astype(jnp.float32)


def split(value):
    first = value.astype(jnp.bfloat16)
    left = value - first.astype(jnp.float32)
    second = left.astype(jnp.bfloat16)
    return first, second, (left - second.astype(jnp.float32)).astype(jnp.bfloat16)


def join(rows, head):
    wide = rows.astype(jnp.float32)
    return wide[3 * head : 3 * head + 1] + (
        wide[3 * head + 1 : 3 * head + 2] + wide[3 * head + 2 : 3 * head + 3]
    )


def decay_rows(totals):
    parts = [part for total in totals for part in split(total)]
    blank = jnp.zeros((EXTRA - len(parts), totals[0].shape[1]), jnp.bfloat16)
    return jnp.concatenate(parts + [blank], axis=0)


def pack_kernel(parts, decay_ref, packed_ref):
    length = packed_ref.shape[2]
    for place in range(packed_ref.shape[0]):
        start = place % parts * length
        packed_ref[place] = decay_ref[0, :, start : start + length]


def state_kernel(dim, owned, parts, slotted, me_ref, *refs):
    keys, values, decays = refs[0:2], refs[2:4], refs[4:6]
    stacked_ref = refs[-1]
    slots = refs[-1 - parts : -1] if slotted else ()
    owners = STEP // owned
    turn = pl.program_id(0)
    part, core = me_ref[0], me_ref[1]
    for source in range(2):
        block = core if source == 0 else 1 - core
        decay = decays[source][0]
        length = decay.shape[1]
        weight = jnp.exp(exact_dot(decay, triangle(length, lambda u, s: u > s), NN))
        whole = jnp.broadcast_to(jnp.sum(decay, axis=1, keepdims=True), (STEP, dim))
        states = []
        for head in range(STEP):
            columns = slice(head * dim, (head + 1) * dim)
            turned = keys[source][0, :, columns].T
            decayed = turned.astype(jnp.float32) * weight[head : head + 1, :]
            states.append(
                dot(decayed.astype(jnp.bfloat16), values[source][0, :, columns], NN)
            )
        for head in range(STEP):
            owner, spot = divmod(head, owned)
            span = slice(spot * dim, (spot + 1) * dim)
            stacked_ref[turn * owners + owner, block, span, :] = states[head].astype(jnp.bfloat16)
        for owner in range(owners):
            stacked_ref[turn * owners + owner, block, owned * dim :, :] = decay_rows(
                [whole[head : head + 1] for head in range(owner * owned, (owner + 1) * owned)]
            )

    if slotted:

        @pl.when(turn == pl.num_programs(0) - 1)
        def _():
            for slot, slot_ref in enumerate(slots):
                slot_ref[...] = stacked_ref[part ^ slot]


def inside_kernel(dim, me_ref, queries_ref, keys_ref, values_ref, decay_ref, *rest):
    inside_ref, done_ref = rest[-2:]
    decay = decay_ref[0]
    length = decay.shape[1]
    down = exact_dot(triangle(length, lambda t, u: u <= t), decay, NT)
    across = exact_dot(decay, triangle(length, lambda u, s: u <= s), NN)
    rows = lax.broadcasted_iota(jnp.int32, (length, length), 0)
    causal = rows >= lax.broadcasted_iota(jnp.int32, (length, length), 1)
    columns = [slice(head * dim, (head + 1) * dim) for head in range(STEP)]
    scores = [dot(queries_ref[0, :, c], keys_ref[0, :, c], NT) for c in columns]
    weights = []
    for head in range(STEP):
        gap = down[:, head : head + 1] - across[head : head + 1, :]
        weight = scores[head] * jnp.exp(jnp.where(causal, gap, -jnp.inf))
        weights.append(weight.astype(jnp.bfloat16))
    for head, c in enumerate(columns):
        inside_ref[:, c] = dot(weights[head], values_ref[0, :, c], NN)
    done_ref[...] = jnp.zeros_like(done_ref)


def pieces_of(part, slots):
    if len(slots) == 1:
        return [(at, slots[0].at[at]) for at in range(slots[0].shape[0])]
    return [(part ^ slot, slot_ref) for slot, slot_ref in enumerate(slots)]


def gather_states(part, slots, stacked_ref):
    pieces = pieces_of(part, slots)
    for at, piece_ref in pieces:
        for block in range(2):
            stacked_ref[block * len(pieces) + at] = piece_ref[block]


def total_kernel(dim, owned, parts, slots, me_ref, *refs):
    total_ref, stacked_ref = refs[-2:]
    gather_states(me_ref[0], refs[:slots], stacked_ref)
    count = 2 * parts
    extra = [stacked_ref[at, owned * dim :, :] for at in range(count)]
    sums = []
    for head in range(owned):
        span = slice(head * dim, (head + 1) * dim)
        after = jnp.zeros((1, dim), jnp.float32)
        total = stacked_ref[count - 1, span, :].astype(jnp.float32)
        for at in range(count - 2, -1, -1):
            after += join(extra[at + 1], head)
            total += jnp.exp(after) * stacked_ref[at, span, :].astype(jnp.float32)
        total_ref[span, :] = total.astype(jnp.bfloat16)
        sums.append(after + join(extra[0], head))
    total_ref[owned * dim :, :] = decay_rows(sums)


def prefix_kernel(dim, owned, parts, slots, stretches, me_ref, gain_ref, *refs):
    stacked_ref, prefix_ref = refs[-2:]
    totals = refs[slots : slots + stretches]
    count = 2 * parts
    results = refs[-2 - slots : -2]
    gather_states(me_ref[0], refs[:slots], stacked_ref)
    extra = [stacked_ref[at, owned * dim :, :] for at in range(count)]
    more = [total_ref[owned * dim :, :] for total_ref in totals]
    for head in range(owned):
        span = slice(head * dim, (head + 1) * dim)
        prefix = jnp.zeros((dim, dim), jnp.float32)
        after = jnp.zeros((1, dim), jnp.float32)
        for turn, total_ref in enumerate(totals):
            prefix += jnp.exp(after) * total_ref[span, :].astype(jnp.float32)
            after += join(more[turn], head)
        for at in range(count):
            prefix_ref[at, span, :] = prefix.astype(jnp.bfloat16)
            if at < count - 1:
                prefix = jnp.exp(join(extra[at], head)) * prefix
                prefix += stacked_ref[at, span, :].astype(jnp.float32)
    size = owned * dim
    for at, result_ref in pieces_of(me_ref[0], results):
        for block in range(2):
            result_ref[block * size : (block + 1) * size, :] = prefix_ref[block * parts + at]
        result_ref[2 * size :, :] = gain_ref[...]


def merge_kernel(slots, me_ref, *refs):
    mine_ref, other_ref, gain_ref = refs[-3:]
    size = mine_ref.shape[1]
    local = gain_ref.shape[0] // mine_ref.shape[0]
    mine = pl.multiple_of(me_ref[1] * size, size)
    other = pl.multiple_of((1 - me_ref[1]) * size, size)
    for owner, piece_ref in pieces_of(me_ref[0], refs[:slots]):
        mine_ref[owner] = piece_ref[pl.ds(mine, size), :]
        other_ref[owner] = piece_ref[pl.ds(other, size), :]
        rows = pl.ds(pl.multiple_of(owner * local, local), local)
        gain_ref[rows, :] = piece_ref[2 * size :, :].astype(jnp.float32)


def output_kernel(
    dim, owned, me_ref, queries_ref, inside_ref, gate_ref, decay_ref, gain_ref, prefix_ref, *refs
):
    out_ref, done_ref = refs[-2:]
    decay = decay_ref[0]
    length = decay.shape[1]
    down = jnp.exp(exact_dot(triangle(length, lambda t, u: u <= t), decay, NT))
    average = jnp.full((dim, dim), 1.0 / dim, jnp.bfloat16)
    columns = [slice(head * dim, (head + 1) * dim) for head in range(STEP)]
    carried = []
    for head, c in enumerate(columns):
        start = head % owned * dim
        prefix = prefix_ref[head // owned, start : start + dim, :]
        carried.append(dot(queries_ref[0, :, c], prefix, NN))
    mixed, means = [], []
    for head, c in enumerate(columns):
        mixed.append(inside_ref[:, c] + carried[head] * down[:, head : head + 1])
        means.append(dot((mixed[head] * mixed[head]).astype(jnp.bfloat16), average, NN))
    for head, c in enumerate(columns):
        half_gain = 0.5 * gain_ref[head : head + 1, :]
        turned = jnp.tanh(0.5 * gate_ref[0, :, c].astype(jnp.float32))
        normed = mixed[head] * lax.rsqrt(means[head] + 1e-06) * (half_gain + half_gain * turned)
        out_ref[0, :, c] = normed.astype(jnp.bfloat16)
    done_ref[...] = jnp.zeros_like(done_ref)


def kernel_call(body, name, grid, in_specs, out_specs, out_shape, scratch=(), aliases={}):
    return pl.pallas_call(
        body,
        grid_spec=pltpu.PrefetchScalarGridSpec(
            num_scalar_prefetch=1,
            grid=grid,
            in_specs=in_specs,
            out_specs=out_specs,
            scratch_shapes=scratch,
        ),
        out_shape=out_shape,
        input_output_aliases=aliases,
        compiler_params=pltpu.CompilerParams(vmem_limit_bytes=VMEM_LIMIT),
        cost_estimate=pl.CostEstimate(flops=1, transcendentals=0, bytes_accessed=1),
        name=name,
    )


def on_device(parts, planes, queries, keys, values, gate, log_decay, norm_gain):
    _, length, width = queries.shape
    local = log_decay.shape[1]
    dim = width // (local * parts)
    count = 2 * parts
    half = local * parts // 2
    owned = half // (GROUPS * parts)
    rows = owned * dim + EXTRA
    per_half, per_group, per_local = half // STEP, half // GROUPS // STEP, local // STEP
    me = jnp.stack([lax.axis_index("head"), lax.axis_index("core")]).astype(jnp.int32)
    swap = [(0, 1), (1, 0)]

    values_other = lax.ppermute(values, "core", swap)
    keys_other = lax.ppermute(keys, "core", swap)
    packed = pl.pallas_call(
        functools.partial(pack_kernel, parts),
        out_shape=jax.ShapeDtypeStruct((count, local, length), jnp.float32),
        name="pack",
    )(log_decay)
    decay = lax.all_to_all(packed, ("core", "head"), 0, 0, tiled=True)
    gain = norm_gain.reshape(local, dim)

    queries, keys, values, gate = (
        pltpu.with_memory_space_constraint(array, pltpu.HBM)
        for array in (queries, keys, values, gate)
    )

    vmem = pl.BlockSpec(memory_space=pltpu.VMEM)
    hbm = pl.BlockSpec(memory_space=pl.ANY)

    def full(shape):
        return pl.BlockSpec(shape, lambda b, me: (0,) * len(shape))

    def features(place):
        return pl.BlockSpec((1, length, STEP * dim), lambda b, me: (0, 0, place(b, me)))

    def decays(place, other=False):
        def block(b, me):
            at = place(b, me)
            which = 1 - me[1] if other else me[1]
            return which * parts + at // per_local, at % per_local, 0

        return pl.BlockSpec((1, STEP, length), block)

    def exchange(slots):
        if len(slots) == 1:
            return [lax.all_to_all(slots[0], "head", 0, 0, tiled=True)]
        arrived = list(slots)
        for slot in sorted(range(1, parts), key=lambda s: -bin(s).count("1")):
            pairs = [(at, at ^ slot) for at in range(parts)]
            arrived[slot] = lax.ppermute(slots[slot], "head", pairs)
        return arrived

    def by_slots(group):
        return group % 2 == 0

    before = ()
    held = []
    state_type = jax.ShapeDtypeStruct((2, rows, dim), jnp.bfloat16)
    for group in range(GROUPS):

        def mine(b, me, group=group):
            return me[1] * per_half + group * per_group + b

        slotted = by_slots(group)
        whole = (parts,) + state_type.shape
        state = kernel_call(
            functools.partial(state_kernel, dim, owned, parts, slotted),
            f"state{group}",
            (per_group,),
            [features(mine)] * 4
            + [decays(mine), decays(mine, other=True)]
            + [hbm] * len(before),
            [full(state_type.shape)] * parts if slotted else [full(whole)],
            [state_type] * parts if slotted else [jax.ShapeDtypeStruct(whole, jnp.bfloat16)],
            [pltpu.VMEM(whole, jnp.bfloat16)] if slotted else [],
        )(me, keys, keys_other, values, values_other, decay, decay, *before)
        before = tuple(state[:1])
        held.append(exchange(state))

    pieces = 2 * GROUPS
    per_piece = 2 * per_half // pieces
    token = jax.ShapeDtypeStruct((8, 128), jnp.float32)

    def inside_part(at, inside, before):
        def place(b, me):
            return at * per_piece + b

        *inside, made = kernel_call(
            functools.partial(inside_kernel, dim),
            f"inside{at}",
            (per_piece,),
            [features(place)] * 3 + [decays(place)] + [hbm] * (len(inside) + len(before)),
            [
                pl.BlockSpec((length, STEP * dim), lambda b, me: (0, place(b, me))),
                full(token.shape),
            ],
            [jax.ShapeDtypeStruct((length, width), jnp.float32), token],
            aliases={5: 0} if inside else {},
        )(me, queries, keys, values, decay, *inside, *before)
        return inside, made

    inside = ()
    arrived = []
    stacked = pltpu.VMEM((count, rows, dim), jnp.bfloat16)
    total_type = jax.ShapeDtypeStruct((rows, dim), jnp.bfloat16)

    def upward(total, far):
        return lax.ppermute(total, "z", [(at, at + far) for at in range(planes - far)])

    for group in range(GROUPS):
        for at in range(group * 2, group * 2 + (1 if group == 0 else 2)):
            inside, made = inside_part(at - min(group, 1), inside, before)
            before = (made,)
        slots = len(held[group])
        total = kernel_call(
            functools.partial(total_kernel, dim, owned, parts, slots),
            f"total{group}",
            (),
            [vmem] * slots + [hbm],
            vmem,
            total_type,
            [stacked],
        )(me, *held[group], *before)
        before = (total,)
        arrived.append([upward(total, far) for far in range(1, planes)])

    prefixes = []
    size = owned * dim
    prefix_type = jax.ShapeDtypeStruct((2 * size + local, dim), jnp.bfloat16)
    for group in range(GROUPS):
        slots = len(held[group])
        whole = jax.ShapeDtypeStruct((parts,) + prefix_type.shape, jnp.bfloat16)
        prefix = kernel_call(
            functools.partial(prefix_kernel, dim, owned, parts, slots, len(arrived[group])),
            f"prefix{group}",
            (),
            [vmem] * (1 + slots + len(arrived[group])) + [hbm],
            [vmem] * slots,
            [whole] if slots == 1 else [prefix_type] * parts,
            [stacked, pltpu.VMEM((count, size, dim), jnp.bfloat16)],
        )(me, gain, *held[group], *arrived[group], *before)
        before = tuple(prefix[:1])
        prefixes.append(exchange(prefix))
        if group == 0:
            inside, made = inside_part(pieces - 1, inside, before)
            before = (made,)

    def merge(group, before):
        part_type = jax.ShapeDtypeStruct((parts, size, dim), jnp.bfloat16)
        return kernel_call(
            functools.partial(merge_kernel, len(prefixes[group])),
            f"merge{group}",
            (),
            [vmem] * len(prefixes[group]) + [hbm] * len(before),
            [vmem] * 3,
            [part_type, part_type, jax.ShapeDtypeStruct((parts * local, dim), jnp.float32)],
        )(me, *prefixes[group], *before)

    def output(group, other, prefix, gains, out, before):
        def place(b, me):
            which = 1 - me[1] if other else me[1]
            return which * per_half + group * per_group + b

        *out, made = kernel_call(
            functools.partial(output_kernel, dim, owned),
            f"output{group}_{other}",
            (per_group,),
            [
                features(place),
                pl.BlockSpec((length, STEP * dim), lambda b, me: (0, place(b, me))),
                features(place),
                decays(place),
                pl.BlockSpec((STEP, dim), lambda b, me: (place(b, me), 0)),
                pl.BlockSpec((STEP // owned, size, dim), lambda b, me: (b, 0, 0)),
            ]
            + [hbm] * (len(out) + len(before)),
            [features(place), full(token.shape)],
            [jax.ShapeDtypeStruct((1, length, width), jnp.bfloat16), token],
            aliases={7: 0} if out else {},
        )(me, queries, *inside, gate, decay, gains, prefix, *out, *before)
        return out, (made,)

    out = ()
    for group in range(GROUPS):
        mine, other, gains = merge(group, before)
        other = lax.ppermute(other, "core", swap)
        out, before = output(group, 0, mine, gains, out, ())
        out, before = output(group, 1, other, gains, out, ())
    return out[0]


def solution(mesh):
    parts, blocks = mesh.shape["head"], mesh.shape["ctx"]
    names = mesh.axis_names
    at = names.index("ctx")
    shape = mesh.devices.shape[:at] + (blocks // 2, 2) + mesh.devices.shape[at + 1 :]
    finer = Mesh(mesh.devices.reshape(shape), names[:at] + ("z", "core") + names[at + 1 :])
    tokens = P(("z", "core"), "head", None)
    return jax.shard_map(
        functools.partial(on_device, parts, blocks // 2),
        mesh=finer,
        in_specs=(tokens,) * 5 + (P("head"),),
        out_specs=tokens,
        check_vma=False,
    )
```

```python
import functools

import jax
import jax.numpy as jnp
from jax import lax
from jax.experimental import pallas as pl
from jax.experimental.pallas import tpu as pltpu
from jax.sharding import Mesh
from jax.sharding import PartitionSpec as P

GROUPS = 2
STEP = 8
EXTRA = 16
VMEM_LIMIT = 24 * 1024 * 1024
NN = (((1,), (0,)), ((), ()))
NT = (((1,), (1,)), ((), ()))
TN = (((0,), (0,)), ((), ()))


def dot(a, b, dims, precision=None):
    return lax.dot_general(a, b, dims, precision=precision, preferred_element_type=jnp.float32)


def exact_dot(a, b, dims):
    return dot(a, b, dims, lax.Precision.HIGHEST)


def triangle(length, keep):
    rows = lax.broadcasted_iota(jnp.int32, (length, length), 0)
    columns = lax.broadcasted_iota(jnp.int32, (length, length), 1)
    return jnp.where(keep(rows, columns), 1.0, 0.0).astype(jnp.float32)


def split(value):
    first = value.astype(jnp.bfloat16)
    left = value - first.astype(jnp.float32)
    second = left.astype(jnp.bfloat16)
    return first, second, (left - second.astype(jnp.float32)).astype(jnp.bfloat16)


def join(rows, head):
    wide = rows.astype(jnp.float32)
    return wide[3 * head : 3 * head + 1] + (
        wide[3 * head + 1 : 3 * head + 2] + wide[3 * head + 2 : 3 * head + 3]
    )


def decay_rows(totals):
    parts = [part for total in totals for part in split(total)]
    blank = jnp.zeros((EXTRA - len(parts), totals[0].shape[1]), jnp.bfloat16)
    return jnp.concatenate(parts + [blank], axis=0)


def pack_kernel(parts, decay_ref, packed_ref):
    length = packed_ref.shape[2]
    for place in range(packed_ref.shape[0]):
        start = place % parts * length
        packed_ref[place] = decay_ref[0, :, start : start + length]


def state_kernel(dim, owned, parts, me_ref, *refs):
    keys, values, decays = refs[0:2], refs[2:4], refs[4:6]
    slots, stacked_ref = refs[-1 - parts : -1], refs[-1]
    owners = STEP // owned
    turn = pl.program_id(0)
    part, core = me_ref[0], me_ref[1]
    for source in range(2):
        block = core if source == 0 else 1 - core
        decay = decays[source][0]
        length = decay.shape[1]
        weight = jnp.exp(exact_dot(decay, triangle(length, lambda u, s: u > s), NN))
        whole = jnp.broadcast_to(jnp.sum(decay, axis=1, keepdims=True), (STEP, dim))
        states = []
        for head in range(STEP):
            columns = slice(head * dim, (head + 1) * dim)
            turned = keys[source][0, :, columns].T
            decayed = turned.astype(jnp.float32) * weight[head : head + 1, :]
            states.append(
                dot(decayed.astype(jnp.bfloat16), values[source][0, :, columns], NN)
            )
        for head in range(STEP):
            owner, spot = divmod(head, owned)
            span = slice(spot * dim, (spot + 1) * dim)
            stacked_ref[turn * owners + owner, block, span, :] = states[head].astype(jnp.bfloat16)
        for owner in range(owners):
            stacked_ref[turn * owners + owner, block, owned * dim :, :] = decay_rows(
                [whole[head : head + 1] for head in range(owner * owned, (owner + 1) * owned)]
            )

    @pl.when(turn == pl.num_programs(0) - 1)
    def _():
        for slot, slot_ref in enumerate(slots):
            slot_ref[...] = stacked_ref[part ^ slot]


def inside_kernel(dim, me_ref, queries_ref, keys_ref, values_ref, decay_ref, *rest):
    inside_ref, done_ref = rest[-2:]
    decay = decay_ref[0]
    length = decay.shape[1]
    down = exact_dot(triangle(length, lambda t, u: u <= t), decay, NT)
    across = exact_dot(decay, triangle(length, lambda u, s: u <= s), NN)
    rows = lax.broadcasted_iota(jnp.int32, (length, length), 0)
    causal = rows >= lax.broadcasted_iota(jnp.int32, (length, length), 1)
    columns = [slice(head * dim, (head + 1) * dim) for head in range(STEP)]
    scores = [dot(queries_ref[0, :, c], keys_ref[0, :, c], NT) for c in columns]
    weights = []
    for head in range(STEP):
        gap = down[:, head : head + 1] - across[head : head + 1, :]
        weight = scores[head] * jnp.exp(jnp.where(causal, gap, -jnp.inf))
        weights.append(weight.astype(jnp.bfloat16))
    for head, c in enumerate(columns):
        inside_ref[:, c] = dot(weights[head], values_ref[0, :, c], NN)
    done_ref[...] = jnp.zeros_like(done_ref)


def gather_states(part, slots, stacked_ref):
    parts = len(slots)
    for slot, slot_ref in enumerate(slots):
        for block in range(2):
            stacked_ref[block * parts + (part ^ slot)] = slot_ref[block]


def total_kernel(dim, owned, parts, me_ref, *refs):
    total_ref, stacked_ref = refs[-2:]
    gather_states(me_ref[0], refs[:parts], stacked_ref)
    count = 2 * parts
    extra = [stacked_ref[at, owned * dim :, :] for at in range(count)]
    sums = []
    for head in range(owned):
        span = slice(head * dim, (head + 1) * dim)
        after = jnp.zeros((1, dim), jnp.float32)
        total = stacked_ref[count - 1, span, :].astype(jnp.float32)
        for at in range(count - 2, -1, -1):
            after += join(extra[at + 1], head)
            total += jnp.exp(after) * stacked_ref[at, span, :].astype(jnp.float32)
        total_ref[span, :] = total.astype(jnp.bfloat16)
        sums.append(after + join(extra[0], head))
    total_ref[owned * dim :, :] = decay_rows(sums)


def widen_kernel(dim, owned, me_ref, later_ref, earlier_ref, *refs):
    out_ref = refs[-1]
    later, earlier = later_ref[owned * dim :, :], earlier_ref[owned * dim :, :]
    sums = []
    for head in range(owned):
        span = slice(head * dim, (head + 1) * dim)
        after = join(later, head)
        total = later_ref[span, :].astype(jnp.float32)
        total += jnp.exp(after) * earlier_ref[span, :].astype(jnp.float32)
        out_ref[span, :] = total.astype(jnp.bfloat16)
        sums.append(after + join(earlier, head))
    out_ref[owned * dim :, :] = decay_rows(sums)


def prefix_kernel(dim, owned, parts, stretches, me_ref, gain_ref, *refs):
    stacked_ref, prefix_ref = refs[-2:]
    slots, totals = refs[:parts], refs[parts : parts + stretches]
    count = 2 * parts
    results = refs[-2 - parts : -2]
    gather_states(me_ref[0], slots, stacked_ref)
    extra = [stacked_ref[at, owned * dim :, :] for at in range(count)]
    more = [total_ref[owned * dim :, :] for total_ref in totals]
    for head in range(owned):
        span = slice(head * dim, (head + 1) * dim)
        prefix = jnp.zeros((dim, dim), jnp.float32)
        after = jnp.zeros((1, dim), jnp.float32)
        for turn, total_ref in enumerate(totals):
            prefix += jnp.exp(after) * total_ref[span, :].astype(jnp.float32)
            after += join(more[turn], head)
        for at in range(count):
            prefix_ref[at, span, :] = prefix.astype(jnp.bfloat16)
            if at < count - 1:
                prefix = jnp.exp(join(extra[at], head)) * prefix
                prefix += stacked_ref[at, span, :].astype(jnp.float32)
    size = owned * dim
    for slot, result_ref in enumerate(results):
        for block in range(2):
            result_ref[block * size : (block + 1) * size, :] = prefix_ref[
                block * parts + (me_ref[0] ^ slot)
            ]
        result_ref[2 * size :, :] = gain_ref[...]


def collect(part, block, slots, prefix_ref, gain_ref):
    parts, size, _ = prefix_ref.shape
    local = gain_ref.shape[0] // parts
    for slot, slot_ref in enumerate(slots):
        owner = part ^ slot
        prefix_ref[owner] = slot_ref[pl.ds(pl.multiple_of(block * size, size), size), :]
        rows = pl.ds(pl.multiple_of(owner * local, local), local)
        gain_ref[rows, :] = slot_ref[2 * size :, :].astype(jnp.float32)


def merge_kernel(parts, me_ref, *refs):
    collect(me_ref[0], 1 - me_ref[1], refs[:parts], *refs[-2:])


def output_kernel(
    dim, owned, parts, place, me_ref, queries_ref, inside_ref, gate_ref, decay_ref, *refs
):
    turn = pl.program_id(0)
    owners = STEP // owned
    if parts is None:
        prefix_ref, gain_ref = refs[:2]
        out_ref, done_ref = refs[-2:]
        first = 0
        gains = gain_ref[...]
    else:
        out_ref, done_ref, prefix_ref, gain_ref = refs[-4:]

        @pl.when(turn == 0)
        def _():
            collect(me_ref[0], me_ref[1], refs[:parts], prefix_ref, gain_ref)

        first = turn * owners
        gains = gain_ref[pl.ds(pl.multiple_of(place(turn, me_ref) * STEP, STEP), STEP), :]
    decay = decay_ref[0]
    length = decay.shape[1]
    down = jnp.exp(exact_dot(triangle(length, lambda t, u: u <= t), decay, NT))
    average = jnp.full((dim, dim), 1.0 / dim, jnp.bfloat16)
    columns = [slice(head * dim, (head + 1) * dim) for head in range(STEP)]
    carried = []
    for head, c in enumerate(columns):
        start = head % owned * dim
        prefix = prefix_ref[first + head // owned, start : start + dim, :]
        carried.append(dot(queries_ref[0, :, c], prefix, NN))
    mixed, means = [], []
    for head, c in enumerate(columns):
        mixed.append(inside_ref[:, c] + carried[head] * down[:, head : head + 1])
        means.append(dot((mixed[head] * mixed[head]).astype(jnp.bfloat16), average, NN))
    for head, c in enumerate(columns):
        half_gain = 0.5 * gains[head : head + 1, :]
        turned = jnp.tanh(0.5 * gate_ref[0, :, c].astype(jnp.float32))
        normed = mixed[head] * lax.rsqrt(means[head] + 1e-06) * (half_gain + half_gain * turned)
        out_ref[0, :, c] = normed.astype(jnp.bfloat16)
    done_ref[...] = jnp.zeros_like(done_ref)


def kernel_call(body, name, grid, in_specs, out_specs, out_shape, scratch=(), aliases={}, cost=0):
    return pl.pallas_call(
        body,
        grid_spec=pltpu.PrefetchScalarGridSpec(
            num_scalar_prefetch=1,
            grid=grid,
            in_specs=in_specs,
            out_specs=out_specs,
            scratch_shapes=scratch,
        ),
        out_shape=out_shape,
        input_output_aliases=aliases,
        compiler_params=pltpu.CompilerParams(vmem_limit_bytes=VMEM_LIMIT),
        cost_estimate=pl.CostEstimate(
            flops=int(1e9 * cost) + 1, transcendentals=0, bytes_accessed=1
        ),
        name=name,
    )


def on_device(parts, planes, queries, keys, values, gate, log_decay, norm_gain):
    _, length, width = queries.shape
    local = log_decay.shape[1]
    dim = width // (local * parts)
    count = 2 * parts
    half = local * parts // 2
    owned = half // (GROUPS * parts)
    rows = owned * dim + EXTRA
    per_half, per_group, per_local = half // STEP, half // GROUPS // STEP, local // STEP
    me = jnp.stack([lax.axis_index("head"), lax.axis_index("core")]).astype(jnp.int32)
    swap = [(0, 1), (1, 0)]

    values_other = lax.ppermute(values, "core", swap)
    keys_other = lax.ppermute(keys, "core", swap)
    packed = pl.pallas_call(
        functools.partial(pack_kernel, parts),
        out_shape=jax.ShapeDtypeStruct((count, local, length), jnp.float32),
        name="pack",
    )(log_decay)
    decay = lax.all_to_all(packed, ("core", "head"), 0, 0, tiled=True)
    gain = norm_gain.reshape(local, dim)

    queries, keys, values, gate = (
        pltpu.with_memory_space_constraint(array, pltpu.HBM)
        for array in (queries, keys, values, gate)
    )

    vmem = pl.BlockSpec(memory_space=pltpu.VMEM)
    hbm = pl.BlockSpec(memory_space=pl.ANY)

    def full(shape):
        return pl.BlockSpec(shape, lambda b, me: (0,) * len(shape))

    def features(place):
        return pl.BlockSpec((1, length, STEP * dim), lambda b, me: (0, 0, place(b, me)))

    def decays(place, other=False):
        def block(b, me):
            at = place(b, me)
            which = 1 - me[1] if other else me[1]
            return which * parts + at // per_local, at % per_local, 0

        return pl.BlockSpec((1, STEP, length), block)

    def exchange(slots):
        arrived = list(slots)
        for slot in sorted(range(1, parts), key=lambda s: -bin(s).count("1")):
            pairs = [(at, at ^ slot) for at in range(parts)]
            arrived[slot] = lax.ppermute(slots[slot], "head", pairs)
        return arrived

    before = ()
    held = []
    state_type = jax.ShapeDtypeStruct((2, rows, dim), jnp.bfloat16)
    for group in range(GROUPS):

        def mine(b, me, group=group):
            return me[1] * per_half + group * per_group + b

        state = kernel_call(
            functools.partial(state_kernel, dim, owned, parts),
            f"state{group}",
            (per_group,),
            [features(mine)] * 4
            + [decays(mine), decays(mine, other=True)]
            + [hbm] * len(before),
            [full(state_type.shape)] * parts,
            [state_type] * parts,
            [pltpu.VMEM((parts,) + state_type.shape, jnp.bfloat16)],
        )(me, keys, keys_other, values, values_other, decay, decay, *before)
        before = tuple(state[:1])
        held.append(exchange(state))

    pieces = 2 * GROUPS
    per_piece = 2 * per_half // pieces
    token = jax.ShapeDtypeStruct((8, 128), jnp.float32)

    def inside_part(turn, inside, before):
        at = turn % 2 * GROUPS + turn // 2

        def place(b, me):
            return at * per_piece + b

        *inside, made = kernel_call(
            functools.partial(inside_kernel, dim),
            f"inside{at}",
            (per_piece,),
            [features(place)] * 3 + [decays(place)] + [hbm] * (len(inside) + len(before)),
            [
                pl.BlockSpec((length, STEP * dim), lambda b, me: (0, place(b, me))),
                full(token.shape),
            ],
            [jax.ShapeDtypeStruct((length, width), jnp.float32), token],
            aliases={5: 0} if inside else {},
        )(me, queries, keys, values, decay, *inside, *before)
        return inside, made

    inside = ()
    arrived = []
    stacked = pltpu.VMEM((count, rows, dim), jnp.bfloat16)
    total_type = jax.ShapeDtypeStruct((rows, dim), jnp.bfloat16)

    def upward(total, far):
        return lax.ppermute(total, "z", [(at, at + far) for at in range(planes - far)])

    def widen(name, total, earlier, before):
        return kernel_call(
            functools.partial(widen_kernel, dim, owned),
            name,
            (),
            [vmem] * 2 + [hbm] * len(before),
            vmem,
            total_type,
        )(me, total, earlier, *before)

    def prefix_of(group, before):
        stretches = arrived[group]
        return kernel_call(
            functools.partial(prefix_kernel, dim, owned, parts, len(stretches)),
            f"prefix{group}",
            (),
            [vmem] * (1 + parts + len(stretches)) + [hbm] * len(before),
            [vmem] * parts,
            [prefix_type] * parts,
            [stacked, pltpu.VMEM((count, size, dim), jnp.bfloat16)],
        )(me, gain, *held[group], *stretches, *before)

    size = owned * dim
    prefix_type = jax.ShapeDtypeStruct((2 * size + local, dim), jnp.bfloat16)
    prefixes = []
    next_piece = 0
    for group in range(GROUPS):
        for _ in range(1 if group == 0 else 0):
            inside, made = inside_part(next_piece, inside, before)
            next_piece, before = next_piece + 1, (made,)
        total = kernel_call(
            functools.partial(total_kernel, dim, owned, parts),
            f"total{group}",
            (),
            [vmem] * parts + [hbm],
            vmem,
            total_type,
            [stacked],
        )(me, *held[group], *before)
        before = (total,)
        stretches, far = [upward(total, 1)], 1
        arrived.append(stretches)
        if group > 0:
            prefix = prefix_of(group - 1, before)
            before = tuple(prefix[:1])
            prefixes.append(exchange(prefix))
        while 2 * far < planes:
            if group == 0 and far == 1:
                inside, made = inside_part(next_piece, inside, before)
                next_piece, before = next_piece + 1, (made,)
            total = widen(f"widen{group}_{far}", total, stretches[-1], before)
            before = (total,)
            far *= 2
            stretches.append(upward(total, far))
        if group < GROUPS - 1:
            inside, made = inside_part(next_piece, inside, before)
            next_piece, before = next_piece + 1, (made,)
    prefix = prefix_of(GROUPS - 1, before)
    before = tuple(prefix[:1])
    prefixes.append(exchange(prefix))

    part_type = jax.ShapeDtypeStruct((parts, size, dim), jnp.bfloat16)
    gain_type = jax.ShapeDtypeStruct((parts * local, dim), jnp.float32)

    def merge(group, before, cost):
        return kernel_call(
            functools.partial(merge_kernel, parts),
            f"merge{group}",
            (),
            [vmem] * parts + [hbm] * len(before),
            [vmem] * 2,
            [part_type, gain_type],
            cost=cost,
        )(me, *prefixes[group], *before)

    def output(group, other, received, out, before, cost=0):
        def place(b, me):
            which = 1 - me[1] if other else me[1]
            return which * per_half + group * per_group + b

        if other:
            specs = [
                pl.BlockSpec((STEP // owned, size, dim), lambda b, me: (b, 0, 0)),
                pl.BlockSpec((STEP, dim), lambda b, me: (place(b, me), 0)),
            ]
            scratch = []
        else:
            specs = [full(prefix_type.shape)] * parts
            scratch = [
                pltpu.VMEM(part_type.shape, part_type.dtype),
                pltpu.VMEM(gain_type.shape, gain_type.dtype),
            ]
        *out, made = kernel_call(
            functools.partial(output_kernel, dim, owned, None if other else parts, place),
            f"output{group}_{other}",
            (per_group,),
            [
                features(place),
                pl.BlockSpec((length, STEP * dim), lambda b, me: (0, place(b, me))),
                features(place),
                decays(place),
            ]
            + specs
            + [hbm] * (len(out) + len(before)),
            [features(place), full(token.shape)],
            [jax.ShapeDtypeStruct((1, length, width), jnp.bfloat16), token],
            scratch,
            aliases={5 + len(specs): 0} if out else {},
            cost=cost,
        )(me, queries, *inside, gate, decay, *received, *out, *before)
        return out, (made,)

    out = ()
    late = None
    for group in range(GROUPS):
        last = group == GROUPS - 1
        if not last:
            out, before = output(group, 0, prefixes[group], out, before)
            while next_piece < 2 * (group + 2):
                inside, made = inside_part(next_piece, inside, before)
                next_piece, before = next_piece + 1, (made,)
        other, gains = merge(group, before, 20 if last else 0)
        other = lax.ppermute(other, "core", swap)
        before = (gains,)
        if late is not None:
            out, before = output(group - 1, 1, late, out, before, cost=20)
        late = (other, gains)
        if last:
            out, before = output(group, 0, prefixes[group], out, before, cost=20)
            out, before = output(group, 1, late, out, before)
    return out[0]


def solution(mesh):
    parts, blocks = mesh.shape["head"], mesh.shape["ctx"]
    names = mesh.axis_names
    at = names.index("ctx")
    shape = mesh.devices.shape[:at] + (blocks // 2, 2) + mesh.devices.shape[at + 1 :]
    finer = Mesh(mesh.devices.reshape(shape), names[:at] + ("z", "core") + names[at + 1 :])
    tokens = P(("z", "core"), "head", None)
    return jax.shard_map(
        functools.partial(on_device, parts, blocks // 2),
        mesh=finer,
        in_specs=(tokens,) * 5 + (P("head"),),
        out_specs=tokens,
        check_vma=False,
    )
```

```python
import functools

import jax
import jax.numpy as jnp
from jax import lax
from jax.experimental import pallas as pl
from jax.experimental.pallas import tpu as pltpu
from jax.sharding import Mesh
from jax.sharding import PartitionSpec as P

GROUPS = 2
STEP = 8
EXTRA = 16
VMEM_LIMIT = 24 * 1024 * 1024
NN = (((1,), (0,)), ((), ()))
NT = (((1,), (1,)), ((), ()))
TN = (((0,), (0,)), ((), ()))


def dot(a, b, dims, precision=None):
    return lax.dot_general(a, b, dims, precision=precision, preferred_element_type=jnp.float32)


def exact_dot(a, b, dims):
    return dot(a, b, dims, lax.Precision.HIGHEST)


def triangle(length, keep):
    rows = lax.broadcasted_iota(jnp.int32, (length, length), 0)
    columns = lax.broadcasted_iota(jnp.int32, (length, length), 1)
    return jnp.where(keep(rows, columns), 1.0, 0.0).astype(jnp.float32)


def split(value):
    first = value.astype(jnp.bfloat16)
    left = value - first.astype(jnp.float32)
    second = left.astype(jnp.bfloat16)
    return first, second, (left - second.astype(jnp.float32)).astype(jnp.bfloat16)


def join(rows, head):
    wide = rows.astype(jnp.float32)
    return wide[3 * head : 3 * head + 1] + (
        wide[3 * head + 1 : 3 * head + 2] + wide[3 * head + 2 : 3 * head + 3]
    )


def decay_rows(totals):
    parts = [part for total in totals for part in split(total)]
    blank = jnp.zeros((EXTRA - len(parts), totals[0].shape[1]), jnp.bfloat16)
    return jnp.concatenate(parts + [blank], axis=0)


def pack_kernel(parts, decay_ref, packed_ref):
    length = packed_ref.shape[2]
    for place in range(packed_ref.shape[0]):
        start = place % parts * length
        packed_ref[place] = decay_ref[0, :, start : start + length]


def state_kernel(dim, owned, parts, me_ref, *refs):
    keys, values, decays = refs[0:2], refs[2:4], refs[4:6]
    slots, stacked_ref = refs[-1 - parts : -1], refs[-1]
    owners = STEP // owned
    turn = pl.program_id(0)
    part, core = me_ref[0], me_ref[1]
    for source in range(2):
        block = core if source == 0 else 1 - core
        decay = decays[source][0]
        length = decay.shape[1]
        weight = jnp.exp(exact_dot(decay, triangle(length, lambda u, s: u > s), NN))
        whole = jnp.broadcast_to(jnp.sum(decay, axis=1, keepdims=True), (STEP, dim))
        states = []
        for head in range(STEP):
            columns = slice(head * dim, (head + 1) * dim)
            turned = keys[source][0, :, columns].T
            decayed = turned.astype(jnp.float32) * weight[head : head + 1, :]
            states.append(
                dot(decayed.astype(jnp.bfloat16), values[source][0, :, columns], NN)
            )
        for head in range(STEP):
            owner, spot = divmod(head, owned)
            span = slice(spot * dim, (spot + 1) * dim)
            stacked_ref[turn * owners + owner, block, span, :] = states[head].astype(jnp.bfloat16)
        for owner in range(owners):
            stacked_ref[turn * owners + owner, block, owned * dim :, :] = decay_rows(
                [whole[head : head + 1] for head in range(owner * owned, (owner + 1) * owned)]
            )

    @pl.when(turn == pl.num_programs(0) - 1)
    def _():
        for slot, slot_ref in enumerate(slots):
            slot_ref[...] = stacked_ref[part ^ slot]


def inside_kernel(dim, me_ref, queries_ref, keys_ref, values_ref, decay_ref, *rest):
    inside_ref, done_ref = rest[-2:]
    decay = decay_ref[0]
    length = decay.shape[1]
    down = exact_dot(triangle(length, lambda t, u: u <= t), decay, NT)
    across = exact_dot(decay, triangle(length, lambda u, s: u <= s), NN)
    rows = lax.broadcasted_iota(jnp.int32, (length, length), 0)
    causal = rows >= lax.broadcasted_iota(jnp.int32, (length, length), 1)
    columns = [slice(head * dim, (head + 1) * dim) for head in range(STEP)]
    scores = [dot(queries_ref[0, :, c], keys_ref[0, :, c], NT) for c in columns]
    weights = []
    for head in range(STEP):
        gap = down[:, head : head + 1] - across[head : head + 1, :]
        weight = scores[head] * jnp.exp(jnp.where(causal, gap, -jnp.inf))
        weights.append(weight.astype(jnp.bfloat16))
    for head, c in enumerate(columns):
        inside_ref[:, c] = dot(weights[head], values_ref[0, :, c], NN)
    done_ref[...] = jnp.zeros_like(done_ref)


def gather_states(part, slots, stacked_ref):
    parts = len(slots)
    for slot, slot_ref in enumerate(slots):
        for block in range(2):
            stacked_ref[block * parts + (part ^ slot)] = slot_ref[block]


def total_kernel(dim, owned, parts, me_ref, *refs):
    total_ref, stacked_ref = refs[-2:]
    gather_states(me_ref[0], refs[:parts], stacked_ref)
    count = 2 * parts
    extra = [stacked_ref[at, owned * dim :, :] for at in range(count)]
    sums = []
    for head in range(owned):
        span = slice(head * dim, (head + 1) * dim)
        after = jnp.zeros((1, dim), jnp.float32)
        total = stacked_ref[count - 1, span, :].astype(jnp.float32)
        for at in range(count - 2, -1, -1):
            after += join(extra[at + 1], head)
            total += jnp.exp(after) * stacked_ref[at, span, :].astype(jnp.float32)
        total_ref[span, :] = total.astype(jnp.bfloat16)
        sums.append(after + join(extra[0], head))
    total_ref[owned * dim :, :] = decay_rows(sums)


def widen_kernel(dim, owned, me_ref, later_ref, earlier_ref, *refs):
    out_ref = refs[-1]
    later, earlier = later_ref[owned * dim :, :], earlier_ref[owned * dim :, :]
    sums = []
    for head in range(owned):
        span = slice(head * dim, (head + 1) * dim)
        after = join(later, head)
        total = later_ref[span, :].astype(jnp.float32)
        total += jnp.exp(after) * earlier_ref[span, :].astype(jnp.float32)
        out_ref[span, :] = total.astype(jnp.bfloat16)
        sums.append(after + join(earlier, head))
    out_ref[owned * dim :, :] = decay_rows(sums)


def prefix_kernel(dim, owned, parts, stretches, me_ref, gain_ref, *refs):
    stacked_ref, prefix_ref = refs[-2:]
    slots, totals = refs[:parts], refs[parts : parts + stretches]
    count = 2 * parts
    results = refs[-2 - parts : -2]
    gather_states(me_ref[0], slots, stacked_ref)
    extra = [stacked_ref[at, owned * dim :, :] for at in range(count)]
    more = [total_ref[owned * dim :, :] for total_ref in totals]
    for head in range(owned):
        span = slice(head * dim, (head + 1) * dim)
        prefix = jnp.zeros((dim, dim), jnp.float32)
        after = jnp.zeros((1, dim), jnp.float32)
        for turn, total_ref in enumerate(totals):
            prefix += jnp.exp(after) * total_ref[span, :].astype(jnp.float32)
            after += join(more[turn], head)
        for at in range(count):
            prefix_ref[at, span, :] = prefix.astype(jnp.bfloat16)
            if at < count - 1:
                prefix = jnp.exp(join(extra[at], head)) * prefix
                prefix += stacked_ref[at, span, :].astype(jnp.float32)
    size = owned * dim
    for slot, result_ref in enumerate(results):
        for block in range(2):
            result_ref[block * size : (block + 1) * size, :] = prefix_ref[
                block * parts + (me_ref[0] ^ slot)
            ]
        result_ref[2 * size :, :] = gain_ref[...]


def collect(part, block, slots, prefix_ref, gain_ref):
    parts, size, _ = prefix_ref.shape
    local = gain_ref.shape[0] // parts
    for slot, slot_ref in enumerate(slots):
        owner = part ^ slot
        prefix_ref[owner] = slot_ref[pl.ds(pl.multiple_of(block * size, size), size), :]
        rows = pl.ds(pl.multiple_of(owner * local, local), local)
        gain_ref[rows, :] = slot_ref[2 * size :, :].astype(jnp.float32)


def merge_kernel(parts, me_ref, *refs):
    *others, gain_ref, prefix_ref = refs[parts:] if len(refs) == parts + 4 else refs[parts + 1 :]
    collect(me_ref[0], 1 - me_ref[1], refs[:parts], prefix_ref, gain_ref)
    each = parts // len(others)
    for turn, other_ref in enumerate(others):
        other_ref[...] = prefix_ref[turn * each : (turn + 1) * each]


def output_kernel(
    dim, owned, parts, place, me_ref, queries_ref, inside_ref, gate_ref, decay_ref, *refs
):
    turn = pl.program_id(0)
    owners = STEP // owned
    out_ref, done_ref, prefix_ref, own_gain_ref = refs[-4:]

    @pl.when(turn == 0)
    def _():
        if parts is None:
            *others, gain_ref = refs[:3]
            each = others[0].shape[0]
            for at, other_ref in enumerate(others):
                prefix_ref[at * each : (at + 1) * each] = other_ref[...]
            own_gain_ref[...] = gain_ref[...]
        else:
            collect(me_ref[0], me_ref[1], refs[:parts], prefix_ref, own_gain_ref)

    first = turn * owners
    gains = own_gain_ref[pl.ds(pl.multiple_of(place(turn, me_ref) * STEP, STEP), STEP), :]
    decay = decay_ref[0]
    length = decay.shape[1]
    down = jnp.exp(exact_dot(triangle(length, lambda t, u: u <= t), decay, NT))
    average = jnp.full((dim, dim), 1.0 / dim, jnp.bfloat16)
    columns = [slice(head * dim, (head + 1) * dim) for head in range(STEP)]
    carried = []
    for head, c in enumerate(columns):
        start = head % owned * dim
        prefix = prefix_ref[first + head // owned, start : start + dim, :]
        carried.append(dot(queries_ref[0, :, c], prefix, NN))
    mixed, means = [], []
    for head, c in enumerate(columns):
        mixed.append(inside_ref[:, c] + carried[head] * down[:, head : head + 1])
        means.append(dot((mixed[head] * mixed[head]).astype(jnp.bfloat16), average, NN))
    for head, c in enumerate(columns):
        half_gain = 0.5 * gains[head : head + 1, :]
        turned = jnp.tanh(0.5 * gate_ref[0, :, c].astype(jnp.float32))
        normed = mixed[head] * lax.rsqrt(means[head] + 1e-06) * (half_gain + half_gain * turned)
        out_ref[0, :, c] = normed.astype(jnp.bfloat16)
    done_ref[...] = jnp.zeros_like(done_ref)


def kernel_call(body, name, grid, in_specs, out_specs, out_shape, scratch=(), aliases={}, cost=0):
    return pl.pallas_call(
        body,
        grid_spec=pltpu.PrefetchScalarGridSpec(
            num_scalar_prefetch=1,
            grid=grid,
            in_specs=in_specs,
            out_specs=out_specs,
            scratch_shapes=scratch,
        ),
        out_shape=out_shape,
        input_output_aliases=aliases,
        compiler_params=pltpu.CompilerParams(vmem_limit_bytes=VMEM_LIMIT),
        cost_estimate=pl.CostEstimate(
            flops=int(1e9 * cost) + 1, transcendentals=0, bytes_accessed=1
        ),
        name=name,
    )


def on_device(parts, planes, queries, keys, values, gate, log_decay, norm_gain):
    _, length, width = queries.shape
    local = log_decay.shape[1]
    dim = width // (local * parts)
    count = 2 * parts
    half = local * parts // 2
    owned = half // (GROUPS * parts)
    rows = owned * dim + EXTRA
    per_half, per_group, per_local = half // STEP, half // GROUPS // STEP, local // STEP
    me = jnp.stack([lax.axis_index("head"), lax.axis_index("core")]).astype(jnp.int32)
    swap = [(0, 1), (1, 0)]

    values_other = lax.ppermute(values, "core", swap)
    keys_other = lax.ppermute(keys, "core", swap)
    packed = pl.pallas_call(
        functools.partial(pack_kernel, parts),
        out_shape=jax.ShapeDtypeStruct((count, local, length), jnp.float32),
        name="pack",
    )(log_decay)
    decay = lax.all_to_all(packed, ("core", "head"), 0, 0, tiled=True)
    gain = norm_gain.reshape(local, dim)

    queries, keys, values, gate = (
        pltpu.with_memory_space_constraint(array, pltpu.HBM)
        for array in (queries, keys, values, gate)
    )

    vmem = pl.BlockSpec(memory_space=pltpu.VMEM)
    hbm = pl.BlockSpec(memory_space=pl.ANY)

    def full(shape):
        return pl.BlockSpec(shape, lambda b, me: (0,) * len(shape))

    def features(place):
        return pl.BlockSpec((1, length, STEP * dim), lambda b, me: (0, 0, place(b, me)))

    def decays(place, other=False):
        def block(b, me):
            at = place(b, me)
            which = 1 - me[1] if other else me[1]
            return which * parts + at // per_local, at % per_local, 0

        return pl.BlockSpec((1, STEP, length), block)

    def exchange(slots):
        arrived = list(slots)
        for slot in sorted(range(1, parts), key=lambda s: -bin(s).count("1")):
            pairs = [(at, at ^ slot) for at in range(parts)]
            arrived[slot] = lax.ppermute(slots[slot], "head", pairs)
        return arrived

    before = ()
    held = []
    state_type = jax.ShapeDtypeStruct((2, rows, dim), jnp.bfloat16)
    for group in range(GROUPS):

        def mine(b, me, group=group):
            return me[1] * per_half + group * per_group + b

        state = kernel_call(
            functools.partial(state_kernel, dim, owned, parts),
            f"state{group}",
            (per_group,),
            [features(mine)] * 4
            + [decays(mine), decays(mine, other=True)]
            + [hbm] * len(before),
            [full(state_type.shape)] * parts,
            [state_type] * parts,
            [pltpu.VMEM((parts,) + state_type.shape, jnp.bfloat16)],
        )(me, keys, keys_other, values, values_other, decay, decay, *before)
        before = tuple(state[:1])
        held.append(exchange(state))

    pieces = 2 * GROUPS
    per_piece = 2 * per_half // pieces
    token = jax.ShapeDtypeStruct((8, 128), jnp.float32)

    def inside_part(turn, inside, before, cost=0):
        at = turn % 2 * GROUPS + turn // 2

        def place(b, me):
            return at * per_piece + b

        *inside, made = kernel_call(
            functools.partial(inside_kernel, dim),
            f"inside{at}",
            (per_piece,),
            [features(place)] * 3 + [decays(place)] + [hbm] * (len(inside) + len(before)),
            [
                pl.BlockSpec((length, STEP * dim), lambda b, me: (0, place(b, me))),
                full(token.shape),
            ],
            [jax.ShapeDtypeStruct((length, width), jnp.float32), token],
            aliases={5: 0} if inside else {},
            cost=cost,
        )(me, queries, keys, values, decay, *inside, *before)
        return inside, made

    inside = ()
    arrived = []
    stacked = pltpu.VMEM((count, rows, dim), jnp.bfloat16)
    total_type = jax.ShapeDtypeStruct((rows, dim), jnp.bfloat16)

    def upward(total, far):
        return lax.ppermute(total, "z", [(at, at + far) for at in range(planes - far)])

    def widen(name, total, earlier, before):
        return kernel_call(
            functools.partial(widen_kernel, dim, owned),
            name,
            (),
            [vmem] * 2 + [hbm] * len(before),
            vmem,
            total_type,
        )(me, total, earlier, *before)

    def prefix_of(group, before):
        stretches = arrived[group]
        return kernel_call(
            functools.partial(prefix_kernel, dim, owned, parts, len(stretches)),
            f"prefix{group}",
            (),
            [vmem] * (1 + parts + len(stretches)) + [hbm] * len(before),
            [vmem] * parts,
            [prefix_type] * parts,
            [stacked, pltpu.VMEM((count, size, dim), jnp.bfloat16)],
        )(me, gain, *held[group], *stretches, *before)

    size = owned * dim
    prefix_type = jax.ShapeDtypeStruct((2 * size + local, dim), jnp.bfloat16)
    prefixes = []
    next_piece = 0
    for group in range(GROUPS):
        for _ in range(1 if group == 0 else 0):
            inside, made = inside_part(next_piece, inside, before)
            next_piece, before = next_piece + 1, (made,)
        total = kernel_call(
            functools.partial(total_kernel, dim, owned, parts),
            f"total{group}",
            (),
            [vmem] * parts + [hbm],
            vmem,
            total_type,
            [stacked],
        )(me, *held[group], *before)
        before = (total,)
        stretches, far = [upward(total, 1)], 1
        arrived.append(stretches)
        if group > 0:
            prefix = prefix_of(group - 1, before)
            before = tuple(prefix[:1])
            prefixes.append(exchange(prefix))
        while 2 * far < planes:
            if group == 0 and far == 1:
                inside, made = inside_part(next_piece, inside, before)
                next_piece, before = next_piece + 1, (made,)
            total = widen(f"widen{group}_{far}", total, stretches[-1], before)
            before = (total,)
            far *= 2
            stretches.append(upward(total, far))
        inside, made = inside_part(next_piece, inside, before, 2 if group > 0 else 0)
        next_piece, before = next_piece + 1, (made,)
    prefix = prefix_of(GROUPS - 1, before)
    before = tuple(prefix[:1])
    prefixes.append(exchange(prefix))

    part_type = jax.ShapeDtypeStruct((parts, size, dim), jnp.bfloat16)
    half_type = jax.ShapeDtypeStruct((parts // 2, size, dim), jnp.bfloat16)
    gain_type = jax.ShapeDtypeStruct((parts * local, dim), jnp.float32)

    def merge(group, before, cost):
        return kernel_call(
            functools.partial(merge_kernel, parts),
            f"merge{group}",
            (),
            [vmem] * parts + [hbm] * len(before),
            [vmem] * 3,
            [half_type, half_type, gain_type],
            [pltpu.VMEM(part_type.shape, part_type.dtype)],
            cost=cost,
        )(me, *prefixes[group], *before)

    def output(group, other, received, out, before, cost=0):
        def place(b, me):
            which = 1 - me[1] if other else me[1]
            return which * per_half + group * per_group + b

        if other:
            specs = [full(half_type.shape)] * 2 + [full(gain_type.shape)]
        else:
            specs = [full(prefix_type.shape)] * parts
        scratch = [
            pltpu.VMEM(part_type.shape, part_type.dtype),
            pltpu.VMEM(gain_type.shape, gain_type.dtype),
        ]
        *out, made = kernel_call(
            functools.partial(output_kernel, dim, owned, None if other else parts, place),
            f"output{group}_{other}",
            (per_group,),
            [
                features(place),
                pl.BlockSpec((length, STEP * dim), lambda b, me: (0, place(b, me))),
                features(place),
                decays(place),
            ]
            + specs
            + [hbm] * (len(out) + len(before)),
            [features(place), full(token.shape)],
            [jax.ShapeDtypeStruct((1, length, width), jnp.bfloat16), token],
            scratch,
            aliases={5 + len(specs): 0} if out else {},
            cost=cost,
        )(me, queries, *inside, gate, decay, *received, *out, *before)
        return out, (made,)

    out = ()
    for group in range(GROUPS):
        last = group == GROUPS - 1
        if not last:
            out, before = output(group, 0, prefixes[group], out, before)
        *others, gains = merge(group, before, 0)
        others = [lax.ppermute(other, "core", swap) for other in others]
        before = (gains,)
        if last:
            out, before = output(group, 0, prefixes[group], out, before, cost=20)
        out, before = output(group, 1, (*others, gains), out, before)
    return out[0]


def solution(mesh):
    parts, blocks = mesh.shape["head"], mesh.shape["ctx"]
    names = mesh.axis_names
    at = names.index("ctx")
    shape = mesh.devices.shape[:at] + (blocks // 2, 2) + mesh.devices.shape[at + 1 :]
    finer = Mesh(mesh.devices.reshape(shape), names[:at] + ("z", "core") + names[at + 1 :])
    tokens = P(("z", "core"), "head", None)
    return jax.shard_map(
        functools.partial(on_device, parts, blocks // 2),
        mesh=finer,
        in_specs=(tokens,) * 5 + (P("head"),),
        out_specs=tokens,
        check_vma=False,
    )
```

```python
import functools

import jax
import jax.numpy as jnp
from jax import lax
from jax.experimental import pallas as pl
from jax.experimental.pallas import tpu as pltpu
from jax.sharding import Mesh
from jax.sharding import PartitionSpec as P

GROUPS = 2
STEP = 8
EXTRA = 16
VMEM_LIMIT = 24 * 1024 * 1024
NN = (((1,), (0,)), ((), ()))
NT = (((1,), (1,)), ((), ()))
TN = (((0,), (0,)), ((), ()))


def dot(a, b, dims, precision=None):
    return lax.dot_general(a, b, dims, precision=precision, preferred_element_type=jnp.float32)


def exact_dot(a, b, dims):
    return dot(a, b, dims, lax.Precision.HIGHEST)


def triangle(length, keep):
    rows = lax.broadcasted_iota(jnp.int32, (length, length), 0)
    columns = lax.broadcasted_iota(jnp.int32, (length, length), 1)
    return jnp.where(keep(rows, columns), 1.0, 0.0).astype(jnp.float32)


def split(value):
    first = value.astype(jnp.bfloat16)
    left = value - first.astype(jnp.float32)
    second = left.astype(jnp.bfloat16)
    return first, second, (left - second.astype(jnp.float32)).astype(jnp.bfloat16)


def join(rows, head):
    wide = rows.astype(jnp.float32)
    return wide[3 * head : 3 * head + 1] + (
        wide[3 * head + 1 : 3 * head + 2] + wide[3 * head + 2 : 3 * head + 3]
    )


def decay_rows(totals):
    parts = [part for total in totals for part in split(total)]
    blank = jnp.zeros((EXTRA - len(parts), totals[0].shape[1]), jnp.bfloat16)
    return jnp.concatenate(parts + [blank], axis=0)


def pack_kernel(parts, decay_ref, packed_ref):
    length = packed_ref.shape[2]
    for place in range(packed_ref.shape[0]):
        start = place % parts * length
        packed_ref[place] = decay_ref[0, :, start : start + length]


def load_kernel(count, *refs):
    sources, copies, done = refs[:count], refs[-1 - count : -1], refs[-1]
    moves = [
        pltpu.make_async_copy(source, copy, done.at[at])
        for at, (source, copy) in enumerate(zip(sources, copies))
    ]
    for move in moves:
        move.start()
    for move in moves:
        move.wait()


def heads_at(first, head, dim):
    return pl.ds(pl.multiple_of((first + head) * dim, dim), dim)


def decays_at(decay_ref, block, first):
    local = decay_ref.shape[1]
    parts = decay_ref.shape[0] // 2
    rows = pl.ds(pl.multiple_of(first % local, STEP), STEP)
    return decay_ref[block * parts + first // local, rows, :]


def state_kernel(dim, owned, parts, half, begin, count, me_ref, *refs):
    keys, values, decay_ref = refs[0:2], refs[2:4], refs[4]
    stacked_ref = refs[-1]
    slots = refs[-1 - parts : -1]
    part, core = me_ref[0], me_ref[1]
    for turn in range(count // STEP):
        first = core * half + begin + turn * STEP
        for source in range(2):
            block = core if source == 0 else 1 - core
            decay = decays_at(decay_ref, block, first)
            length = decay.shape[1]
            weight = jnp.exp(exact_dot(decay, triangle(length, lambda u, s: u > s), NN))
            whole = jnp.broadcast_to(jnp.sum(decay, axis=1, keepdims=True), (STEP, dim))
            states = []
            for head in range(STEP):
                columns = heads_at(first, head, dim)
                turned = keys[source][0, :, columns].T
                decayed = turned.astype(jnp.float32) * weight[head : head + 1, :]
                states.append(
                    dot(decayed.astype(jnp.bfloat16), values[source][0, :, columns], NN)
                )
            for head in range(STEP):
                owner, spot = divmod(turn * STEP + head, owned)
                span = slice(spot * dim, (spot + 1) * dim)
                stacked_ref[owner, block, span, :] = states[head].astype(jnp.bfloat16)
            for at in range(STEP // owned):
                stacked_ref[turn * STEP // owned + at, block, owned * dim :, :] = decay_rows(
                    [whole[head : head + 1] for head in range(at * owned, (at + 1) * owned)]
                )
    for slot, slot_ref in enumerate(slots):
        slot_ref[...] = stacked_ref[part ^ slot]


def inside_kernel(
    dim, half, begin, count, other, me_ref, queries_ref, keys_ref, values_ref, decay_ref, *rest
):
    inside_ref, done_ref = rest[-2:]
    core = me_ref[1]
    length = decay_ref.shape[2]
    rows = lax.broadcasted_iota(jnp.int32, (length, length), 0)
    causal = rows >= lax.broadcasted_iota(jnp.int32, (length, length), 1)
    for turn in range(count // STEP):
        first = (1 - core if other else core) * half + begin + turn * STEP
        decay = decays_at(decay_ref, core, first)
        down = exact_dot(triangle(length, lambda t, u: u <= t), decay, NT)
        across = exact_dot(decay, triangle(length, lambda u, s: u <= s), NN)
        columns = [heads_at(first, head, dim) for head in range(STEP)]
        scores = [dot(queries_ref[0, :, c], keys_ref[0, :, c], NT) for c in columns]
        weights = []
        for head in range(STEP):
            gap = down[:, head : head + 1] - across[head : head + 1, :]
            weight = scores[head] * jnp.exp(jnp.where(causal, gap, -jnp.inf))
            weights.append(weight.astype(jnp.bfloat16))
        for head, c in enumerate(columns):
            at = (turn * STEP + head) * dim
            inside_ref[:, at : at + dim] = dot(weights[head], values_ref[0, :, c], NN)
    done_ref[...] = jnp.zeros_like(done_ref)


def gather_states(part, slots, stacked_ref):
    parts = len(slots)
    for slot, slot_ref in enumerate(slots):
        for block in range(2):
            stacked_ref[block * parts + (part ^ slot)] = slot_ref[block]


def total_kernel(dim, owned, parts, me_ref, *refs):
    total_ref, stacked_ref = refs[-2:]
    gather_states(me_ref[0], refs[:parts], stacked_ref)
    count = 2 * parts
    extra = [stacked_ref[at, owned * dim :, :] for at in range(count)]
    sums = []
    for head in range(owned):
        span = slice(head * dim, (head + 1) * dim)
        after = jnp.zeros((1, dim), jnp.float32)
        total = stacked_ref[count - 1, span, :].astype(jnp.float32)
        for at in range(count - 2, -1, -1):
            after += join(extra[at + 1], head)
            total += jnp.exp(after) * stacked_ref[at, span, :].astype(jnp.float32)
        total_ref[span, :] = total.astype(jnp.bfloat16)
        sums.append(after + join(extra[0], head))
    total_ref[owned * dim :, :] = decay_rows(sums)


def widen_kernel(dim, owned, me_ref, later_ref, earlier_ref, *refs):
    out_ref = refs[-1]
    later, earlier = later_ref[owned * dim :, :], earlier_ref[owned * dim :, :]
    sums = []
    for head in range(owned):
        span = slice(head * dim, (head + 1) * dim)
        after = join(later, head)
        total = later_ref[span, :].astype(jnp.float32)
        total += jnp.exp(after) * earlier_ref[span, :].astype(jnp.float32)
        out_ref[span, :] = total.astype(jnp.bfloat16)
        sums.append(after + join(earlier, head))
    out_ref[owned * dim :, :] = decay_rows(sums)


def prefix_kernel(dim, owned, parts, stretches, me_ref, gain_ref, *refs):
    stacked_ref, prefix_ref = refs[-2:]
    slots, totals = refs[:parts], refs[parts : parts + stretches]
    count = 2 * parts
    results = refs[-2 - parts : -2]
    gather_states(me_ref[0], slots, stacked_ref)
    extra = [stacked_ref[at, owned * dim :, :] for at in range(count)]
    more = [total_ref[owned * dim :, :] for total_ref in totals]
    for head in range(owned):
        span = slice(head * dim, (head + 1) * dim)
        prefix = jnp.zeros((dim, dim), jnp.float32)
        after = jnp.zeros((1, dim), jnp.float32)
        for turn, total_ref in enumerate(totals):
            prefix += jnp.exp(after) * total_ref[span, :].astype(jnp.float32)
            after += join(more[turn], head)
        for at in range(count):
            prefix_ref[at, span, :] = prefix.astype(jnp.bfloat16)
            if at < count - 1:
                prefix = jnp.exp(join(extra[at], head)) * prefix
                prefix += stacked_ref[at, span, :].astype(jnp.float32)
    size = owned * dim
    for slot, result_ref in enumerate(results):
        for block in range(2):
            result_ref[block * size : (block + 1) * size, :] = prefix_ref[
                block * parts + (me_ref[0] ^ slot)
            ]
        result_ref[2 * size :, :] = gain_ref[...]


def collect(part, block, slots, prefix_ref, gain_ref):
    parts, size, _ = prefix_ref.shape
    local = gain_ref.shape[0] // parts
    for slot, slot_ref in enumerate(slots):
        owner = part ^ slot
        prefix_ref[owner] = slot_ref[pl.ds(pl.multiple_of(block * size, size), size), :]
        rows = pl.ds(pl.multiple_of(owner * local, local), local)
        gain_ref[rows, :] = slot_ref[2 * size :, :].astype(jnp.float32)


def merge_kernel(parts, me_ref, *refs):
    *others, gain_ref, prefix_ref = refs[parts:] if len(refs) == parts + 4 else refs[parts + 1 :]
    collect(me_ref[0], 1 - me_ref[1], refs[:parts], prefix_ref, gain_ref)
    each = parts // len(others)
    for turn, other_ref in enumerate(others):
        other_ref[...] = prefix_ref[turn * each : (turn + 1) * each]


def output_kernel(
    dim, owned, half, begin, count, parts, me_ref,
    queries_ref, inside_ref, gate_ref, decay_ref, *refs,
):
    out_ref, done_ref, prefix_ref, gain_ref, result_ref, sent = refs[-6:]
    core = me_ref[1]
    if parts is None:
        *others, gains = refs[:3]
        each = others[0].shape[0]
        prefixes = [others[at // each].at[at % each] for at in range(each * len(others))]
    else:
        collect(me_ref[0], core, refs[:parts], prefix_ref, gain_ref)
        prefixes, gains = [prefix_ref.at[at] for at in range(parts)], gain_ref
    length = decay_ref.shape[2]
    average = jnp.full((dim, dim), 1.0 / dim, jnp.bfloat16)
    moves = []
    for turn in range(count // STEP):
        first = (1 - core if parts is None else core) * half + begin + turn * STEP
        decay = decays_at(decay_ref, core, first)
        gain = gains[pl.ds(pl.multiple_of(first, STEP), STEP), :]
        down = jnp.exp(exact_dot(triangle(length, lambda t, u: u <= t), decay, NT))
        columns = [heads_at(first, head, dim) for head in range(STEP)]
        carried = []
        for head, c in enumerate(columns):
            owner, spot = divmod(turn * STEP + head, owned)
            prefix = prefixes[owner][spot * dim : (spot + 1) * dim, :]
            carried.append(dot(queries_ref[0, :, c], prefix, NN))
        mixed, means = [], []
        for head in range(STEP):
            at = (turn * STEP + head) * dim
            mixed.append(inside_ref[:, at : at + dim] + carried[head] * down[:, head : head + 1])
            means.append(dot((mixed[head] * mixed[head]).astype(jnp.bfloat16), average, NN))
        for head, c in enumerate(columns):
            half_gain = 0.5 * gain[head : head + 1, :]
            turned = jnp.tanh(0.5 * gate_ref[0, :, c].astype(jnp.float32))
            normed = mixed[head] * lax.rsqrt(means[head] + 1e-06) * (half_gain + half_gain * turned)
            result_ref[turn, :, head * dim : (head + 1) * dim] = normed.astype(jnp.bfloat16)
        width = STEP * dim
        moves.append(
            pltpu.make_async_copy(
                result_ref.at[turn],
                out_ref.at[0, :, pl.ds(pl.multiple_of(first * dim, width), width)],
                sent.at[turn],
            )
        )
        moves[-1].start()
    done_ref[...] = jnp.zeros_like(done_ref)
    for move in moves:
        move.wait()


def kernel_call(body, name, in_specs, out_specs, out_shape, scratch=(), aliases={}, cost=0):
    return pl.pallas_call(
        body,
        grid_spec=pltpu.PrefetchScalarGridSpec(
            num_scalar_prefetch=1,
            grid=(),
            in_specs=in_specs,
            out_specs=out_specs,
            scratch_shapes=scratch,
        ),
        out_shape=out_shape,
        input_output_aliases=aliases,
        compiler_params=pltpu.CompilerParams(vmem_limit_bytes=VMEM_LIMIT),
        cost_estimate=pl.CostEstimate(
            flops=int(1e9 * cost) + 1, transcendentals=0, bytes_accessed=1
        ),
        name=name,
    )


def on_device(parts, planes, queries, keys, values, gate, log_decay, norm_gain):
    _, length, width = queries.shape
    local = log_decay.shape[1]
    dim = width // (local * parts)
    count = 2 * parts
    half = local * parts // 2
    owned = half // (GROUPS * parts)
    rows = owned * dim + EXTRA
    me = jnp.stack([lax.axis_index("head"), lax.axis_index("core")]).astype(jnp.int32)
    swap = [(0, 1), (1, 0)]

    values_other = lax.ppermute(values, "core", swap)
    keys_other = lax.ppermute(keys, "core", swap)
    packed = pl.pallas_call(
        functools.partial(pack_kernel, parts),
        out_shape=jax.ShapeDtypeStruct((count, local, length), jnp.float32),
        name="pack",
    )(log_decay)
    decay = lax.all_to_all(packed, ("core", "head"), 0, 0, tiled=True)
    gain = norm_gain.reshape(local, dim)

    vmem = pl.BlockSpec(memory_space=pltpu.VMEM)
    hbm = pl.BlockSpec(memory_space=pl.ANY)

    def in_vmem(array):
        return pltpu.with_memory_space_constraint(array, pltpu.VMEM)

    sources = [
        pltpu.with_memory_space_constraint(array, pltpu.HBM)
        for array in (keys, values, queries, gate)
    ]
    loaded = pl.pallas_call(
        functools.partial(load_kernel, len(sources)),
        in_specs=[hbm] * (len(sources) + 1),
        out_specs=[vmem] * len(sources),
        out_shape=[pltpu.VMEM(array.shape, array.dtype) for array in sources],
        scratch_shapes=[pltpu.SemaphoreType.DMA((len(sources),))],
        compiler_params=pltpu.CompilerParams(vmem_limit_bytes=VMEM_LIMIT),
        cost_estimate=pl.CostEstimate(flops=1, transcendentals=0, bytes_accessed=1),
        name="load",
    )(*sources, packed)
    keys, values, queries, gate = (in_vmem(array) for array in loaded)
    keys_other, values_other = in_vmem(keys_other), in_vmem(values_other)

    def exchange(slots):
        arrived = list(slots)
        for slot in sorted(range(1, parts), key=lambda s: -bin(s).count("1")):
            pairs = [(at, at ^ slot) for at in range(parts)]
            arrived[slot] = lax.ppermute(slots[slot], "head", pairs)
        return arrived

    before = ()
    held = []
    state_type = jax.ShapeDtypeStruct((2, rows, dim), jnp.bfloat16)
    share = half // GROUPS
    for group in range(GROUPS):
        state = kernel_call(
            functools.partial(state_kernel, dim, owned, parts, half, group * share, share),
            f"state{group}",
            [vmem] * 5 + [hbm] * len(before),
            [vmem] * parts,
            [state_type] * parts,
            [pltpu.VMEM((parts,) + state_type.shape, jnp.bfloat16)],
        )(me, keys, keys_other, values, values_other, decay, *before)
        before = tuple(state[:1])
        held.append(exchange(state))

    token = jax.ShapeDtypeStruct((8, 128), jnp.float32)
    inside = {}

    def inside_part(before, cost=0):
        group, other = divmod(len(inside), 2)
        inside[group, other], made = kernel_call(
            functools.partial(inside_kernel, dim, half, group * share, share, other),
            f"inside{group}_{other}",
            [vmem] * 4 + [hbm] * len(before),
            [vmem] * 2,
            [pltpu.VMEM((length, share * dim), jnp.float32), token],
            cost=cost,
        )(me, queries, keys, values, decay, *before)
        return (made,)

    arrived = []
    stacked = pltpu.VMEM((count, rows, dim), jnp.bfloat16)
    total_type = jax.ShapeDtypeStruct((rows, dim), jnp.bfloat16)

    def upward(total, far):
        return lax.ppermute(total, "z", [(at, at + far) for at in range(planes - far)])

    def widen(name, total, earlier, before):
        return kernel_call(
            functools.partial(widen_kernel, dim, owned),
            name,
            [vmem] * 2 + [hbm] * len(before),
            vmem,
            total_type,
        )(me, total, earlier, *before)

    def prefix_of(group, before):
        stretches = arrived[group]
        return kernel_call(
            functools.partial(prefix_kernel, dim, owned, parts, len(stretches)),
            f"prefix{group}",
            [vmem] * (1 + parts + len(stretches)) + [hbm] * len(before),
            [vmem] * parts,
            [prefix_type] * parts,
            [stacked, pltpu.VMEM((count, size, dim), jnp.bfloat16)],
        )(me, gain, *held[group], *stretches, *before)

    size = owned * dim
    prefix_type = jax.ShapeDtypeStruct((2 * size + local, dim), jnp.bfloat16)
    prefixes = []
    for group in range(GROUPS):
        if group == 0:
            before = inside_part(before)
        total = kernel_call(
            functools.partial(total_kernel, dim, owned, parts),
            f"total{group}",
            [vmem] * parts + [hbm],
            vmem,
            total_type,
            [stacked],
        )(me, *held[group], *before)
        before = (total,)
        stretches, far = [upward(total, 1)], 1
        arrived.append(stretches)
        if group > 0:
            prefix = prefix_of(group - 1, before)
            before = tuple(prefix[:1])
            prefixes.append(exchange(prefix))
        while 2 * far < planes:
            if group == 0 and far == 1:
                before = inside_part(before)
            total = widen(f"widen{group}_{far}", total, stretches[-1], before)
            before = (total,)
            far *= 2
            stretches.append(upward(total, far))
        before = inside_part(before, 2 if group > 0 else 0)
    while len(inside) < 2 * GROUPS:
        before = inside_part(before)
    prefix = prefix_of(GROUPS - 1, before)
    before = tuple(prefix[:1])
    prefixes.append(exchange(prefix))

    part_type = jax.ShapeDtypeStruct((parts, size, dim), jnp.bfloat16)
    half_type = jax.ShapeDtypeStruct((parts // 2, size, dim), jnp.bfloat16)
    gain_type = jax.ShapeDtypeStruct((parts * local, dim), jnp.float32)

    def merge(group, before, cost):
        return kernel_call(
            functools.partial(merge_kernel, parts),
            f"merge{group}",
            [vmem] * parts + [hbm] * len(before),
            [vmem] * 3,
            [half_type, half_type, gain_type],
            [pltpu.VMEM(part_type.shape, part_type.dtype)],
            cost=cost,
        )(me, *prefixes[group], *before)

    def output(group, other, received, out, before, cost=0):
        *out, made = kernel_call(
            functools.partial(
                output_kernel, dim, owned, half, group * share, share, None if other else parts
            ),
            f"output{group}_{other}",
            [vmem] * (4 + len(received)) + [hbm] * (len(out) + len(before)),
            [hbm, vmem],
            [pltpu.HBM((1, length, width), jnp.bfloat16), token],
            [
                pltpu.VMEM(part_type.shape, part_type.dtype),
                pltpu.VMEM(gain_type.shape, gain_type.dtype),
                pltpu.VMEM((share // STEP, length, STEP * dim), jnp.bfloat16),
                pltpu.SemaphoreType.DMA((share // STEP,)),
            ],
            aliases={5 + len(received): 0} if out else {},
            cost=cost,
        )(me, queries, in_vmem(inside[group, other]), gate, decay, *received, *out, *before)
        return out, (made,)

    out = ()
    for group in range(GROUPS):
        last = group == GROUPS - 1
        if not last:
            out, before = output(group, 0, prefixes[group], out, before)
        *others, gains = merge(group, before, 0)
        others = [lax.ppermute(other, "core", swap) for other in others]
        before = (gains,)
        if last:
            out, before = output(group, 0, prefixes[group], out, before, cost=20)
        out, before = output(group, 1, (*others, gains), out, before)
    return out[0]


def solution(mesh):
    parts, blocks = mesh.shape["head"], mesh.shape["ctx"]
    names = mesh.axis_names
    at = names.index("ctx")
    shape = mesh.devices.shape[:at] + (blocks // 2, 2) + mesh.devices.shape[at + 1 :]
    finer = Mesh(mesh.devices.reshape(shape), names[:at] + ("z", "core") + names[at + 1 :])
    tokens = P(("z", "core"), "head", None)
    return jax.shard_map(
        functools.partial(on_device, parts, blocks // 2),
        mesh=finer,
        in_specs=(tokens,) * 5 + (P("head"),),
        out_specs=tokens,
        check_vma=False,
    )
```

```python
import functools

import jax
import jax.numpy as jnp
from jax import lax
from jax.experimental import pallas as pl
from jax.experimental.pallas import tpu as pltpu
from jax.sharding import Mesh
from jax.sharding import PartitionSpec as P

GROUPS = 2
STEP = 8
EXTRA = 16
VMEM_LIMIT = 8 * 1024 * 1024
NN = (((1,), (0,)), ((), ()))
NT = (((1,), (1,)), ((), ()))
TN = (((0,), (0,)), ((), ()))


def dot(a, b, dims, precision=None):
    return lax.dot_general(a, b, dims, precision=precision, preferred_element_type=jnp.float32)


def exact_dot(a, b, dims):
    return dot(a, b, dims, lax.Precision.HIGHEST)


def triangle(length, keep):
    rows = lax.broadcasted_iota(jnp.int32, (length, length), 0)
    columns = lax.broadcasted_iota(jnp.int32, (length, length), 1)
    return jnp.where(keep(rows, columns), 1.0, 0.0).astype(jnp.float32)


def split(value):
    first = value.astype(jnp.bfloat16)
    left = value - first.astype(jnp.float32)
    second = left.astype(jnp.bfloat16)
    return first, second, (left - second.astype(jnp.float32)).astype(jnp.bfloat16)


def join(rows, head):
    wide = rows.astype(jnp.float32)
    return wide[3 * head : 3 * head + 1] + (
        wide[3 * head + 1 : 3 * head + 2] + wide[3 * head + 2 : 3 * head + 3]
    )


def decay_rows(totals):
    parts = [part for total in totals for part in split(total)]
    blank = jnp.zeros((EXTRA - len(parts), totals[0].shape[1]), jnp.bfloat16)
    return jnp.concatenate(parts + [blank], axis=0)


def pack_kernel(parts, decay_ref, packed_ref):
    length = packed_ref.shape[2]
    for place in range(packed_ref.shape[0]):
        start = place % parts * length
        packed_ref[place] = decay_ref[0, :, start : start + length]


def load_kernel(count, *refs):
    sources, copies, done = refs[:count], refs[-1 - count : -1], refs[-1]
    moves = [
        pltpu.make_async_copy(source, copy, done.at[at])
        for at, (source, copy) in enumerate(zip(sources, copies))
    ]
    for move in moves:
        move.start()
    for move in moves:
        move.wait()


def heads_at(first, head, dim):
    return pl.ds(pl.multiple_of((first + head) * dim, dim), dim)


def decays_at(decay_ref, block, first):
    local = decay_ref.shape[1]
    parts = decay_ref.shape[0] // 2
    rows = pl.ds(pl.multiple_of(first % local, STEP), STEP)
    return decay_ref[block * parts + first // local, rows, :]


def state_kernel(dim, owned, parts, half, begin, count, me_ref, *refs):
    keys_ref, values_ref, decay_ref, *others = refs[:5]
    stacked_ref, other_ref, done = refs[-3:]
    slots = refs[-3 - parts : -3]
    part, core = me_ref[0], me_ref[1]
    width = count * dim
    columns = pl.ds(pl.multiple_of((core * half + begin) * dim, width), width)
    moves = [
        pltpu.make_async_copy(ref.at[0, :, columns], other_ref.at[at], done.at[at])
        for at, ref in enumerate(others)
    ]
    for move in moves:
        move.start()
    for source in range(2):
        block = core if source == 0 else 1 - core
        if source == 1:
            for move in moves:
                move.wait()
        for turn in range(count // STEP):
            first = core * half + begin + turn * STEP
            decay = decays_at(decay_ref, block, first)
            length = decay.shape[1]
            weight = jnp.exp(exact_dot(decay, triangle(length, lambda u, s: u > s), NN))
            whole = jnp.broadcast_to(jnp.sum(decay, axis=1, keepdims=True), (STEP, dim))
            states = []
            for head in range(STEP):
                if source == 0:
                    c = heads_at(first, head, dim)
                    key, value = keys_ref[0, :, c], values_ref[0, :, c]
                else:
                    at = (turn * STEP + head) * dim
                    key, value = other_ref[0, :, at : at + dim], other_ref[1, :, at : at + dim]
                decayed = key.T.astype(jnp.float32) * weight[head : head + 1, :]
                states.append(dot(decayed.astype(jnp.bfloat16), value, NN))
            for head in range(STEP):
                owner, spot = divmod(turn * STEP + head, owned)
                span = slice(spot * dim, (spot + 1) * dim)
                stacked_ref[owner, block, span, :] = states[head].astype(jnp.bfloat16)
            for at in range(STEP // owned):
                stacked_ref[turn * STEP // owned + at, block, owned * dim :, :] = decay_rows(
                    [whole[head : head + 1] for head in range(at * owned, (at + 1) * owned)]
                )
    for slot, slot_ref in enumerate(slots):
        slot_ref[...] = stacked_ref[part ^ slot]


def inside_kernel(
    dim, half, begin, count, other, me_ref, queries_ref, keys_ref, values_ref, decay_ref, *rest
):
    inside_ref, done_ref = rest[-2:]
    core = me_ref[1]
    length = decay_ref.shape[2]
    rows = lax.broadcasted_iota(jnp.int32, (length, length), 0)
    causal = rows >= lax.broadcasted_iota(jnp.int32, (length, length), 1)
    for turn in range(count // STEP):
        first = (1 - core if other else core) * half + begin + turn * STEP
        decay = decays_at(decay_ref, core, first)
        down = exact_dot(triangle(length, lambda t, u: u <= t), decay, NT)
        across = exact_dot(decay, triangle(length, lambda u, s: u <= s), NN)
        columns = [heads_at(first, head, dim) for head in range(STEP)]
        scores = [dot(queries_ref[0, :, c], keys_ref[0, :, c], NT) for c in columns]
        weights = []
        for head in range(STEP):
            gap = down[:, head : head + 1] - across[head : head + 1, :]
            weight = scores[head] * jnp.exp(jnp.where(causal, gap, -jnp.inf))
            weights.append(weight.astype(jnp.bfloat16))
        for head, c in enumerate(columns):
            at = (turn * STEP + head) * dim
            inside_ref[:, at : at + dim] = dot(weights[head], values_ref[0, :, c], NN)
    done_ref[...] = jnp.zeros_like(done_ref)


def gather_states(part, slots, stacked_ref):
    parts = len(slots)
    for slot, slot_ref in enumerate(slots):
        for block in range(2):
            stacked_ref[block * parts + (part ^ slot)] = slot_ref[block]


def total_kernel(dim, owned, parts, me_ref, *refs):
    total_ref, stacked_ref = refs[-2:]
    gather_states(me_ref[0], refs[:parts], stacked_ref)
    count = 2 * parts
    extra = [stacked_ref[at, owned * dim :, :] for at in range(count)]
    sums = []
    for head in range(owned):
        span = slice(head * dim, (head + 1) * dim)
        after = jnp.zeros((1, dim), jnp.float32)
        total = stacked_ref[count - 1, span, :].astype(jnp.float32)
        for at in range(count - 2, -1, -1):
            after += join(extra[at + 1], head)
            total += jnp.exp(after) * stacked_ref[at, span, :].astype(jnp.float32)
        total_ref[span, :] = total.astype(jnp.bfloat16)
        sums.append(after + join(extra[0], head))
    total_ref[owned * dim :, :] = decay_rows(sums)


def widen_kernel(dim, owned, me_ref, later_ref, earlier_ref, *refs):
    out_ref = refs[-1]
    later, earlier = later_ref[owned * dim :, :], earlier_ref[owned * dim :, :]
    sums = []
    for head in range(owned):
        span = slice(head * dim, (head + 1) * dim)
        after = join(later, head)
        total = later_ref[span, :].astype(jnp.float32)
        total += jnp.exp(after) * earlier_ref[span, :].astype(jnp.float32)
        out_ref[span, :] = total.astype(jnp.bfloat16)
        sums.append(after + join(earlier, head))
    out_ref[owned * dim :, :] = decay_rows(sums)


def prefix_kernel(dim, owned, parts, stretches, me_ref, gain_ref, *refs):
    stacked_ref, prefix_ref = refs[-2:]
    slots, totals = refs[:parts], refs[parts : parts + stretches]
    count = 2 * parts
    results = refs[-2 - parts : -2]
    gather_states(me_ref[0], slots, stacked_ref)
    extra = [stacked_ref[at, owned * dim :, :] for at in range(count)]
    more = [total_ref[owned * dim :, :] for total_ref in totals]
    for head in range(owned):
        span = slice(head * dim, (head + 1) * dim)
        prefix = jnp.zeros((dim, dim), jnp.float32)
        after = jnp.zeros((1, dim), jnp.float32)
        for turn, total_ref in enumerate(totals):
            prefix += jnp.exp(after) * total_ref[span, :].astype(jnp.float32)
            after += join(more[turn], head)
        for at in range(count):
            prefix_ref[at, span, :] = prefix.astype(jnp.bfloat16)
            if at < count - 1:
                prefix = jnp.exp(join(extra[at], head)) * prefix
                prefix += stacked_ref[at, span, :].astype(jnp.float32)
    size = owned * dim
    for slot, result_ref in enumerate(results):
        for block in range(2):
            result_ref[block * size : (block + 1) * size, :] = prefix_ref[
                block * parts + (me_ref[0] ^ slot)
            ]
        result_ref[2 * size :, :] = gain_ref[...]


def collect(part, block, slots, prefix_ref, gain_ref):
    parts, size, _ = prefix_ref.shape
    local = gain_ref.shape[0] // parts
    for slot, slot_ref in enumerate(slots):
        owner = part ^ slot
        prefix_ref[owner] = slot_ref[pl.ds(pl.multiple_of(block * size, size), size), :]
        rows = pl.ds(pl.multiple_of(owner * local, local), local)
        gain_ref[rows, :] = slot_ref[2 * size :, :].astype(jnp.float32)


def merge_kernel(parts, me_ref, *refs):
    *others, gain_ref, prefix_ref = refs[parts:] if len(refs) == parts + 4 else refs[parts + 1 :]
    collect(me_ref[0], 1 - me_ref[1], refs[:parts], prefix_ref, gain_ref)
    each = parts // len(others)
    for turn, other_ref in enumerate(others):
        other_ref[...] = prefix_ref[turn * each : (turn + 1) * each]


def output_kernel(
    dim, owned, half, begin, count, parts, me_ref,
    queries_ref, inside_ref, gate_ref, decay_ref, *refs,
):
    out_ref, done_ref, prefix_ref, gain_ref, result_ref, sent = refs[-6:]
    core = me_ref[1]
    if parts is None:
        *others, gains = refs[:3]
        each = others[0].shape[0]
        prefixes = [others[at // each].at[at % each] for at in range(each * len(others))]
    else:
        collect(me_ref[0], core, refs[:parts], prefix_ref, gain_ref)
        prefixes, gains = [prefix_ref.at[at] for at in range(parts)], gain_ref
    length = decay_ref.shape[2]
    average = jnp.full((dim, dim), 1.0 / dim, jnp.bfloat16)
    moves = []
    for turn in range(count // STEP):
        first = (1 - core if parts is None else core) * half + begin + turn * STEP
        decay = decays_at(decay_ref, core, first)
        gain = gains[pl.ds(pl.multiple_of(first, STEP), STEP), :]
        down = jnp.exp(exact_dot(triangle(length, lambda t, u: u <= t), decay, NT))
        columns = [heads_at(first, head, dim) for head in range(STEP)]
        carried = []
        for head, c in enumerate(columns):
            owner, spot = divmod(turn * STEP + head, owned)
            prefix = prefixes[owner][spot * dim : (spot + 1) * dim, :]
            carried.append(dot(queries_ref[0, :, c], prefix, NN))
        mixed, means = [], []
        for head in range(STEP):
            at = (turn * STEP + head) * dim
            mixed.append(inside_ref[:, at : at + dim] + carried[head] * down[:, head : head + 1])
            means.append(dot((mixed[head] * mixed[head]).astype(jnp.bfloat16), average, NN))
        for head, c in enumerate(columns):
            half_gain = 0.5 * gain[head : head + 1, :]
            turned = jnp.tanh(0.5 * gate_ref[0, :, c].astype(jnp.float32))
            normed = mixed[head] * lax.rsqrt(means[head] + 1e-06) * (half_gain + half_gain * turned)
            result_ref[turn, :, head * dim : (head + 1) * dim] = normed.astype(jnp.bfloat16)
        width = STEP * dim
        moves.append(
            pltpu.make_async_copy(
                result_ref.at[turn],
                out_ref.at[0, :, pl.ds(pl.multiple_of(first * dim, width), width)],
                sent.at[turn],
            )
        )
        moves[-1].start()
    done_ref[...] = jnp.zeros_like(done_ref)
    for move in moves:
        move.wait()


def kernel_call(body, name, in_specs, out_specs, out_shape, scratch=(), aliases={}, cost=0):
    return pl.pallas_call(
        body,
        grid_spec=pltpu.PrefetchScalarGridSpec(
            num_scalar_prefetch=1,
            grid=(),
            in_specs=in_specs,
            out_specs=out_specs,
            scratch_shapes=scratch,
        ),
        out_shape=out_shape,
        input_output_aliases=aliases,
        compiler_params=pltpu.CompilerParams(vmem_limit_bytes=VMEM_LIMIT),
        cost_estimate=pl.CostEstimate(
            flops=int(1e9 * cost) + 1, transcendentals=0, bytes_accessed=1
        ),
        name=name,
    )


def on_device(parts, planes, queries, keys, values, gate, log_decay, norm_gain):
    _, length, width = queries.shape
    local = log_decay.shape[1]
    dim = width // (local * parts)
    count = 2 * parts
    half = local * parts // 2
    owned = half // (GROUPS * parts)
    rows = owned * dim + EXTRA
    me = jnp.stack([lax.axis_index("head"), lax.axis_index("core")]).astype(jnp.int32)
    swap = [(0, 1), (1, 0)]

    values_other = lax.ppermute(values, "core", swap)
    keys_other = lax.ppermute(keys, "core", swap)
    packed = pl.pallas_call(
        functools.partial(pack_kernel, parts),
        out_shape=jax.ShapeDtypeStruct((count, local, length), jnp.float32),
        name="pack",
    )(log_decay)
    decay = lax.all_to_all(packed, ("core", "head"), 0, 0, tiled=True)
    gain = norm_gain.reshape(local, dim)

    vmem = pl.BlockSpec(memory_space=pltpu.VMEM)
    hbm = pl.BlockSpec(memory_space=pl.ANY)

    def in_vmem(array):
        return pltpu.with_memory_space_constraint(array, pltpu.VMEM)

    sources = [
        pltpu.with_memory_space_constraint(array, pltpu.HBM)
        for array in (keys, values, queries, gate)
    ]
    loaded = pl.pallas_call(
        functools.partial(load_kernel, len(sources)),
        in_specs=[hbm] * (len(sources) + 1),
        out_specs=[vmem] * len(sources),
        out_shape=[pltpu.VMEM(array.shape, array.dtype) for array in sources],
        scratch_shapes=[pltpu.SemaphoreType.DMA((len(sources),))],
        compiler_params=pltpu.CompilerParams(vmem_limit_bytes=VMEM_LIMIT),
        cost_estimate=pl.CostEstimate(flops=1, transcendentals=0, bytes_accessed=1),
        name="load",
    )(*sources, packed)
    keys, values, queries, gate = (in_vmem(array) for array in loaded)

    def exchange(slots):
        arrived = list(slots)
        for slot in sorted(range(1, parts), key=lambda s: -bin(s).count("1")):
            pairs = [(at, at ^ slot) for at in range(parts)]
            arrived[slot] = lax.ppermute(slots[slot], "head", pairs)
        return arrived

    before = ()
    held = []
    state_type = jax.ShapeDtypeStruct((2, rows, dim), jnp.bfloat16)
    share = half // GROUPS
    for group in range(GROUPS):
        state = kernel_call(
            functools.partial(state_kernel, dim, owned, parts, half, group * share, share),
            f"state{group}",
            [vmem] * 3 + [hbm] * (2 + len(before)),
            [vmem] * parts,
            [state_type] * parts,
            [
                pltpu.VMEM((parts,) + state_type.shape, jnp.bfloat16),
                pltpu.VMEM((2, length, share * dim), jnp.bfloat16),
                pltpu.SemaphoreType.DMA((2,)),
            ],
        )(me, keys, values, decay, keys_other, values_other, *before)
        before = tuple(state[:1])
        held.append(exchange(state))

    token = jax.ShapeDtypeStruct((8, 128), jnp.float32)
    inside = {}

    def inside_part(before, cost=0):
        group, other = divmod(len(inside), 2)
        inside[group, other], made = kernel_call(
            functools.partial(inside_kernel, dim, half, group * share, share, other),
            f"inside{group}_{other}",
            [vmem] * 4 + [hbm] * len(before),
            [vmem] * 2,
            [pltpu.VMEM((length, share * dim), jnp.float32), token],
            cost=cost,
        )(me, queries, keys, values, decay, *before)
        return (made,)

    arrived = []
    stacked = pltpu.VMEM((count, rows, dim), jnp.bfloat16)
    total_type = jax.ShapeDtypeStruct((rows, dim), jnp.bfloat16)

    def upward(total, far):
        return lax.ppermute(total, "z", [(at, at + far) for at in range(planes - far)])

    def widen(name, total, earlier, before):
        return kernel_call(
            functools.partial(widen_kernel, dim, owned),
            name,
            [vmem] * 2 + [hbm] * len(before),
            vmem,
            total_type,
        )(me, total, earlier, *before)

    def prefix_of(group, before):
        stretches = arrived[group]
        return kernel_call(
            functools.partial(prefix_kernel, dim, owned, parts, len(stretches)),
            f"prefix{group}",
            [vmem] * (1 + parts + len(stretches)) + [hbm] * len(before),
            [vmem] * parts,
            [prefix_type] * parts,
            [stacked, pltpu.VMEM((count, size, dim), jnp.bfloat16)],
        )(me, gain, *held[group], *stretches, *before)

    size = owned * dim
    prefix_type = jax.ShapeDtypeStruct((2 * size + local, dim), jnp.bfloat16)
    prefixes = []
    for group in range(GROUPS):
        if group == 0:
            before = inside_part(before)
        total = kernel_call(
            functools.partial(total_kernel, dim, owned, parts),
            f"total{group}",
            [vmem] * parts + [hbm],
            vmem,
            total_type,
            [stacked],
        )(me, *held[group], *before)
        before = (total,)
        stretches, far = [upward(total, 1)], 1
        arrived.append(stretches)
        if group > 0:
            prefix = prefix_of(group - 1, before)
            before = tuple(prefix[:1])
            prefixes.append(exchange(prefix))
        while 2 * far < planes:
            if group == 0 and far == 1:
                before = inside_part(before)
            total = widen(f"widen{group}_{far}", total, stretches[-1], before)
            before = (total,)
            far *= 2
            stretches.append(upward(total, far))
        before = inside_part(before, 2 if group > 0 else 0)
    while len(inside) < 2 * GROUPS:
        before = inside_part(before)
    prefix = prefix_of(GROUPS - 1, before)
    before = tuple(prefix[:1])
    prefixes.append(exchange(prefix))

    part_type = jax.ShapeDtypeStruct((parts, size, dim), jnp.bfloat16)
    half_type = jax.ShapeDtypeStruct((parts // 2, size, dim), jnp.bfloat16)
    gain_type = jax.ShapeDtypeStruct((parts * local, dim), jnp.float32)

    def merge(group, before, cost):
        return kernel_call(
            functools.partial(merge_kernel, parts),
            f"merge{group}",
            [vmem] * parts + [hbm] * len(before),
            [vmem] * 3,
            [half_type, half_type, gain_type],
            [pltpu.VMEM(part_type.shape, part_type.dtype)],
            cost=cost,
        )(me, *prefixes[group], *before)

    def output(group, other, received, out, before, cost=0):
        *out, made = kernel_call(
            functools.partial(
                output_kernel, dim, owned, half, group * share, share, None if other else parts
            ),
            f"output{group}_{other}",
            [vmem] * (4 + len(received)) + [hbm] * (len(out) + len(before)),
            [hbm, vmem],
            [pltpu.HBM((1, length, width), jnp.bfloat16), token],
            [
                pltpu.VMEM(part_type.shape, part_type.dtype),
                pltpu.VMEM(gain_type.shape, gain_type.dtype),
                pltpu.VMEM((share // STEP, length, STEP * dim), jnp.bfloat16),
                pltpu.SemaphoreType.DMA((share // STEP,)),
            ],
            aliases={5 + len(received): 0} if out else {},
            cost=cost,
        )(me, queries, in_vmem(inside[group, other]), gate, decay, *received, *out, *before)
        return out, (made,)

    out = ()
    for group in range(GROUPS):
        last = group == GROUPS - 1
        if not last:
            out, before = output(group, 0, prefixes[group], out, before)
        *others, gains = merge(group, before, 0)
        others = [lax.ppermute(other, "core", swap) for other in others]
        before = (gains,)
        if last:
            out, before = output(group, 0, prefixes[group], out, before, cost=20)
        out, before = output(group, 1, (*others, gains), out, before)
    return out[0]


def solution(mesh):
    parts, blocks = mesh.shape["head"], mesh.shape["ctx"]
    names = mesh.axis_names
    at = names.index("ctx")
    shape = mesh.devices.shape[:at] + (blocks // 2, 2) + mesh.devices.shape[at + 1 :]
    finer = Mesh(mesh.devices.reshape(shape), names[:at] + ("z", "core") + names[at + 1 :])
    tokens = P(("z", "core"), "head", None)
    return jax.shard_map(
        functools.partial(on_device, parts, blocks // 2),
        mesh=finer,
        in_specs=(tokens,) * 5 + (P("head"),),
        out_specs=tokens,
        check_vma=False,
    )
```

```python
import functools

import jax
import jax.numpy as jnp
from jax import lax
from jax.experimental import pallas as pl
from jax.experimental.pallas import tpu as pltpu
from jax.sharding import Mesh
from jax.sharding import PartitionSpec as P

GROUPS = 2
STEP = 8
EXTRA = 16
VMEM_LIMIT = 8 * 1024 * 1024
NN = (((1,), (0,)), ((), ()))
NT = (((1,), (1,)), ((), ()))
TN = (((0,), (0,)), ((), ()))


def dot(a, b, dims, precision=None):
    return lax.dot_general(a, b, dims, precision=precision, preferred_element_type=jnp.float32)


def exact_dot(a, b, dims):
    return dot(a, b, dims, lax.Precision.HIGHEST)


def triangle(length, keep):
    rows = lax.broadcasted_iota(jnp.int32, (length, length), 0)
    columns = lax.broadcasted_iota(jnp.int32, (length, length), 1)
    return jnp.where(keep(rows, columns), 1.0, 0.0).astype(jnp.float32)


def split(value):
    first = value.astype(jnp.bfloat16)
    left = value - first.astype(jnp.float32)
    second = left.astype(jnp.bfloat16)
    return first, second, (left - second.astype(jnp.float32)).astype(jnp.bfloat16)


def join(rows, head):
    wide = rows.astype(jnp.float32)
    return wide[3 * head : 3 * head + 1] + (
        wide[3 * head + 1 : 3 * head + 2] + wide[3 * head + 2 : 3 * head + 3]
    )


def decay_rows(totals):
    parts = [part for total in totals for part in split(total)]
    blank = jnp.zeros((EXTRA - len(parts), totals[0].shape[1]), jnp.bfloat16)
    return jnp.concatenate(parts + [blank], axis=0)


def pack_kernel(parts, decay_ref, packed_ref):
    length = packed_ref.shape[2]
    for place in range(packed_ref.shape[0]):
        start = place % parts * length
        packed_ref[place] = decay_ref[0, :, start : start + length]


def heads_at(first, head, dim):
    return pl.ds(pl.multiple_of((first + head) * dim, dim), dim)


def decays_at(decay_ref, block, first):
    local = decay_ref.shape[1]
    parts = decay_ref.shape[0] // 2
    rows = pl.ds(pl.multiple_of(first % local, STEP), STEP)
    return decay_ref[block * parts + first // local, rows, :]


def state_kernel(dim, owned, parts, half, begin, count, me_ref, *refs):
    decay_ref, *arrays = refs[:5]
    stacked_ref, copy_ref, done = refs[-3:]
    slots = refs[-3 - parts : -3]
    part, core = me_ref[0], me_ref[1]
    width = count * dim
    columns = pl.ds(pl.multiple_of((core * half + begin) * dim, width), width)
    moves = [
        pltpu.make_async_copy(ref.at[0, :, columns], copy_ref.at[at], done.at[at])
        for at, ref in enumerate(arrays)
    ]
    for move in moves:
        move.start()
    for source in range(2):
        block = core if source == 0 else 1 - core
        for move in moves[2 * source : 2 * source + 2]:
            move.wait()
        for turn in range(count // STEP):
            first = core * half + begin + turn * STEP
            decay = decays_at(decay_ref, block, first)
            length = decay.shape[1]
            weight = jnp.exp(exact_dot(decay, triangle(length, lambda u, s: u > s), NN))
            whole = jnp.broadcast_to(jnp.sum(decay, axis=1, keepdims=True), (STEP, dim))
            states = []
            for head in range(STEP):
                at = (turn * STEP + head) * dim
                key = copy_ref[2 * source, :, at : at + dim]
                value = copy_ref[2 * source + 1, :, at : at + dim]
                decayed = key.T.astype(jnp.float32) * weight[head : head + 1, :]
                states.append(dot(decayed.astype(jnp.bfloat16), value, NN))
            for head in range(STEP):
                owner, spot = divmod(turn * STEP + head, owned)
                span = slice(spot * dim, (spot + 1) * dim)
                stacked_ref[owner, block, span, :] = states[head].astype(jnp.bfloat16)
            for at in range(STEP // owned):
                stacked_ref[turn * STEP // owned + at, block, owned * dim :, :] = decay_rows(
                    [whole[head : head + 1] for head in range(at * owned, (at + 1) * owned)]
                )
    for slot, slot_ref in enumerate(slots):
        slot_ref[...] = stacked_ref[part ^ slot]


def inside_kernel(
    dim, half, begin, count, other, me_ref, queries_ref, keys_ref, values_ref, decay_ref, *rest
):
    inside_ref, done_ref = rest[-2:]
    core = me_ref[1]
    length = decay_ref.shape[2]
    rows = lax.broadcasted_iota(jnp.int32, (length, length), 0)
    causal = rows >= lax.broadcasted_iota(jnp.int32, (length, length), 1)
    for turn in range(count // STEP):
        first = (1 - core if other else core) * half + begin + turn * STEP
        decay = decays_at(decay_ref, core, first)
        down = exact_dot(triangle(length, lambda t, u: u <= t), decay, NT)
        across = exact_dot(decay, triangle(length, lambda u, s: u <= s), NN)
        columns = [heads_at(first, head, dim) for head in range(STEP)]
        scores = [dot(queries_ref[0, :, c], keys_ref[0, :, c], NT) for c in columns]
        weights = []
        for head in range(STEP):
            gap = down[:, head : head + 1] - across[head : head + 1, :]
            weight = scores[head] * jnp.exp(jnp.where(causal, gap, -jnp.inf))
            weights.append(weight.astype(jnp.bfloat16))
        for head, c in enumerate(columns):
            at = (turn * STEP + head) * dim
            inside_ref[:, at : at + dim] = dot(weights[head], values_ref[0, :, c], NN)
    done_ref[...] = jnp.zeros_like(done_ref)


def gather_states(part, slots, stacked_ref):
    parts = len(slots)
    for slot, slot_ref in enumerate(slots):
        for block in range(2):
            stacked_ref[block * parts + (part ^ slot)] = slot_ref[block]


def total_kernel(dim, owned, parts, me_ref, *refs):
    total_ref, stacked_ref = refs[-2:]
    gather_states(me_ref[0], refs[:parts], stacked_ref)
    count = 2 * parts
    extra = [stacked_ref[at, owned * dim :, :] for at in range(count)]
    sums = []
    for head in range(owned):
        span = slice(head * dim, (head + 1) * dim)
        after = jnp.zeros((1, dim), jnp.float32)
        total = stacked_ref[count - 1, span, :].astype(jnp.float32)
        for at in range(count - 2, -1, -1):
            after += join(extra[at + 1], head)
            total += jnp.exp(after) * stacked_ref[at, span, :].astype(jnp.float32)
        total_ref[span, :] = total.astype(jnp.bfloat16)
        sums.append(after + join(extra[0], head))
    total_ref[owned * dim :, :] = decay_rows(sums)


def widen_kernel(dim, owned, me_ref, later_ref, earlier_ref, *refs):
    out_ref = refs[-1]
    later, earlier = later_ref[owned * dim :, :], earlier_ref[owned * dim :, :]
    sums = []
    for head in range(owned):
        span = slice(head * dim, (head + 1) * dim)
        after = join(later, head)
        total = later_ref[span, :].astype(jnp.float32)
        total += jnp.exp(after) * earlier_ref[span, :].astype(jnp.float32)
        out_ref[span, :] = total.astype(jnp.bfloat16)
        sums.append(after + join(earlier, head))
    out_ref[owned * dim :, :] = decay_rows(sums)


def prefix_kernel(dim, owned, parts, stretches, me_ref, gain_ref, *refs):
    stacked_ref, prefix_ref = refs[-2:]
    slots, totals = refs[:parts], refs[parts : parts + stretches]
    count = 2 * parts
    results = refs[-2 - parts : -2]
    gather_states(me_ref[0], slots, stacked_ref)
    extra = [stacked_ref[at, owned * dim :, :] for at in range(count)]
    more = [total_ref[owned * dim :, :] for total_ref in totals]
    for head in range(owned):
        span = slice(head * dim, (head + 1) * dim)
        prefix = jnp.zeros((dim, dim), jnp.float32)
        after = jnp.zeros((1, dim), jnp.float32)
        for turn, total_ref in enumerate(totals):
            prefix += jnp.exp(after) * total_ref[span, :].astype(jnp.float32)
            after += join(more[turn], head)
        for at in range(count):
            prefix_ref[at, span, :] = prefix.astype(jnp.bfloat16)
            if at < count - 1:
                prefix = jnp.exp(join(extra[at], head)) * prefix
                prefix += stacked_ref[at, span, :].astype(jnp.float32)
    size = owned * dim
    for slot, result_ref in enumerate(results):
        for block in range(2):
            result_ref[block * size : (block + 1) * size, :] = prefix_ref[
                block * parts + (me_ref[0] ^ slot)
            ]
        result_ref[2 * size :, :] = gain_ref[...]


def collect(part, block, slots, prefix_ref, gain_ref):
    parts, size, _ = prefix_ref.shape
    local = gain_ref.shape[0] // parts
    for slot, slot_ref in enumerate(slots):
        owner = part ^ slot
        prefix_ref[owner] = slot_ref[pl.ds(pl.multiple_of(block * size, size), size), :]
        rows = pl.ds(pl.multiple_of(owner * local, local), local)
        gain_ref[rows, :] = slot_ref[2 * size :, :].astype(jnp.float32)


def merge_kernel(parts, me_ref, *refs):
    *others, gain_ref, prefix_ref = refs[parts:] if len(refs) == parts + 4 else refs[parts + 1 :]
    collect(me_ref[0], 1 - me_ref[1], refs[:parts], prefix_ref, gain_ref)
    each = parts // len(others)
    for turn, other_ref in enumerate(others):
        other_ref[...] = prefix_ref[turn * each : (turn + 1) * each]


def output_kernel(
    dim, owned, half, begin, count, parts, me_ref,
    queries_ref, inside_ref, gate_ref, decay_ref, *refs,
):
    out_ref, done_ref, prefix_ref, gain_ref, result_ref, sent = refs[-6:]
    core = me_ref[1]
    if parts is None:
        *others, gains = refs[:3]
        each = others[0].shape[0]
        prefixes = [others[at // each].at[at % each] for at in range(each * len(others))]
    else:
        collect(me_ref[0], core, refs[:parts], prefix_ref, gain_ref)
        prefixes, gains = [prefix_ref.at[at] for at in range(parts)], gain_ref
    length = decay_ref.shape[2]
    average = jnp.full((dim, dim), 1.0 / dim, jnp.bfloat16)
    moves = []
    for turn in range(count // STEP):
        first = (1 - core if parts is None else core) * half + begin + turn * STEP
        decay = decays_at(decay_ref, core, first)
        gain = gains[pl.ds(pl.multiple_of(first, STEP), STEP), :]
        down = jnp.exp(exact_dot(triangle(length, lambda t, u: u <= t), decay, NT))
        columns = [heads_at(first, head, dim) for head in range(STEP)]
        carried = []
        for head, c in enumerate(columns):
            owner, spot = divmod(turn * STEP + head, owned)
            prefix = prefixes[owner][spot * dim : (spot + 1) * dim, :]
            carried.append(dot(queries_ref[0, :, c], prefix, NN))
        mixed, means = [], []
        for head in range(STEP):
            at = (turn * STEP + head) * dim
            mixed.append(inside_ref[:, at : at + dim] + carried[head] * down[:, head : head + 1])
            means.append(dot((mixed[head] * mixed[head]).astype(jnp.bfloat16), average, NN))
        for head, c in enumerate(columns):
            half_gain = 0.5 * gain[head : head + 1, :]
            turned = jnp.tanh(0.5 * gate_ref[0, :, c].astype(jnp.float32))
            normed = mixed[head] * lax.rsqrt(means[head] + 1e-06) * (half_gain + half_gain * turned)
            result_ref[turn, :, head * dim : (head + 1) * dim] = normed.astype(jnp.bfloat16)
        width = STEP * dim
        moves.append(
            pltpu.make_async_copy(
                result_ref.at[turn],
                out_ref.at[0, :, pl.ds(pl.multiple_of(first * dim, width), width)],
                sent.at[turn],
            )
        )
        moves[-1].start()
    done_ref[...] = jnp.zeros_like(done_ref)
    for move in moves:
        move.wait()


def kernel_call(body, name, in_specs, out_specs, out_shape, scratch=(), aliases={}, cost=0):
    return pl.pallas_call(
        body,
        grid_spec=pltpu.PrefetchScalarGridSpec(
            num_scalar_prefetch=1,
            grid=(),
            in_specs=in_specs,
            out_specs=out_specs,
            scratch_shapes=scratch,
        ),
        out_shape=out_shape,
        input_output_aliases=aliases,
        compiler_params=pltpu.CompilerParams(vmem_limit_bytes=VMEM_LIMIT),
        cost_estimate=pl.CostEstimate(
            flops=int(1e9 * cost) + 1, transcendentals=0, bytes_accessed=1
        ),
        name=name,
    )


def on_device(parts, planes, queries, keys, values, gate, log_decay, norm_gain):
    _, length, width = queries.shape
    local = log_decay.shape[1]
    dim = width // (local * parts)
    count = 2 * parts
    half = local * parts // 2
    owned = half // (GROUPS * parts)
    rows = owned * dim + EXTRA
    me = jnp.stack([lax.axis_index("head"), lax.axis_index("core")]).astype(jnp.int32)
    swap = [(0, 1), (1, 0)]

    values_other = lax.ppermute(values, "core", swap)
    keys_other = lax.ppermute(keys, "core", swap)
    packed = pl.pallas_call(
        functools.partial(pack_kernel, parts),
        out_shape=jax.ShapeDtypeStruct((count, local, length), jnp.float32),
        name="pack",
    )(log_decay)
    decay = lax.all_to_all(packed, ("core", "head"), 0, 0, tiled=True)
    gain = norm_gain.reshape(local, dim)

    vmem = pl.BlockSpec(memory_space=pltpu.VMEM)
    hbm = pl.BlockSpec(memory_space=pl.ANY)

    def in_vmem(array):
        return pltpu.with_memory_space_constraint(array, pltpu.VMEM)

    def in_hbm(array):
        return pltpu.with_memory_space_constraint(array, pltpu.HBM)

    own = in_hbm(keys), in_hbm(values)
    keys, values, queries, gate = (in_vmem(array) for array in (keys, values, queries, gate))

    def exchange(slots):
        arrived = list(slots)
        for slot in sorted(range(1, parts), key=lambda s: -bin(s).count("1")):
            pairs = [(at, at ^ slot) for at in range(parts)]
            arrived[slot] = lax.ppermute(slots[slot], "head", pairs)
        return arrived

    before = ()
    held = []
    state_type = jax.ShapeDtypeStruct((2, rows, dim), jnp.bfloat16)
    share = half // GROUPS
    for group in range(GROUPS):
        state = kernel_call(
            functools.partial(state_kernel, dim, owned, parts, half, group * share, share),
            f"state{group}",
            [vmem] + [hbm] * (4 + len(before)),
            [vmem] * parts,
            [state_type] * parts,
            [
                pltpu.VMEM((parts,) + state_type.shape, jnp.bfloat16),
                pltpu.VMEM((4, length, share * dim), jnp.bfloat16),
                pltpu.SemaphoreType.DMA((4,)),
            ],
        )(me, decay, *own, keys_other, values_other, *before)
        before = tuple(state[:1])
        held.append(exchange(state))

    token = jax.ShapeDtypeStruct((8, 128), jnp.float32)
    inside = {}

    def inside_part(before, cost=0):
        group, other = divmod(len(inside), 2)
        inside[group, other], made = kernel_call(
            functools.partial(inside_kernel, dim, half, group * share, share, other),
            f"inside{group}_{other}",
            [vmem] * 4 + [hbm] * len(before),
            [vmem] * 2,
            [pltpu.VMEM((length, share * dim), jnp.float32), token],
            cost=cost,
        )(me, queries, keys, values, decay, *before)
        return (made,)

    arrived = []
    stacked = pltpu.VMEM((count, rows, dim), jnp.bfloat16)
    total_type = jax.ShapeDtypeStruct((rows, dim), jnp.bfloat16)

    def upward(total, far):
        return lax.ppermute(total, "z", [(at, at + far) for at in range(planes - far)])

    def widen(name, total, earlier, before):
        return kernel_call(
            functools.partial(widen_kernel, dim, owned),
            name,
            [vmem] * 2 + [hbm] * len(before),
            vmem,
            total_type,
        )(me, total, earlier, *before)

    def prefix_of(group, before):
        stretches = arrived[group]
        return kernel_call(
            functools.partial(prefix_kernel, dim, owned, parts, len(stretches)),
            f"prefix{group}",
            [vmem] * (1 + parts + len(stretches)) + [hbm] * len(before),
            [vmem] * parts,
            [prefix_type] * parts,
            [stacked, pltpu.VMEM((count, size, dim), jnp.bfloat16)],
        )(me, gain, *held[group], *stretches, *before)

    size = owned * dim
    prefix_type = jax.ShapeDtypeStruct((2 * size + local, dim), jnp.bfloat16)
    prefixes = []
    for group in range(GROUPS):
        if group == 0:
            before = inside_part(before)
        total = kernel_call(
            functools.partial(total_kernel, dim, owned, parts),
            f"total{group}",
            [vmem] * parts + [hbm],
            vmem,
            total_type,
            [stacked],
        )(me, *held[group], *before)
        before = (total,)
        stretches, far = [upward(total, 1)], 1
        arrived.append(stretches)
        if group > 0:
            prefix = prefix_of(group - 1, before)
            before = tuple(prefix[:1])
            prefixes.append(exchange(prefix))
        while 2 * far < planes:
            if group == 0 and far == 1:
                before = inside_part(before)
            total = widen(f"widen{group}_{far}", total, stretches[-1], before)
            before = (total,)
            far *= 2
            stretches.append(upward(total, far))
        before = inside_part(before, 2 if group > 0 else 0)
    while len(inside) < 2 * GROUPS:
        before = inside_part(before)
    prefix = prefix_of(GROUPS - 1, before)
    before = tuple(prefix[:1])
    prefixes.append(exchange(prefix))

    part_type = jax.ShapeDtypeStruct((parts, size, dim), jnp.bfloat16)
    half_type = jax.ShapeDtypeStruct((parts // 2, size, dim), jnp.bfloat16)
    gain_type = jax.ShapeDtypeStruct((parts * local, dim), jnp.float32)

    def merge(group, before, cost):
        return kernel_call(
            functools.partial(merge_kernel, parts),
            f"merge{group}",
            [vmem] * parts + [hbm] * len(before),
            [vmem] * 3,
            [half_type, half_type, gain_type],
            [pltpu.VMEM(part_type.shape, part_type.dtype)],
            cost=cost,
        )(me, *prefixes[group], *before)

    def output(group, other, received, out, before, cost=0):
        *out, made = kernel_call(
            functools.partial(
                output_kernel, dim, owned, half, group * share, share, None if other else parts
            ),
            f"output{group}_{other}",
            [vmem] * (4 + len(received)) + [hbm] * (len(out) + len(before)),
            [hbm, vmem],
            [pltpu.HBM((1, length, width), jnp.bfloat16), token],
            [
                pltpu.VMEM(part_type.shape, part_type.dtype),
                pltpu.VMEM(gain_type.shape, gain_type.dtype),
                pltpu.VMEM((share // STEP, length, STEP * dim), jnp.bfloat16),
                pltpu.SemaphoreType.DMA((share // STEP,)),
            ],
            aliases={5 + len(received): 0} if out else {},
            cost=cost,
        )(me, queries, in_vmem(inside[group, other]), gate, decay, *received, *out, *before)
        return out, (made,)

    out = ()
    for group in range(GROUPS):
        last = group == GROUPS - 1
        if not last:
            out, before = output(group, 0, prefixes[group], out, before)
        *others, gains = merge(group, before, 0)
        others = [lax.ppermute(other, "core", swap) for other in others]
        before = (gains,)
        if last:
            out, before = output(group, 0, prefixes[group], out, before, cost=20)
        out, before = output(group, 1, (*others, gains), out, before)
    return out[0]


def solution(mesh):
    parts, blocks = mesh.shape["head"], mesh.shape["ctx"]
    names = mesh.axis_names
    at = names.index("ctx")
    shape = mesh.devices.shape[:at] + (blocks // 2, 2) + mesh.devices.shape[at + 1 :]
    finer = Mesh(mesh.devices.reshape(shape), names[:at] + ("z", "core") + names[at + 1 :])
    tokens = P(("z", "core"), "head", None)
    return jax.shard_map(
        functools.partial(on_device, parts, blocks // 2),
        mesh=finer,
        in_specs=(tokens,) * 5 + (P("head"),),
        out_specs=tokens,
        check_vma=False,
    )
```

```python
import functools

import jax
import jax.numpy as jnp
from jax import lax
from jax.experimental import pallas as pl
from jax.experimental.pallas import tpu as pltpu
from jax.sharding import Mesh
from jax.sharding import PartitionSpec as P

GROUPS = 2
STEP = 8
EXTRA = 16
VMEM_LIMIT = 8 * 1024 * 1024
NN = (((1,), (0,)), ((), ()))
NT = (((1,), (1,)), ((), ()))
TN = (((0,), (0,)), ((), ()))


def dot(a, b, dims, precision=None):
    return lax.dot_general(a, b, dims, precision=precision, preferred_element_type=jnp.float32)


def exact_dot(a, b, dims):
    return dot(a, b, dims, lax.Precision.HIGHEST)


def triangle(length, keep):
    rows = lax.broadcasted_iota(jnp.int32, (length, length), 0)
    columns = lax.broadcasted_iota(jnp.int32, (length, length), 1)
    return jnp.where(keep(rows, columns), 1.0, 0.0).astype(jnp.float32)


def split(value):
    first = value.astype(jnp.bfloat16)
    left = value - first.astype(jnp.float32)
    second = left.astype(jnp.bfloat16)
    return first, second, (left - second.astype(jnp.float32)).astype(jnp.bfloat16)


def join(rows, head):
    wide = rows.astype(jnp.float32)
    return wide[3 * head : 3 * head + 1] + (
        wide[3 * head + 1 : 3 * head + 2] + wide[3 * head + 2 : 3 * head + 3]
    )


def decay_rows(totals):
    parts = [part for total in totals for part in split(total)]
    blank = jnp.zeros((EXTRA - len(parts), totals[0].shape[1]), jnp.bfloat16)
    return jnp.concatenate(parts + [blank], axis=0)


def pack_kernel(parts, decay_ref, packed_ref):
    length = packed_ref.shape[2]
    for place in range(packed_ref.shape[0]):
        start = place % parts * length
        packed_ref[place] = decay_ref[0, :, start : start + length]


def heads_at(first, head, dim):
    return pl.ds(pl.multiple_of((first + head) * dim, dim), dim)


def decays_at(decay_ref, block, first):
    local = decay_ref.shape[1]
    parts = decay_ref.shape[0] // 2
    rows = pl.ds(pl.multiple_of(first % local, STEP), STEP)
    return decay_ref[block * parts + first // local, rows, :]


def state_kernel(dim, owned, parts, half, begin, count, me_ref, *refs):
    decay_ref, *arrays = refs[:5]
    stacked_ref, copy_ref, done = refs[-3:]
    slots = refs[-3 - parts : -3]
    part, core = me_ref[0], me_ref[1]
    width = count * dim
    columns = pl.ds(pl.multiple_of((core * half + begin) * dim, width), width)
    moves = [
        pltpu.make_async_copy(ref.at[0, :, columns], copy_ref.at[at], done.at[at])
        for at, ref in enumerate(arrays)
    ]
    for move in moves:
        move.start()
    for source in range(2):
        block = core if source == 0 else 1 - core
        for move in moves[2 * source : 2 * source + 2]:
            move.wait()
        for turn in range(count // STEP):
            first = core * half + begin + turn * STEP
            decay = decays_at(decay_ref, block, first)
            length = decay.shape[1]
            weight = jnp.exp(exact_dot(decay, triangle(length, lambda u, s: u > s), NN))
            whole = jnp.broadcast_to(jnp.sum(decay, axis=1, keepdims=True), (STEP, dim))
            states = []
            for head in range(STEP):
                at = (turn * STEP + head) * dim
                key = copy_ref[2 * source, :, at : at + dim]
                value = copy_ref[2 * source + 1, :, at : at + dim]
                decayed = key.T.astype(jnp.float32) * weight[head : head + 1, :]
                states.append(dot(decayed.astype(jnp.bfloat16), value, NN))
            for head in range(STEP):
                owner, spot = divmod(turn * STEP + head, owned)
                span = slice(spot * dim, (spot + 1) * dim)
                stacked_ref[owner, block, span, :] = states[head].astype(jnp.bfloat16)
            for at in range(STEP // owned):
                stacked_ref[turn * STEP // owned + at, block, owned * dim :, :] = decay_rows(
                    [whole[head : head + 1] for head in range(at * owned, (at + 1) * owned)]
                )
    for slot, slot_ref in enumerate(slots):
        slot_ref[...] = stacked_ref[part ^ slot]


def inside_kernel(
    dim, half, begin, count, other, me_ref, queries_ref, keys_ref, values_ref, decay_ref, *rest
):
    inside_ref, done_ref = rest[-2:]
    core = me_ref[1]
    length = decay_ref.shape[2]
    rows = lax.broadcasted_iota(jnp.int32, (length, length), 0)
    causal = rows >= lax.broadcasted_iota(jnp.int32, (length, length), 1)
    for turn in range(count // STEP):
        first = (1 - core if other else core) * half + begin + turn * STEP
        decay = decays_at(decay_ref, core, first)
        down = exact_dot(triangle(length, lambda t, u: u <= t), decay, NT)
        across = exact_dot(decay, triangle(length, lambda u, s: u <= s), NN)
        columns = [heads_at(first, head, dim) for head in range(STEP)]
        scores = [dot(queries_ref[0, :, c], keys_ref[0, :, c], NT) for c in columns]
        weights = []
        for head in range(STEP):
            gap = down[:, head : head + 1] - across[head : head + 1, :]
            weight = scores[head] * jnp.exp(jnp.where(causal, gap, -jnp.inf))
            weights.append(weight.astype(jnp.bfloat16))
        for head, c in enumerate(columns):
            at = (turn * STEP + head) * dim
            inside_ref[:, at : at + dim] = dot(weights[head], values_ref[0, :, c], NN)
    done_ref[...] = jnp.zeros_like(done_ref)


def gather_states(part, slots, stacked_ref):
    parts = len(slots)
    for slot, slot_ref in enumerate(slots):
        for block in range(2):
            stacked_ref[block * parts + (part ^ slot)] = slot_ref[block]


def total_kernel(dim, owned, parts, me_ref, *refs):
    total_ref, stacked_ref = refs[-2:]
    gather_states(me_ref[0], refs[:parts], stacked_ref)
    count = 2 * parts
    extra = [stacked_ref[at, owned * dim :, :] for at in range(count)]
    sums = []
    for head in range(owned):
        span = slice(head * dim, (head + 1) * dim)
        after = jnp.zeros((1, dim), jnp.float32)
        total = stacked_ref[count - 1, span, :].astype(jnp.float32)
        for at in range(count - 2, -1, -1):
            after += join(extra[at + 1], head)
            total += jnp.exp(after) * stacked_ref[at, span, :].astype(jnp.float32)
        total_ref[span, :] = total.astype(jnp.bfloat16)
        sums.append(after + join(extra[0], head))
    total_ref[owned * dim :, :] = decay_rows(sums)


def widen_kernel(dim, owned, me_ref, later_ref, earlier_ref, *refs):
    out_ref = refs[-1]
    later, earlier = later_ref[owned * dim :, :], earlier_ref[owned * dim :, :]
    sums = []
    for head in range(owned):
        span = slice(head * dim, (head + 1) * dim)
        after = join(later, head)
        total = later_ref[span, :].astype(jnp.float32)
        total += jnp.exp(after) * earlier_ref[span, :].astype(jnp.float32)
        out_ref[span, :] = total.astype(jnp.bfloat16)
        sums.append(after + join(earlier, head))
    out_ref[owned * dim :, :] = decay_rows(sums)


def prefix_kernel(dim, owned, parts, stretches, me_ref, gain_ref, *refs):
    stacked_ref, prefix_ref = refs[-2:]
    slots, totals = refs[:parts], refs[parts : parts + stretches]
    count = 2 * parts
    results = refs[-2 - parts : -2]
    gather_states(me_ref[0], slots, stacked_ref)
    extra = [stacked_ref[at, owned * dim :, :] for at in range(count)]
    more = [total_ref[owned * dim :, :] for total_ref in totals]
    for head in range(owned):
        span = slice(head * dim, (head + 1) * dim)
        prefix = jnp.zeros((dim, dim), jnp.float32)
        after = jnp.zeros((1, dim), jnp.float32)
        for turn, total_ref in enumerate(totals):
            prefix += jnp.exp(after) * total_ref[span, :].astype(jnp.float32)
            after += join(more[turn], head)
        for at in range(count):
            prefix_ref[at, span, :] = prefix.astype(jnp.bfloat16)
            if at < count - 1:
                prefix = jnp.exp(join(extra[at], head)) * prefix
                prefix += stacked_ref[at, span, :].astype(jnp.float32)
    size = owned * dim
    for slot, result_ref in enumerate(results):
        for block in range(2):
            result_ref[block * size : (block + 1) * size, :] = prefix_ref[
                block * parts + (me_ref[0] ^ slot)
            ]
        result_ref[2 * size :, :] = gain_ref[...]


def collect(part, block, slots, prefix_ref, gain_ref):
    parts, size, _ = prefix_ref.shape
    local = gain_ref.shape[0] // parts
    for slot, slot_ref in enumerate(slots):
        owner = part ^ slot
        prefix_ref[owner] = slot_ref[pl.ds(pl.multiple_of(block * size, size), size), :]
        rows = pl.ds(pl.multiple_of(owner * local, local), local)
        gain_ref[rows, :] = slot_ref[2 * size :, :].astype(jnp.float32)


def merge_kernel(parts, me_ref, *refs):
    *others, gain_ref, prefix_ref = refs[parts:] if len(refs) == parts + 4 else refs[parts + 1 :]
    collect(me_ref[0], 1 - me_ref[1], refs[:parts], prefix_ref, gain_ref)
    each = parts // len(others)
    for turn, other_ref in enumerate(others):
        other_ref[...] = prefix_ref[turn * each : (turn + 1) * each]


def output_kernel(
    dim, owned, half, begin, count, parts, me_ref,
    queries_ref, inside_ref, gate_ref, decay_ref, *refs,
):
    out_ref, done_ref, prefix_ref, gain_ref, result_ref, sent = refs[-6:]
    core = me_ref[1]
    if parts is None:
        *others, gains = refs[:3]
        each = others[0].shape[0]
        prefixes = [others[at // each].at[at % each] for at in range(each * len(others))]
    else:
        collect(me_ref[0], core, refs[:parts], prefix_ref, gain_ref)
        prefixes, gains = [prefix_ref.at[at] for at in range(parts)], gain_ref
    length = decay_ref.shape[2]
    average = jnp.full((dim, dim), 1.0 / dim, jnp.bfloat16)
    moves = []
    for turn in range(count // STEP):
        first = (1 - core if parts is None else core) * half + begin + turn * STEP
        decay = decays_at(decay_ref, core, first)
        gain = gains[pl.ds(pl.multiple_of(first, STEP), STEP), :]
        down = jnp.exp(exact_dot(triangle(length, lambda t, u: u <= t), decay, NT))
        columns = [heads_at(first, head, dim) for head in range(STEP)]
        carried = []
        for head, c in enumerate(columns):
            owner, spot = divmod(turn * STEP + head, owned)
            prefix = prefixes[owner][spot * dim : (spot + 1) * dim, :]
            carried.append(dot(queries_ref[0, :, c], prefix, NN))
        mixed, means = [], []
        for head in range(STEP):
            at = (turn * STEP + head) * dim
            mixed.append(inside_ref[:, at : at + dim] + carried[head] * down[:, head : head + 1])
            means.append(dot((mixed[head] * mixed[head]).astype(jnp.bfloat16), average, NN))
        for head, c in enumerate(columns):
            half_gain = 0.5 * gain[head : head + 1, :]
            turned = jnp.tanh(0.5 * gate_ref[0, :, c].astype(jnp.float32))
            normed = mixed[head] * lax.rsqrt(means[head] + 1e-06) * (half_gain + half_gain * turned)
            result_ref[turn, :, head * dim : (head + 1) * dim] = normed.astype(jnp.bfloat16)
        width = STEP * dim
        moves.append(
            pltpu.make_async_copy(
                result_ref.at[turn],
                out_ref.at[0, :, pl.ds(pl.multiple_of(first * dim, width), width)],
                sent.at[turn],
            )
        )
        moves[-1].start()
    done_ref[...] = jnp.zeros_like(done_ref)
    for move in moves:
        move.wait()


def kernel_call(body, name, in_specs, out_specs, out_shape, scratch=(), aliases={}, cost=0):
    return pl.pallas_call(
        body,
        grid_spec=pltpu.PrefetchScalarGridSpec(
            num_scalar_prefetch=1,
            grid=(),
            in_specs=in_specs,
            out_specs=out_specs,
            scratch_shapes=scratch,
        ),
        out_shape=out_shape,
        input_output_aliases=aliases,
        compiler_params=pltpu.CompilerParams(vmem_limit_bytes=VMEM_LIMIT),
        cost_estimate=pl.CostEstimate(
            flops=int(1e9 * cost) + 1, transcendentals=0, bytes_accessed=1
        ),
        name=name,
    )


def on_device(parts, planes, queries, keys, values, gate, log_decay, norm_gain):
    _, length, width = queries.shape
    local = log_decay.shape[1]
    dim = width // (local * parts)
    count = 2 * parts
    half = local * parts // 2
    owned = half // (GROUPS * parts)
    rows = owned * dim + EXTRA
    me = jnp.stack([lax.axis_index("head"), lax.axis_index("core")]).astype(jnp.int32)
    swap = [(0, 1), (1, 0)]

    values_other = lax.ppermute(values, "core", swap)
    keys_other = lax.ppermute(keys, "core", swap)
    packed = pl.pallas_call(
        functools.partial(pack_kernel, parts),
        out_shape=jax.ShapeDtypeStruct((count, local, length), jnp.float32),
        name="pack",
    )(log_decay)
    decay = lax.all_to_all(packed, ("core", "head"), 0, 0, tiled=True)
    gain = norm_gain.reshape(local, dim)

    vmem = pl.BlockSpec(memory_space=pltpu.VMEM)
    hbm = pl.BlockSpec(memory_space=pl.ANY)

    def in_vmem(array):
        return pltpu.with_memory_space_constraint(array, pltpu.VMEM)

    def in_hbm(array):
        return pltpu.with_memory_space_constraint(array, pltpu.HBM)

    own = in_hbm(keys), in_hbm(values)
    keys, values, queries, gate = (in_vmem(array) for array in (keys, values, queries, gate))

    def exchange(slots):
        arrived = list(slots)
        for slot in sorted(range(1, parts), key=lambda s: -bin(s).count("1")):
            pairs = [(at, at ^ slot) for at in range(parts)]
            arrived[slot] = lax.ppermute(slots[slot], "head", pairs)
        return arrived

    before = ()
    held = []
    state_type = jax.ShapeDtypeStruct((2, rows, dim), jnp.bfloat16)
    share = half // GROUPS
    token = jax.ShapeDtypeStruct((8, 128), jnp.float32)
    inside = {}

    def inside_part(before, cost=0):
        group, other = divmod(len(inside), 2)
        inside[group, other], made = kernel_call(
            functools.partial(inside_kernel, dim, half, group * share, share, other),
            f"inside{group}_{other}",
            [vmem] * 4 + [hbm] * len(before),
            [vmem] * 2,
            [pltpu.VMEM((length, share * dim), jnp.float32), token],
            cost=cost,
        )(me, queries, keys, values, decay, *before)
        return (made,)

    for group in range(GROUPS):
        state = kernel_call(
            functools.partial(state_kernel, dim, owned, parts, half, group * share, share),
            f"state{group}",
            [vmem] + [hbm] * (4 + len(before)),
            [vmem] * parts,
            [state_type] * parts,
            [
                pltpu.VMEM((parts,) + state_type.shape, jnp.bfloat16),
                pltpu.VMEM((4, length, share * dim), jnp.bfloat16),
                pltpu.SemaphoreType.DMA((4,)),
            ],
        )(me, decay, *own, keys_other, values_other, *before)
        before = tuple(state[:1])
        held.append(exchange(state))
        if group == 0:
            before = inside_part(inside_part(before))

    arrived = []
    stacked = pltpu.VMEM((count, rows, dim), jnp.bfloat16)
    total_type = jax.ShapeDtypeStruct((rows, dim), jnp.bfloat16)

    def upward(total, far):
        return lax.ppermute(total, "z", [(at, at + far) for at in range(planes - far)])

    def widen(name, total, earlier, before):
        return kernel_call(
            functools.partial(widen_kernel, dim, owned),
            name,
            [vmem] * 2 + [hbm] * len(before),
            vmem,
            total_type,
        )(me, total, earlier, *before)

    def prefix_of(group, before):
        stretches = arrived[group]
        return kernel_call(
            functools.partial(prefix_kernel, dim, owned, parts, len(stretches)),
            f"prefix{group}",
            [vmem] * (1 + parts + len(stretches)) + [hbm] * len(before),
            [vmem] * parts,
            [prefix_type] * parts,
            [stacked, pltpu.VMEM((count, size, dim), jnp.bfloat16)],
        )(me, gain, *held[group], *stretches, *before)

    size = owned * dim
    prefix_type = jax.ShapeDtypeStruct((2 * size + local, dim), jnp.bfloat16)
    prefixes = []
    for group in range(GROUPS):
        total = kernel_call(
            functools.partial(total_kernel, dim, owned, parts),
            f"total{group}",
            [vmem] * parts + [hbm],
            vmem,
            total_type,
            [stacked],
        )(me, *held[group], *before)
        before = (total,)
        stretches, far = [upward(total, 1)], 1
        arrived.append(stretches)
        if group > 0:
            prefix = prefix_of(group - 1, before)
            before = tuple(prefix[:1])
            prefixes.append(exchange(prefix))
        while 2 * far < planes:
            if group == 0 and far == 1:
                before = inside_part(before)
            total = widen(f"widen{group}_{far}", total, stretches[-1], before)
            before = (total,)
            far *= 2
            stretches.append(upward(total, far))
        if group == GROUPS - 1:
            before = inside_part(before, 2)
    while len(inside) < 2 * GROUPS:
        before = inside_part(before)
    prefix = prefix_of(GROUPS - 1, before)
    before = tuple(prefix[:1])
    prefixes.append(exchange(prefix))

    part_type = jax.ShapeDtypeStruct((parts, size, dim), jnp.bfloat16)
    half_type = jax.ShapeDtypeStruct((parts // 2, size, dim), jnp.bfloat16)
    gain_type = jax.ShapeDtypeStruct((parts * local, dim), jnp.float32)

    def merge(group, before, cost):
        return kernel_call(
            functools.partial(merge_kernel, parts),
            f"merge{group}",
            [vmem] * parts + [hbm] * len(before),
            [vmem] * 3,
            [half_type, half_type, gain_type],
            [pltpu.VMEM(part_type.shape, part_type.dtype)],
            cost=cost,
        )(me, *prefixes[group], *before)

    def output(group, other, received, out, before, cost=0):
        *out, made = kernel_call(
            functools.partial(
                output_kernel, dim, owned, half, group * share, share, None if other else parts
            ),
            f"output{group}_{other}",
            [vmem] * (4 + len(received)) + [hbm] * (len(out) + len(before)),
            [hbm, vmem],
            [pltpu.HBM((1, length, width), jnp.bfloat16), token],
            [
                pltpu.VMEM(part_type.shape, part_type.dtype),
                pltpu.VMEM(gain_type.shape, gain_type.dtype),
                pltpu.VMEM((share // STEP, length, STEP * dim), jnp.bfloat16),
                pltpu.SemaphoreType.DMA((share // STEP,)),
            ],
            aliases={5 + len(received): 0} if out else {},
            cost=cost,
        )(me, queries, in_vmem(inside[group, other]), gate, decay, *received, *out, *before)
        return out, (made,)

    out = ()
    for group in range(GROUPS):
        last = group == GROUPS - 1
        if not last:
            out, before = output(group, 0, prefixes[group], out, before)
        *others, gains = merge(group, before, 0)
        others = [lax.ppermute(other, "core", swap) for other in others]
        before = (gains,)
        if last:
            out, before = output(group, 0, prefixes[group], out, before, cost=20)
        out, before = output(group, 1, (*others, gains), out, before)
    return out[0]


def solution(mesh):
    parts, blocks = mesh.shape["head"], mesh.shape["ctx"]
    names = mesh.axis_names
    at = names.index("ctx")
    shape = mesh.devices.shape[:at] + (blocks // 2, 2) + mesh.devices.shape[at + 1 :]
    finer = Mesh(mesh.devices.reshape(shape), names[:at] + ("z", "core") + names[at + 1 :])
    tokens = P(("z", "core"), "head", None)
    return jax.shard_map(
        functools.partial(on_device, parts, blocks // 2),
        mesh=finer,
        in_specs=(tokens,) * 5 + (P("head"),),
        out_specs=tokens,
        check_vma=False,
    )
```

```python
import functools

import jax
import jax.numpy as jnp
from jax import lax
from jax.experimental import pallas as pl
from jax.experimental.pallas import tpu as pltpu
from jax.sharding import Mesh
from jax.sharding import PartitionSpec as P

GROUPS = 2
STEP = 8
EXTRA = 16
VMEM_LIMIT = 8 * 1024 * 1024
NN = (((1,), (0,)), ((), ()))
NT = (((1,), (1,)), ((), ()))
TN = (((0,), (0,)), ((), ()))


def dot(a, b, dims, precision=None):
    return lax.dot_general(a, b, dims, precision=precision, preferred_element_type=jnp.float32)


def exact_dot(a, b, dims):
    return dot(a, b, dims, lax.Precision.HIGHEST)


def triangle(length, keep):
    rows = lax.broadcasted_iota(jnp.int32, (length, length), 0)
    columns = lax.broadcasted_iota(jnp.int32, (length, length), 1)
    return jnp.where(keep(rows, columns), 1.0, 0.0).astype(jnp.float32)


def split(value):
    first = value.astype(jnp.bfloat16)
    left = value - first.astype(jnp.float32)
    second = left.astype(jnp.bfloat16)
    return first, second, (left - second.astype(jnp.float32)).astype(jnp.bfloat16)


def join(rows, head):
    wide = rows.astype(jnp.float32)
    return wide[3 * head : 3 * head + 1] + (
        wide[3 * head + 1 : 3 * head + 2] + wide[3 * head + 2 : 3 * head + 3]
    )


def decay_rows(totals):
    parts = [part for total in totals for part in split(total)]
    blank = jnp.zeros((EXTRA - len(parts), totals[0].shape[1]), jnp.bfloat16)
    return jnp.concatenate(parts + [blank], axis=0)


def pack_kernel(parts, decay_ref, packed_ref, done):
    length = packed_ref.shape[2]
    moves = [
        pltpu.make_async_copy(
            decay_ref.at[0, :, place % parts * length : (place % parts + 1) * length],
            packed_ref.at[place],
            done.at[place],
        )
        for place in range(packed_ref.shape[0])
    ]
    for move in moves:
        move.start()
    for move in moves:
        move.wait()


def heads_at(first, head, dim):
    return pl.ds(pl.multiple_of((first + head) * dim, dim), dim)


def decays_at(decay_ref, block, first):
    local = decay_ref.shape[1]
    parts = decay_ref.shape[0] // 2
    rows = pl.ds(pl.multiple_of(first % local, STEP), STEP)
    return decay_ref[block * parts + first // local, rows, :]


def state_kernel(dim, owned, parts, half, begin, count, me_ref, *refs):
    decay_ref, *arrays = refs[:5]
    stacked_ref, copy_ref, done = refs[-3:]
    slots = refs[-3 - parts : -3]
    part, core = me_ref[0], me_ref[1]
    width = count * dim
    columns = pl.ds(pl.multiple_of((core * half + begin) * dim, width), width)
    moves = [
        pltpu.make_async_copy(ref.at[0, :, columns], copy_ref.at[at], done.at[at])
        for at, ref in enumerate(arrays)
    ]
    for move in moves:
        move.start()
    for source in range(2):
        block = core if source == 0 else 1 - core
        for move in moves[2 * source : 2 * source + 2]:
            move.wait()
        for turn in range(count // STEP):
            first = core * half + begin + turn * STEP
            decay = decays_at(decay_ref, block, first)
            length = decay.shape[1]
            weight = jnp.exp(exact_dot(decay, triangle(length, lambda u, s: u > s), NN))
            whole = jnp.broadcast_to(jnp.sum(decay, axis=1, keepdims=True), (STEP, dim))
            states = []
            for head in range(STEP):
                at = (turn * STEP + head) * dim
                key = copy_ref[2 * source, :, at : at + dim]
                value = copy_ref[2 * source + 1, :, at : at + dim]
                decayed = key.T.astype(jnp.float32) * weight[head : head + 1, :]
                states.append(dot(decayed.astype(jnp.bfloat16), value, NN))
            for head in range(STEP):
                owner, spot = divmod(turn * STEP + head, owned)
                span = slice(spot * dim, (spot + 1) * dim)
                stacked_ref[owner, block, span, :] = states[head].astype(jnp.bfloat16)
            for at in range(STEP // owned):
                stacked_ref[turn * STEP // owned + at, block, owned * dim :, :] = decay_rows(
                    [whole[head : head + 1] for head in range(at * owned, (at + 1) * owned)]
                )
    for slot, slot_ref in enumerate(slots):
        slot_ref[...] = stacked_ref[part ^ slot]


def inside_kernel(
    dim, half, begin, count, other, me_ref, queries_ref, keys_ref, values_ref, decay_ref, *rest
):
    inside_ref, done_ref = rest[-2:]
    core = me_ref[1]
    length = decay_ref.shape[2]
    rows = lax.broadcasted_iota(jnp.int32, (length, length), 0)
    causal = rows >= lax.broadcasted_iota(jnp.int32, (length, length), 1)
    for turn in range(count // STEP):
        first = (1 - core if other else core) * half + begin + turn * STEP
        decay = decays_at(decay_ref, core, first)
        down = exact_dot(triangle(length, lambda t, u: u <= t), decay, NT)
        across = exact_dot(decay, triangle(length, lambda u, s: u <= s), NN)
        columns = [heads_at(first, head, dim) for head in range(STEP)]
        scores = [dot(queries_ref[0, :, c], keys_ref[0, :, c], NT) for c in columns]
        weights = []
        for head in range(STEP):
            gap = down[:, head : head + 1] - across[head : head + 1, :]
            weight = scores[head] * jnp.exp(jnp.where(causal, gap, -jnp.inf))
            weights.append(weight.astype(jnp.bfloat16))
        for head, c in enumerate(columns):
            at = (turn * STEP + head) * dim
            inside_ref[:, at : at + dim] = dot(weights[head], values_ref[0, :, c], NN)
    done_ref[...] = jnp.zeros_like(done_ref)


def gather_states(part, slots, stacked_ref):
    parts = len(slots)
    for slot, slot_ref in enumerate(slots):
        for block in range(2):
            stacked_ref[block * parts + (part ^ slot)] = slot_ref[block]


def total_kernel(dim, owned, parts, me_ref, *refs):
    total_ref, stacked_ref = refs[-2:]
    gather_states(me_ref[0], refs[:parts], stacked_ref)
    count = 2 * parts
    extra = [stacked_ref[at, owned * dim :, :] for at in range(count)]
    sums = []
    for head in range(owned):
        span = slice(head * dim, (head + 1) * dim)
        after = jnp.zeros((1, dim), jnp.float32)
        total = stacked_ref[count - 1, span, :].astype(jnp.float32)
        for at in range(count - 2, -1, -1):
            after += join(extra[at + 1], head)
            total += jnp.exp(after) * stacked_ref[at, span, :].astype(jnp.float32)
        total_ref[span, :] = total.astype(jnp.bfloat16)
        sums.append(after + join(extra[0], head))
    total_ref[owned * dim :, :] = decay_rows(sums)


def widen_kernel(dim, owned, step, me_ref, mine_ref, other_ref, *refs):
    out_ref = refs[-1]
    later = (me_ref[2] >> step) % 2 == 1
    extra = mine_ref[owned * dim :, :], other_ref[owned * dim :, :]
    sums = []
    for head in range(owned):
        span = slice(head * dim, (head + 1) * dim)
        mine, other = join(extra[0], head), join(extra[1], head)
        total = jnp.where(later, 1.0, jnp.exp(other)) * mine_ref[span, :].astype(jnp.float32)
        total += jnp.where(later, jnp.exp(mine), 1.0) * other_ref[span, :].astype(jnp.float32)
        out_ref[span, :] = total.astype(jnp.bfloat16)
        sums.append(mine + other)
    out_ref[owned * dim :, :] = decay_rows(sums)


def prefix_kernel(dim, owned, parts, stretches, me_ref, gain_ref, *refs):
    stacked_ref, prefix_ref = refs[-2:]
    slots, totals = refs[:parts], refs[parts : parts + stretches]
    count = 2 * parts
    results = refs[-2 - parts : -2]
    gather_states(me_ref[0], slots, stacked_ref)
    extra = [stacked_ref[at, owned * dim :, :] for at in range(count)]
    more = [total_ref[owned * dim :, :] for total_ref in totals]
    earlier = [
        ((me_ref[2] >> step) % 2).astype(jnp.float32) for step in range(len(totals))
    ]
    for head in range(owned):
        span = slice(head * dim, (head + 1) * dim)
        prefix = jnp.zeros((dim, dim), jnp.float32)
        after = jnp.zeros((1, dim), jnp.float32)
        for turn, total_ref in enumerate(totals):
            factor = earlier[turn] * jnp.exp(after)
            prefix += factor * total_ref[span, :].astype(jnp.float32)
            after += earlier[turn] * join(more[turn], head)
        for at in range(count):
            prefix_ref[at, span, :] = prefix.astype(jnp.bfloat16)
            if at < count - 1:
                prefix = jnp.exp(join(extra[at], head)) * prefix
                prefix += stacked_ref[at, span, :].astype(jnp.float32)
    size = owned * dim
    for slot, result_ref in enumerate(results):
        for block in range(2):
            result_ref[block * size : (block + 1) * size, :] = prefix_ref[
                block * parts + (me_ref[0] ^ slot)
            ]
        result_ref[2 * size :, :] = gain_ref[...]


def collect(part, block, slots, prefix_ref, gain_ref):
    parts, size, _ = prefix_ref.shape
    local = gain_ref.shape[0] // parts
    for slot, slot_ref in enumerate(slots):
        owner = part ^ slot
        prefix_ref[owner] = slot_ref[pl.ds(pl.multiple_of(block * size, size), size), :]
        rows = pl.ds(pl.multiple_of(owner * local, local), local)
        gain_ref[rows, :] = slot_ref[2 * size :, :].astype(jnp.float32)


def merge_kernel(parts, me_ref, *refs):
    *others, gain_ref, prefix_ref = refs[parts:] if len(refs) == parts + 4 else refs[parts + 1 :]
    collect(me_ref[0], 1 - me_ref[1], refs[:parts], prefix_ref, gain_ref)
    each = parts // len(others)
    for turn, other_ref in enumerate(others):
        other_ref[...] = prefix_ref[turn * each : (turn + 1) * each]


def output_kernel(
    dim, owned, half, begin, count, parts, me_ref,
    queries_ref, inside_ref, gate_ref, decay_ref, *refs,
):
    out_ref, done_ref, prefix_ref, gain_ref, result_ref, sent = refs[-6:]
    core = me_ref[1]
    if parts is None:
        *others, gains = refs[:3]
        each = others[0].shape[0]
        prefixes = [others[at // each].at[at % each] for at in range(each * len(others))]
    else:
        collect(me_ref[0], core, refs[:parts], prefix_ref, gain_ref)
        prefixes, gains = [prefix_ref.at[at] for at in range(parts)], gain_ref
    length = decay_ref.shape[2]
    average = jnp.full((dim, dim), 1.0 / dim, jnp.bfloat16)
    moves = []
    for turn in range(count // STEP):
        first = (1 - core if parts is None else core) * half + begin + turn * STEP
        decay = decays_at(decay_ref, core, first)
        gain = gains[pl.ds(pl.multiple_of(first, STEP), STEP), :]
        down = jnp.exp(exact_dot(triangle(length, lambda t, u: u <= t), decay, NT))
        columns = [heads_at(first, head, dim) for head in range(STEP)]
        carried = []
        for head, c in enumerate(columns):
            owner, spot = divmod(turn * STEP + head, owned)
            prefix = prefixes[owner][spot * dim : (spot + 1) * dim, :]
            carried.append(dot(queries_ref[0, :, c], prefix, NN))
        mixed, means = [], []
        for head in range(STEP):
            at = (turn * STEP + head) * dim
            mixed.append(inside_ref[:, at : at + dim] + carried[head] * down[:, head : head + 1])
            means.append(dot((mixed[head] * mixed[head]).astype(jnp.bfloat16), average, NN))
        for head, c in enumerate(columns):
            half_gain = 0.5 * gain[head : head + 1, :]
            turned = jnp.tanh(0.5 * gate_ref[0, :, c].astype(jnp.float32))
            normed = mixed[head] * lax.rsqrt(means[head] + 1e-06) * (half_gain + half_gain * turned)
            result_ref[turn, :, head * dim : (head + 1) * dim] = normed.astype(jnp.bfloat16)
        width = STEP * dim
        moves.append(
            pltpu.make_async_copy(
                result_ref.at[turn],
                out_ref.at[0, :, pl.ds(pl.multiple_of(first * dim, width), width)],
                sent.at[turn],
            )
        )
        moves[-1].start()
    done_ref[...] = jnp.zeros_like(done_ref)
    for move in moves:
        move.wait()


def kernel_call(body, name, in_specs, out_specs, out_shape, scratch=(), aliases={}, cost=0):
    return pl.pallas_call(
        body,
        grid_spec=pltpu.PrefetchScalarGridSpec(
            num_scalar_prefetch=1,
            grid=(),
            in_specs=in_specs,
            out_specs=out_specs,
            scratch_shapes=scratch,
        ),
        out_shape=out_shape,
        input_output_aliases=aliases,
        compiler_params=pltpu.CompilerParams(vmem_limit_bytes=VMEM_LIMIT),
        cost_estimate=pl.CostEstimate(
            flops=int(1e9 * cost) + 1, transcendentals=0, bytes_accessed=1
        ),
        name=name,
    )


def on_device(parts, planes, queries, keys, values, gate, log_decay, norm_gain):
    _, length, width = queries.shape
    local = log_decay.shape[1]
    dim = width // (local * parts)
    count = 2 * parts
    half = local * parts // 2
    owned = half // (GROUPS * parts)
    rows = owned * dim + EXTRA
    me = jnp.stack([lax.axis_index(axis) for axis in ("head", "core", "z")]).astype(jnp.int32)
    swap = [(0, 1), (1, 0)]

    values_other = lax.ppermute(values, "core", swap)
    keys_other = lax.ppermute(keys, "core", swap)
    packed = pl.pallas_call(
        functools.partial(pack_kernel, parts),
        in_specs=[pl.BlockSpec(memory_space=pl.ANY)],
        out_specs=pl.BlockSpec(memory_space=pl.ANY),
        out_shape=pltpu.HBM((count, local, length), jnp.float32),
        scratch_shapes=[pltpu.SemaphoreType.DMA((count,))],
        name="pack",
    )(pltpu.with_memory_space_constraint(log_decay, pltpu.HBM))
    decay = lax.all_to_all(packed, ("core", "head"), 0, 0, tiled=True)
    gain = norm_gain.reshape(local, dim)

    vmem = pl.BlockSpec(memory_space=pltpu.VMEM)
    hbm = pl.BlockSpec(memory_space=pl.ANY)

    def in_vmem(array):
        return pltpu.with_memory_space_constraint(array, pltpu.VMEM)

    def in_hbm(array):
        return pltpu.with_memory_space_constraint(array, pltpu.HBM)

    own = in_hbm(keys), in_hbm(values)
    keys, values, queries, gate = (in_vmem(array) for array in (keys, values, queries, gate))

    def exchange(slots):
        arrived = list(slots)
        for slot in sorted(range(1, parts), key=lambda s: -bin(s).count("1")):
            pairs = [(at, at ^ slot) for at in range(parts)]
            arrived[slot] = lax.ppermute(slots[slot], "head", pairs)
        return arrived

    before = ()
    held = []
    state_type = jax.ShapeDtypeStruct((2, rows, dim), jnp.bfloat16)
    share = half // GROUPS
    token = jax.ShapeDtypeStruct((8, 128), jnp.float32)
    inside = {}

    def inside_part(before, cost=0):
        group, other = divmod(len(inside), 2)
        inside[group, other], made = kernel_call(
            functools.partial(inside_kernel, dim, half, group * share, share, other),
            f"inside{group}_{other}",
            [vmem] * 4 + [hbm] * len(before),
            [vmem] * 2,
            [pltpu.VMEM((length, share * dim), jnp.float32), token],
            cost=cost,
        )(me, queries, keys, values, decay, *before)
        return (made,)

    for group in range(GROUPS):
        state = kernel_call(
            functools.partial(state_kernel, dim, owned, parts, half, group * share, share),
            f"state{group}",
            [vmem] + [hbm] * (4 + len(before)),
            [vmem] * parts,
            [state_type] * parts,
            [
                pltpu.VMEM((parts,) + state_type.shape, jnp.bfloat16),
                pltpu.VMEM((4, length, share * dim), jnp.bfloat16),
                pltpu.SemaphoreType.DMA((4,)),
            ],
        )(me, decay, *own, keys_other, values_other, *before)
        before = tuple(state[:1])
        held.append(exchange(state))
        if group == 0:
            before = inside_part(inside_part(before))

    arrived = []
    stacked = pltpu.VMEM((count, rows, dim), jnp.bfloat16)
    total_type = jax.ShapeDtypeStruct((rows, dim), jnp.bfloat16)

    def with_plane(total, step):
        pairs = [(at, at ^ (1 << step)) for at in range(planes)]
        return lax.ppermute(total, "z", pairs)

    def widen(group, step, total, other, before):
        return kernel_call(
            functools.partial(widen_kernel, dim, owned, step),
            f"widen{group}_{step}",
            [vmem] * 2 + [hbm] * len(before),
            vmem,
            total_type,
        )(me, total, other, *before)

    def prefix_of(group, before):
        stretches = arrived[group]
        return kernel_call(
            functools.partial(prefix_kernel, dim, owned, parts, len(stretches)),
            f"prefix{group}",
            [vmem] * (1 + parts + len(stretches)) + [hbm] * len(before),
            [vmem] * parts,
            [prefix_type] * parts,
            [stacked, pltpu.VMEM((count, size, dim), jnp.bfloat16)],
        )(me, gain, *held[group], *stretches, *before)

    size = owned * dim
    prefix_type = jax.ShapeDtypeStruct((2 * size + local, dim), jnp.bfloat16)
    prefixes = []
    for group in range(GROUPS):
        total = kernel_call(
            functools.partial(total_kernel, dim, owned, parts),
            f"total{group}",
            [vmem] * parts + [hbm],
            vmem,
            total_type,
            [stacked],
        )(me, *held[group], *before)
        before = (total,)
        stretches = [with_plane(total, 0)]
        arrived.append(stretches)
        if group > 0:
            prefix = prefix_of(group - 1, before)
            before = tuple(prefix[:1])
            prefixes.append(exchange(prefix))
        for step in range(1, planes.bit_length() - 1):
            if group == 0 and step == 1:
                before = inside_part(before)
            total = widen(group, step - 1, total, stretches[-1], before)
            before = (total,)
            stretches.append(with_plane(total, step))
        if group == GROUPS - 1:
            before = inside_part(before, 2)
    while len(inside) < 2 * GROUPS:
        before = inside_part(before)
    prefix = prefix_of(GROUPS - 1, before)
    before = tuple(prefix[:1])
    prefixes.append(exchange(prefix))

    part_type = jax.ShapeDtypeStruct((parts, size, dim), jnp.bfloat16)
    half_type = jax.ShapeDtypeStruct((parts // 2, size, dim), jnp.bfloat16)
    gain_type = jax.ShapeDtypeStruct((parts * local, dim), jnp.float32)

    def merge(group, before, cost):
        return kernel_call(
            functools.partial(merge_kernel, parts),
            f"merge{group}",
            [vmem] * parts + [hbm] * len(before),
            [vmem] * 3,
            [half_type, half_type, gain_type],
            [pltpu.VMEM(part_type.shape, part_type.dtype)],
            cost=cost,
        )(me, *prefixes[group], *before)

    def output(group, other, received, out, before, cost=0):
        *out, made = kernel_call(
            functools.partial(
                output_kernel, dim, owned, half, group * share, share, None if other else parts
            ),
            f"output{group}_{other}",
            [vmem] * (4 + len(received)) + [hbm] * (len(out) + len(before)),
            [hbm, vmem],
            [pltpu.HBM((1, length, width), jnp.bfloat16), token],
            [
                pltpu.VMEM(part_type.shape, part_type.dtype),
                pltpu.VMEM(gain_type.shape, gain_type.dtype),
                pltpu.VMEM((share // STEP, length, STEP * dim), jnp.bfloat16),
                pltpu.SemaphoreType.DMA((share // STEP,)),
            ],
            aliases={5 + len(received): 0} if out else {},
            cost=cost,
        )(me, queries, in_vmem(inside[group, other]), gate, decay, *received, *out, *before)
        return out, (made,)

    out = ()
    for group in range(GROUPS):
        last = group == GROUPS - 1
        if not last:
            out, before = output(group, 0, prefixes[group], out, before)
        *others, gains = merge(group, before, 0)
        others = [lax.ppermute(other, "core", swap) for other in others]
        before = (gains,)
        if last:
            out, before = output(group, 0, prefixes[group], out, before, cost=20)
        out, before = output(group, 1, (*others, gains), out, before)
    return out[0]


def solution(mesh):
    parts, blocks = mesh.shape["head"], mesh.shape["ctx"]
    names = mesh.axis_names
    at = names.index("ctx")
    shape = mesh.devices.shape[:at] + (blocks // 2, 2) + mesh.devices.shape[at + 1 :]
    finer = Mesh(mesh.devices.reshape(shape), names[:at] + ("z", "core") + names[at + 1 :])
    tokens = P(("z", "core"), "head", None)
    return jax.shard_map(
        functools.partial(on_device, parts, blocks // 2),
        mesh=finer,
        in_specs=(tokens,) * 5 + (P("head"),),
        out_specs=tokens,
        check_vma=False,
    )
```

```python
import functools

import jax
import jax.numpy as jnp
from jax import lax
from jax.experimental import pallas as pl
from jax.experimental.pallas import tpu as pltpu
from jax.sharding import Mesh
from jax.sharding import PartitionSpec as P

GROUPS = 2
STEP = 8
EXTRA = 16
VMEM_LIMIT = 8 * 1024 * 1024
NN = (((1,), (0,)), ((), ()))
NT = (((1,), (1,)), ((), ()))
TN = (((0,), (0,)), ((), ()))


def dot(a, b, dims, precision=None):
    return lax.dot_general(a, b, dims, precision=precision, preferred_element_type=jnp.float32)


def exact_dot(a, b, dims):
    return dot(a, b, dims, lax.Precision.HIGHEST)


def triangle(length, keep):
    rows = lax.broadcasted_iota(jnp.int32, (length, length), 0)
    columns = lax.broadcasted_iota(jnp.int32, (length, length), 1)
    return jnp.where(keep(rows, columns), 1.0, 0.0).astype(jnp.float32)


def split(value):
    first = value.astype(jnp.bfloat16)
    left = value - first.astype(jnp.float32)
    second = left.astype(jnp.bfloat16)
    return first, second, (left - second.astype(jnp.float32)).astype(jnp.bfloat16)


def join(rows, head):
    wide = rows.astype(jnp.float32)
    return wide[3 * head : 3 * head + 1] + (
        wide[3 * head + 1 : 3 * head + 2] + wide[3 * head + 2 : 3 * head + 3]
    )


def decay_rows(totals):
    parts = [part for total in totals for part in split(total)]
    blank = jnp.zeros((EXTRA - len(parts), totals[0].shape[1]), jnp.bfloat16)
    return jnp.concatenate(parts + [blank], axis=0)


def pack_kernel(parts, decay_ref, packed_ref):
    length = packed_ref.shape[2]
    for place in range(packed_ref.shape[0]):
        start = place % parts * length
        packed_ref[place] = decay_ref[0, :, start : start + length]


def heads_at(first, head, dim):
    return pl.ds(pl.multiple_of((first + head) * dim, dim), dim)


def decays_at(decay_ref, block, first):
    local = decay_ref.shape[1]
    parts = decay_ref.shape[0] // 2
    rows = pl.ds(pl.multiple_of(first % local, STEP), STEP)
    return decay_ref[block * parts + first // local, rows, :]


def state_kernel(dim, owned, half, begin, masks, me_ref, decay_ref, *refs):
    arrays, slots = refs[:4], refs[-3 - 2 * len(masks) : -3]
    stacked_ref, copy_ref, done = refs[-3:]
    part, core = me_ref[0], me_ref[1]
    firsts = [core * half + begin + ((part >> 1) ^ mask) * STEP for mask in masks]
    width = STEP * dim
    moves = [
        [
            pltpu.make_async_copy(
                ref.at[0, :, pl.ds(pl.multiple_of(first * dim, width), width)],
                copy_ref.at[turn, at],
                done.at[turn, at],
            )
            for at, ref in enumerate(arrays)
        ]
        for turn, first in enumerate(firsts)
    ]
    for move in sum(moves, []):
        move.start()
    for turn, first in enumerate(firsts):
        for source in range(2):
            block = core if source == 0 else 1 - core
            decay = decays_at(decay_ref, block, first)
            length = decay.shape[1]
            weight = jnp.exp(exact_dot(decay, triangle(length, lambda u, s: u > s), NN))
            whole = jnp.broadcast_to(jnp.sum(decay, axis=1, keepdims=True), (STEP, dim))
            for move in moves[turn][2 * source : 2 * source + 2]:
                move.wait()
            states = []
            for head in range(STEP):
                c = slice(head * dim, (head + 1) * dim)
                decayed = copy_ref[turn, 2 * source, :, c].T.astype(jnp.float32)
                decayed = (decayed * weight[head : head + 1, :]).astype(jnp.bfloat16)
                states.append(dot(decayed, copy_ref[turn, 2 * source + 1, :, c], NN))
            for head in range(STEP):
                owner, spot = divmod(head, owned)
                span = slice(spot * dim, (spot + 1) * dim)
                stacked_ref[turn, owner, block, span, :] = states[head].astype(jnp.bfloat16)
            for at in range(2):
                stacked_ref[turn, at, block, owned * dim :, :] = decay_rows(
                    [whole[head : head + 1] for head in range(at * owned, (at + 1) * owned)]
                )
        for at in range(2):
            slots[2 * turn + at][...] = stacked_ref[turn, (part & 1) ^ at]


def inside_kernel(
    dim, half, begin, count, other, me_ref, queries_ref, keys_ref, values_ref, decay_ref, *rest
):
    inside_ref, done_ref = rest[-2:]
    core = me_ref[1]
    length = decay_ref.shape[2]
    rows = lax.broadcasted_iota(jnp.int32, (length, length), 0)
    causal = rows >= lax.broadcasted_iota(jnp.int32, (length, length), 1)
    for turn in range(count // STEP):
        first = (1 - core if other else core) * half + begin + turn * STEP
        decay = decays_at(decay_ref, core, first)
        down = exact_dot(triangle(length, lambda t, u: u <= t), decay, NT)
        across = exact_dot(decay, triangle(length, lambda u, s: u <= s), NN)
        columns = [heads_at(first, head, dim) for head in range(STEP)]
        scores = [dot(queries_ref[0, :, c], keys_ref[0, :, c], NT) for c in columns]
        weights = []
        for head in range(STEP):
            gap = down[:, head : head + 1] - across[head : head + 1, :]
            weight = scores[head] * jnp.exp(jnp.where(causal, gap, -jnp.inf))
            weights.append(weight.astype(jnp.bfloat16))
        for head, c in enumerate(columns):
            at = (turn * STEP + head) * dim
            inside_ref[:, at : at + dim] = dot(weights[head], values_ref[0, :, c], NN)
    done_ref[...] = jnp.zeros_like(done_ref)


def gather_states(part, slots, stacked_ref):
    parts = len(slots)
    for slot, slot_ref in enumerate(slots):
        for block in range(2):
            stacked_ref[block * parts + (part ^ slot)] = slot_ref[block]


def total_kernel(dim, owned, parts, me_ref, *refs):
    total_ref, stacked_ref = refs[-2:]
    gather_states(me_ref[0], refs[:parts], stacked_ref)
    count = 2 * parts
    extra = [stacked_ref[at, owned * dim :, :] for at in range(count)]
    sums = []
    for head in range(owned):
        span = slice(head * dim, (head + 1) * dim)
        after = jnp.zeros((1, dim), jnp.float32)
        total = stacked_ref[count - 1, span, :].astype(jnp.float32)
        for at in range(count - 2, -1, -1):
            after += join(extra[at + 1], head)
            total += jnp.exp(after) * stacked_ref[at, span, :].astype(jnp.float32)
        total_ref[span, :] = total.astype(jnp.bfloat16)
        sums.append(after + join(extra[0], head))
    total_ref[owned * dim :, :] = decay_rows(sums)


def widen_kernel(dim, owned, step, me_ref, mine_ref, other_ref, *refs):
    out_ref = refs[-1]
    later = (me_ref[2] >> step) % 2 == 1
    extra = mine_ref[owned * dim :, :], other_ref[owned * dim :, :]
    sums = []
    for head in range(owned):
        span = slice(head * dim, (head + 1) * dim)
        mine, other = join(extra[0], head), join(extra[1], head)
        total = jnp.where(later, 1.0, jnp.exp(other)) * mine_ref[span, :].astype(jnp.float32)
        total += jnp.where(later, jnp.exp(mine), 1.0) * other_ref[span, :].astype(jnp.float32)
        out_ref[span, :] = total.astype(jnp.bfloat16)
        sums.append(mine + other)
    out_ref[owned * dim :, :] = decay_rows(sums)


def prefix_kernel(dim, owned, parts, stretches, me_ref, gain_ref, *refs):
    stacked_ref, prefix_ref = refs[-2:]
    slots, totals = refs[:parts], refs[parts : parts + stretches]
    count = 2 * parts
    results = refs[-2 - parts : -2]
    gather_states(me_ref[0], slots, stacked_ref)
    extra = [stacked_ref[at, owned * dim :, :] for at in range(count)]
    more = [total_ref[owned * dim :, :] for total_ref in totals]
    earlier = [
        ((me_ref[2] >> step) % 2).astype(jnp.float32) for step in range(len(totals))
    ]
    for head in range(owned):
        span = slice(head * dim, (head + 1) * dim)
        prefix = jnp.zeros((dim, dim), jnp.float32)
        after = jnp.zeros((1, dim), jnp.float32)
        for turn, total_ref in enumerate(totals):
            factor = earlier[turn] * jnp.exp(after)
            prefix += factor * total_ref[span, :].astype(jnp.float32)
            after += earlier[turn] * join(more[turn], head)
        for at in range(count):
            prefix_ref[at, span, :] = prefix.astype(jnp.bfloat16)
            if at < count - 1:
                prefix = jnp.exp(join(extra[at], head)) * prefix
                prefix += stacked_ref[at, span, :].astype(jnp.float32)
    size = owned * dim
    for slot, result_ref in enumerate(results):
        for block in range(2):
            result_ref[block * size : (block + 1) * size, :] = prefix_ref[
                block * parts + (me_ref[0] ^ slot)
            ]
        result_ref[2 * size :, :] = gain_ref[...]


def collect(part, block, slots, prefix_ref, gain_ref):
    parts, size, _ = prefix_ref.shape
    local = gain_ref.shape[0] // parts
    for slot, slot_ref in enumerate(slots):
        owner = part ^ slot
        prefix_ref[owner] = slot_ref[pl.ds(pl.multiple_of(block * size, size), size), :]
        rows = pl.ds(pl.multiple_of(owner * local, local), local)
        gain_ref[rows, :] = slot_ref[2 * size :, :].astype(jnp.float32)


def merge_kernel(parts, me_ref, *refs):
    *others, gain_ref, prefix_ref = refs[parts:] if len(refs) == parts + 4 else refs[parts + 1 :]
    collect(me_ref[0], 1 - me_ref[1], refs[:parts], prefix_ref, gain_ref)
    each = parts // len(others)
    for turn, other_ref in enumerate(others):
        other_ref[...] = prefix_ref[turn * each : (turn + 1) * each]


def output_kernel(
    dim, owned, half, begin, count, parts, me_ref,
    queries_ref, inside_ref, gate_ref, decay_ref, *refs,
):
    out_ref, done_ref, prefix_ref, gain_ref, result_ref, sent = refs[-6:]
    core = me_ref[1]
    if parts is None:
        *others, gains = refs[:3]
        each = others[0].shape[0]
        prefixes = [others[at // each].at[at % each] for at in range(each * len(others))]
    else:
        collect(me_ref[0], core, refs[:parts], prefix_ref, gain_ref)
        prefixes, gains = [prefix_ref.at[at] for at in range(parts)], gain_ref
    length = decay_ref.shape[2]
    average = jnp.full((dim, dim), 1.0 / dim, jnp.bfloat16)
    moves = []
    for turn in range(count // STEP):
        first = (1 - core if parts is None else core) * half + begin + turn * STEP
        decay = decays_at(decay_ref, core, first)
        gain = gains[pl.ds(pl.multiple_of(first, STEP), STEP), :]
        down = jnp.exp(exact_dot(triangle(length, lambda t, u: u <= t), decay, NT))
        columns = [heads_at(first, head, dim) for head in range(STEP)]
        carried = []
        for head, c in enumerate(columns):
            owner, spot = divmod(turn * STEP + head, owned)
            prefix = prefixes[owner][spot * dim : (spot + 1) * dim, :]
            carried.append(dot(queries_ref[0, :, c], prefix, NN))
        mixed, means = [], []
        for head in range(STEP):
            at = (turn * STEP + head) * dim
            mixed.append(inside_ref[:, at : at + dim] + carried[head] * down[:, head : head + 1])
            means.append(dot((mixed[head] * mixed[head]).astype(jnp.bfloat16), average, NN))
        for head, c in enumerate(columns):
            half_gain = 0.5 * gain[head : head + 1, :]
            turned = jnp.tanh(0.5 * gate_ref[0, :, c].astype(jnp.float32))
            normed = mixed[head] * lax.rsqrt(means[head] + 1e-06) * (half_gain + half_gain * turned)
            result_ref[turn, :, head * dim : (head + 1) * dim] = normed.astype(jnp.bfloat16)
        width = STEP * dim
        moves.append(
            pltpu.make_async_copy(
                result_ref.at[turn],
                out_ref.at[0, :, pl.ds(pl.multiple_of(first * dim, width), width)],
                sent.at[turn],
            )
        )
        moves[-1].start()
    done_ref[...] = jnp.zeros_like(done_ref)
    for move in moves:
        move.wait()


def kernel_call(body, name, in_specs, out_specs, out_shape, scratch=(), aliases={}, cost=0):
    return pl.pallas_call(
        body,
        grid_spec=pltpu.PrefetchScalarGridSpec(
            num_scalar_prefetch=1,
            grid=(),
            in_specs=in_specs,
            out_specs=out_specs,
            scratch_shapes=scratch,
        ),
        out_shape=out_shape,
        input_output_aliases=aliases,
        compiler_params=pltpu.CompilerParams(vmem_limit_bytes=VMEM_LIMIT),
        cost_estimate=pl.CostEstimate(
            flops=int(1e9 * cost) + 1, transcendentals=0, bytes_accessed=1
        ),
        name=name,
    )


def on_device(parts, planes, queries, keys, values, gate, log_decay, norm_gain):
    _, length, width = queries.shape
    local = log_decay.shape[1]
    dim = width // (local * parts)
    count = 2 * parts
    half = local * parts // 2
    owned = half // (GROUPS * parts)
    rows = owned * dim + EXTRA
    me = jnp.stack([lax.axis_index(axis) for axis in ("head", "core", "z")]).astype(jnp.int32)
    swap = [(0, 1), (1, 0)]

    values_other = lax.ppermute(values, "core", swap)
    keys_other = lax.ppermute(keys, "core", swap)
    packed = pl.pallas_call(
        functools.partial(pack_kernel, parts),
        out_shape=jax.ShapeDtypeStruct((count, local, length), jnp.float32),
        name="pack",
    )(log_decay)
    decay = lax.all_to_all(packed, ("core", "head"), 0, 0, tiled=True)
    gain = norm_gain.reshape(local, dim)

    vmem = pl.BlockSpec(memory_space=pltpu.VMEM)
    hbm = pl.BlockSpec(memory_space=pl.ANY)

    def in_vmem(array):
        return pltpu.with_memory_space_constraint(array, pltpu.VMEM)

    def in_hbm(array):
        return pltpu.with_memory_space_constraint(array, pltpu.HBM)

    own = in_hbm(keys), in_hbm(values)
    keys, values, queries, gate = (in_vmem(array) for array in (keys, values, queries, gate))

    def exchange(slots):
        arrived = list(slots)
        for slot in sorted(range(1, parts), key=lambda s: -bin(s).count("1")):
            pairs = [(at, at ^ slot) for at in range(parts)]
            arrived[slot] = lax.ppermute(slots[slot], "head", pairs)
        return arrived

    before = ()
    held = []
    state_type = jax.ShapeDtypeStruct((2, rows, dim), jnp.bfloat16)
    share = half // GROUPS
    token = jax.ShapeDtypeStruct((8, 128), jnp.float32)
    inside = {}

    def inside_part(before, cost=0):
        group, other = divmod(len(inside), 2)
        inside[group, other], made = kernel_call(
            functools.partial(inside_kernel, dim, half, group * share, share, other),
            f"inside{group}_{other}",
            [vmem] * 4 + [hbm] * len(before),
            [vmem] * 2,
            [pltpu.VMEM((length, share * dim), jnp.float32), token],
            cost=cost,
        )(me, queries, keys, values, decay, *before)
        return (made,)

    for group in range(GROUPS):
        slots = {}
        for masks in ((1,), (0,)) if group == 0 else ((1, 0),):
            state = kernel_call(
                functools.partial(state_kernel, dim, owned, half, group * share, masks),
                f"state{group}_{masks[0]}",
                [vmem] + [hbm] * (4 + len(before)),
                [vmem] * (2 * len(masks)),
                [state_type] * (2 * len(masks)),
                [
                    pltpu.VMEM((len(masks), 2) + state_type.shape, jnp.bfloat16),
                    pltpu.VMEM((len(masks), 4, length, STEP * dim), jnp.bfloat16),
                    pltpu.SemaphoreType.DMA((len(masks), 4)),
                ],
            )(me, decay, *own, keys_other, values_other, *before)
            before = tuple(state[:1])
            for at, array in enumerate(state):
                slots[2 * masks[at // 2] + at % 2] = array
        held.append(exchange([slots[slot] for slot in range(parts)]))
        if group == 0:
            before = inside_part(inside_part(before))

    arrived = []
    stacked = pltpu.VMEM((count, rows, dim), jnp.bfloat16)
    total_type = jax.ShapeDtypeStruct((rows, dim), jnp.bfloat16)

    def with_plane(total, step):
        pairs = [(at, at ^ (1 << step)) for at in range(planes)]
        return lax.ppermute(total, "z", pairs)

    def widen(group, step, total, other, before):
        return kernel_call(
            functools.partial(widen_kernel, dim, owned, step),
            f"widen{group}_{step}",
            [vmem] * 2 + [hbm] * len(before),
            vmem,
            total_type,
        )(me, total, other, *before)

    def prefix_of(group, before):
        stretches = arrived[group]
        return kernel_call(
            functools.partial(prefix_kernel, dim, owned, parts, len(stretches)),
            f"prefix{group}",
            [vmem] * (1 + parts + len(stretches)) + [hbm] * len(before),
            [vmem] * parts,
            [prefix_type] * parts,
            [stacked, pltpu.VMEM((count, size, dim), jnp.bfloat16)],
        )(me, gain, *held[group], *stretches, *before)

    size = owned * dim
    prefix_type = jax.ShapeDtypeStruct((2 * size + local, dim), jnp.bfloat16)
    prefixes = []
    for group in range(GROUPS):
        total = kernel_call(
            functools.partial(total_kernel, dim, owned, parts),
            f"total{group}",
            [vmem] * parts + [hbm],
            vmem,
            total_type,
            [stacked],
        )(me, *held[group], *before)
        before = (total,)
        stretches = [with_plane(total, 0)]
        arrived.append(stretches)
        if group > 0:
            prefix = prefix_of(group - 1, before)
            before = tuple(prefix[:1])
            prefixes.append(exchange(prefix))
        if group < GROUPS - 1:
            before = inside_part(before)
        for step in range(1, planes.bit_length() - 1):
            total = widen(group, step - 1, total, stretches[-1], before)
            before = (total,)
            stretches.append(with_plane(total, step))
        while group == GROUPS - 1 and len(inside) < 2 * GROUPS:
            before = inside_part(before, 2)
    prefix = prefix_of(GROUPS - 1, before)
    before = tuple(prefix[:1])
    prefixes.append(exchange(prefix))

    part_type = jax.ShapeDtypeStruct((parts, size, dim), jnp.bfloat16)
    half_type = jax.ShapeDtypeStruct((parts // 2, size, dim), jnp.bfloat16)
    gain_type = jax.ShapeDtypeStruct((parts * local, dim), jnp.float32)

    def merge(group, before, cost):
        return kernel_call(
            functools.partial(merge_kernel, parts),
            f"merge{group}",
            [vmem] * parts + [hbm] * len(before),
            [vmem] * 3,
            [half_type, half_type, gain_type],
            [pltpu.VMEM(part_type.shape, part_type.dtype)],
            cost=cost,
        )(me, *prefixes[group], *before)

    def output(group, other, received, out, before, cost=0):
        *out, made = kernel_call(
            functools.partial(
                output_kernel, dim, owned, half, group * share, share, None if other else parts
            ),
            f"output{group}_{other}",
            [vmem] * (4 + len(received)) + [hbm] * (len(out) + len(before)),
            [hbm, vmem],
            [pltpu.HBM((1, length, width), jnp.bfloat16), token],
            [
                pltpu.VMEM(part_type.shape, part_type.dtype),
                pltpu.VMEM(gain_type.shape, gain_type.dtype),
                pltpu.VMEM((share // STEP, length, STEP * dim), jnp.bfloat16),
                pltpu.SemaphoreType.DMA((share // STEP,)),
            ],
            aliases={5 + len(received): 0} if out else {},
            cost=cost,
        )(me, queries, in_vmem(inside[group, other]), gate, decay, *received, *out, *before)
        return out, (made,)

    out = ()
    for group in range(GROUPS):
        last = group == GROUPS - 1
        if not last:
            out, before = output(group, 0, prefixes[group], out, before)
        *others, gains = merge(group, before, 0)
        others = [lax.ppermute(other, "core", swap) for other in others]
        before = (gains,)
        if last:
            out, before = output(group, 0, prefixes[group], out, before, cost=20)
        out, before = output(group, 1, (*others, gains), out, before)
    return out[0]


def solution(mesh):
    parts, blocks = mesh.shape["head"], mesh.shape["ctx"]
    names = mesh.axis_names
    at = names.index("ctx")
    shape = mesh.devices.shape[:at] + (blocks // 2, 2) + mesh.devices.shape[at + 1 :]
    finer = Mesh(mesh.devices.reshape(shape), names[:at] + ("z", "core") + names[at + 1 :])
    tokens = P(("z", "core"), "head", None)
    return jax.shard_map(
        functools.partial(on_device, parts, blocks // 2),
        mesh=finer,
        in_specs=(tokens,) * 5 + (P("head"),),
        out_specs=tokens,
        check_vma=False,
    )
```

```python
import functools

import jax
import jax.numpy as jnp
from jax import lax
from jax.experimental import pallas as pl
from jax.experimental.pallas import tpu as pltpu
from jax.sharding import Mesh
from jax.sharding import PartitionSpec as P

GROUPS = 2
STEP = 8
EXTRA = 16
VMEM_LIMIT = 8 * 1024 * 1024
NN = (((1,), (0,)), ((), ()))
NT = (((1,), (1,)), ((), ()))
TN = (((0,), (0,)), ((), ()))


def dot(a, b, dims, precision=None):
    return lax.dot_general(a, b, dims, precision=precision, preferred_element_type=jnp.float32)


def split(value):
    first = value.astype(jnp.bfloat16)
    left = value - first.astype(jnp.float32)
    second = left.astype(jnp.bfloat16)
    return first, second, (left - second.astype(jnp.float32)).astype(jnp.bfloat16)


def sums_over(decay, keep):
    heads, length = decay.shape
    rows = lax.broadcasted_iota(jnp.int32, (length, length), 0)
    columns = lax.broadcasted_iota(jnp.int32, (length, length), 1)
    chosen = jnp.where(keep(rows, columns), 1.0, 0.0).astype(jnp.bfloat16)
    parts = [part.astype(jnp.float32) for part in split(decay)]
    both = dot(jnp.concatenate(parts, axis=0).astype(jnp.bfloat16), chosen, NN)
    return both[:heads] + (both[heads : 2 * heads] + both[2 * heads :])


def join(rows, head):
    wide = rows.astype(jnp.float32)
    return wide[3 * head : 3 * head + 1] + (
        wide[3 * head + 1 : 3 * head + 2] + wide[3 * head + 2 : 3 * head + 3]
    )


def decay_rows(totals):
    parts = [part for total in totals for part in split(total)]
    blank = jnp.zeros((EXTRA - len(parts), totals[0].shape[1]), jnp.bfloat16)
    return jnp.concatenate(parts + [blank], axis=0)


def pack_kernel(parts, decay_ref, packed_ref):
    length = packed_ref.shape[2]
    for place in range(packed_ref.shape[0]):
        start = place % parts * length
        packed_ref[place] = decay_ref[0, :, start : start + length]


def heads_at(first, head, dim):
    return pl.ds(pl.multiple_of((first + head) * dim, dim), dim)


def decays_at(decay_ref, block, first):
    local = decay_ref.shape[1]
    parts = decay_ref.shape[0] // 2
    rows = pl.ds(pl.multiple_of(first % local, STEP), STEP)
    return decay_ref[block * parts + first // local, rows, :]


def state_kernel(dim, owned, half, begin, masks, me_ref, decay_ref, *refs):
    arrays, slots = refs[:4], refs[-3 - 2 * len(masks) : -3]
    stacked_ref, copy_ref, done = refs[-3:]
    part, core = me_ref[0], me_ref[1]
    firsts = [core * half + begin + ((part >> 1) ^ mask) * STEP for mask in masks]
    width = STEP * dim
    moves = [
        [
            pltpu.make_async_copy(
                ref.at[0, :, pl.ds(pl.multiple_of(first * dim, width), width)],
                copy_ref.at[turn, at],
                done.at[turn, at],
            )
            for at, ref in enumerate(arrays)
        ]
        for turn, first in enumerate(firsts)
    ]
    for move in sum(moves, []):
        move.start()
    for turn, first in enumerate(firsts):
        for source in range(2):
            block = core if source == 0 else 1 - core
            decay = decays_at(decay_ref, block, first)
            weight = jnp.exp(sums_over(decay, lambda u, s: u > s))
            whole = jnp.broadcast_to(jnp.sum(decay, axis=1, keepdims=True), (STEP, dim))
            for move in moves[turn][2 * source : 2 * source + 2]:
                move.wait()
            states = []
            for head in range(STEP):
                c = slice(head * dim, (head + 1) * dim)
                decayed = copy_ref[turn, 2 * source, :, c].T.astype(jnp.float32)
                decayed = (decayed * weight[head : head + 1, :]).astype(jnp.bfloat16)
                states.append(dot(decayed, copy_ref[turn, 2 * source + 1, :, c], NN))
            for head in range(STEP):
                owner, spot = divmod(head, owned)
                span = slice(spot * dim, (spot + 1) * dim)
                stacked_ref[turn, owner, block, span, :] = states[head].astype(jnp.bfloat16)
            for at in range(2):
                stacked_ref[turn, at, block, owned * dim :, :] = decay_rows(
                    [whole[head : head + 1] for head in range(at * owned, (at + 1) * owned)]
                )
        for at in range(2):
            slots[2 * turn + at][...] = stacked_ref[turn, (part & 1) ^ at]


def inside_kernel(
    dim, half, begin, count, other, me_ref, queries_ref, keys_ref, values_ref, decay_ref, *rest
):
    inside_ref, done_ref = rest[-2:]
    core = me_ref[1]
    length = decay_ref.shape[2]
    rows = lax.broadcasted_iota(jnp.int32, (length, length), 0)
    causal = rows >= lax.broadcasted_iota(jnp.int32, (length, length), 1)
    for turn in range(count // STEP):
        first = (1 - core if other else core) * half + begin + turn * STEP
        decay = decays_at(decay_ref, core, first)
        across = sums_over(decay, lambda u, s: u <= s)
        down = across.T
        columns = [heads_at(first, head, dim) for head in range(STEP)]
        scores = [dot(queries_ref[0, :, c], keys_ref[0, :, c], NT) for c in columns]
        weights = []
        for head in range(STEP):
            gap = down[:, head : head + 1] - across[head : head + 1, :]
            weight = scores[head] * jnp.exp(jnp.where(causal, gap, -jnp.inf))
            weights.append(weight.astype(jnp.bfloat16))
        for head, c in enumerate(columns):
            at = (turn * STEP + head) * dim
            inside_ref[:, at : at + dim] = dot(weights[head], values_ref[0, :, c], NN)
    done_ref[...] = jnp.zeros_like(done_ref)


def gather_states(part, slots, stacked_ref):
    parts = len(slots)
    for slot, slot_ref in enumerate(slots):
        for block in range(2):
            stacked_ref[block * parts + (part ^ slot)] = slot_ref[block]


def total_kernel(dim, owned, parts, me_ref, *refs):
    total_ref, stacked_ref = refs[-2:]
    gather_states(me_ref[0], refs[:parts], stacked_ref)
    count = 2 * parts
    extra = [stacked_ref[at, owned * dim :, :] for at in range(count)]
    sums = []
    for head in range(owned):
        span = slice(head * dim, (head + 1) * dim)
        after = jnp.zeros((1, dim), jnp.float32)
        total = stacked_ref[count - 1, span, :].astype(jnp.float32)
        for at in range(count - 2, -1, -1):
            after += join(extra[at + 1], head)
            total += jnp.exp(after) * stacked_ref[at, span, :].astype(jnp.float32)
        total_ref[span, :] = total.astype(jnp.bfloat16)
        sums.append(after + join(extra[0], head))
    total_ref[owned * dim :, :] = decay_rows(sums)


def widen_kernel(dim, owned, step, me_ref, mine_ref, other_ref, *refs):
    out_ref = refs[-1]
    later = (me_ref[2] >> step) % 2 == 1
    extra = mine_ref[owned * dim :, :], other_ref[owned * dim :, :]
    sums = []
    for head in range(owned):
        span = slice(head * dim, (head + 1) * dim)
        mine, other = join(extra[0], head), join(extra[1], head)
        total = jnp.where(later, 1.0, jnp.exp(other)) * mine_ref[span, :].astype(jnp.float32)
        total += jnp.where(later, jnp.exp(mine), 1.0) * other_ref[span, :].astype(jnp.float32)
        out_ref[span, :] = total.astype(jnp.bfloat16)
        sums.append(mine + other)
    out_ref[owned * dim :, :] = decay_rows(sums)


def prefix_kernel(dim, owned, parts, stretches, me_ref, gain_ref, *refs):
    stacked_ref, prefix_ref = refs[-2:]
    slots, totals = refs[:parts], refs[parts : parts + stretches]
    count = 2 * parts
    results = refs[-2 - parts : -2]
    gather_states(me_ref[0], slots, stacked_ref)
    extra = [stacked_ref[at, owned * dim :, :] for at in range(count)]
    more = [total_ref[owned * dim :, :] for total_ref in totals]
    earlier = [
        ((me_ref[2] >> step) % 2).astype(jnp.float32) for step in range(len(totals))
    ]
    for head in range(owned):
        span = slice(head * dim, (head + 1) * dim)
        prefix = jnp.zeros((dim, dim), jnp.float32)
        after = jnp.zeros((1, dim), jnp.float32)
        for turn, total_ref in enumerate(totals):
            factor = earlier[turn] * jnp.exp(after)
            prefix += factor * total_ref[span, :].astype(jnp.float32)
            after += earlier[turn] * join(more[turn], head)
        for at in range(count):
            prefix_ref[at, span, :] = prefix.astype(jnp.bfloat16)
            if at < count - 1:
                prefix = jnp.exp(join(extra[at], head)) * prefix
                prefix += stacked_ref[at, span, :].astype(jnp.float32)
    size = owned * dim
    for slot, result_ref in enumerate(results):
        for block in range(2):
            result_ref[block * size : (block + 1) * size, :] = prefix_ref[
                block * parts + (me_ref[0] ^ slot)
            ]
        result_ref[2 * size :, :] = gain_ref[...]


def collect(part, block, slots, prefix_ref, gain_ref):
    parts, size, _ = prefix_ref.shape
    local = gain_ref.shape[0] // parts
    for slot, slot_ref in enumerate(slots):
        owner = part ^ slot
        prefix_ref[owner] = slot_ref[pl.ds(pl.multiple_of(block * size, size), size), :]
        rows = pl.ds(pl.multiple_of(owner * local, local), local)
        gain_ref[rows, :] = slot_ref[2 * size :, :].astype(jnp.float32)


def merge_kernel(parts, me_ref, *refs):
    *others, gain_ref, prefix_ref = refs[parts:] if len(refs) == parts + 4 else refs[parts + 1 :]
    collect(me_ref[0], 1 - me_ref[1], refs[:parts], prefix_ref, gain_ref)
    each = parts // len(others)
    for turn, other_ref in enumerate(others):
        other_ref[...] = prefix_ref[turn * each : (turn + 1) * each]


def output_kernel(
    dim, owned, half, begin, count, parts, me_ref,
    queries_ref, inside_ref, gate_ref, decay_ref, *refs,
):
    out_ref, done_ref, prefix_ref, gain_ref, result_ref, sent = refs[-6:]
    core = me_ref[1]
    if parts is None:
        *others, gains = refs[:3]
        each = others[0].shape[0]
        prefixes = [others[at // each].at[at % each] for at in range(each * len(others))]
    else:
        collect(me_ref[0], core, refs[:parts], prefix_ref, gain_ref)
        prefixes, gains = [prefix_ref.at[at] for at in range(parts)], gain_ref
    length = decay_ref.shape[2]
    average = jnp.full((dim, dim), 1.0 / dim, jnp.bfloat16)
    moves = []
    for turn in range(count // STEP):
        first = (1 - core if parts is None else core) * half + begin + turn * STEP
        decay = decays_at(decay_ref, core, first)
        gain = gains[pl.ds(pl.multiple_of(first, STEP), STEP), :]
        down = jnp.exp(sums_over(decay, lambda u, t: u <= t)).T
        columns = [heads_at(first, head, dim) for head in range(STEP)]
        carried = []
        for head, c in enumerate(columns):
            owner, spot = divmod(turn * STEP + head, owned)
            prefix = prefixes[owner][spot * dim : (spot + 1) * dim, :]
            carried.append(dot(queries_ref[0, :, c], prefix, NN))
        mixed, means = [], []
        for head in range(STEP):
            at = (turn * STEP + head) * dim
            mixed.append(inside_ref[:, at : at + dim] + carried[head] * down[:, head : head + 1])
            means.append(dot((mixed[head] * mixed[head]).astype(jnp.bfloat16), average, NN))
        for head, c in enumerate(columns):
            half_gain = 0.5 * gain[head : head + 1, :]
            turned = jnp.tanh(0.5 * gate_ref[0, :, c].astype(jnp.float32))
            normed = mixed[head] * lax.rsqrt(means[head] + 1e-06) * (half_gain + half_gain * turned)
            result_ref[turn, :, head * dim : (head + 1) * dim] = normed.astype(jnp.bfloat16)
        width = STEP * dim
        moves.append(
            pltpu.make_async_copy(
                result_ref.at[turn],
                out_ref.at[0, :, pl.ds(pl.multiple_of(first * dim, width), width)],
                sent.at[turn],
            )
        )
        moves[-1].start()
    done_ref[...] = jnp.zeros_like(done_ref)
    for move in moves:
        move.wait()


def kernel_call(body, name, in_specs, out_specs, out_shape, scratch=(), aliases={}, cost=0):
    return pl.pallas_call(
        body,
        grid_spec=pltpu.PrefetchScalarGridSpec(
            num_scalar_prefetch=1,
            grid=(),
            in_specs=in_specs,
            out_specs=out_specs,
            scratch_shapes=scratch,
        ),
        out_shape=out_shape,
        input_output_aliases=aliases,
        compiler_params=pltpu.CompilerParams(vmem_limit_bytes=VMEM_LIMIT),
        cost_estimate=pl.CostEstimate(
            flops=int(1e9 * cost) + 1, transcendentals=0, bytes_accessed=1
        ),
        name=name,
    )


def on_device(parts, planes, queries, keys, values, gate, log_decay, norm_gain):
    _, length, width = queries.shape
    local = log_decay.shape[1]
    dim = width // (local * parts)
    count = 2 * parts
    half = local * parts // 2
    owned = half // (GROUPS * parts)
    rows = owned * dim + EXTRA
    me = jnp.stack([lax.axis_index(axis) for axis in ("head", "core", "z")]).astype(jnp.int32)
    swap = [(0, 1), (1, 0)]

    values_other = lax.ppermute(values, "core", swap)
    keys_other = lax.ppermute(keys, "core", swap)
    packed = pl.pallas_call(
        functools.partial(pack_kernel, parts),
        out_shape=jax.ShapeDtypeStruct((count, local, length), jnp.float32),
        name="pack",
    )(log_decay)
    decay = lax.all_to_all(packed, ("core", "head"), 0, 0, tiled=True)
    gain = norm_gain.reshape(local, dim)

    vmem = pl.BlockSpec(memory_space=pltpu.VMEM)
    hbm = pl.BlockSpec(memory_space=pl.ANY)

    def in_vmem(array):
        return pltpu.with_memory_space_constraint(array, pltpu.VMEM)

    def in_hbm(array):
        return pltpu.with_memory_space_constraint(array, pltpu.HBM)

    own = in_hbm(keys), in_hbm(values)
    keys, values, queries, gate = (in_vmem(array) for array in (keys, values, queries, gate))

    def exchange(slots):
        arrived = list(slots)
        for slot in sorted(range(1, parts), key=lambda s: -bin(s).count("1")):
            pairs = [(at, at ^ slot) for at in range(parts)]
            arrived[slot] = lax.ppermute(slots[slot], "head", pairs)
        return arrived

    before = ()
    held = []
    state_type = jax.ShapeDtypeStruct((2, rows, dim), jnp.bfloat16)
    share = half // GROUPS
    token = jax.ShapeDtypeStruct((8, 128), jnp.float32)
    inside = {}

    def inside_part(before, cost=0):
        group, other = divmod(len(inside), 2)
        inside[group, other], made = kernel_call(
            functools.partial(inside_kernel, dim, half, group * share, share, other),
            f"inside{group}_{other}",
            [vmem] * 4 + [hbm] * len(before),
            [vmem] * 2,
            [pltpu.VMEM((length, share * dim), jnp.float32), token],
            cost=cost,
        )(me, queries, keys, values, decay, *before)
        return (made,)

    for group in range(GROUPS):
        slots = {}
        for masks in ((1,), (0,)) if group == 0 else ((1, 0),):
            state = kernel_call(
                functools.partial(state_kernel, dim, owned, half, group * share, masks),
                f"state{group}_{masks[0]}",
                [vmem] + [hbm] * (4 + len(before)),
                [vmem] * (2 * len(masks)),
                [state_type] * (2 * len(masks)),
                [
                    pltpu.VMEM((len(masks), 2) + state_type.shape, jnp.bfloat16),
                    pltpu.VMEM((len(masks), 4, length, STEP * dim), jnp.bfloat16),
                    pltpu.SemaphoreType.DMA((len(masks), 4)),
                ],
            )(me, decay, *own, keys_other, values_other, *before)
            before = tuple(state[:1])
            for at, array in enumerate(state):
                slots[2 * masks[at // 2] + at % 2] = array
        held.append(exchange([slots[slot] for slot in range(parts)]))
        if group == 0:
            before = inside_part(inside_part(before))

    arrived = []
    stacked = pltpu.VMEM((count, rows, dim), jnp.bfloat16)
    total_type = jax.ShapeDtypeStruct((rows, dim), jnp.bfloat16)

    def with_plane(total, step):
        pairs = [(at, at ^ (1 << step)) for at in range(planes)]
        return lax.ppermute(total, "z", pairs)

    def widen(group, step, total, other, before):
        return kernel_call(
            functools.partial(widen_kernel, dim, owned, step),
            f"widen{group}_{step}",
            [vmem] * 2 + [hbm] * len(before),
            vmem,
            total_type,
        )(me, total, other, *before)

    def prefix_of(group, before):
        stretches = arrived[group]
        return kernel_call(
            functools.partial(prefix_kernel, dim, owned, parts, len(stretches)),
            f"prefix{group}",
            [vmem] * (1 + parts + len(stretches)) + [hbm] * len(before),
            [vmem] * parts,
            [prefix_type] * parts,
            [stacked, pltpu.VMEM((count, size, dim), jnp.bfloat16)],
        )(me, gain, *held[group], *stretches, *before)

    size = owned * dim
    prefix_type = jax.ShapeDtypeStruct((2 * size + local, dim), jnp.bfloat16)
    prefixes = []
    for group in range(GROUPS):
        total = kernel_call(
            functools.partial(total_kernel, dim, owned, parts),
            f"total{group}",
            [vmem] * parts + [hbm],
            vmem,
            total_type,
            [stacked],
        )(me, *held[group], *before)
        before = (total,)
        stretches = [with_plane(total, 0)]
        arrived.append(stretches)
        if group > 0:
            prefix = prefix_of(group - 1, before)
            before = tuple(prefix[:1])
            prefixes.append(exchange(prefix))
        if group < GROUPS - 1:
            before = inside_part(before)
        for step in range(1, planes.bit_length() - 1):
            total = widen(group, step - 1, total, stretches[-1], before)
            before = (total,)
            stretches.append(with_plane(total, step))
        while group == GROUPS - 1 and len(inside) < 2 * GROUPS:
            before = inside_part(before, 2)
    prefix = prefix_of(GROUPS - 1, before)
    before = tuple(prefix[:1])
    prefixes.append(exchange(prefix))

    part_type = jax.ShapeDtypeStruct((parts, size, dim), jnp.bfloat16)
    half_type = jax.ShapeDtypeStruct((parts // 2, size, dim), jnp.bfloat16)
    gain_type = jax.ShapeDtypeStruct((parts * local, dim), jnp.float32)

    def merge(group, before, cost):
        return kernel_call(
            functools.partial(merge_kernel, parts),
            f"merge{group}",
            [vmem] * parts + [hbm] * len(before),
            [vmem] * 3,
            [half_type, half_type, gain_type],
            [pltpu.VMEM(part_type.shape, part_type.dtype)],
            cost=cost,
        )(me, *prefixes[group], *before)

    def output(group, other, received, out, before, cost=0):
        *out, made = kernel_call(
            functools.partial(
                output_kernel, dim, owned, half, group * share, share, None if other else parts
            ),
            f"output{group}_{other}",
            [vmem] * (4 + len(received)) + [hbm] * (len(out) + len(before)),
            [hbm, vmem],
            [pltpu.HBM((1, length, width), jnp.bfloat16), token],
            [
                pltpu.VMEM(part_type.shape, part_type.dtype),
                pltpu.VMEM(gain_type.shape, gain_type.dtype),
                pltpu.VMEM((share // STEP, length, STEP * dim), jnp.bfloat16),
                pltpu.SemaphoreType.DMA((share // STEP,)),
            ],
            aliases={5 + len(received): 0} if out else {},
            cost=cost,
        )(me, queries, in_vmem(inside[group, other]), gate, decay, *received, *out, *before)
        return out, (made,)

    out = ()
    for group in range(GROUPS):
        last = group == GROUPS - 1
        if not last:
            out, before = output(group, 0, prefixes[group], out, before)
        *others, gains = merge(group, before, 0)
        others = [lax.ppermute(other, "core", swap) for other in others]
        before = (gains,)
        if last:
            out, before = output(group, 0, prefixes[group], out, before, cost=20)
        out, before = output(group, 1, (*others, gains), out, before)
    return out[0]


def solution(mesh):
    parts, blocks = mesh.shape["head"], mesh.shape["ctx"]
    names = mesh.axis_names
    at = names.index("ctx")
    shape = mesh.devices.shape[:at] + (blocks // 2, 2) + mesh.devices.shape[at + 1 :]
    finer = Mesh(mesh.devices.reshape(shape), names[:at] + ("z", "core") + names[at + 1 :])
    tokens = P(("z", "core"), "head", None)
    return jax.shard_map(
        functools.partial(on_device, parts, blocks // 2),
        mesh=finer,
        in_specs=(tokens,) * 5 + (P("head"),),
        out_specs=tokens,
        check_vma=False,
    )
```

```python
import functools

import jax
import jax.numpy as jnp
from jax import lax
from jax.experimental import pallas as pl
from jax.experimental.pallas import tpu as pltpu
from jax.sharding import Mesh
from jax.sharding import PartitionSpec as P

GROUPS = 2
STEP = 8
EXTRA = 16
VMEM_LIMIT = 8 * 1024 * 1024
NN = (((1,), (0,)), ((), ()))
NT = (((1,), (1,)), ((), ()))
TN = (((0,), (0,)), ((), ()))


def dot(a, b, dims, precision=None):
    return lax.dot_general(a, b, dims, precision=precision, preferred_element_type=jnp.float32)


def split(value):
    first = value.astype(jnp.bfloat16)
    left = value - first.astype(jnp.float32)
    second = left.astype(jnp.bfloat16)
    return first, second, (left - second.astype(jnp.float32)).astype(jnp.bfloat16)


def sums_over(decay, keep):
    heads, length = decay.shape
    rows = lax.broadcasted_iota(jnp.int32, (length, length), 0)
    columns = lax.broadcasted_iota(jnp.int32, (length, length), 1)
    chosen = jnp.where(keep(rows, columns), 1.0, 0.0).astype(jnp.bfloat16)
    parts = [part.astype(jnp.float32) for part in split(decay)]
    both = dot(jnp.concatenate(parts, axis=0).astype(jnp.bfloat16), chosen, NN)
    return both[:heads] + (both[heads : 2 * heads] + both[2 * heads :])


def join(rows, head):
    wide = rows.astype(jnp.float32)
    return wide[3 * head : 3 * head + 1] + (
        wide[3 * head + 1 : 3 * head + 2] + wide[3 * head + 2 : 3 * head + 3]
    )


def decay_rows(totals):
    parts = [part for total in totals for part in split(total)]
    blank = jnp.zeros((EXTRA - len(parts), totals[0].shape[1]), jnp.bfloat16)
    return jnp.concatenate(parts + [blank], axis=0)


def pack_kernel(parts, decay_ref, packed_ref):
    length = packed_ref.shape[2]
    for place in range(packed_ref.shape[0]):
        start = place % parts * length
        packed_ref[place] = decay_ref[0, :, start : start + length]


def gate_kernel(half, share, dim, me_ref, gate_ref, *refs):
    *results, copy_ref, result_ref, done = refs[1:]
    load = pltpu.make_async_copy(gate_ref.at[0], copy_ref, done.at[len(results)])
    load.start()
    load.wait()
    moves = []
    for at, out_ref in enumerate(results):
        group, other = divmod(at, 2)
        which = 1 - me_ref[1] if other else me_ref[1]
        for head in range(share):
            gate = copy_ref[:, heads_at(which * half + group * share, head, dim)]
            turned = jnp.tanh(0.5 * gate.astype(jnp.float32))
            result_ref[at, :, head * dim : (head + 1) * dim] = 0.5 + 0.5 * turned
        moves.append(pltpu.make_async_copy(result_ref.at[at], out_ref, done.at[at]))
        moves[-1].start()
    for move in moves:
        move.wait()


def heads_at(first, head, dim):
    return pl.ds(pl.multiple_of((first + head) * dim, dim), dim)


def decays_at(decay_ref, block, first):
    local = decay_ref.shape[1]
    parts = decay_ref.shape[0] // 2
    rows = pl.ds(pl.multiple_of(first % local, STEP), STEP)
    return decay_ref[block * parts + first // local, rows, :]


def state_kernel(dim, owned, half, begin, masks, me_ref, decay_ref, *refs):
    arrays, slots = refs[:4], refs[-3 - 2 * len(masks) : -3]
    stacked_ref, copy_ref, done = refs[-3:]
    part, core = me_ref[0], me_ref[1]
    firsts = [core * half + begin + ((part >> 1) ^ mask) * STEP for mask in masks]
    width = STEP * dim
    moves = [
        [
            pltpu.make_async_copy(
                ref.at[0, :, pl.ds(pl.multiple_of(first * dim, width), width)],
                copy_ref.at[turn, at],
                done.at[turn, at],
            )
            for at, ref in enumerate(arrays)
        ]
        for turn, first in enumerate(firsts)
    ]
    for move in sum(moves, []):
        move.start()
    for turn, first in enumerate(firsts):
        for source in range(2):
            block = core if source == 0 else 1 - core
            decay = decays_at(decay_ref, block, first)
            weight = jnp.exp(sums_over(decay, lambda u, s: u > s))
            whole = jnp.broadcast_to(jnp.sum(decay, axis=1, keepdims=True), (STEP, dim))
            for move in moves[turn][2 * source : 2 * source + 2]:
                move.wait()
            states = []
            for head in range(STEP):
                c = slice(head * dim, (head + 1) * dim)
                decayed = copy_ref[turn, 2 * source, :, c].T.astype(jnp.float32)
                decayed = (decayed * weight[head : head + 1, :]).astype(jnp.bfloat16)
                states.append(dot(decayed, copy_ref[turn, 2 * source + 1, :, c], NN))
            for head in range(STEP):
                owner, spot = divmod(head, owned)
                span = slice(spot * dim, (spot + 1) * dim)
                stacked_ref[turn, owner, block, span, :] = states[head].astype(jnp.bfloat16)
            for at in range(2):
                stacked_ref[turn, at, block, owned * dim :, :] = decay_rows(
                    [whole[head : head + 1] for head in range(at * owned, (at + 1) * owned)]
                )
        for at in range(2):
            slots[2 * turn + at][...] = stacked_ref[turn, (part & 1) ^ at]


def inside_kernel(
    dim, half, begin, count, other, me_ref, queries_ref, keys_ref, values_ref, decay_ref, *rest
):
    inside_ref, down_ref, done_ref = rest[-3:]
    core = me_ref[1]
    length = decay_ref.shape[2]
    rows = lax.broadcasted_iota(jnp.int32, (length, length), 0)
    causal = rows >= lax.broadcasted_iota(jnp.int32, (length, length), 1)
    for turn in range(count // STEP):
        first = (1 - core if other else core) * half + begin + turn * STEP
        decay = decays_at(decay_ref, core, first)
        across = sums_over(decay, lambda u, s: u <= s)
        down = across.T
        down_ref[turn] = jnp.exp(down)
        columns = [heads_at(first, head, dim) for head in range(STEP)]
        scores = [dot(queries_ref[0, :, c], keys_ref[0, :, c], NT) for c in columns]
        weights = []
        for head in range(STEP):
            gap = down[:, head : head + 1] - across[head : head + 1, :]
            weight = scores[head] * jnp.exp(jnp.where(causal, gap, -jnp.inf))
            weights.append(weight.astype(jnp.bfloat16))
        for head, c in enumerate(columns):
            at = (turn * STEP + head) * dim
            inside_ref[:, at : at + dim] = dot(weights[head], values_ref[0, :, c], NN)
    done_ref[...] = jnp.zeros_like(done_ref)


def gather_states(part, slots, stacked_ref):
    parts = len(slots)
    for slot, slot_ref in enumerate(slots):
        for block in range(2):
            stacked_ref[block * parts + (part ^ slot)] = slot_ref[block]


def total_kernel(dim, owned, parts, me_ref, *refs):
    total_ref, stacked_ref = refs[-2:]
    gather_states(me_ref[0], refs[:parts], stacked_ref)
    count = 2 * parts
    extra = [stacked_ref[at, owned * dim :, :] for at in range(count)]
    sums = []
    for head in range(owned):
        span = slice(head * dim, (head + 1) * dim)
        after = jnp.zeros((1, dim), jnp.float32)
        total = stacked_ref[count - 1, span, :].astype(jnp.float32)
        for at in range(count - 2, -1, -1):
            after += join(extra[at + 1], head)
            total += jnp.exp(after) * stacked_ref[at, span, :].astype(jnp.float32)
        total_ref[span, :] = total.astype(jnp.bfloat16)
        sums.append(after + join(extra[0], head))
    total_ref[owned * dim :, :] = decay_rows(sums)


def widen_kernel(dim, owned, step, me_ref, mine_ref, other_ref, *refs):
    out_ref = refs[-1]
    later = (me_ref[2] >> step) % 2 == 1
    extra = mine_ref[owned * dim :, :], other_ref[owned * dim :, :]
    sums = []
    for head in range(owned):
        span = slice(head * dim, (head + 1) * dim)
        mine, other = join(extra[0], head), join(extra[1], head)
        total = jnp.where(later, 1.0, jnp.exp(other)) * mine_ref[span, :].astype(jnp.float32)
        total += jnp.where(later, jnp.exp(mine), 1.0) * other_ref[span, :].astype(jnp.float32)
        out_ref[span, :] = total.astype(jnp.bfloat16)
        sums.append(mine + other)
    out_ref[owned * dim :, :] = decay_rows(sums)


def prefix_kernel(dim, owned, parts, stretches, me_ref, gain_ref, *refs):
    stacked_ref, prefix_ref = refs[-2:]
    slots, totals = refs[:parts], refs[parts : parts + stretches]
    count = 2 * parts
    results = refs[-2 - parts : -2]
    gather_states(me_ref[0], slots, stacked_ref)
    extra = [stacked_ref[at, owned * dim :, :] for at in range(count)]
    more = [total_ref[owned * dim :, :] for total_ref in totals]
    earlier = [
        ((me_ref[2] >> step) % 2).astype(jnp.float32) for step in range(len(totals))
    ]
    for head in range(owned):
        span = slice(head * dim, (head + 1) * dim)
        prefix = jnp.zeros((dim, dim), jnp.float32)
        after = jnp.zeros((1, dim), jnp.float32)
        for turn, total_ref in enumerate(totals):
            factor = earlier[turn] * jnp.exp(after)
            prefix += factor * total_ref[span, :].astype(jnp.float32)
            after += earlier[turn] * join(more[turn], head)
        for at in range(count):
            prefix_ref[at, span, :] = prefix.astype(jnp.bfloat16)
            if at < count - 1:
                prefix = jnp.exp(join(extra[at], head)) * prefix
                prefix += stacked_ref[at, span, :].astype(jnp.float32)
    size = owned * dim
    for slot, result_ref in enumerate(results):
        for block in range(2):
            result_ref[block * size : (block + 1) * size, :] = prefix_ref[
                block * parts + (me_ref[0] ^ slot)
            ]
        result_ref[2 * size :, :] = gain_ref[...]


def collect(part, block, slots, prefix_ref, gain_ref):
    parts, size, _ = prefix_ref.shape
    local = gain_ref.shape[0] // parts
    for slot, slot_ref in enumerate(slots):
        owner = part ^ slot
        prefix_ref[owner] = slot_ref[pl.ds(pl.multiple_of(block * size, size), size), :]
        rows = pl.ds(pl.multiple_of(owner * local, local), local)
        gain_ref[rows, :] = slot_ref[2 * size :, :].astype(jnp.float32)


def merge_kernel(parts, me_ref, *refs):
    *others, gain_ref, prefix_ref = refs[parts:] if len(refs) == parts + 4 else refs[parts + 1 :]
    collect(me_ref[0], 1 - me_ref[1], refs[:parts], prefix_ref, gain_ref)
    each = parts // len(others)
    for turn, other_ref in enumerate(others):
        other_ref[...] = prefix_ref[turn * each : (turn + 1) * each]


def output_kernel(
    dim, owned, half, begin, count, parts, me_ref,
    queries_ref, inside_ref, down_ref, gate_ref, *refs,
):
    out_ref, done_ref, prefix_ref, gain_ref, result_ref, sent = refs[-6:]
    core = me_ref[1]
    if parts is None:
        *others, gains = refs[:3]
        each = others[0].shape[0]
        prefixes = [others[at // each].at[at % each] for at in range(each * len(others))]
    else:
        collect(me_ref[0], core, refs[:parts], prefix_ref, gain_ref)
        prefixes, gains = [prefix_ref.at[at] for at in range(parts)], gain_ref
    average = jnp.full((dim, dim), 1.0 / dim, jnp.bfloat16)
    moves = []
    for turn in range(count // STEP):
        first = (1 - core if parts is None else core) * half + begin + turn * STEP
        gain = gains[pl.ds(pl.multiple_of(first, STEP), STEP), :]
        down = down_ref[turn]
        columns = [heads_at(first, head, dim) for head in range(STEP)]
        carried = []
        for head, c in enumerate(columns):
            owner, spot = divmod(turn * STEP + head, owned)
            prefix = prefixes[owner][spot * dim : (spot + 1) * dim, :]
            carried.append(dot(queries_ref[0, :, c], prefix, NN))
        mixed, means = [], []
        for head in range(STEP):
            at = (turn * STEP + head) * dim
            mixed.append(inside_ref[:, at : at + dim] + carried[head] * down[:, head : head + 1])
            means.append(dot((mixed[head] * mixed[head]).astype(jnp.bfloat16), average, NN))
        for head in range(STEP):
            at = (turn * STEP + head) * dim
            factor = gain[head : head + 1, :] * gate_ref[:, at : at + dim]
            normed = mixed[head] * lax.rsqrt(means[head] + 1e-06) * factor
            result_ref[turn, :, head * dim : (head + 1) * dim] = normed.astype(jnp.bfloat16)
        width = STEP * dim
        moves.append(
            pltpu.make_async_copy(
                result_ref.at[turn],
                out_ref.at[0, :, pl.ds(pl.multiple_of(first * dim, width), width)],
                sent.at[turn],
            )
        )
        moves[-1].start()
    done_ref[...] = jnp.zeros_like(done_ref)
    for move in moves:
        move.wait()


def kernel_call(body, name, in_specs, out_specs, out_shape, scratch=(), aliases={}, cost=0):
    return pl.pallas_call(
        body,
        grid_spec=pltpu.PrefetchScalarGridSpec(
            num_scalar_prefetch=1,
            grid=(),
            in_specs=in_specs,
            out_specs=out_specs,
            scratch_shapes=scratch,
        ),
        out_shape=out_shape,
        input_output_aliases=aliases,
        compiler_params=pltpu.CompilerParams(vmem_limit_bytes=VMEM_LIMIT),
        cost_estimate=pl.CostEstimate(
            flops=int(1e9 * cost) + 1, transcendentals=0, bytes_accessed=1
        ),
        name=name,
    )


def on_device(parts, planes, queries, keys, values, gate, log_decay, norm_gain):
    _, length, width = queries.shape
    local = log_decay.shape[1]
    dim = width // (local * parts)
    count = 2 * parts
    half = local * parts // 2
    owned = half // (GROUPS * parts)
    rows = owned * dim + EXTRA
    me = jnp.stack([lax.axis_index(axis) for axis in ("head", "core", "z")]).astype(jnp.int32)
    swap = [(0, 1), (1, 0)]

    values_other = lax.ppermute(values, "core", swap)
    keys_other = lax.ppermute(keys, "core", swap)
    packed = pl.pallas_call(
        functools.partial(pack_kernel, parts),
        out_shape=jax.ShapeDtypeStruct((count, local, length), jnp.float32),
        name="pack",
    )(log_decay)
    decay = lax.all_to_all(packed, ("core", "head"), 0, 0, tiled=True)
    gain = norm_gain.reshape(local, dim)

    vmem = pl.BlockSpec(memory_space=pltpu.VMEM)
    hbm = pl.BlockSpec(memory_space=pl.ANY)

    def in_vmem(array):
        return pltpu.with_memory_space_constraint(array, pltpu.VMEM)

    def in_hbm(array):
        return pltpu.with_memory_space_constraint(array, pltpu.HBM)

    own = in_hbm(keys), in_hbm(values)
    share = half // GROUPS
    gate_type = jax.ShapeDtypeStruct((length, share * dim), jnp.float32)
    gates = kernel_call(
        functools.partial(gate_kernel, half, share, dim),
        "gates",
        [hbm] * 2,
        [hbm] * (2 * GROUPS),
        [pltpu.HBM(gate_type.shape, gate_type.dtype)] * (2 * GROUPS),
        [
            pltpu.VMEM((length, width), jnp.bfloat16),
            pltpu.VMEM((2 * GROUPS,) + gate_type.shape, jnp.float32),
            pltpu.SemaphoreType.DMA((2 * GROUPS + 1,)),
        ],
    )(me, in_hbm(gate), packed)
    keys, values, queries = (in_vmem(array) for array in (keys, values, queries))

    def exchange(slots):
        arrived = list(slots)
        for slot in sorted(range(1, parts), key=lambda s: -bin(s).count("1")):
            pairs = [(at, at ^ slot) for at in range(parts)]
            arrived[slot] = lax.ppermute(slots[slot], "head", pairs)
        return arrived

    before = tuple(gates[:1])
    held = []
    state_type = jax.ShapeDtypeStruct((2, rows, dim), jnp.bfloat16)
    token = jax.ShapeDtypeStruct((8, 128), jnp.float32)
    inside = {}

    def inside_part(before, cost=0):
        group, other = divmod(len(inside), 2)
        *inside[group, other], made = kernel_call(
            functools.partial(inside_kernel, dim, half, group * share, share, other),
            f"inside{group}_{other}",
            [vmem] * 4 + [hbm] * len(before),
            [vmem] * 3,
            [
                pltpu.VMEM((length, share * dim), jnp.float32),
                jax.ShapeDtypeStruct((share // STEP, length, STEP), jnp.float32),
                token,
            ],
            cost=cost,
        )(me, queries, keys, values, decay, *before)
        return (made,)

    for group in range(GROUPS):
        slots = {}
        for masks in ((1,), (0,)) if group == 0 else ((1, 0),):
            state = kernel_call(
                functools.partial(state_kernel, dim, owned, half, group * share, masks),
                f"state{group}_{masks[0]}",
                [vmem] + [hbm] * (4 + len(before)),
                [vmem] * (2 * len(masks)),
                [state_type] * (2 * len(masks)),
                [
                    pltpu.VMEM((len(masks), 2) + state_type.shape, jnp.bfloat16),
                    pltpu.VMEM((len(masks), 4, length, STEP * dim), jnp.bfloat16),
                    pltpu.SemaphoreType.DMA((len(masks), 4)),
                ],
            )(me, decay, *own, keys_other, values_other, *before)
            before = tuple(state[:1])
            for at, array in enumerate(state):
                slots[2 * masks[at // 2] + at % 2] = array
        held.append(exchange([slots[slot] for slot in range(parts)]))
        if group == 0:
            before = inside_part(inside_part(before))

    arrived = []
    stacked = pltpu.VMEM((count, rows, dim), jnp.bfloat16)
    total_type = jax.ShapeDtypeStruct((rows, dim), jnp.bfloat16)

    def with_plane(total, step):
        pairs = [(at, at ^ (1 << step)) for at in range(planes)]
        return lax.ppermute(total, "z", pairs)

    def widen(group, step, total, other, before):
        return kernel_call(
            functools.partial(widen_kernel, dim, owned, step),
            f"widen{group}_{step}",
            [vmem] * 2 + [hbm] * len(before),
            vmem,
            total_type,
        )(me, total, other, *before)

    def prefix_of(group, before):
        stretches = arrived[group]
        return kernel_call(
            functools.partial(prefix_kernel, dim, owned, parts, len(stretches)),
            f"prefix{group}",
            [vmem] * (1 + parts + len(stretches)) + [hbm] * len(before),
            [vmem] * parts,
            [prefix_type] * parts,
            [stacked, pltpu.VMEM((count, size, dim), jnp.bfloat16)],
        )(me, gain, *held[group], *stretches, *before)

    size = owned * dim
    prefix_type = jax.ShapeDtypeStruct((2 * size + local, dim), jnp.bfloat16)
    prefixes = []
    for group in range(GROUPS):
        total = kernel_call(
            functools.partial(total_kernel, dim, owned, parts),
            f"total{group}",
            [vmem] * parts + [hbm],
            vmem,
            total_type,
            [stacked],
        )(me, *held[group], *before)
        before = (total,)
        stretches = [with_plane(total, 0)]
        arrived.append(stretches)
        if group > 0:
            prefix = prefix_of(group - 1, before)
            before = tuple(prefix[:1])
            prefixes.append(exchange(prefix))
        if group < GROUPS - 1:
            before = inside_part(before)
        for step in range(1, planes.bit_length() - 1):
            total = widen(group, step - 1, total, stretches[-1], before)
            before = (total,)
            stretches.append(with_plane(total, step))
        while group == GROUPS - 1 and len(inside) < 2 * GROUPS:
            before = inside_part(before, 2)
    prefix = prefix_of(GROUPS - 1, before)
    before = tuple(prefix[:1])
    prefixes.append(exchange(prefix))

    part_type = jax.ShapeDtypeStruct((parts, size, dim), jnp.bfloat16)
    half_type = jax.ShapeDtypeStruct((parts // 2, size, dim), jnp.bfloat16)
    gain_type = jax.ShapeDtypeStruct((parts * local, dim), jnp.float32)

    def merge(group, before, cost):
        return kernel_call(
            functools.partial(merge_kernel, parts),
            f"merge{group}",
            [vmem] * parts + [hbm] * len(before),
            [vmem] * 3,
            [half_type, half_type, gain_type],
            [pltpu.VMEM(part_type.shape, part_type.dtype)],
            cost=cost,
        )(me, *prefixes[group], *before)

    def output(group, other, received, out, before, cost=0):
        *out, made = kernel_call(
            functools.partial(
                output_kernel, dim, owned, half, group * share, share, None if other else parts
            ),
            f"output{group}_{other}",
            [vmem] * (4 + len(received)) + [hbm] * (len(out) + len(before)),
            [hbm, vmem],
            [pltpu.HBM((1, length, width), jnp.bfloat16), token],
            [
                pltpu.VMEM(part_type.shape, part_type.dtype),
                pltpu.VMEM(gain_type.shape, gain_type.dtype),
                pltpu.VMEM((share // STEP, length, STEP * dim), jnp.bfloat16),
                pltpu.SemaphoreType.DMA((share // STEP,)),
            ],
            aliases={5 + len(received): 0} if out else {},
            cost=cost,
        )(
            me, queries, in_vmem(inside[group, other][0]), inside[group, other][1],
            in_vmem(gates[2 * group + other]), *received, *out, *before,
        )
        return out, (made,)

    out = ()
    for group in range(GROUPS):
        last = group == GROUPS - 1
        if not last:
            out, before = output(group, 0, prefixes[group], out, before)
        *others, gains = merge(group, before, 0)
        others = [lax.ppermute(other, "core", swap) for other in others]
        before = (gains,)
        if last:
            out, before = output(group, 0, prefixes[group], out, before, cost=20)
        out, before = output(group, 1, (*others, gains), out, before)
    return out[0]


def solution(mesh):
    parts, blocks = mesh.shape["head"], mesh.shape["ctx"]
    names = mesh.axis_names
    at = names.index("ctx")
    shape = mesh.devices.shape[:at] + (blocks // 2, 2) + mesh.devices.shape[at + 1 :]
    finer = Mesh(mesh.devices.reshape(shape), names[:at] + ("z", "core") + names[at + 1 :])
    tokens = P(("z", "core"), "head", None)
    return jax.shard_map(
        functools.partial(on_device, parts, blocks // 2),
        mesh=finer,
        in_specs=(tokens,) * 5 + (P("head"),),
        out_specs=tokens,
        check_vma=False,
    )
```

```python
import functools

import jax
import jax.numpy as jnp
from jax import lax
from jax.experimental import pallas as pl
from jax.experimental.pallas import tpu as pltpu
from jax.sharding import Mesh
from jax.sharding import PartitionSpec as P

GROUPS = 2
STEP = 8
EXTRA = 16
VMEM_LIMIT = 8 * 1024 * 1024
NN = (((1,), (0,)), ((), ()))
NT = (((1,), (1,)), ((), ()))
TN = (((0,), (0,)), ((), ()))


def dot(a, b, dims, precision=None):
    return lax.dot_general(a, b, dims, precision=precision, preferred_element_type=jnp.float32)


def split(value):
    first = value.astype(jnp.bfloat16)
    left = value - first.astype(jnp.float32)
    second = left.astype(jnp.bfloat16)
    return first, second, (left - second.astype(jnp.float32)).astype(jnp.bfloat16)


def sums_over(decay, keep):
    heads, length = decay.shape
    rows = lax.broadcasted_iota(jnp.int32, (length, length), 0)
    columns = lax.broadcasted_iota(jnp.int32, (length, length), 1)
    chosen = jnp.where(keep(rows, columns), 1.0, 0.0).astype(jnp.bfloat16)
    parts = [part.astype(jnp.float32) for part in split(decay)]
    both = dot(jnp.concatenate(parts, axis=0).astype(jnp.bfloat16), chosen, NN)
    return both[:heads] + (both[heads : 2 * heads] + both[2 * heads :])


def join(rows, head):
    wide = rows.astype(jnp.float32)
    return wide[3 * head : 3 * head + 1] + (
        wide[3 * head + 1 : 3 * head + 2] + wide[3 * head + 2 : 3 * head + 3]
    )


def decay_rows(totals):
    parts = [part for total in totals for part in split(total)]
    blank = jnp.zeros((EXTRA - len(parts), totals[0].shape[1]), jnp.bfloat16)
    return jnp.concatenate(parts + [blank], axis=0)


def pack_kernel(parts, decay_ref, packed_ref):
    length = packed_ref.shape[2]
    for place in range(packed_ref.shape[0]):
        start = place % parts * length
        packed_ref[place] = decay_ref[0, :, start : start + length]


def gate_kernel(half, begin, share, dim, me_ref, gate_ref, *refs):
    *results, done_ref, copy_ref, result_ref, done = refs[-6:]
    width = share * dim
    loads, stores = [], []
    for at, out_ref in enumerate(results):
        first = (me_ref[1] if at == 0 else 1 - me_ref[1]) * half + begin
        columns = pl.ds(pl.multiple_of(first * dim, width), width)
        loads.append(pltpu.make_async_copy(gate_ref.at[0, :, columns], copy_ref.at[at], done.at[at]))
        stores.append(pltpu.make_async_copy(result_ref.at[at], out_ref, done.at[2 + at]))
        loads[-1].start()
    for at in range(len(results)):
        loads[at].wait()
        for head in range(share):
            c = slice(head * dim, (head + 1) * dim)
            turned = jnp.tanh(0.5 * copy_ref[at, :, c].astype(jnp.float32))
            result_ref[at, :, c] = 0.5 + 0.5 * turned
        stores[at].start()
    done_ref[...] = jnp.zeros_like(done_ref)
    for store in stores:
        store.wait()


def heads_at(first, head, dim):
    return pl.ds(pl.multiple_of((first + head) * dim, dim), dim)


def decays_at(decay_ref, block, first):
    local = decay_ref.shape[1]
    parts = decay_ref.shape[0] // 2
    rows = pl.ds(pl.multiple_of(first % local, STEP), STEP)
    return decay_ref[block * parts + first // local, rows, :]


def state_kernel(dim, owned, half, begin, masks, me_ref, decay_ref, *refs):
    arrays, slots = refs[:4], refs[-3 - 2 * len(masks) : -3]
    stacked_ref, copy_ref, done = refs[-3:]
    part, core = me_ref[0], me_ref[1]
    firsts = [core * half + begin + ((part >> 1) ^ mask) * STEP for mask in masks]
    width = STEP * dim
    moves = [
        [
            pltpu.make_async_copy(
                ref.at[0, :, pl.ds(pl.multiple_of(first * dim, width), width)],
                copy_ref.at[turn, at],
                done.at[turn, at],
            )
            for at, ref in enumerate(arrays)
        ]
        for turn, first in enumerate(firsts)
    ]
    for move in sum(moves, []):
        move.start()
    for turn, first in enumerate(firsts):
        for source in range(2):
            block = core if source == 0 else 1 - core
            decay = decays_at(decay_ref, block, first)
            weight = jnp.exp(sums_over(decay, lambda u, s: u > s))
            whole = jnp.broadcast_to(jnp.sum(decay, axis=1, keepdims=True), (STEP, dim))
            for move in moves[turn][2 * source : 2 * source + 2]:
                move.wait()
            states = []
            for head in range(STEP):
                c = slice(head * dim, (head + 1) * dim)
                decayed = copy_ref[turn, 2 * source, :, c].T.astype(jnp.float32)
                decayed = (decayed * weight[head : head + 1, :]).astype(jnp.bfloat16)
                states.append(dot(decayed, copy_ref[turn, 2 * source + 1, :, c], NN))
            for head in range(STEP):
                owner, spot = divmod(head, owned)
                span = slice(spot * dim, (spot + 1) * dim)
                stacked_ref[turn, owner, block, span, :] = states[head].astype(jnp.bfloat16)
            for at in range(2):
                stacked_ref[turn, at, block, owned * dim :, :] = decay_rows(
                    [whole[head : head + 1] for head in range(at * owned, (at + 1) * owned)]
                )
        for at in range(2):
            slots[2 * turn + at][...] = stacked_ref[turn, (part & 1) ^ at]


def inside_kernel(
    dim, half, begin, count, other, me_ref, queries_ref, keys_ref, values_ref, decay_ref, *rest
):
    inside_ref, down_ref, done_ref = rest[-3:]
    core = me_ref[1]
    length = decay_ref.shape[2]
    rows = lax.broadcasted_iota(jnp.int32, (length, length), 0)
    causal = rows >= lax.broadcasted_iota(jnp.int32, (length, length), 1)
    for turn in range(count // STEP):
        first = (1 - core if other else core) * half + begin + turn * STEP
        decay = decays_at(decay_ref, core, first)
        across = sums_over(decay, lambda u, s: u <= s)
        down = across.T
        down_ref[turn] = jnp.exp(down)
        columns = [heads_at(first, head, dim) for head in range(STEP)]
        scores = [dot(queries_ref[0, :, c], keys_ref[0, :, c], NT) for c in columns]
        weights = []
        for head in range(STEP):
            gap = down[:, head : head + 1] - across[head : head + 1, :]
            weight = scores[head] * jnp.exp(jnp.where(causal, gap, -jnp.inf))
            weights.append(weight.astype(jnp.bfloat16))
        for head, c in enumerate(columns):
            at = (turn * STEP + head) * dim
            inside_ref[:, at : at + dim] = dot(weights[head], values_ref[0, :, c], NN)
    done_ref[...] = jnp.zeros_like(done_ref)


def gather_states(part, slots, stacked_ref):
    parts = len(slots)
    for slot, slot_ref in enumerate(slots):
        for block in range(2):
            stacked_ref[block * parts + (part ^ slot)] = slot_ref[block]


def total_kernel(dim, owned, parts, me_ref, *refs):
    total_ref, stacked_ref = refs[-2:]
    gather_states(me_ref[0], refs[:parts], stacked_ref)
    count = 2 * parts
    extra = [stacked_ref[at, owned * dim :, :] for at in range(count)]
    sums = []
    for head in range(owned):
        span = slice(head * dim, (head + 1) * dim)
        after = jnp.zeros((1, dim), jnp.float32)
        total = stacked_ref[count - 1, span, :].astype(jnp.float32)
        for at in range(count - 2, -1, -1):
            after += join(extra[at + 1], head)
            total += jnp.exp(after) * stacked_ref[at, span, :].astype(jnp.float32)
        total_ref[span, :] = total.astype(jnp.bfloat16)
        sums.append(after + join(extra[0], head))
    total_ref[owned * dim :, :] = decay_rows(sums)


def widen_kernel(dim, owned, step, me_ref, mine_ref, other_ref, *refs):
    out_ref = refs[-1]
    later = (me_ref[2] >> step) % 2 == 1
    extra = mine_ref[owned * dim :, :], other_ref[owned * dim :, :]
    sums = []
    for head in range(owned):
        span = slice(head * dim, (head + 1) * dim)
        mine, other = join(extra[0], head), join(extra[1], head)
        total = jnp.where(later, 1.0, jnp.exp(other)) * mine_ref[span, :].astype(jnp.float32)
        total += jnp.where(later, jnp.exp(mine), 1.0) * other_ref[span, :].astype(jnp.float32)
        out_ref[span, :] = total.astype(jnp.bfloat16)
        sums.append(mine + other)
    out_ref[owned * dim :, :] = decay_rows(sums)


def prefix_kernel(dim, owned, parts, stretches, me_ref, gain_ref, *refs):
    stacked_ref, prefix_ref = refs[-2:]
    slots, totals = refs[:parts], refs[parts : parts + stretches]
    count = 2 * parts
    results = refs[-2 - parts : -2]
    gather_states(me_ref[0], slots, stacked_ref)
    extra = [stacked_ref[at, owned * dim :, :] for at in range(count)]
    more = [total_ref[owned * dim :, :] for total_ref in totals]
    earlier = [
        ((me_ref[2] >> step) % 2).astype(jnp.float32) for step in range(len(totals))
    ]
    for head in range(owned):
        span = slice(head * dim, (head + 1) * dim)
        prefix = jnp.zeros((dim, dim), jnp.float32)
        after = jnp.zeros((1, dim), jnp.float32)
        for turn, total_ref in enumerate(totals):
            factor = earlier[turn] * jnp.exp(after)
            prefix += factor * total_ref[span, :].astype(jnp.float32)
            after += earlier[turn] * join(more[turn], head)
        for at in range(count):
            prefix_ref[at, span, :] = prefix.astype(jnp.bfloat16)
            if at < count - 1:
                prefix = jnp.exp(join(extra[at], head)) * prefix
                prefix += stacked_ref[at, span, :].astype(jnp.float32)
    size = owned * dim
    for slot, result_ref in enumerate(results):
        for block in range(2):
            result_ref[block * size : (block + 1) * size, :] = prefix_ref[
                block * parts + (me_ref[0] ^ slot)
            ]
        result_ref[2 * size :, :] = gain_ref[...]


def collect(part, block, slots, prefix_ref, gain_ref):
    parts, size, _ = prefix_ref.shape
    local = gain_ref.shape[0] // parts
    for slot, slot_ref in enumerate(slots):
        owner = part ^ slot
        prefix_ref[owner] = slot_ref[pl.ds(pl.multiple_of(block * size, size), size), :]
        rows = pl.ds(pl.multiple_of(owner * local, local), local)
        gain_ref[rows, :] = slot_ref[2 * size :, :].astype(jnp.float32)


def merge_kernel(parts, me_ref, *refs):
    *others, gain_ref, prefix_ref = refs[parts:] if len(refs) == parts + 4 else refs[parts + 1 :]
    collect(me_ref[0], 1 - me_ref[1], refs[:parts], prefix_ref, gain_ref)
    each = parts // len(others)
    for turn, other_ref in enumerate(others):
        other_ref[...] = prefix_ref[turn * each : (turn + 1) * each]


def output_kernel(
    dim, owned, half, begin, count, parts, me_ref,
    queries_ref, inside_ref, down_ref, gate_ref, *refs,
):
    out_ref, done_ref, prefix_ref, gain_ref, result_ref, sent = refs[-6:]
    core = me_ref[1]
    if parts is None:
        *others, gains = refs[:3]
        each = others[0].shape[0]
        prefixes = [others[at // each].at[at % each] for at in range(each * len(others))]
    else:
        collect(me_ref[0], core, refs[:parts], prefix_ref, gain_ref)
        prefixes, gains = [prefix_ref.at[at] for at in range(parts)], gain_ref
    average = jnp.full((dim, dim), 1.0 / dim, jnp.bfloat16)
    moves = []
    for turn in range(count // STEP):
        first = (1 - core if parts is None else core) * half + begin + turn * STEP
        gain = gains[pl.ds(pl.multiple_of(first, STEP), STEP), :]
        down = down_ref[turn]
        columns = [heads_at(first, head, dim) for head in range(STEP)]
        carried = []
        for head, c in enumerate(columns):
            owner, spot = divmod(turn * STEP + head, owned)
            prefix = prefixes[owner][spot * dim : (spot + 1) * dim, :]
            carried.append(dot(queries_ref[0, :, c], prefix, NN))
        mixed, means = [], []
        for head in range(STEP):
            at = (turn * STEP + head) * dim
            mixed.append(inside_ref[:, at : at + dim] + carried[head] * down[:, head : head + 1])
            means.append(dot((mixed[head] * mixed[head]).astype(jnp.bfloat16), average, NN))
        for head in range(STEP):
            at = (turn * STEP + head) * dim
            factor = gain[head : head + 1, :] * gate_ref[:, at : at + dim]
            normed = mixed[head] * lax.rsqrt(means[head] + 1e-06) * factor
            result_ref[turn, :, head * dim : (head + 1) * dim] = normed.astype(jnp.bfloat16)
        width = STEP * dim
        moves.append(
            pltpu.make_async_copy(
                result_ref.at[turn],
                out_ref.at[0, :, pl.ds(pl.multiple_of(first * dim, width), width)],
                sent.at[turn],
            )
        )
        moves[-1].start()
    done_ref[...] = jnp.zeros_like(done_ref)
    for move in moves:
        move.wait()


def kernel_call(body, name, in_specs, out_specs, out_shape, scratch=(), aliases={}, cost=0):
    return pl.pallas_call(
        body,
        grid_spec=pltpu.PrefetchScalarGridSpec(
            num_scalar_prefetch=1,
            grid=(),
            in_specs=in_specs,
            out_specs=out_specs,
            scratch_shapes=scratch,
        ),
        out_shape=out_shape,
        input_output_aliases=aliases,
        compiler_params=pltpu.CompilerParams(vmem_limit_bytes=VMEM_LIMIT),
        cost_estimate=pl.CostEstimate(
            flops=int(1e9 * cost) + 1, transcendentals=0, bytes_accessed=1
        ),
        name=name,
    )


def on_device(parts, planes, queries, keys, values, gate, log_decay, norm_gain):
    _, length, width = queries.shape
    local = log_decay.shape[1]
    dim = width // (local * parts)
    count = 2 * parts
    half = local * parts // 2
    owned = half // (GROUPS * parts)
    rows = owned * dim + EXTRA
    me = jnp.stack([lax.axis_index(axis) for axis in ("head", "core", "z")]).astype(jnp.int32)
    swap = [(0, 1), (1, 0)]

    values_other = lax.ppermute(values, "core", swap)
    keys_other = lax.ppermute(keys, "core", swap)
    packed = pl.pallas_call(
        functools.partial(pack_kernel, parts),
        out_shape=jax.ShapeDtypeStruct((count, local, length), jnp.float32),
        name="pack",
    )(log_decay)
    decay = lax.all_to_all(packed, ("core", "head"), 0, 0, tiled=True)
    gain = norm_gain.reshape(local, dim)

    vmem = pl.BlockSpec(memory_space=pltpu.VMEM)
    hbm = pl.BlockSpec(memory_space=pl.ANY)

    def in_vmem(array):
        return pltpu.with_memory_space_constraint(array, pltpu.VMEM)

    def in_hbm(array):
        return pltpu.with_memory_space_constraint(array, pltpu.HBM)

    own = in_hbm(keys), in_hbm(values)
    share = half // GROUPS
    keys, values, queries = (in_vmem(array) for array in (keys, values, queries))

    def exchange(slots):
        arrived = list(slots)
        for slot in sorted(range(1, parts), key=lambda s: -bin(s).count("1")):
            pairs = [(at, at ^ slot) for at in range(parts)]
            arrived[slot] = lax.ppermute(slots[slot], "head", pairs)
        return arrived

    before = ()
    held = []
    state_type = jax.ShapeDtypeStruct((2, rows, dim), jnp.bfloat16)
    token = jax.ShapeDtypeStruct((8, 128), jnp.float32)
    inside = {}

    def inside_part(before, cost=0):
        group, other = divmod(len(inside), 2)
        *inside[group, other], made = kernel_call(
            functools.partial(inside_kernel, dim, half, group * share, share, other),
            f"inside{group}_{other}",
            [vmem] * 4 + [hbm] * len(before),
            [vmem] * 3,
            [
                pltpu.VMEM((length, share * dim), jnp.float32),
                jax.ShapeDtypeStruct((share // STEP, length, STEP), jnp.float32),
                token,
            ],
            cost=cost,
        )(me, queries, keys, values, decay, *before)
        return (made,)

    gate_type = jax.ShapeDtypeStruct((length, share * dim), jnp.float32)
    gates = {}

    def gates_of(group, before):
        gates[group, 0], gates[group, 1], made = kernel_call(
            functools.partial(gate_kernel, half, group * share, share, dim),
            f"gates{group}",
            [hbm] * (1 + len(before)),
            [hbm, hbm, vmem],
            [pltpu.HBM(gate_type.shape, gate_type.dtype)] * 2 + [token],
            [
                pltpu.VMEM((2, length, share * dim), jnp.bfloat16),
                pltpu.VMEM((2,) + gate_type.shape, jnp.float32),
                pltpu.SemaphoreType.DMA((4,)),
            ],
        )(me, in_hbm(gate), *before)
        return (made,)

    for group in range(GROUPS):
        slots = {}
        for masks in ((1,), (0,)) if group == 0 else ((1, 0),):
            state = kernel_call(
                functools.partial(state_kernel, dim, owned, half, group * share, masks),
                f"state{group}_{masks[0]}",
                [vmem] + [hbm] * (4 + len(before)),
                [vmem] * (2 * len(masks)),
                [state_type] * (2 * len(masks)),
                [
                    pltpu.VMEM((len(masks), 2) + state_type.shape, jnp.bfloat16),
                    pltpu.VMEM((len(masks), 4, length, STEP * dim), jnp.bfloat16),
                    pltpu.SemaphoreType.DMA((len(masks), 4)),
                ],
            )(me, decay, *own, keys_other, values_other, *before)
            before = tuple(state[:1])
            for at, array in enumerate(state):
                slots[2 * masks[at // 2] + at % 2] = array
        held.append(exchange([slots[slot] for slot in range(parts)]))
        if group == 0:
            before = inside_part(inside_part(before))

    arrived = []
    stacked = pltpu.VMEM((count, rows, dim), jnp.bfloat16)
    total_type = jax.ShapeDtypeStruct((rows, dim), jnp.bfloat16)

    def with_plane(total, step):
        pairs = [(at, at ^ (1 << step)) for at in range(planes)]
        return lax.ppermute(total, "z", pairs)

    def widen(group, step, total, other, before):
        return kernel_call(
            functools.partial(widen_kernel, dim, owned, step),
            f"widen{group}_{step}",
            [vmem] * 2 + [hbm] * len(before),
            vmem,
            total_type,
        )(me, total, other, *before)

    def prefix_of(group, before):
        stretches = arrived[group]
        return kernel_call(
            functools.partial(prefix_kernel, dim, owned, parts, len(stretches)),
            f"prefix{group}",
            [vmem] * (1 + parts + len(stretches)) + [hbm] * len(before),
            [vmem] * parts,
            [prefix_type] * parts,
            [stacked, pltpu.VMEM((count, size, dim), jnp.bfloat16)],
        )(me, gain, *held[group], *stretches, *before)

    size = owned * dim
    prefix_type = jax.ShapeDtypeStruct((2 * size + local, dim), jnp.bfloat16)
    prefixes = []
    for group in range(GROUPS):
        total = kernel_call(
            functools.partial(total_kernel, dim, owned, parts),
            f"total{group}",
            [vmem] * parts + [hbm],
            vmem,
            total_type,
            [stacked],
        )(me, *held[group], *before)
        before = (total,)
        stretches = [with_plane(total, 0)]
        arrived.append(stretches)
        if group > 0:
            prefix = prefix_of(group - 1, before)
            before = tuple(prefix[:1])
            prefixes.append(exchange(prefix))
        if group < GROUPS - 1:
            before = inside_part(before)
        for step in range(1, planes.bit_length() - 1):
            total = widen(group, step - 1, total, stretches[-1], before)
            before = (total,)
            stretches.append(with_plane(total, step))
        while group == GROUPS - 1 and len(inside) < 2 * GROUPS:
            before = inside_part(before, 2)
        before = gates_of(group, before)
    prefix = prefix_of(GROUPS - 1, before)
    before = tuple(prefix[:1])
    prefixes.append(exchange(prefix))

    part_type = jax.ShapeDtypeStruct((parts, size, dim), jnp.bfloat16)
    half_type = jax.ShapeDtypeStruct((parts // 2, size, dim), jnp.bfloat16)
    gain_type = jax.ShapeDtypeStruct((parts * local, dim), jnp.float32)

    def merge(group, before, cost):
        return kernel_call(
            functools.partial(merge_kernel, parts),
            f"merge{group}",
            [vmem] * parts + [hbm] * len(before),
            [vmem] * 3,
            [half_type, half_type, gain_type],
            [pltpu.VMEM(part_type.shape, part_type.dtype)],
            cost=cost,
        )(me, *prefixes[group], *before)

    def output(group, other, received, out, before, cost=0):
        *out, made = kernel_call(
            functools.partial(
                output_kernel, dim, owned, half, group * share, share, None if other else parts
            ),
            f"output{group}_{other}",
            [vmem] * (4 + len(received)) + [hbm] * (len(out) + len(before)),
            [hbm, vmem],
            [pltpu.HBM((1, length, width), jnp.bfloat16), token],
            [
                pltpu.VMEM(part_type.shape, part_type.dtype),
                pltpu.VMEM(gain_type.shape, gain_type.dtype),
                pltpu.VMEM((share // STEP, length, STEP * dim), jnp.bfloat16),
                pltpu.SemaphoreType.DMA((share // STEP,)),
            ],
            aliases={5 + len(received): 0} if out else {},
            cost=cost,
        )(
            me, queries, in_vmem(inside[group, other][0]), inside[group, other][1],
            in_vmem(gates[group, other]), *received, *out, *before,
        )
        return out, (made,)

    out = ()
    for group in range(GROUPS):
        last = group == GROUPS - 1
        if not last:
            out, before = output(group, 0, prefixes[group], out, before)
        *others, gains = merge(group, before, 0)
        others = [lax.ppermute(other, "core", swap) for other in others]
        before = (gains,)
        if last:
            out, before = output(group, 0, prefixes[group], out, before, cost=20)
        out, before = output(group, 1, (*others, gains), out, before)
    return out[0]


def solution(mesh):
    parts, blocks = mesh.shape["head"], mesh.shape["ctx"]
    names = mesh.axis_names
    at = names.index("ctx")
    shape = mesh.devices.shape[:at] + (blocks // 2, 2) + mesh.devices.shape[at + 1 :]
    finer = Mesh(mesh.devices.reshape(shape), names[:at] + ("z", "core") + names[at + 1 :])
    tokens = P(("z", "core"), "head", None)
    return jax.shard_map(
        functools.partial(on_device, parts, blocks // 2),
        mesh=finer,
        in_specs=(tokens,) * 5 + (P("head"),),
        out_specs=tokens,
        check_vma=False,
    )
```

```python
import functools

import jax
import jax.numpy as jnp
from jax import lax
from jax.experimental import pallas as pl
from jax.experimental.pallas import tpu as pltpu
from jax.sharding import Mesh
from jax.sharding import PartitionSpec as P

GROUPS = 2
STEP = 8
EXTRA = 16
VMEM_LIMIT = 8 * 1024 * 1024
NN = (((1,), (0,)), ((), ()))
NT = (((1,), (1,)), ((), ()))
TN = (((0,), (0,)), ((), ()))


def dot(a, b, dims, precision=None):
    return lax.dot_general(a, b, dims, precision=precision, preferred_element_type=jnp.float32)


def split(value):
    first = value.astype(jnp.bfloat16)
    left = value - first.astype(jnp.float32)
    second = left.astype(jnp.bfloat16)
    return first, second, (left - second.astype(jnp.float32)).astype(jnp.bfloat16)


def sums_over(decay, keep):
    heads, length = decay.shape
    rows = lax.broadcasted_iota(jnp.int32, (length, length), 0)
    columns = lax.broadcasted_iota(jnp.int32, (length, length), 1)
    chosen = jnp.where(keep(rows, columns), 1.0, 0.0).astype(jnp.bfloat16)
    parts = [part.astype(jnp.float32) for part in split(decay)]
    both = dot(jnp.concatenate(parts, axis=0).astype(jnp.bfloat16), chosen, NN)
    return both[:heads] + (both[heads : 2 * heads] + both[2 * heads :])


def join(rows, head):
    wide = rows.astype(jnp.float32)
    return wide[3 * head : 3 * head + 1] + (
        wide[3 * head + 1 : 3 * head + 2] + wide[3 * head + 2 : 3 * head + 3]
    )


def decay_rows(totals):
    parts = [part for total in totals for part in split(total)]
    blank = jnp.zeros((EXTRA - len(parts), totals[0].shape[1]), jnp.bfloat16)
    return jnp.concatenate(parts + [blank], axis=0)


def pack_kernel(parts, decay_ref, packed_ref):
    length = packed_ref.shape[2]
    for place in range(packed_ref.shape[0]):
        start = place % parts * length
        packed_ref[place] = decay_ref[0, :, start : start + length]


def gate_kernel(half, begin, share, dim, me_ref, gate_ref, *refs):
    *results, done_ref, copy_ref, result_ref, done = refs[-6:]
    width = share * dim
    loads, stores = [], []
    for at, out_ref in enumerate(results):
        first = (me_ref[1] if at == 0 else 1 - me_ref[1]) * half + begin
        columns = pl.ds(pl.multiple_of(first * dim, width), width)
        loads.append(pltpu.make_async_copy(gate_ref.at[0, :, columns], copy_ref.at[at], done.at[at]))
        stores.append(pltpu.make_async_copy(result_ref.at[at], out_ref, done.at[2 + at]))
        loads[-1].start()
    for at in range(len(results)):
        loads[at].wait()
        for head in range(share):
            c = slice(head * dim, (head + 1) * dim)
            turned = jnp.tanh(0.5 * copy_ref[at, :, c].astype(jnp.float32))
            result_ref[at, :, c] = 0.5 + 0.5 * turned
        stores[at].start()
    done_ref[...] = jnp.zeros_like(done_ref)
    for store in stores:
        store.wait()


def heads_at(first, head, dim):
    return pl.ds(pl.multiple_of((first + head) * dim, dim), dim)


def decays_at(decay_ref, block, first):
    local = decay_ref.shape[1]
    parts = decay_ref.shape[0] // 2
    rows = pl.ds(pl.multiple_of(first % local, STEP), STEP)
    return decay_ref[block * parts + first // local, rows, :]


def state_kernel(dim, owned, half, begin, masks, me_ref, decay_ref, *refs):
    arrays, slots = refs[:4], refs[-3 - 2 * len(masks) : -3]
    stacked_ref, copy_ref, done = refs[-3:]
    part, core = me_ref[0], me_ref[1]
    firsts = [core * half + begin + ((part >> 1) ^ mask) * STEP for mask in masks]
    width = STEP * dim
    moves = [
        [
            pltpu.make_async_copy(
                ref.at[0, :, pl.ds(pl.multiple_of(first * dim, width), width)],
                copy_ref.at[turn, at],
                done.at[turn, at],
            )
            for at, ref in enumerate(arrays)
        ]
        for turn, first in enumerate(firsts)
    ]
    for move in sum(moves, []):
        move.start()
    for turn, first in enumerate(firsts):
        for source in range(2):
            block = core if source == 0 else 1 - core
            decay = decays_at(decay_ref, block, first)
            weight = jnp.exp(sums_over(decay, lambda u, s: u > s))
            whole = jnp.broadcast_to(jnp.sum(decay, axis=1, keepdims=True), (STEP, dim))
            for move in moves[turn][2 * source : 2 * source + 2]:
                move.wait()
            states = []
            for head in range(STEP):
                c = slice(head * dim, (head + 1) * dim)
                decayed = copy_ref[turn, 2 * source, :, c].T.astype(jnp.float32)
                decayed = (decayed * weight[head : head + 1, :]).astype(jnp.bfloat16)
                states.append(dot(decayed, copy_ref[turn, 2 * source + 1, :, c], NN))
            for head in range(STEP):
                owner, spot = divmod(head, owned)
                span = slice(spot * dim, (spot + 1) * dim)
                stacked_ref[turn, owner, block, span, :] = states[head].astype(jnp.bfloat16)
            for at in range(2):
                stacked_ref[turn, at, block, owned * dim :, :] = decay_rows(
                    [whole[head : head + 1] for head in range(at * owned, (at + 1) * owned)]
                )
        for at in range(2):
            slots[2 * turn + at][...] = stacked_ref[turn, (part & 1) ^ at]


def inside_kernel(
    dim, half, begin, count, other, me_ref, queries_ref, keys_ref, values_ref, decay_ref, *rest
):
    inside_ref, down_ref, done_ref = rest[-3:]
    core = me_ref[1]
    length = decay_ref.shape[2]
    rows = lax.broadcasted_iota(jnp.int32, (length, length), 0)
    causal = rows >= lax.broadcasted_iota(jnp.int32, (length, length), 1)
    for turn in range(count // STEP):
        first = (1 - core if other else core) * half + begin + turn * STEP
        decay = decays_at(decay_ref, core, first)
        across = sums_over(decay, lambda u, s: u <= s)
        down = across.T
        down_ref[turn] = jnp.exp(down)
        columns = [heads_at(first, head, dim) for head in range(STEP)]
        scores = [dot(queries_ref[0, :, c], keys_ref[0, :, c], NT) for c in columns]
        weights = []
        for head in range(STEP):
            gap = down[:, head : head + 1] - across[head : head + 1, :]
            weight = scores[head] * jnp.exp(jnp.where(causal, gap, -jnp.inf))
            weights.append(weight.astype(jnp.bfloat16))
        for head, c in enumerate(columns):
            at = (turn * STEP + head) * dim
            inside_ref[:, at : at + dim] = dot(weights[head], values_ref[0, :, c], NN)
    done_ref[...] = jnp.zeros_like(done_ref)


def gather_states(part, slots, stacked_ref):
    parts = len(slots)
    for slot, slot_ref in enumerate(slots):
        for block in range(2):
            stacked_ref[block * parts + (part ^ slot)] = slot_ref[block]


def total_kernel(dim, owned, parts, me_ref, *refs):
    total_ref, stacked_ref = refs[-2:]
    gather_states(me_ref[0], refs[:parts], stacked_ref)
    count = 2 * parts
    extra = [stacked_ref[at, owned * dim :, :] for at in range(count)]
    sums = []
    for head in range(owned):
        span = slice(head * dim, (head + 1) * dim)
        after = jnp.zeros((1, dim), jnp.float32)
        total = stacked_ref[count - 1, span, :].astype(jnp.float32)
        for at in range(count - 2, -1, -1):
            after += join(extra[at + 1], head)
            total += jnp.exp(after) * stacked_ref[at, span, :].astype(jnp.float32)
        total_ref[span, :] = total.astype(jnp.bfloat16)
        sums.append(after + join(extra[0], head))
    total_ref[owned * dim :, :] = decay_rows(sums)


def widen_kernel(dim, owned, step, me_ref, mine_ref, other_ref, *refs):
    out_ref = refs[-1]
    later = (me_ref[2] >> step) % 2 == 1
    extra = mine_ref[owned * dim :, :], other_ref[owned * dim :, :]
    sums = []
    for head in range(owned):
        span = slice(head * dim, (head + 1) * dim)
        mine, other = join(extra[0], head), join(extra[1], head)
        total = jnp.where(later, 1.0, jnp.exp(other)) * mine_ref[span, :].astype(jnp.float32)
        total += jnp.where(later, jnp.exp(mine), 1.0) * other_ref[span, :].astype(jnp.float32)
        out_ref[span, :] = total.astype(jnp.bfloat16)
        sums.append(mine + other)
    out_ref[owned * dim :, :] = decay_rows(sums)


def prefix_kernel(dim, owned, parts, stretches, me_ref, gain_ref, *refs):
    stacked_ref, prefix_ref = refs[-2:]
    slots, totals = refs[:parts], refs[parts : parts + stretches]
    count = 2 * parts
    results = refs[-2 - parts : -2]
    gather_states(me_ref[0], slots, stacked_ref)
    extra = [stacked_ref[at, owned * dim :, :] for at in range(count)]
    more = [total_ref[owned * dim :, :] for total_ref in totals]
    earlier = [
        ((me_ref[2] >> step) % 2).astype(jnp.float32) for step in range(len(totals))
    ]
    for head in range(owned):
        span = slice(head * dim, (head + 1) * dim)
        prefix = jnp.zeros((dim, dim), jnp.float32)
        after = jnp.zeros((1, dim), jnp.float32)
        for turn, total_ref in enumerate(totals):
            factor = earlier[turn] * jnp.exp(after)
            prefix += factor * total_ref[span, :].astype(jnp.float32)
            after += earlier[turn] * join(more[turn], head)
        for at in range(count):
            prefix_ref[at, span, :] = prefix.astype(jnp.bfloat16)
            if at < count - 1:
                prefix = jnp.exp(join(extra[at], head)) * prefix
                prefix += stacked_ref[at, span, :].astype(jnp.float32)
    size = owned * dim
    for slot, result_ref in enumerate(results):
        for block in range(2):
            result_ref[block * size : (block + 1) * size, :] = prefix_ref[
                block * parts + (me_ref[0] ^ slot)
            ]
        result_ref[2 * size :, :] = gain_ref[...]


def collect(part, block, slots, prefix_ref, gain_ref):
    parts, size, _ = prefix_ref.shape
    local = gain_ref.shape[0] // parts
    for slot, slot_ref in enumerate(slots):
        owner = part ^ slot
        prefix_ref[owner] = slot_ref[pl.ds(pl.multiple_of(block * size, size), size), :]
        rows = pl.ds(pl.multiple_of(owner * local, local), local)
        gain_ref[rows, :] = slot_ref[2 * size :, :].astype(jnp.float32)


def merge_kernel(parts, me_ref, *refs):
    *others, gain_ref, prefix_ref = refs[parts:] if len(refs) == parts + 4 else refs[parts + 1 :]
    collect(me_ref[0], 1 - me_ref[1], refs[:parts], prefix_ref, gain_ref)
    each = parts // len(others)
    for turn, other_ref in enumerate(others):
        other_ref[...] = prefix_ref[turn * each : (turn + 1) * each]


def output_kernel(
    dim, owned, half, begin, count, parts, me_ref,
    queries_ref, inside_ref, down_ref, gate_ref, *refs,
):
    out_ref, done_ref, prefix_ref, gain_ref, result_ref, sent = refs[-6:]
    core = me_ref[1]
    if parts is None:
        *others, gains = refs[:3]
        each = others[0].shape[0]
        prefixes = [others[at // each].at[at % each] for at in range(each * len(others))]
    else:
        collect(me_ref[0], core, refs[:parts], prefix_ref, gain_ref)
        prefixes, gains = [prefix_ref.at[at] for at in range(parts)], gain_ref
    average = jnp.full((dim, dim), 1.0 / dim, jnp.bfloat16)
    batch = STEP // 2
    width = batch * dim
    moves = []
    for turn in range(count // batch):
        first = (1 - core if parts is None else core) * half + begin + turn * batch
        block, offset = divmod(turn * batch, STEP)
        gain = gains[pl.ds(pl.multiple_of(first - offset, STEP), STEP), :]
        down = down_ref[block]
        places = [turn * batch + head for head in range(batch)]
        carried = []
        for place in places:
            owner, spot = divmod(place, owned)
            query = queries_ref[0, :, heads_at(first - turn * batch, place, dim)]
            carried.append(dot(query, prefixes[owner][spot * dim : (spot + 1) * dim, :], NN))
        mixed, means = [], []
        for head, place in enumerate(places):
            c = slice(place * dim, (place + 1) * dim)
            at = offset + head
            mixed.append(inside_ref[:, c] + carried[head] * down[:, at : at + 1])
            means.append(dot((mixed[head] * mixed[head]).astype(jnp.bfloat16), average, NN))
        for head, place in enumerate(places):
            c = slice(place * dim, (place + 1) * dim)
            factor = gain[offset + head : offset + head + 1, :] * gate_ref[:, c]
            normed = mixed[head] * lax.rsqrt(means[head] + 1e-06) * factor
            result_ref[turn, :, head * dim : (head + 1) * dim] = normed.astype(jnp.bfloat16)
        moves.append(
            pltpu.make_async_copy(
                result_ref.at[turn],
                out_ref.at[0, :, pl.ds(pl.multiple_of(first * dim, width), width)],
                sent.at[turn],
            )
        )
        moves[-1].start()
    done_ref[...] = jnp.zeros_like(done_ref)
    for move in moves:
        move.wait()


def kernel_call(body, name, in_specs, out_specs, out_shape, scratch=(), aliases={}, cost=0):
    return pl.pallas_call(
        body,
        grid_spec=pltpu.PrefetchScalarGridSpec(
            num_scalar_prefetch=1,
            grid=(),
            in_specs=in_specs,
            out_specs=out_specs,
            scratch_shapes=scratch,
        ),
        out_shape=out_shape,
        input_output_aliases=aliases,
        compiler_params=pltpu.CompilerParams(vmem_limit_bytes=VMEM_LIMIT),
        cost_estimate=pl.CostEstimate(
            flops=int(1e9 * cost) + 1, transcendentals=0, bytes_accessed=1
        ),
        name=name,
    )


def on_device(parts, planes, queries, keys, values, gate, log_decay, norm_gain):
    _, length, width = queries.shape
    local = log_decay.shape[1]
    dim = width // (local * parts)
    count = 2 * parts
    half = local * parts // 2
    owned = half // (GROUPS * parts)
    rows = owned * dim + EXTRA
    me = jnp.stack([lax.axis_index(axis) for axis in ("head", "core", "z")]).astype(jnp.int32)
    swap = [(0, 1), (1, 0)]

    values_other = lax.ppermute(values, "core", swap)
    keys_other = lax.ppermute(keys, "core", swap)
    packed = pl.pallas_call(
        functools.partial(pack_kernel, parts),
        out_shape=jax.ShapeDtypeStruct((count, local, length), jnp.float32),
        name="pack",
    )(log_decay)
    decay = lax.all_to_all(packed, ("core", "head"), 0, 0, tiled=True)
    gain = norm_gain.reshape(local, dim)

    vmem = pl.BlockSpec(memory_space=pltpu.VMEM)
    hbm = pl.BlockSpec(memory_space=pl.ANY)

    def in_vmem(array):
        return pltpu.with_memory_space_constraint(array, pltpu.VMEM)

    def in_hbm(array):
        return pltpu.with_memory_space_constraint(array, pltpu.HBM)

    own = in_hbm(keys), in_hbm(values)
    share = half // GROUPS
    keys, values, queries = (in_vmem(array) for array in (keys, values, queries))

    def exchange(slots):
        arrived = list(slots)
        for slot in sorted(range(1, parts), key=lambda s: -bin(s).count("1")):
            pairs = [(at, at ^ slot) for at in range(parts)]
            arrived[slot] = lax.ppermute(slots[slot], "head", pairs)
        return arrived

    before = ()
    held = []
    state_type = jax.ShapeDtypeStruct((2, rows, dim), jnp.bfloat16)
    token = jax.ShapeDtypeStruct((8, 128), jnp.float32)
    inside = {}

    def inside_part(before, cost=0):
        group, other = divmod(len(inside), 2)
        *inside[group, other], made = kernel_call(
            functools.partial(inside_kernel, dim, half, group * share, share, other),
            f"inside{group}_{other}",
            [vmem] * 4 + [hbm] * len(before),
            [vmem] * 3,
            [
                pltpu.VMEM((length, share * dim), jnp.float32),
                jax.ShapeDtypeStruct((share // STEP, length, STEP), jnp.float32),
                token,
            ],
            cost=cost,
        )(me, queries, keys, values, decay, *before)
        return (made,)

    gate_type = jax.ShapeDtypeStruct((length, share * dim), jnp.float32)
    gates = {}

    def gates_of(group, before):
        gates[group, 0], gates[group, 1], made = kernel_call(
            functools.partial(gate_kernel, half, group * share, share, dim),
            f"gates{group}",
            [hbm] * (1 + len(before)),
            [hbm, hbm, vmem],
            [pltpu.HBM(gate_type.shape, gate_type.dtype)] * 2 + [token],
            [
                pltpu.VMEM((2, length, share * dim), jnp.bfloat16),
                pltpu.VMEM((2,) + gate_type.shape, jnp.float32),
                pltpu.SemaphoreType.DMA((4,)),
            ],
        )(me, in_hbm(gate), *before)
        return (made,)

    for group in range(GROUPS):
        slots = {}
        for masks in ((1,), (0,)) if group == 0 else ((1, 0),):
            state = kernel_call(
                functools.partial(state_kernel, dim, owned, half, group * share, masks),
                f"state{group}_{masks[0]}",
                [vmem] + [hbm] * (4 + len(before)),
                [vmem] * (2 * len(masks)),
                [state_type] * (2 * len(masks)),
                [
                    pltpu.VMEM((len(masks), 2) + state_type.shape, jnp.bfloat16),
                    pltpu.VMEM((len(masks), 4, length, STEP * dim), jnp.bfloat16),
                    pltpu.SemaphoreType.DMA((len(masks), 4)),
                ],
            )(me, decay, *own, keys_other, values_other, *before)
            before = tuple(state[:1])
            for at, array in enumerate(state):
                slots[2 * masks[at // 2] + at % 2] = array
        held.append(exchange([slots[slot] for slot in range(parts)]))
        if group == 0:
            before = inside_part(inside_part(before))

    arrived = []
    stacked = pltpu.VMEM((count, rows, dim), jnp.bfloat16)
    total_type = jax.ShapeDtypeStruct((rows, dim), jnp.bfloat16)

    def with_plane(total, step):
        pairs = [(at, at ^ (1 << step)) for at in range(planes)]
        return lax.ppermute(total, "z", pairs)

    def widen(group, step, total, other, before):
        return kernel_call(
            functools.partial(widen_kernel, dim, owned, step),
            f"widen{group}_{step}",
            [vmem] * 2 + [hbm] * len(before),
            vmem,
            total_type,
        )(me, total, other, *before)

    def prefix_of(group, before):
        stretches = arrived[group]
        return kernel_call(
            functools.partial(prefix_kernel, dim, owned, parts, len(stretches)),
            f"prefix{group}",
            [vmem] * (1 + parts + len(stretches)) + [hbm] * len(before),
            [vmem] * parts,
            [prefix_type] * parts,
            [stacked, pltpu.VMEM((count, size, dim), jnp.bfloat16)],
        )(me, gain, *held[group], *stretches, *before)

    size = owned * dim
    prefix_type = jax.ShapeDtypeStruct((2 * size + local, dim), jnp.bfloat16)
    prefixes = []
    for group in range(GROUPS):
        total = kernel_call(
            functools.partial(total_kernel, dim, owned, parts),
            f"total{group}",
            [vmem] * parts + [hbm],
            vmem,
            total_type,
            [stacked],
        )(me, *held[group], *before)
        before = (total,)
        stretches = [with_plane(total, 0)]
        arrived.append(stretches)
        if group > 0:
            prefix = prefix_of(group - 1, before)
            before = tuple(prefix[:1])
            prefixes.append(exchange(prefix))
        if group < GROUPS - 1:
            before = inside_part(before)
        for step in range(1, planes.bit_length() - 1):
            total = widen(group, step - 1, total, stretches[-1], before)
            before = (total,)
            stretches.append(with_plane(total, step))
        while group == GROUPS - 1 and len(inside) < 2 * GROUPS:
            before = inside_part(before, 2)
        before = gates_of(group, before)
    prefix = prefix_of(GROUPS - 1, before)
    before = tuple(prefix[:1])
    prefixes.append(exchange(prefix))

    part_type = jax.ShapeDtypeStruct((parts, size, dim), jnp.bfloat16)
    half_type = jax.ShapeDtypeStruct((parts // 2, size, dim), jnp.bfloat16)
    gain_type = jax.ShapeDtypeStruct((parts * local, dim), jnp.float32)

    def merge(group, before, cost):
        return kernel_call(
            functools.partial(merge_kernel, parts),
            f"merge{group}",
            [vmem] * parts + [hbm] * len(before),
            [vmem] * 3,
            [half_type, half_type, gain_type],
            [pltpu.VMEM(part_type.shape, part_type.dtype)],
            cost=cost,
        )(me, *prefixes[group], *before)

    def output(group, other, received, out, before, cost=0):
        *out, made = kernel_call(
            functools.partial(
                output_kernel, dim, owned, half, group * share, share, None if other else parts
            ),
            f"output{group}_{other}",
            [vmem] * (4 + len(received)) + [hbm] * (len(out) + len(before)),
            [hbm, vmem],
            [pltpu.HBM((1, length, width), jnp.bfloat16), token],
            [
                pltpu.VMEM(part_type.shape, part_type.dtype),
                pltpu.VMEM(gain_type.shape, gain_type.dtype),
                pltpu.VMEM((2 * share // STEP, length, STEP // 2 * dim), jnp.bfloat16),
                pltpu.SemaphoreType.DMA((2 * share // STEP,)),
            ],
            aliases={5 + len(received): 0} if out else {},
            cost=cost,
        )(
            me, queries, in_vmem(inside[group, other][0]), inside[group, other][1],
            in_vmem(gates[group, other]), *received, *out, *before,
        )
        return out, (made,)

    out = ()
    for group in range(GROUPS):
        last = group == GROUPS - 1
        *others, gains = merge(group, before, 0)
        others = [lax.ppermute(other, "core", swap) for other in others]
        before = (gains,)
        out, before = output(group, 0, prefixes[group], out, before, cost=20 if last else 0)
        out, before = output(group, 1, (*others, gains), out, before)
    return out[0]


def solution(mesh):
    parts, blocks = mesh.shape["head"], mesh.shape["ctx"]
    names = mesh.axis_names
    at = names.index("ctx")
    shape = mesh.devices.shape[:at] + (blocks // 2, 2) + mesh.devices.shape[at + 1 :]
    finer = Mesh(mesh.devices.reshape(shape), names[:at] + ("z", "core") + names[at + 1 :])
    tokens = P(("z", "core"), "head", None)
    return jax.shard_map(
        functools.partial(on_device, parts, blocks // 2),
        mesh=finer,
        in_specs=(tokens,) * 5 + (P("head"),),
        out_specs=tokens,
        check_vma=False,
    )
```

```python
import functools

import jax
import jax.numpy as jnp
from jax import lax
from jax.experimental import pallas as pl
from jax.experimental.pallas import tpu as pltpu
from jax.sharding import Mesh
from jax.sharding import PartitionSpec as P

GROUPS = 2
STEP = 8
EXTRA = 16
VMEM_LIMIT = 8 * 1024 * 1024
NN = (((1,), (0,)), ((), ()))
NT = (((1,), (1,)), ((), ()))
TN = (((0,), (0,)), ((), ()))


def dot(a, b, dims, precision=None):
    return lax.dot_general(a, b, dims, precision=precision, preferred_element_type=jnp.float32)


def split(value):
    first = value.astype(jnp.bfloat16)
    left = value - first.astype(jnp.float32)
    second = left.astype(jnp.bfloat16)
    return first, second, (left - second.astype(jnp.float32)).astype(jnp.bfloat16)


def sums_over(decay, keep):
    heads, length = decay.shape
    rows = lax.broadcasted_iota(jnp.int32, (length, length), 0)
    columns = lax.broadcasted_iota(jnp.int32, (length, length), 1)
    chosen = jnp.where(keep(rows, columns), 1.0, 0.0).astype(jnp.bfloat16)
    parts = [part.astype(jnp.float32) for part in split(decay)]
    both = dot(jnp.concatenate(parts, axis=0).astype(jnp.bfloat16), chosen, NN)
    return both[:heads] + (both[heads : 2 * heads] + both[2 * heads :])


def join(rows, head):
    wide = rows.astype(jnp.float32)
    return wide[3 * head : 3 * head + 1] + (
        wide[3 * head + 1 : 3 * head + 2] + wide[3 * head + 2 : 3 * head + 3]
    )


def decay_rows(totals):
    parts = [part for total in totals for part in split(total)]
    blank = jnp.zeros((EXTRA - len(parts), totals[0].shape[1]), jnp.bfloat16)
    return jnp.concatenate(parts + [blank], axis=0)


def pack_kernel(parts, decay_ref, packed_ref):
    length = packed_ref.shape[2]
    for place in range(packed_ref.shape[0]):
        start = place % parts * length
        packed_ref[place] = decay_ref[0, :, start : start + length]


def gate_kernel(half, begin, share, dim, me_ref, gate_ref, *refs):
    *results, done_ref, copy_ref, result_ref, done = refs[-6:]
    width = share * dim
    loads, stores = [], []
    for at, out_ref in enumerate(results):
        first = (me_ref[1] if at == 0 else 1 - me_ref[1]) * half + begin
        columns = pl.ds(pl.multiple_of(first * dim, width), width)
        loads.append(pltpu.make_async_copy(gate_ref.at[0, :, columns], copy_ref.at[at], done.at[at]))
        stores.append(pltpu.make_async_copy(result_ref.at[at], out_ref, done.at[2 + at]))
        loads[-1].start()
    for at in range(len(results)):
        loads[at].wait()
        for head in range(share):
            c = slice(head * dim, (head + 1) * dim)
            turned = jnp.tanh(0.5 * copy_ref[at, :, c].astype(jnp.float32))
            result_ref[at, :, c] = 0.5 + 0.5 * turned
        stores[at].start()
    done_ref[...] = jnp.zeros_like(done_ref)
    for store in stores:
        store.wait()


def heads_at(first, head, dim):
    return pl.ds(pl.multiple_of((first + head) * dim, dim), dim)


def decays_at(decay_ref, block, first):
    local = decay_ref.shape[1]
    parts = decay_ref.shape[0] // 2
    rows = pl.ds(pl.multiple_of(first % local, STEP), STEP)
    return decay_ref[block * parts + first // local, rows, :]


def state_kernel(dim, owned, half, begin, masks, me_ref, decay_ref, *refs):
    arrays, slots = refs[:4], refs[-3 - 2 * len(masks) : -3]
    stacked_ref, copy_ref, done = refs[-3:]
    part, core = me_ref[0], me_ref[1]
    firsts = [core * half + begin + ((part >> 1) ^ mask) * STEP for mask in masks]
    width = STEP * dim
    moves = [
        [
            pltpu.make_async_copy(
                ref.at[0, :, pl.ds(pl.multiple_of(first * dim, width), width)],
                copy_ref.at[turn, at],
                done.at[turn, at],
            )
            for at, ref in enumerate(arrays)
        ]
        for turn, first in enumerate(firsts)
    ]
    for move in sum(moves, []):
        move.start()
    for turn, first in enumerate(firsts):
        for source in range(2):
            block = core if source == 0 else 1 - core
            decay = decays_at(decay_ref, block, first)
            weight = jnp.exp(sums_over(decay, lambda u, s: u > s))
            whole = jnp.broadcast_to(jnp.sum(decay, axis=1, keepdims=True), (STEP, dim))
            for move in moves[turn][2 * source : 2 * source + 2]:
                move.wait()
            states = []
            for head in range(STEP):
                c = slice(head * dim, (head + 1) * dim)
                decayed = copy_ref[turn, 2 * source, :, c].T.astype(jnp.float32)
                decayed = (decayed * weight[head : head + 1, :]).astype(jnp.bfloat16)
                states.append(dot(decayed, copy_ref[turn, 2 * source + 1, :, c], NN))
            for head in range(STEP):
                owner, spot = divmod(head, owned)
                span = slice(spot * dim, (spot + 1) * dim)
                stacked_ref[turn, owner, block, span, :] = states[head].astype(jnp.bfloat16)
            for at in range(2):
                stacked_ref[turn, at, block, owned * dim :, :] = decay_rows(
                    [whole[head : head + 1] for head in range(at * owned, (at + 1) * owned)]
                )
        for at in range(2):
            slots[2 * turn + at][...] = stacked_ref[turn, (part & 1) ^ at]


def inside_kernel(
    dim, half, begin, count, other, me_ref, queries_ref, keys_ref, values_ref, decay_ref, *rest
):
    inside_ref, down_ref, done_ref = rest[-3:]
    core = me_ref[1]
    length = decay_ref.shape[2]
    rows = lax.broadcasted_iota(jnp.int32, (length, length), 0)
    causal = rows >= lax.broadcasted_iota(jnp.int32, (length, length), 1)
    for turn in range(count // STEP):
        first = (1 - core if other else core) * half + begin + turn * STEP
        decay = decays_at(decay_ref, core, first)
        across = sums_over(decay, lambda u, s: u <= s)
        down = across.T
        down_ref[turn] = jnp.exp(down)
        columns = [heads_at(first, head, dim) for head in range(STEP)]
        scores = [dot(queries_ref[0, :, c], keys_ref[0, :, c], NT) for c in columns]
        weights = []
        for head in range(STEP):
            gap = down[:, head : head + 1] - across[head : head + 1, :]
            weight = scores[head] * jnp.exp(jnp.where(causal, gap, -jnp.inf))
            weights.append(weight.astype(jnp.bfloat16))
        for head, c in enumerate(columns):
            at = (turn * STEP + head) * dim
            inside_ref[:, at : at + dim] = dot(weights[head], values_ref[0, :, c], NN)
    done_ref[...] = jnp.zeros_like(done_ref)


def gather_states(part, slots, stacked_ref):
    parts = len(slots)
    for slot, slot_ref in enumerate(slots):
        for block in range(2):
            stacked_ref[block * parts + (part ^ slot)] = slot_ref[block]


def total_kernel(dim, owned, parts, me_ref, *refs):
    total_ref, stacked_ref = refs[-2:]
    gather_states(me_ref[0], refs[:parts], stacked_ref)
    count = 2 * parts
    extra = [stacked_ref[at, owned * dim :, :] for at in range(count)]
    sums = []
    for head in range(owned):
        span = slice(head * dim, (head + 1) * dim)
        after = jnp.zeros((1, dim), jnp.float32)
        total = stacked_ref[count - 1, span, :].astype(jnp.float32)
        for at in range(count - 2, -1, -1):
            after += join(extra[at + 1], head)
            total += jnp.exp(after) * stacked_ref[at, span, :].astype(jnp.float32)
        total_ref[span, :] = total.astype(jnp.bfloat16)
        sums.append(after + join(extra[0], head))
    total_ref[owned * dim :, :] = decay_rows(sums)


def widen_kernel(dim, owned, step, me_ref, mine_ref, other_ref, *refs):
    out_ref = refs[-1]
    later = (me_ref[2] >> step) % 2 == 1
    extra = mine_ref[owned * dim :, :], other_ref[owned * dim :, :]
    sums = []
    for head in range(owned):
        span = slice(head * dim, (head + 1) * dim)
        mine, other = join(extra[0], head), join(extra[1], head)
        total = jnp.where(later, 1.0, jnp.exp(other)) * mine_ref[span, :].astype(jnp.float32)
        total += jnp.where(later, jnp.exp(mine), 1.0) * other_ref[span, :].astype(jnp.float32)
        out_ref[span, :] = total.astype(jnp.bfloat16)
        sums.append(mine + other)
    out_ref[owned * dim :, :] = decay_rows(sums)


def prefix_kernel(dim, owned, parts, stretches, me_ref, gain_ref, *refs):
    stacked_ref, prefix_ref = refs[-2:]
    slots, totals = refs[:parts], refs[parts : parts + stretches]
    count = 2 * parts
    results = refs[-2 - parts : -2]
    gather_states(me_ref[0], slots, stacked_ref)
    extra = [stacked_ref[at, owned * dim :, :] for at in range(count)]
    more = [total_ref[owned * dim :, :] for total_ref in totals]
    earlier = [
        ((me_ref[2] >> step) % 2).astype(jnp.float32) for step in range(len(totals))
    ]
    for head in range(owned):
        span = slice(head * dim, (head + 1) * dim)
        prefix = jnp.zeros((dim, dim), jnp.float32)
        after = jnp.zeros((1, dim), jnp.float32)
        for turn, total_ref in enumerate(totals):
            factor = earlier[turn] * jnp.exp(after)
            prefix += factor * total_ref[span, :].astype(jnp.float32)
            after += earlier[turn] * join(more[turn], head)
        for at in range(count):
            prefix_ref[at, span, :] = prefix.astype(jnp.bfloat16)
            if at < count - 1:
                prefix = jnp.exp(join(extra[at], head)) * prefix
                prefix += stacked_ref[at, span, :].astype(jnp.float32)
    size = owned * dim
    for slot, result_ref in enumerate(results):
        for block in range(2):
            result_ref[block * size : (block + 1) * size, :] = prefix_ref[
                block * parts + (me_ref[0] ^ slot)
            ]
        result_ref[2 * size :, :] = gain_ref[...]


def collect(part, block, slots, prefix_ref, gain_ref):
    parts, size, _ = prefix_ref.shape
    local = gain_ref.shape[0] // parts
    for slot, slot_ref in enumerate(slots):
        owner = part ^ slot
        prefix_ref[owner] = slot_ref[pl.ds(pl.multiple_of(block * size, size), size), :]
        rows = pl.ds(pl.multiple_of(owner * local, local), local)
        gain_ref[rows, :] = slot_ref[2 * size :, :].astype(jnp.float32)


def merge_kernel(parts, me_ref, *refs):
    *others, gain_ref, prefix_ref = refs[parts:] if len(refs) == parts + 4 else refs[parts + 1 :]
    collect(me_ref[0], 1 - me_ref[1], refs[:parts], prefix_ref, gain_ref)
    each = parts // len(others)
    for turn, other_ref in enumerate(others):
        other_ref[...] = prefix_ref[turn * each : (turn + 1) * each]


def output_kernel(
    dim, owned, half, begin, count, parts, me_ref,
    queries_ref, inside_ref, down_ref, gate_ref, *refs,
):
    out_ref, done_ref, prefix_ref, gain_ref, result_ref, sent = refs[-6:]
    core = me_ref[1]
    if parts is None:
        *others, gains = refs[:3]
        each = others[0].shape[0]
        prefixes = [others[at // each].at[at % each] for at in range(each * len(others))]
    else:
        collect(me_ref[0], core, refs[:parts], prefix_ref, gain_ref)
        prefixes, gains = [prefix_ref.at[at] for at in range(parts)], gain_ref
    blocks = [lax.broadcasted_iota(jnp.int32, (2 * dim, 2 * dim), axis) // dim for axis in (0, 1)]
    average = jnp.where(blocks[0] == blocks[1], 1.0 / dim, 0.0).astype(jnp.bfloat16)
    moves = []
    for turn in range(count // STEP):
        first = (1 - core if parts is None else core) * half + begin + turn * STEP
        gain = gains[pl.ds(pl.multiple_of(first, STEP), STEP), :]
        down = down_ref[turn]
        columns = [heads_at(first, head, dim) for head in range(STEP)]
        carried = []
        for head, c in enumerate(columns):
            owner, spot = divmod(turn * STEP + head, owned)
            prefix = prefixes[owner][spot * dim : (spot + 1) * dim, :]
            carried.append(dot(queries_ref[0, :, c], prefix, NN))
        mixed, means = [], []
        for head in range(STEP):
            at = (turn * STEP + head) * dim
            mixed.append(inside_ref[:, at : at + dim] + carried[head] * down[:, head : head + 1])
        for head in range(0, STEP, 2):
            squares = [(mixed[at] * mixed[at]).astype(jnp.bfloat16) for at in (head, head + 1)]
            both = dot(jnp.concatenate(squares, axis=1), average, NN)
            means += [both[:, :dim], both[:, dim:]]
        for head in range(STEP):
            at = (turn * STEP + head) * dim
            factor = gain[head : head + 1, :] * gate_ref[:, at : at + dim]
            normed = mixed[head] * lax.rsqrt(means[head] + 1e-06) * factor
            result_ref[turn, :, head * dim : (head + 1) * dim] = normed.astype(jnp.bfloat16)
        width = STEP * dim
        moves.append(
            pltpu.make_async_copy(
                result_ref.at[turn],
                out_ref.at[0, :, pl.ds(pl.multiple_of(first * dim, width), width)],
                sent.at[turn],
            )
        )
        moves[-1].start()
    done_ref[...] = jnp.zeros_like(done_ref)
    for move in moves:
        move.wait()


def kernel_call(body, name, in_specs, out_specs, out_shape, scratch=(), aliases={}, cost=0):
    return pl.pallas_call(
        body,
        grid_spec=pltpu.PrefetchScalarGridSpec(
            num_scalar_prefetch=1,
            grid=(),
            in_specs=in_specs,
            out_specs=out_specs,
            scratch_shapes=scratch,
        ),
        out_shape=out_shape,
        input_output_aliases=aliases,
        compiler_params=pltpu.CompilerParams(vmem_limit_bytes=VMEM_LIMIT),
        cost_estimate=pl.CostEstimate(
            flops=int(1e9 * cost) + 1, transcendentals=0, bytes_accessed=1
        ),
        name=name,
    )


def on_device(parts, planes, queries, keys, values, gate, log_decay, norm_gain):
    _, length, width = queries.shape
    local = log_decay.shape[1]
    dim = width // (local * parts)
    count = 2 * parts
    half = local * parts // 2
    owned = half // (GROUPS * parts)
    rows = owned * dim + EXTRA
    me = jnp.stack([lax.axis_index(axis) for axis in ("head", "core", "z")]).astype(jnp.int32)
    swap = [(0, 1), (1, 0)]

    values_other = lax.ppermute(values, "core", swap)
    keys_other = lax.ppermute(keys, "core", swap)
    packed = pl.pallas_call(
        functools.partial(pack_kernel, parts),
        out_shape=jax.ShapeDtypeStruct((count, local, length), jnp.float32),
        name="pack",
    )(log_decay)
    decay = lax.all_to_all(packed, ("core", "head"), 0, 0, tiled=True)
    gain = norm_gain.reshape(local, dim)

    vmem = pl.BlockSpec(memory_space=pltpu.VMEM)
    hbm = pl.BlockSpec(memory_space=pl.ANY)

    def in_vmem(array):
        return pltpu.with_memory_space_constraint(array, pltpu.VMEM)

    def in_hbm(array):
        return pltpu.with_memory_space_constraint(array, pltpu.HBM)

    own = in_hbm(keys), in_hbm(values)
    share = half // GROUPS
    keys, values, queries = (in_vmem(array) for array in (keys, values, queries))

    def exchange(slots):
        arrived = list(slots)
        for slot in sorted(range(1, parts), key=lambda s: -bin(s).count("1")):
            pairs = [(at, at ^ slot) for at in range(parts)]
            arrived[slot] = lax.ppermute(slots[slot], "head", pairs)
        return arrived

    before = ()
    held = []
    state_type = jax.ShapeDtypeStruct((2, rows, dim), jnp.bfloat16)
    token = jax.ShapeDtypeStruct((8, 128), jnp.float32)
    inside = {}

    def inside_part(before, cost=0):
        group, other = divmod(len(inside), 2)
        *inside[group, other], made = kernel_call(
            functools.partial(inside_kernel, dim, half, group * share, share, other),
            f"inside{group}_{other}",
            [vmem] * 4 + [hbm] * len(before),
            [vmem] * 3,
            [
                pltpu.VMEM((length, share * dim), jnp.float32),
                jax.ShapeDtypeStruct((share // STEP, length, STEP), jnp.float32),
                token,
            ],
            cost=cost,
        )(me, queries, keys, values, decay, *before)
        return (made,)

    gate_type = jax.ShapeDtypeStruct((length, share * dim), jnp.float32)
    gates = {}

    def gates_of(group, before):
        gates[group, 0], gates[group, 1], made = kernel_call(
            functools.partial(gate_kernel, half, group * share, share, dim),
            f"gates{group}",
            [hbm] * (1 + len(before)),
            [hbm, hbm, vmem],
            [pltpu.HBM(gate_type.shape, gate_type.dtype)] * 2 + [token],
            [
                pltpu.VMEM((2, length, share * dim), jnp.bfloat16),
                pltpu.VMEM((2,) + gate_type.shape, jnp.float32),
                pltpu.SemaphoreType.DMA((4,)),
            ],
        )(me, in_hbm(gate), *before)
        return (made,)

    for group in range(GROUPS):
        slots = {}
        for masks in ((1,), (0,)) if group == 0 else ((1, 0),):
            state = kernel_call(
                functools.partial(state_kernel, dim, owned, half, group * share, masks),
                f"state{group}_{masks[0]}",
                [vmem] + [hbm] * (4 + len(before)),
                [vmem] * (2 * len(masks)),
                [state_type] * (2 * len(masks)),
                [
                    pltpu.VMEM((len(masks), 2) + state_type.shape, jnp.bfloat16),
                    pltpu.VMEM((len(masks), 4, length, STEP * dim), jnp.bfloat16),
                    pltpu.SemaphoreType.DMA((len(masks), 4)),
                ],
            )(me, decay, *own, keys_other, values_other, *before)
            before = tuple(state[:1])
            for at, array in enumerate(state):
                slots[2 * masks[at // 2] + at % 2] = array
        held.append(exchange([slots[slot] for slot in range(parts)]))
    before = inside_part(inside_part(before))

    arrived = []
    stacked = pltpu.VMEM((count, rows, dim), jnp.bfloat16)
    total_type = jax.ShapeDtypeStruct((rows, dim), jnp.bfloat16)

    def with_plane(total, step):
        pairs = [(at, at ^ (1 << step)) for at in range(planes)]
        return lax.ppermute(total, "z", pairs)

    def widen(group, step, total, other, before):
        return kernel_call(
            functools.partial(widen_kernel, dim, owned, step),
            f"widen{group}_{step}",
            [vmem] * 2 + [hbm] * len(before),
            vmem,
            total_type,
        )(me, total, other, *before)

    def prefix_of(group, before):
        stretches = arrived[group]
        return kernel_call(
            functools.partial(prefix_kernel, dim, owned, parts, len(stretches)),
            f"prefix{group}",
            [vmem] * (1 + parts + len(stretches)) + [hbm] * len(before),
            [vmem] * parts,
            [prefix_type] * parts,
            [stacked, pltpu.VMEM((count, size, dim), jnp.bfloat16)],
        )(me, gain, *held[group], *stretches, *before)

    size = owned * dim
    prefix_type = jax.ShapeDtypeStruct((2 * size + local, dim), jnp.bfloat16)
    prefixes = []
    for group in range(GROUPS):
        total = kernel_call(
            functools.partial(total_kernel, dim, owned, parts),
            f"total{group}",
            [vmem] * parts + [hbm],
            vmem,
            total_type,
            [stacked],
        )(me, *held[group], *before)
        before = (total,)
        stretches = [with_plane(total, 0)]
        arrived.append(stretches)
        if group > 0:
            prefix = prefix_of(group - 1, before)
            before = tuple(prefix[:1])
            prefixes.append(exchange(prefix))
        if group < GROUPS - 1:
            before = inside_part(before)
        for step in range(1, planes.bit_length() - 1):
            total = widen(group, step - 1, total, stretches[-1], before)
            before = (total,)
            stretches.append(with_plane(total, step))
        while group == GROUPS - 1 and len(inside) < 2 * GROUPS:
            before = inside_part(before, 2)
        before = gates_of(group, before)
    prefix = prefix_of(GROUPS - 1, before)
    before = tuple(prefix[:1])
    prefixes.append(exchange(prefix))

    part_type = jax.ShapeDtypeStruct((parts, size, dim), jnp.bfloat16)
    half_type = jax.ShapeDtypeStruct((parts // 2, size, dim), jnp.bfloat16)
    gain_type = jax.ShapeDtypeStruct((parts * local, dim), jnp.float32)

    def merge(group, before, cost):
        return kernel_call(
            functools.partial(merge_kernel, parts),
            f"merge{group}",
            [vmem] * parts + [hbm] * len(before),
            [vmem] * 3,
            [half_type, half_type, gain_type],
            [pltpu.VMEM(part_type.shape, part_type.dtype)],
            cost=cost,
        )(me, *prefixes[group], *before)

    def output(group, other, received, out, before, cost=0):
        *out, made = kernel_call(
            functools.partial(
                output_kernel, dim, owned, half, group * share, share, None if other else parts
            ),
            f"output{group}_{other}",
            [vmem] * (4 + len(received)) + [hbm] * (len(out) + len(before)),
            [hbm, vmem],
            [pltpu.HBM((1, length, width), jnp.bfloat16), token],
            [
                pltpu.VMEM(part_type.shape, part_type.dtype),
                pltpu.VMEM(gain_type.shape, gain_type.dtype),
                pltpu.VMEM((share // STEP, length, STEP * dim), jnp.bfloat16),
                pltpu.SemaphoreType.DMA((share // STEP,)),
            ],
            aliases={5 + len(received): 0} if out else {},
            cost=cost,
        )(
            me, queries, in_vmem(inside[group, other][0]), inside[group, other][1],
            in_vmem(gates[group, other]), *received, *out, *before,
        )
        return out, (made,)

    out = ()
    for group in range(GROUPS):
        last = group == GROUPS - 1
        *others, gains = merge(group, before, 0)
        others = [lax.ppermute(other, "core", swap) for other in others]
        before = (gains,)
        out, before = output(group, 0, prefixes[group], out, before, cost=20 if last else 0)
        out, before = output(group, 1, (*others, gains), out, before)
    return out[0]


def solution(mesh):
    parts, blocks = mesh.shape["head"], mesh.shape["ctx"]
    names = mesh.axis_names
    at = names.index("ctx")
    shape = mesh.devices.shape[:at] + (blocks // 2, 2) + mesh.devices.shape[at + 1 :]
    finer = Mesh(mesh.devices.reshape(shape), names[:at] + ("z", "core") + names[at + 1 :])
    tokens = P(("z", "core"), "head", None)
    return jax.shard_map(
        functools.partial(on_device, parts, blocks // 2),
        mesh=finer,
        in_specs=(tokens,) * 5 + (P("head"),),
        out_specs=tokens,
        check_vma=False,
    )
```

```python
import functools

import jax
import jax.numpy as jnp
from jax import lax
from jax.experimental import pallas as pl
from jax.experimental.pallas import tpu as pltpu
from jax.sharding import Mesh
from jax.sharding import PartitionSpec as P

GROUPS = 2
STEP = 8
EXTRA = 16
VMEM_LIMIT = 8 * 1024 * 1024
NN = (((1,), (0,)), ((), ()))
NT = (((1,), (1,)), ((), ()))
TN = (((0,), (0,)), ((), ()))


def dot(a, b, dims, precision=None):
    return lax.dot_general(a, b, dims, precision=precision, preferred_element_type=jnp.float32)


def split(value):
    first = value.astype(jnp.bfloat16)
    left = value - first.astype(jnp.float32)
    second = left.astype(jnp.bfloat16)
    return first, second, (left - second.astype(jnp.float32)).astype(jnp.bfloat16)


def sums_over(decay, keep):
    heads, length = decay.shape
    rows = lax.broadcasted_iota(jnp.int32, (length, length), 0)
    columns = lax.broadcasted_iota(jnp.int32, (length, length), 1)
    chosen = jnp.where(keep(rows, columns), 1.0, 0.0).astype(jnp.bfloat16)
    parts = [part.astype(jnp.float32) for part in split(decay)]
    both = dot(jnp.concatenate(parts, axis=0).astype(jnp.bfloat16), chosen, NN)
    return both[:heads] + (both[heads : 2 * heads] + both[2 * heads :])


def join(rows, head):
    wide = rows.astype(jnp.float32)
    return wide[3 * head : 3 * head + 1] + (
        wide[3 * head + 1 : 3 * head + 2] + wide[3 * head + 2 : 3 * head + 3]
    )


def decay_rows(totals):
    parts = [part for total in totals for part in split(total)]
    blank = jnp.zeros((EXTRA - len(parts), totals[0].shape[1]), jnp.bfloat16)
    return jnp.concatenate(parts + [blank], axis=0)


def pack_kernel(parts, decay_ref, packed_ref):
    length = packed_ref.shape[2]
    for place in range(packed_ref.shape[0]):
        start = place % parts * length
        packed_ref[place] = decay_ref[0, :, start : start + length]


def gate_kernel(half, begin, share, dim, me_ref, gate_ref, *refs):
    *results, done_ref, copy_ref, result_ref, done = refs[-6:]
    width = share * dim
    loads, stores = [], []
    for at, out_ref in enumerate(results):
        first = (me_ref[1] if at == 0 else 1 - me_ref[1]) * half + begin
        columns = pl.ds(pl.multiple_of(first * dim, width), width)
        loads.append(pltpu.make_async_copy(gate_ref.at[0, :, columns], copy_ref.at[at], done.at[at]))
        stores.append(pltpu.make_async_copy(result_ref.at[at], out_ref, done.at[2 + at]))
        loads[-1].start()
    for at in range(len(results)):
        loads[at].wait()
        for head in range(share):
            c = slice(head * dim, (head + 1) * dim)
            turned = jnp.tanh(0.5 * copy_ref[at, :, c].astype(jnp.float32))
            result_ref[at, :, c] = 0.5 + 0.5 * turned
        stores[at].start()
    done_ref[...] = jnp.zeros_like(done_ref)
    for store in stores:
        store.wait()


def heads_at(first, head, dim):
    return pl.ds(pl.multiple_of((first + head) * dim, dim), dim)


def decays_at(decay_ref, block, first):
    local = decay_ref.shape[1]
    parts = decay_ref.shape[0] // 2
    rows = pl.ds(pl.multiple_of(first % local, STEP), STEP)
    return decay_ref[block * parts + first // local, rows, :]


def load_kernel(half, begin, count, dim, me_ref, *refs):
    sources, copies, done = refs[:4], refs[-5:-1], refs[-1]
    width = count * dim
    columns = pl.ds(pl.multiple_of((me_ref[1] * half + begin) * dim, width), width)
    moves = [
        pltpu.make_async_copy(source.at[0, :, columns], copy, done.at[at])
        for at, (source, copy) in enumerate(zip(sources, copies))
    ]
    for move in moves:
        move.start()
    for move in moves:
        move.wait()


def state_kernel(dim, owned, half, begin, masks, loaded, me_ref, decay_ref, *refs):
    arrays = refs[:4]
    outs = refs[len(refs) - (1 if loaded else 3) - 2 * len(masks) :]
    slots, stacked_ref = outs[: 2 * len(masks)], outs[2 * len(masks)]
    part, core = me_ref[0], me_ref[1]
    turns = [(part >> 1) ^ mask for mask in masks]
    firsts = [core * half + begin + turn * STEP for turn in turns]
    width = STEP * dim
    moves = []
    if not loaded:
        copy_ref, done = outs[-2:]
        moves = [
            [
                pltpu.make_async_copy(
                    ref.at[0, :, pl.ds(pl.multiple_of(first * dim, width), width)],
                    copy_ref.at[turn, at],
                    done.at[turn, at],
                )
                for at, ref in enumerate(arrays)
            ]
            for turn, first in enumerate(firsts)
        ]
    for move in sum(moves, []):
        move.start()

    def piece(turn, at, head):
        if loaded:
            return arrays[at][:, heads_at(turns[turn] * STEP, head, dim)]
        return copy_ref[turn, at, :, head * dim : (head + 1) * dim]

    for turn, first in enumerate(firsts):
        for source in range(2):
            block = core if source == 0 else 1 - core
            decay = decays_at(decay_ref, block, first)
            weight = jnp.exp(sums_over(decay, lambda u, s: u > s))
            whole = jnp.broadcast_to(jnp.sum(decay, axis=1, keepdims=True), (STEP, dim))
            if moves:
                for move in moves[turn][2 * source : 2 * source + 2]:
                    move.wait()
            states = []
            for head in range(STEP):
                decayed = piece(turn, 2 * source, head).T.astype(jnp.float32)
                decayed = (decayed * weight[head : head + 1, :]).astype(jnp.bfloat16)
                states.append(dot(decayed, piece(turn, 2 * source + 1, head), NN))
            for head in range(STEP):
                owner, spot = divmod(head, owned)
                span = slice(spot * dim, (spot + 1) * dim)
                stacked_ref[turn, owner, block, span, :] = states[head].astype(jnp.bfloat16)
            for at in range(2):
                stacked_ref[turn, at, block, owned * dim :, :] = decay_rows(
                    [whole[head : head + 1] for head in range(at * owned, (at + 1) * owned)]
                )
        for at in range(2):
            slots[2 * turn + at][...] = stacked_ref[turn, (part & 1) ^ at]


def inside_kernel(
    dim, half, begin, count, other, me_ref, queries_ref, keys_ref, values_ref, decay_ref, *rest
):
    inside_ref, down_ref, done_ref = rest[-3:]
    core = me_ref[1]
    length = decay_ref.shape[2]
    rows = lax.broadcasted_iota(jnp.int32, (length, length), 0)
    causal = rows >= lax.broadcasted_iota(jnp.int32, (length, length), 1)
    for turn in range(count // STEP):
        first = (1 - core if other else core) * half + begin + turn * STEP
        decay = decays_at(decay_ref, core, first)
        across = sums_over(decay, lambda u, s: u <= s)
        down = across.T
        down_ref[turn] = jnp.exp(down)
        columns = [heads_at(first, head, dim) for head in range(STEP)]
        scores = [dot(queries_ref[0, :, c], keys_ref[0, :, c], NT) for c in columns]
        weights = []
        for head in range(STEP):
            gap = down[:, head : head + 1] - across[head : head + 1, :]
            weight = scores[head] * jnp.exp(jnp.where(causal, gap, -jnp.inf))
            weights.append(weight.astype(jnp.bfloat16))
        for head, c in enumerate(columns):
            at = (turn * STEP + head) * dim
            inside_ref[:, at : at + dim] = dot(weights[head], values_ref[0, :, c], NN)
    done_ref[...] = jnp.zeros_like(done_ref)


def gather_states(part, slots, stacked_ref):
    parts = len(slots)
    for slot, slot_ref in enumerate(slots):
        for block in range(2):
            stacked_ref[block * parts + (part ^ slot)] = slot_ref[block]


def total_kernel(dim, owned, parts, me_ref, *refs):
    total_ref, stacked_ref = refs[-2:]
    gather_states(me_ref[0], refs[:parts], stacked_ref)
    count = 2 * parts
    extra = [stacked_ref[at, owned * dim :, :] for at in range(count)]
    sums = []
    for head in range(owned):
        span = slice(head * dim, (head + 1) * dim)
        after = jnp.zeros((1, dim), jnp.float32)
        total = stacked_ref[count - 1, span, :].astype(jnp.float32)
        for at in range(count - 2, -1, -1):
            after += join(extra[at + 1], head)
            total += jnp.exp(after) * stacked_ref[at, span, :].astype(jnp.float32)
        total_ref[span, :] = total.astype(jnp.bfloat16)
        sums.append(after + join(extra[0], head))
    total_ref[owned * dim :, :] = decay_rows(sums)


def widen_kernel(dim, owned, step, me_ref, mine_ref, other_ref, *refs):
    out_ref = refs[-1]
    later = (me_ref[2] >> step) % 2 == 1
    extra = mine_ref[owned * dim :, :], other_ref[owned * dim :, :]
    sums = []
    for head in range(owned):
        span = slice(head * dim, (head + 1) * dim)
        mine, other = join(extra[0], head), join(extra[1], head)
        total = jnp.where(later, 1.0, jnp.exp(other)) * mine_ref[span, :].astype(jnp.float32)
        total += jnp.where(later, jnp.exp(mine), 1.0) * other_ref[span, :].astype(jnp.float32)
        out_ref[span, :] = total.astype(jnp.bfloat16)
        sums.append(mine + other)
    out_ref[owned * dim :, :] = decay_rows(sums)


def prefix_kernel(dim, owned, parts, stretches, me_ref, gain_ref, *refs):
    stacked_ref, prefix_ref = refs[-2:]
    slots, totals = refs[:parts], refs[parts : parts + stretches]
    count = 2 * parts
    results = refs[-2 - parts : -2]
    gather_states(me_ref[0], slots, stacked_ref)
    extra = [stacked_ref[at, owned * dim :, :] for at in range(count)]
    more = [total_ref[owned * dim :, :] for total_ref in totals]
    earlier = [
        ((me_ref[2] >> step) % 2).astype(jnp.float32) for step in range(len(totals))
    ]
    for head in range(owned):
        span = slice(head * dim, (head + 1) * dim)
        prefix = jnp.zeros((dim, dim), jnp.float32)
        after = jnp.zeros((1, dim), jnp.float32)
        for turn, total_ref in enumerate(totals):
            factor = earlier[turn] * jnp.exp(after)
            prefix += factor * total_ref[span, :].astype(jnp.float32)
            after += earlier[turn] * join(more[turn], head)
        for at in range(count):
            prefix_ref[at, span, :] = prefix.astype(jnp.bfloat16)
            if at < count - 1:
                prefix = jnp.exp(join(extra[at], head)) * prefix
                prefix += stacked_ref[at, span, :].astype(jnp.float32)
    size = owned * dim
    for slot, result_ref in enumerate(results):
        for block in range(2):
            result_ref[block * size : (block + 1) * size, :] = prefix_ref[
                block * parts + (me_ref[0] ^ slot)
            ]
        if result_ref.shape[0] > 2 * size:
            result_ref[2 * size :, :] = gain_ref[...]


def merge_kernel(parts, me_ref, *refs):
    slots, gain_ref, prefix_ref = refs[:parts], refs[-2], refs[-1]
    others = refs[-4:-2]
    size = prefix_ref.shape[1]
    local = gain_ref.shape[0] // parts
    block = 1 - me_ref[1]
    for slot, slot_ref in enumerate(slots):
        owner = me_ref[0] ^ slot
        prefix_ref[owner] = slot_ref[pl.ds(pl.multiple_of(block * size, size), size), :]
        if slot_ref.shape[0] > 2 * size:
            rows = pl.ds(pl.multiple_of(owner * local, local), local)
            gain_ref[rows, :] = slot_ref[2 * size :, :].astype(jnp.float32)
    if slots[0].shape[0] == 2 * size:
        gain_ref[...] = jnp.zeros_like(gain_ref)
    each = parts // len(others)
    for turn, other_ref in enumerate(others):
        other_ref[...] = prefix_ref[turn * each : (turn + 1) * each]


def output_kernel(
    dim, owned, half, begin, masks, other, me_ref,
    queries_ref, inside_ref, down_ref, gate_ref, gains, *refs,
):
    out_ref, done_ref, prefix_ref, result_ref, sent = refs[-5:]
    part, core = me_ref[0], me_ref[1]
    size = owned * dim
    if other:
        turns, prefixes = [0, 1], [refs[0], refs[1]]
    else:
        turns = [(part >> 1) ^ mask for mask in masks]
        prefixes = [prefix_ref.at[turn] for turn in range(len(masks))]
        rows = pl.ds(pl.multiple_of(core * size, size), size)
        for turn in range(len(masks)):
            for at in range(2):
                prefix_ref[turn, (part & 1) ^ at] = refs[2 * turn + at][rows, :]
    blocks = [lax.broadcasted_iota(jnp.int32, (2 * dim, 2 * dim), axis) // dim for axis in (0, 1)]
    average = jnp.where(blocks[0] == blocks[1], 1.0 / dim, 0.0).astype(jnp.bfloat16)
    moves = []
    for at, turn in enumerate(turns):
        first = (1 - core if other else core) * half + begin + turn * STEP
        gain = gains[pl.ds(pl.multiple_of(first, STEP), STEP), :]
        down = down_ref[turn]
        columns = [heads_at(first, head, dim) for head in range(STEP)]
        here = [heads_at(turn * STEP, head, dim) for head in range(STEP)]
        carried = []
        for head, c in enumerate(columns):
            owner, spot = divmod(head, owned)
            prefix = prefixes[at][owner, spot * dim : (spot + 1) * dim, :]
            carried.append(dot(queries_ref[0, :, c], prefix, NN))
        mixed, means = [], []
        for head in range(STEP):
            mixed.append(inside_ref[:, here[head]] + carried[head] * down[:, head : head + 1])
        for head in range(0, STEP, 2):
            squares = [(value * value).astype(jnp.bfloat16) for value in mixed[head : head + 2]]
            both = dot(jnp.concatenate(squares, axis=1), average, NN)
            means += [both[:, :dim], both[:, dim:]]
        for head in range(STEP):
            factor = gain[head : head + 1, :] * gate_ref[:, here[head]]
            normed = mixed[head] * lax.rsqrt(means[head] + 1e-06) * factor
            result_ref[at, :, head * dim : (head + 1) * dim] = normed.astype(jnp.bfloat16)
        width = STEP * dim
        moves.append(
            pltpu.make_async_copy(
                result_ref.at[at],
                out_ref.at[0, :, pl.ds(pl.multiple_of(first * dim, width), width)],
                sent.at[at],
            )
        )
        moves[-1].start()
    done_ref[...] = jnp.zeros_like(done_ref)
    for move in moves:
        move.wait()


def kernel_call(body, name, in_specs, out_specs, out_shape, scratch=(), aliases={}, cost=0):
    return pl.pallas_call(
        body,
        grid_spec=pltpu.PrefetchScalarGridSpec(
            num_scalar_prefetch=1,
            grid=(),
            in_specs=in_specs,
            out_specs=out_specs,
            scratch_shapes=scratch,
        ),
        out_shape=out_shape,
        input_output_aliases=aliases,
        compiler_params=pltpu.CompilerParams(vmem_limit_bytes=VMEM_LIMIT),
        cost_estimate=pl.CostEstimate(
            flops=int(1e9 * cost) + 1, transcendentals=0, bytes_accessed=1
        ),
        name=name,
    )


def on_device(parts, planes, queries, keys, values, gate, log_decay, norm_gain):
    _, length, width = queries.shape
    local = log_decay.shape[1]
    dim = width // (local * parts)
    count = 2 * parts
    half = local * parts // 2
    owned = half // (GROUPS * parts)
    rows = owned * dim + EXTRA
    me = jnp.stack([lax.axis_index(axis) for axis in ("head", "core", "z")]).astype(jnp.int32)
    swap = [(0, 1), (1, 0)]

    values_other = lax.ppermute(values, "core", swap)
    keys_other = lax.ppermute(keys, "core", swap)
    packed = pl.pallas_call(
        functools.partial(pack_kernel, parts),
        out_shape=jax.ShapeDtypeStruct((count, local, length), jnp.float32),
        name="pack",
    )(log_decay)
    decay = lax.all_to_all(packed, ("core", "head"), 0, 0, tiled=True)
    gain = norm_gain.reshape(local, dim)

    vmem = pl.BlockSpec(memory_space=pltpu.VMEM)
    hbm = pl.BlockSpec(memory_space=pl.ANY)

    def in_vmem(array):
        return pltpu.with_memory_space_constraint(array, pltpu.VMEM)

    def in_hbm(array):
        return pltpu.with_memory_space_constraint(array, pltpu.HBM)

    own = in_hbm(keys), in_hbm(values)
    share = half // GROUPS
    keys, values, queries = (in_vmem(array) for array in (keys, values, queries))

    def exchange(slots):
        arrived = list(slots)
        for slot in sorted(range(1, parts), key=lambda s: -bin(s).count("1")):
            pairs = [(at, at ^ slot) for at in range(parts)]
            arrived[slot] = lax.ppermute(slots[slot], "head", pairs)
        return arrived

    before = ()
    held = []
    state_type = jax.ShapeDtypeStruct((2, rows, dim), jnp.bfloat16)
    token = jax.ShapeDtypeStruct((8, 128), jnp.float32)
    inside = {}

    def inside_part(before, cost=0):
        group, other = divmod(len(inside), 2)
        *inside[group, other], made = kernel_call(
            functools.partial(inside_kernel, dim, half, group * share, share, other),
            f"inside{group}_{other}",
            [vmem] * 4 + [hbm] * len(before),
            [vmem] * 3,
            [
                pltpu.VMEM((length, share * dim), jnp.float32),
                jax.ShapeDtypeStruct((share // STEP, length, STEP), jnp.float32),
                token,
            ],
            cost=cost,
        )(me, queries, keys, values, decay, *before)
        return (made,)

    gate_type = jax.ShapeDtypeStruct((length, share * dim), jnp.float32)
    gates = {}

    def gates_of(group, before):
        gates[group, 0], gates[group, 1], made = kernel_call(
            functools.partial(gate_kernel, half, group * share, share, dim),
            f"gates{group}",
            [hbm] * (1 + len(before)),
            [hbm, hbm, vmem],
            [pltpu.HBM(gate_type.shape, gate_type.dtype)] * 2 + [token],
            [
                pltpu.VMEM((2, length, share * dim), jnp.bfloat16),
                pltpu.VMEM((2,) + gate_type.shape, jnp.float32),
                pltpu.SemaphoreType.DMA((4,)),
            ],
        )(me, in_hbm(gate), *before)
        return (made,)

    slices = (*own, keys_other, values_other)
    first_slices = kernel_call(
        functools.partial(load_kernel, half, 0, share, dim),
        "load",
        [hbm] * 4,
        [vmem] * 4,
        [pltpu.VMEM((length, share * dim), jnp.bfloat16)] * 4,
        [pltpu.SemaphoreType.DMA((4,))],
    )(me, *slices)
    first_slices = [in_vmem(array) for array in first_slices]
    for group in range(GROUPS):
        slots = {}
        for masks in ((1, 0),):
            loaded = group == 0
            scratch = [pltpu.VMEM((len(masks), 2) + state_type.shape, jnp.bfloat16)]
            if not loaded:
                scratch += [
                    pltpu.VMEM((len(masks), 4, length, STEP * dim), jnp.bfloat16),
                    pltpu.SemaphoreType.DMA((len(masks), 4)),
                ]
            state = kernel_call(
                functools.partial(state_kernel, dim, owned, half, group * share, masks, loaded),
                f"state{group}_{masks[0]}",
                [vmem] + [vmem if loaded else hbm] * 4 + [hbm] * len(before),
                [vmem] * (2 * len(masks)),
                [state_type] * (2 * len(masks)),
                scratch,
            )(me, decay, *(first_slices if loaded else slices), *before)
            before = tuple(state[:1])
            for at, array in enumerate(state):
                slots[2 * masks[at // 2] + at % 2] = array
        held.append(exchange([slots[slot] for slot in range(parts)]))
    before = inside_part(inside_part(before))

    arrived = []
    stacked = pltpu.VMEM((count, rows, dim), jnp.bfloat16)
    total_type = jax.ShapeDtypeStruct((rows, dim), jnp.bfloat16)

    def with_plane(total, step):
        pairs = [(at, at ^ (1 << step)) for at in range(planes)]
        return lax.ppermute(total, "z", pairs)

    def widen(group, step, total, other, before):
        return kernel_call(
            functools.partial(widen_kernel, dim, owned, step),
            f"widen{group}_{step}",
            [vmem] * 2 + [hbm] * len(before),
            vmem,
            total_type,
        )(me, total, other, *before)

    def prefix_of(group, before):
        stretches = arrived[group]
        return kernel_call(
            functools.partial(prefix_kernel, dim, owned, parts, len(stretches)),
            f"prefix{group}",
            [vmem] * (1 + parts + len(stretches)) + [hbm] * len(before),
            [vmem] * parts,
            [prefix_type] * parts,
            [stacked, pltpu.VMEM((count, size, dim), jnp.bfloat16)],
        )(me, gain, *held[group], *stretches, *before)

    size = owned * dim
    prefix_type = jax.ShapeDtypeStruct((2 * size + local, dim), jnp.bfloat16)
    prefixes = []
    for group in range(GROUPS):
        total = kernel_call(
            functools.partial(total_kernel, dim, owned, parts),
            f"total{group}",
            [vmem] * parts + [hbm],
            vmem,
            total_type,
            [stacked],
        )(me, *held[group], *before)
        before = (total,)
        stretches = [with_plane(total, 0)]
        arrived.append(stretches)
        if group > 0:
            prefix = prefix_of(group - 1, before)
            before = tuple(prefix[:1])
            prefixes.append(exchange(prefix))
        if group < GROUPS - 1:
            before = inside_part(before)
        for step in range(1, planes.bit_length() - 1):
            total = widen(group, step - 1, total, stretches[-1], before)
            before = (total,)
            stretches.append(with_plane(total, step))
        while group == GROUPS - 1 and len(inside) < 2 * GROUPS:
            before = inside_part(before, 2)
        before = gates_of(group, before)
    prefix = prefix_of(GROUPS - 1, before)
    before = tuple(prefix[:1])
    prefixes.append(exchange(prefix))

    part_type = jax.ShapeDtypeStruct((parts, size, dim), jnp.bfloat16)
    half_type = jax.ShapeDtypeStruct((parts // 2, size, dim), jnp.bfloat16)
    gain_type = jax.ShapeDtypeStruct((parts * local, dim), jnp.float32)

    def merge(group, before, cost):
        return kernel_call(
            functools.partial(merge_kernel, parts),
            f"merge{group}",
            [vmem] * parts + [hbm] * len(before),
            [vmem] * 3,
            [half_type, half_type, gain_type],
            [pltpu.VMEM(part_type.shape, part_type.dtype)],
            cost=cost,
        )(me, *prefixes[group], *before)

    def output(group, other, masks, received, out, before, cost=0):
        *out, made = kernel_call(
            functools.partial(output_kernel, dim, owned, half, group * share, masks, other),
            f"output{group}_{other}_{masks[0]}",
            [vmem] * (5 + len(received)) + [hbm] * (len(out) + len(before)),
            [hbm, vmem],
            [pltpu.HBM((1, length, width), jnp.bfloat16), token],
            [
                pltpu.VMEM((len(masks), 2, size, dim), jnp.bfloat16),
                pltpu.VMEM((len(masks), length, STEP * dim), jnp.bfloat16),
                pltpu.SemaphoreType.DMA((len(masks),)),
            ],
            aliases={6 + len(received): 0} if out else {},
            cost=cost,
        )(
            me, queries, in_vmem(inside[group, other][0]), inside[group, other][1],
            in_vmem(gates[group, other]), gains, *received, *out, *before,
        )
        return out, (made,)

    out = ()
    for group in range(GROUPS):
        last = group == GROUPS - 1
        slots = prefixes[group]
        if last:
            out, before = output(group, 0, (0,), slots[:2], out, before)
        *others, came = merge(group, before, 0)
        if group == 0:
            gains = came
        others = [lax.ppermute(other, "core", swap) for other in others]
        before = (came,)
        if last:
            out, before = output(group, 0, (1,), slots[2:], out, before, cost=20)
        else:
            out, before = output(group, 0, (0, 1), slots, out, before)
        out, before = output(group, 1, (0, 1), others, out, before)
    return out[0]


def solution(mesh):
    parts, blocks = mesh.shape["head"], mesh.shape["ctx"]
    names = mesh.axis_names
    at = names.index("ctx")
    shape = mesh.devices.shape[:at] + (blocks // 2, 2) + mesh.devices.shape[at + 1 :]
    finer = Mesh(mesh.devices.reshape(shape), names[:at] + ("z", "core") + names[at + 1 :])
    tokens = P(("z", "core"), "head", None)
    return jax.shard_map(
        functools.partial(on_device, parts, blocks // 2),
        mesh=finer,
        in_specs=(tokens,) * 5 + (P("head"),),
        out_specs=tokens,
        check_vma=False,
    )
```

```python
import functools

import jax
import jax.numpy as jnp
from jax import lax
from jax.experimental import pallas as pl
from jax.experimental.pallas import tpu as pltpu
from jax.sharding import Mesh
from jax.sharding import PartitionSpec as P

GROUPS = 2
STEP = 8
EXTRA = 16
VMEM_LIMIT = 8 * 1024 * 1024
NN = (((1,), (0,)), ((), ()))
NT = (((1,), (1,)), ((), ()))
TN = (((0,), (0,)), ((), ()))


def dot(a, b, dims, precision=None):
    return lax.dot_general(a, b, dims, precision=precision, preferred_element_type=jnp.float32)


def split(value):
    first = value.astype(jnp.bfloat16)
    left = value - first.astype(jnp.float32)
    second = left.astype(jnp.bfloat16)
    return first, second, (left - second.astype(jnp.float32)).astype(jnp.bfloat16)


def sums_over(decay, keep):
    heads, length = decay.shape
    rows = lax.broadcasted_iota(jnp.int32, (length, length), 0)
    columns = lax.broadcasted_iota(jnp.int32, (length, length), 1)
    chosen = jnp.where(keep(rows, columns), 1.0, 0.0).astype(jnp.bfloat16)
    parts = [part.astype(jnp.float32) for part in split(decay)]
    both = dot(jnp.concatenate(parts, axis=0).astype(jnp.bfloat16), chosen, NN)
    return both[:heads] + (both[heads : 2 * heads] + both[2 * heads :])


def join(rows, head):
    wide = rows.astype(jnp.float32)
    return wide[3 * head : 3 * head + 1] + (
        wide[3 * head + 1 : 3 * head + 2] + wide[3 * head + 2 : 3 * head + 3]
    )


def decay_rows(totals):
    parts = [part for total in totals for part in split(total)]
    blank = jnp.zeros((EXTRA - len(parts), totals[0].shape[1]), jnp.bfloat16)
    return jnp.concatenate(parts + [blank], axis=0)


def pack_kernel(parts, decay_ref, packed_ref):
    length = packed_ref.shape[2]
    for place in range(packed_ref.shape[0]):
        start = place % parts * length
        packed_ref[place] = decay_ref[0, :, start : start + length]


def gate_kernel(half, begin, share, dim, me_ref, gate_ref, *refs):
    *results, done_ref, copy_ref, result_ref, done = refs[-6:]
    width = share * dim
    loads, stores = [], []
    for at, out_ref in enumerate(results):
        first = (me_ref[1] if at == 0 else 1 - me_ref[1]) * half + begin
        columns = pl.ds(pl.multiple_of(first * dim, width), width)
        loads.append(pltpu.make_async_copy(gate_ref.at[0, :, columns], copy_ref.at[at], done.at[at]))
        stores.append(pltpu.make_async_copy(result_ref.at[at], out_ref, done.at[2 + at]))
        loads[-1].start()
    for at in range(len(results)):
        loads[at].wait()
        for head in range(share):
            c = slice(head * dim, (head + 1) * dim)
            turned = jnp.tanh(0.5 * copy_ref[at, :, c].astype(jnp.float32))
            result_ref[at, :, c] = 0.5 + 0.5 * turned
        stores[at].start()
    done_ref[...] = jnp.zeros_like(done_ref)
    for store in stores:
        store.wait()


def heads_at(first, head, dim):
    return pl.ds(pl.multiple_of((first + head) * dim, dim), dim)


def decays_at(decay_ref, block, first):
    local = decay_ref.shape[1]
    parts = decay_ref.shape[0] // 2
    rows = pl.ds(pl.multiple_of(first % local, STEP), STEP)
    return decay_ref[block * parts + first // local, rows, :]


def load_kernel(half, begin, count, dim, me_ref, *refs):
    sources, copies, done = refs[:4], refs[-5:-1], refs[-1]
    width = count * dim
    columns = pl.ds(pl.multiple_of((me_ref[1] * half + begin) * dim, width), width)
    moves = [
        pltpu.make_async_copy(source.at[0, :, columns], copy, done.at[at])
        for at, (source, copy) in enumerate(zip(sources, copies))
    ]
    for move in moves:
        move.start()
    for move in moves:
        move.wait()


def state_kernel(dim, owned, half, begin, masks, loaded, me_ref, decay_ref, *refs):
    arrays = refs[:4]
    outs = refs[len(refs) - (1 if loaded else 3) - 2 * len(masks) :]
    slots, stacked_ref = outs[: 2 * len(masks)], outs[2 * len(masks)]
    part, core = me_ref[0], me_ref[1]
    turns = [(part >> 1) ^ mask for mask in masks]
    firsts = [core * half + begin + turn * STEP for turn in turns]
    width = STEP * dim
    moves = []
    if not loaded:
        copy_ref, done = outs[-2:]
        moves = [
            [
                pltpu.make_async_copy(
                    ref.at[0, :, pl.ds(pl.multiple_of(first * dim, width), width)],
                    copy_ref.at[turn, at],
                    done.at[turn, at],
                )
                for at, ref in enumerate(arrays)
            ]
            for turn, first in enumerate(firsts)
        ]
    for move in sum(moves, []):
        move.start()

    def piece(turn, at, head):
        if loaded:
            return arrays[at][:, heads_at(turns[turn] * STEP, head, dim)]
        return copy_ref[turn, at, :, head * dim : (head + 1) * dim]

    for turn, first in enumerate(firsts):
        for source in range(2):
            block = core if source == 0 else 1 - core
            decay = decays_at(decay_ref, block, first)
            weight = jnp.exp(sums_over(decay, lambda u, s: u > s))
            whole = jnp.broadcast_to(jnp.sum(decay, axis=1, keepdims=True), (STEP, dim))
            if moves:
                for move in moves[turn][2 * source : 2 * source + 2]:
                    move.wait()
            states = []
            for head in range(STEP):
                decayed = piece(turn, 2 * source, head).T.astype(jnp.float32)
                decayed = (decayed * weight[head : head + 1, :]).astype(jnp.bfloat16)
                states.append(dot(decayed, piece(turn, 2 * source + 1, head), NN))
            for head in range(STEP):
                owner, spot = divmod(head, owned)
                span = slice(spot * dim, (spot + 1) * dim)
                stacked_ref[turn, owner, block, span, :] = states[head].astype(jnp.bfloat16)
            for at in range(2):
                stacked_ref[turn, at, block, owned * dim :, :] = decay_rows(
                    [whole[head : head + 1] for head in range(at * owned, (at + 1) * owned)]
                )
        for at in range(2):
            slots[2 * turn + at][...] = stacked_ref[turn, (part & 1) ^ at]


def inside_kernel(
    dim, half, begin, count, other, me_ref, queries_ref, keys_ref, values_ref, decay_ref, *rest
):
    inside_ref, down_ref, done_ref = rest[-3:]
    core = me_ref[1]
    length = decay_ref.shape[2]
    rows = lax.broadcasted_iota(jnp.int32, (length, length), 0)
    causal = rows >= lax.broadcasted_iota(jnp.int32, (length, length), 1)
    for turn in range(count // STEP):
        first = (1 - core if other else core) * half + begin + turn * STEP
        decay = decays_at(decay_ref, core, first)
        across = sums_over(decay, lambda u, s: u <= s)
        down = across.T
        down_ref[turn] = jnp.exp(down)
        columns = [heads_at(first, head, dim) for head in range(STEP)]
        scores = [dot(queries_ref[0, :, c], keys_ref[0, :, c], NT) for c in columns]
        weights = []
        for head in range(STEP):
            gap = down[:, head : head + 1] - across[head : head + 1, :]
            weight = scores[head] * jnp.exp(jnp.where(causal, gap, -jnp.inf))
            weights.append(weight.astype(jnp.bfloat16))
        for head, c in enumerate(columns):
            at = (turn * STEP + head) * dim
            inside_ref[:, at : at + dim] = dot(weights[head], values_ref[0, :, c], NN)
    done_ref[...] = jnp.zeros_like(done_ref)


def gather_states(part, slots, stacked_ref):
    parts = len(slots)
    for slot, slot_ref in enumerate(slots):
        for block in range(2):
            stacked_ref[block * parts + (part ^ slot)] = slot_ref[block]


def total_kernel(dim, owned, parts, me_ref, *refs):
    total_ref, stacked_ref = refs[-2:]
    gather_states(me_ref[0], refs[:parts], stacked_ref)
    count = 2 * parts
    extra = [stacked_ref[at, owned * dim :, :] for at in range(count)]
    sums = []
    for head in range(owned):
        span = slice(head * dim, (head + 1) * dim)
        after = jnp.zeros((1, dim), jnp.float32)
        total = stacked_ref[count - 1, span, :].astype(jnp.float32)
        for at in range(count - 2, -1, -1):
            after += join(extra[at + 1], head)
            total += jnp.exp(after) * stacked_ref[at, span, :].astype(jnp.float32)
        total_ref[span, :] = total.astype(jnp.bfloat16)
        sums.append(after + join(extra[0], head))
    total_ref[owned * dim :, :] = decay_rows(sums)


def widen_kernel(dim, owned, step, me_ref, mine_ref, other_ref, *refs):
    out_ref = refs[-1]
    later = (me_ref[2] >> step) % 2 == 1
    extra = mine_ref[owned * dim :, :], other_ref[owned * dim :, :]
    sums = []
    for head in range(owned):
        span = slice(head * dim, (head + 1) * dim)
        mine, other = join(extra[0], head), join(extra[1], head)
        total = jnp.where(later, 1.0, jnp.exp(other)) * mine_ref[span, :].astype(jnp.float32)
        total += jnp.where(later, jnp.exp(mine), 1.0) * other_ref[span, :].astype(jnp.float32)
        out_ref[span, :] = total.astype(jnp.bfloat16)
        sums.append(mine + other)
    out_ref[owned * dim :, :] = decay_rows(sums)


def prefix_kernel(dim, owned, parts, stretches, me_ref, gain_ref, *refs):
    stacked_ref, prefix_ref = refs[-2:]
    slots, totals = refs[:parts], refs[parts : parts + stretches]
    count = 2 * parts
    results = refs[-2 - parts : -2]
    gather_states(me_ref[0], slots, stacked_ref)
    extra = [stacked_ref[at, owned * dim :, :] for at in range(count)]
    more = [total_ref[owned * dim :, :] for total_ref in totals]
    earlier = [
        ((me_ref[2] >> step) % 2).astype(jnp.float32) for step in range(len(totals))
    ]
    for head in range(owned):
        span = slice(head * dim, (head + 1) * dim)
        prefix = jnp.zeros((dim, dim), jnp.float32)
        after = jnp.zeros((1, dim), jnp.float32)
        for turn, total_ref in enumerate(totals):
            factor = earlier[turn] * jnp.exp(after)
            prefix += factor * total_ref[span, :].astype(jnp.float32)
            after += earlier[turn] * join(more[turn], head)
        for at in range(count):
            prefix_ref[at, span, :] = prefix.astype(jnp.bfloat16)
            if at < count - 1:
                prefix = jnp.exp(join(extra[at], head)) * prefix
                prefix += stacked_ref[at, span, :].astype(jnp.float32)
    size = owned * dim
    for slot, result_ref in enumerate(results):
        for block in range(2):
            result_ref[block * size : (block + 1) * size, :] = prefix_ref[
                block * parts + (me_ref[0] ^ slot)
            ]
        if result_ref.shape[0] > 2 * size:
            result_ref[2 * size :, :] = gain_ref[...]


def merge_kernel(parts, me_ref, *refs):
    slots, gain_ref, prefix_ref = refs[:parts], refs[-2], refs[-1]
    others = refs[-4:-2]
    size = prefix_ref.shape[1]
    local = gain_ref.shape[0] // parts
    block = 1 - me_ref[1]
    for slot, slot_ref in enumerate(slots):
        owner = me_ref[0] ^ slot
        prefix_ref[owner] = slot_ref[pl.ds(pl.multiple_of(block * size, size), size), :]
        if slot_ref.shape[0] > 2 * size:
            rows = pl.ds(pl.multiple_of(owner * local, local), local)
            gain_ref[rows, :] = slot_ref[2 * size :, :].astype(jnp.float32)
    if slots[0].shape[0] == 2 * size:
        gain_ref[...] = jnp.zeros_like(gain_ref)
    each = parts // len(others)
    for turn, other_ref in enumerate(others):
        other_ref[...] = prefix_ref[turn * each : (turn + 1) * each]


def output_kernel(
    dim, owned, half, begin, masks, other, me_ref,
    queries_ref, inside_ref, down_ref, gate_ref, gains, *refs,
):
    out_ref, done_ref, prefix_ref, result_ref, sent = refs[-5:]
    part, core = me_ref[0], me_ref[1]
    size = owned * dim
    if other:
        turns, prefixes = [0, 1], [refs[0], refs[1]]
    else:
        turns = [(part >> 1) ^ mask for mask in masks]
        prefixes = [prefix_ref.at[turn] for turn in range(len(masks))]
        rows = pl.ds(pl.multiple_of(core * size, size), size)
        for turn in range(len(masks)):
            for at in range(2):
                prefix_ref[turn, (part & 1) ^ at] = refs[2 * turn + at][rows, :]
    blocks = [lax.broadcasted_iota(jnp.int32, (2 * dim, 2 * dim), axis) // dim for axis in (0, 1)]
    average = jnp.where(blocks[0] == blocks[1], 1.0 / dim, 0.0).astype(jnp.bfloat16)
    moves = []
    for at, turn in enumerate(turns):
        first = (1 - core if other else core) * half + begin + turn * STEP
        gain = gains[pl.ds(pl.multiple_of(first, STEP), STEP), :]
        down = down_ref[turn]
        columns = [heads_at(first, head, dim) for head in range(STEP)]
        here = [heads_at(turn * STEP, head, dim) for head in range(STEP)]
        carried = []
        for head, c in enumerate(columns):
            owner, spot = divmod(head, owned)
            prefix = prefixes[at][owner, spot * dim : (spot + 1) * dim, :]
            carried.append(dot(queries_ref[0, :, c], prefix, NN))
        mixed, means = [], []
        for head in range(STEP):
            mixed.append(inside_ref[:, here[head]] + carried[head] * down[:, head : head + 1])
        for head in range(0, STEP, 2):
            squares = [(value * value).astype(jnp.bfloat16) for value in mixed[head : head + 2]]
            both = dot(jnp.concatenate(squares, axis=1), average, NN)
            means += [both[:, :dim], both[:, dim:]]
        for head in range(STEP):
            factor = gain[head : head + 1, :] * gate_ref[:, here[head]]
            normed = mixed[head] * lax.rsqrt(means[head] + 1e-06) * factor
            result_ref[at, :, head * dim : (head + 1) * dim] = normed.astype(jnp.bfloat16)
            if head % 2 == 1:
                start = pl.multiple_of((first + head - 1) * dim, 2 * dim)
                moves.append(
                    pltpu.make_async_copy(
                        result_ref.at[at, :, (head - 1) * dim : (head + 1) * dim],
                        out_ref.at[0, :, pl.ds(start, 2 * dim)],
                        sent.at[at, head // 2],
                    )
                )
                moves[-1].start()
    done_ref[...] = jnp.zeros_like(done_ref)
    for move in moves:
        move.wait()


def kernel_call(body, name, in_specs, out_specs, out_shape, scratch=(), aliases={}, cost=0):
    return pl.pallas_call(
        body,
        grid_spec=pltpu.PrefetchScalarGridSpec(
            num_scalar_prefetch=1,
            grid=(),
            in_specs=in_specs,
            out_specs=out_specs,
            scratch_shapes=scratch,
        ),
        out_shape=out_shape,
        input_output_aliases=aliases,
        compiler_params=pltpu.CompilerParams(vmem_limit_bytes=VMEM_LIMIT),
        cost_estimate=pl.CostEstimate(
            flops=int(1e9 * cost) + 1, transcendentals=0, bytes_accessed=1
        ),
        name=name,
    )


def on_device(parts, planes, queries, keys, values, gate, log_decay, norm_gain):
    _, length, width = queries.shape
    local = log_decay.shape[1]
    dim = width // (local * parts)
    count = 2 * parts
    half = local * parts // 2
    owned = half // (GROUPS * parts)
    rows = owned * dim + EXTRA
    me = jnp.stack([lax.axis_index(axis) for axis in ("head", "core", "z")]).astype(jnp.int32)
    swap = [(0, 1), (1, 0)]

    values_other = lax.ppermute(values, "core", swap)
    keys_other = lax.ppermute(keys, "core", swap)
    packed = pl.pallas_call(
        functools.partial(pack_kernel, parts),
        out_shape=jax.ShapeDtypeStruct((count, local, length), jnp.float32),
        name="pack",
    )(log_decay)
    decay = lax.all_to_all(packed, ("core", "head"), 0, 0, tiled=True)
    gain = norm_gain.reshape(local, dim)

    vmem = pl.BlockSpec(memory_space=pltpu.VMEM)
    hbm = pl.BlockSpec(memory_space=pl.ANY)

    def in_vmem(array):
        return pltpu.with_memory_space_constraint(array, pltpu.VMEM)

    def in_hbm(array):
        return pltpu.with_memory_space_constraint(array, pltpu.HBM)

    own = in_hbm(keys), in_hbm(values)
    share = half // GROUPS
    keys, values, queries = (in_vmem(array) for array in (keys, values, queries))

    def exchange(slots):
        arrived = list(slots)
        for slot in sorted(range(1, parts), key=lambda s: -bin(s).count("1")):
            pairs = [(at, at ^ slot) for at in range(parts)]
            arrived[slot] = lax.ppermute(slots[slot], "head", pairs)
        return arrived

    before = ()
    held = []
    state_type = jax.ShapeDtypeStruct((2, rows, dim), jnp.bfloat16)
    token = jax.ShapeDtypeStruct((8, 128), jnp.float32)
    inside = {}

    def inside_part(before, cost=0):
        group, other = divmod(len(inside), 2)
        *inside[group, other], made = kernel_call(
            functools.partial(inside_kernel, dim, half, group * share, share, other),
            f"inside{group}_{other}",
            [vmem] * 4 + [hbm] * len(before),
            [vmem] * 3,
            [
                pltpu.VMEM((length, share * dim), jnp.float32),
                jax.ShapeDtypeStruct((share // STEP, length, STEP), jnp.float32),
                token,
            ],
            cost=cost,
        )(me, queries, keys, values, decay, *before)
        return (made,)

    gate_type = jax.ShapeDtypeStruct((length, share * dim), jnp.float32)
    gates = {}

    def gates_of(group, before):
        gates[group, 0], gates[group, 1], made = kernel_call(
            functools.partial(gate_kernel, half, group * share, share, dim),
            f"gates{group}",
            [hbm] * (1 + len(before)),
            [hbm, hbm, vmem],
            [pltpu.HBM(gate_type.shape, gate_type.dtype)] * 2 + [token],
            [
                pltpu.VMEM((2, length, share * dim), jnp.bfloat16),
                pltpu.VMEM((2,) + gate_type.shape, jnp.float32),
                pltpu.SemaphoreType.DMA((4,)),
            ],
        )(me, in_hbm(gate), *before)
        return (made,)

    slices = (*own, keys_other, values_other)
    first_slices = kernel_call(
        functools.partial(load_kernel, half, 0, share, dim),
        "load",
        [hbm] * 4,
        [vmem] * 4,
        [jax.ShapeDtypeStruct((length, share * dim), jnp.bfloat16)] * 4,
        [pltpu.SemaphoreType.DMA((4,))],
    )(me, *slices)
    for group in range(GROUPS):
        slots = {}
        for masks in ((1, 0),):
            loaded = group == 0
            scratch = [pltpu.VMEM((len(masks), 2) + state_type.shape, jnp.bfloat16)]
            if not loaded:
                scratch += [
                    pltpu.VMEM((len(masks), 4, length, STEP * dim), jnp.bfloat16),
                    pltpu.SemaphoreType.DMA((len(masks), 4)),
                ]
            state = kernel_call(
                functools.partial(state_kernel, dim, owned, half, group * share, masks, loaded),
                f"state{group}_{masks[0]}",
                [vmem] + [vmem if loaded else hbm] * 4 + [hbm] * len(before),
                [vmem] * (2 * len(masks)),
                [state_type] * (2 * len(masks)),
                scratch,
            )(me, decay, *(first_slices if loaded else slices), *before)
            before = tuple(state[:1])
            for at, array in enumerate(state):
                slots[2 * masks[at // 2] + at % 2] = array
        held.append(exchange([slots[slot] for slot in range(parts)]))
    before = inside_part(inside_part(before))

    arrived = []
    stacked = pltpu.VMEM((count, rows, dim), jnp.bfloat16)
    total_type = jax.ShapeDtypeStruct((rows, dim), jnp.bfloat16)

    def with_plane(total, step):
        pairs = [(at, at ^ (1 << step)) for at in range(planes)]
        return lax.ppermute(total, "z", pairs)

    def widen(group, step, total, other, before):
        return kernel_call(
            functools.partial(widen_kernel, dim, owned, step),
            f"widen{group}_{step}",
            [vmem] * 2 + [hbm] * len(before),
            vmem,
            total_type,
        )(me, total, other, *before)

    def prefix_of(group, before):
        stretches = arrived[group]
        return kernel_call(
            functools.partial(prefix_kernel, dim, owned, parts, len(stretches)),
            f"prefix{group}",
            [vmem] * (1 + parts + len(stretches)) + [hbm] * len(before),
            [vmem] * parts,
            [prefix_type] * parts,
            [stacked, pltpu.VMEM((count, size, dim), jnp.bfloat16)],
        )(me, gain, *held[group], *stretches, *before)

    size = owned * dim
    prefix_type = jax.ShapeDtypeStruct((2 * size + local, dim), jnp.bfloat16)
    prefixes = []
    for group in range(GROUPS):
        total = kernel_call(
            functools.partial(total_kernel, dim, owned, parts),
            f"total{group}",
            [vmem] * parts + [hbm],
            vmem,
            total_type,
            [stacked],
        )(me, *held[group], *before)
        before = (total,)
        stretches = [with_plane(total, 0)]
        arrived.append(stretches)
        if group > 0:
            prefix = prefix_of(group - 1, before)
            before = tuple(prefix[:1])
            prefixes.append(exchange(prefix))
        if group < GROUPS - 1:
            before = inside_part(before)
        for step in range(1, planes.bit_length() - 1):
            total = widen(group, step - 1, total, stretches[-1], before)
            before = (total,)
            stretches.append(with_plane(total, step))
        while group == GROUPS - 1 and len(inside) < 2 * GROUPS:
            before = inside_part(before, 2)
        before = gates_of(group, before)
    prefix = prefix_of(GROUPS - 1, before)
    before = tuple(prefix[:1])
    prefixes.append(exchange(prefix))

    part_type = jax.ShapeDtypeStruct((parts, size, dim), jnp.bfloat16)
    half_type = jax.ShapeDtypeStruct((parts // 2, size, dim), jnp.bfloat16)
    gain_type = jax.ShapeDtypeStruct((parts * local, dim), jnp.float32)

    def merge(group, before, cost):
        return kernel_call(
            functools.partial(merge_kernel, parts),
            f"merge{group}",
            [vmem] * parts + [hbm] * len(before),
            [vmem] * 3,
            [half_type, half_type, gain_type],
            [pltpu.VMEM(part_type.shape, part_type.dtype)],
            cost=cost,
        )(me, *prefixes[group], *before)

    def output(group, other, masks, received, out, before, cost=0):
        *out, made = kernel_call(
            functools.partial(output_kernel, dim, owned, half, group * share, masks, other),
            f"output{group}_{other}_{masks[0]}",
            [vmem] * (5 + len(received)) + [hbm] * (len(out) + len(before)),
            [hbm, vmem],
            [pltpu.HBM((1, length, width), jnp.bfloat16), token],
            [
                pltpu.VMEM((len(masks), 2, size, dim), jnp.bfloat16),
                pltpu.VMEM((len(masks), length, STEP * dim), jnp.bfloat16),
                pltpu.SemaphoreType.DMA((len(masks), STEP // 2)),
            ],
            aliases={6 + len(received): 0} if out else {},
            cost=cost,
        )(
            me, queries, in_vmem(inside[group, other][0]), inside[group, other][1],
            in_vmem(gates[group, other]), gains, *received, *out, *before,
        )
        return out, (made,)

    out = ()
    for group in range(GROUPS):
        last = group == GROUPS - 1
        slots = prefixes[group]
        if last:
            out, before = output(group, 0, (0,), slots[:2], out, before)
        *others, came = merge(group, before, 0)
        if group == 0:
            gains = came
        others = [lax.ppermute(other, "core", swap) for other in others]
        before = (came,)
        if last:
            out, before = output(group, 0, (1,), slots[2:], out, before, cost=20)
        else:
            out, before = output(group, 0, (0, 1), slots, out, before)
        out, before = output(group, 1, (0, 1), others, out, before)
    return out[0]


def solution(mesh):
    parts, blocks = mesh.shape["head"], mesh.shape["ctx"]
    names = mesh.axis_names
    at = names.index("ctx")
    shape = mesh.devices.shape[:at] + (blocks // 2, 2) + mesh.devices.shape[at + 1 :]
    finer = Mesh(mesh.devices.reshape(shape), names[:at] + ("z", "core") + names[at + 1 :])
    tokens = P(("z", "core"), "head", None)
    return jax.shard_map(
        functools.partial(on_device, parts, blocks // 2),
        mesh=finer,
        in_specs=(tokens,) * 5 + (P("head"),),
        out_specs=tokens,
        check_vma=False,
    )
```

```python
import functools

import jax
import jax.numpy as jnp
from jax import lax
from jax.experimental import pallas as pl
from jax.experimental.pallas import tpu as pltpu
from jax.sharding import Mesh
from jax.sharding import PartitionSpec as P

GROUPS = 2
STEP = 8
EXTRA = 16
VMEM_LIMIT = 8 * 1024 * 1024
NN = (((1,), (0,)), ((), ()))
NT = (((1,), (1,)), ((), ()))
TN = (((0,), (0,)), ((), ()))


def dot(a, b, dims, precision=None):
    return lax.dot_general(a, b, dims, precision=precision, preferred_element_type=jnp.float32)


def split(value):
    first = value.astype(jnp.bfloat16)
    left = value - first.astype(jnp.float32)
    second = left.astype(jnp.bfloat16)
    return first, second, (left - second.astype(jnp.float32)).astype(jnp.bfloat16)


def sums_over(decay, keep):
    heads, length = decay.shape
    rows = lax.broadcasted_iota(jnp.int32, (length, length), 0)
    columns = lax.broadcasted_iota(jnp.int32, (length, length), 1)
    chosen = jnp.where(keep(rows, columns), 1.0, 0.0).astype(jnp.bfloat16)
    parts = [part.astype(jnp.float32) for part in split(decay)]
    both = dot(jnp.concatenate(parts, axis=0).astype(jnp.bfloat16), chosen, NN)
    return both[:heads] + (both[heads : 2 * heads] + both[2 * heads :])


def join(rows, head):
    wide = rows.astype(jnp.float32)
    return wide[3 * head : 3 * head + 1] + (
        wide[3 * head + 1 : 3 * head + 2] + wide[3 * head + 2 : 3 * head + 3]
    )


def decay_rows(totals):
    parts = [part for total in totals for part in split(total)]
    blank = jnp.zeros((EXTRA - len(parts), totals[0].shape[1]), jnp.bfloat16)
    return jnp.concatenate(parts + [blank], axis=0)


def pack_kernel(parts, decay_ref, packed_ref):
    length = packed_ref.shape[2]
    for place in range(packed_ref.shape[0]):
        start = place % parts * length
        packed_ref[place] = decay_ref[0, :, start : start + length]


def gate_kernel(half, begin, share, dim, me_ref, gate_ref, *refs):
    *results, done_ref, copy_ref, result_ref, done = refs[-6:]
    width = share * dim
    loads, stores = [], []
    for at, out_ref in enumerate(results):
        first = (me_ref[1] if at == 0 else 1 - me_ref[1]) * half + begin
        columns = pl.ds(pl.multiple_of(first * dim, width), width)
        loads.append(pltpu.make_async_copy(gate_ref.at[0, :, columns], copy_ref.at[at], done.at[at]))
        stores.append(pltpu.make_async_copy(result_ref.at[at], out_ref, done.at[2 + at]))
        loads[-1].start()
    for at in range(len(results)):
        loads[at].wait()
        for head in range(share):
            c = slice(head * dim, (head + 1) * dim)
            turned = jnp.tanh(0.5 * copy_ref[at, :, c].astype(jnp.float32))
            result_ref[at, :, c] = 0.5 + 0.5 * turned
        stores[at].start()
    done_ref[...] = jnp.zeros_like(done_ref)
    for store in stores:
        store.wait()


def heads_at(first, head, dim):
    return pl.ds(pl.multiple_of((first + head) * dim, dim), dim)


def decays_at(decay_ref, block, first):
    local = decay_ref.shape[1]
    parts = decay_ref.shape[0] // 2
    rows = pl.ds(pl.multiple_of(first % local, STEP), STEP)
    return decay_ref[block * parts + first // local, rows, :]


def load_kernel(half, begin, count, dim, me_ref, *refs):
    sources, copies, done = refs[:2], refs[-3:-1], refs[-1]
    width = count * dim
    columns = pl.ds(pl.multiple_of((me_ref[1] * half + begin) * dim, width), width)
    moves = [
        pltpu.make_async_copy(source.at[0, :, columns], copy, done.at[at])
        for at, (source, copy) in enumerate(zip(sources, copies))
    ]
    for move in moves:
        move.start()
    for move in moves:
        move.wait()


def state_kernel(dim, owned, half, begin, masks, loaded, me_ref, decay_ref, *refs):
    arrays = refs[:4]
    stacked_ref, copy_ref, done = refs[-3:]
    slots = refs[-3 - 2 * len(masks) : -3]
    part, core = me_ref[0], me_ref[1]
    turns = [(part >> 1) ^ mask for mask in masks]
    firsts = [core * half + begin + turn * STEP for turn in turns]
    width = STEP * dim
    moves = {}
    for at in range(2 if loaded else 0, 4):
        for turn, first in enumerate(firsts):
            columns = pl.ds(pl.multiple_of(first * dim, width), width)
            moves[at, turn] = pltpu.make_async_copy(
                arrays[at].at[0, :, columns], copy_ref.at[turn, at], done.at[turn, at]
            )
            moves[at, turn].start()

    def piece(turn, at, head):
        if loaded and at < 2:
            return arrays[at][:, heads_at(turns[turn] * STEP, head, dim)]
        return copy_ref[turn, at, :, head * dim : (head + 1) * dim]

    for source in range(2):
        block = core if source == 0 else 1 - core
        for turn, first in enumerate(firsts):
            decay = decays_at(decay_ref, block, first)
            weight = jnp.exp(sums_over(decay, lambda u, s: u > s))
            whole = jnp.broadcast_to(jnp.sum(decay, axis=1, keepdims=True), (STEP, dim))
            for at in (2 * source, 2 * source + 1):
                if (at, turn) in moves:
                    moves[at, turn].wait()
            states = []
            for head in range(STEP):
                decayed = piece(turn, 2 * source, head).T.astype(jnp.float32)
                decayed = (decayed * weight[head : head + 1, :]).astype(jnp.bfloat16)
                states.append(dot(decayed, piece(turn, 2 * source + 1, head), NN))
            for head in range(STEP):
                owner, spot = divmod(head, owned)
                span = slice(spot * dim, (spot + 1) * dim)
                stacked_ref[turn, owner, block, span, :] = states[head].astype(jnp.bfloat16)
            for at in range(2):
                stacked_ref[turn, at, block, owned * dim :, :] = decay_rows(
                    [whole[head : head + 1] for head in range(at * owned, (at + 1) * owned)]
                )
    for turn in range(len(masks)):
        for at in range(2):
            slots[2 * turn + at][...] = stacked_ref[turn, (part & 1) ^ at]


def inside_kernel(
    dim, half, begin, count, other, me_ref, queries_ref, keys_ref, values_ref, decay_ref, *rest
):
    inside_ref, down_ref, done_ref = rest[-3:]
    core = me_ref[1]
    length = decay_ref.shape[2]
    rows = lax.broadcasted_iota(jnp.int32, (length, length), 0)
    causal = rows >= lax.broadcasted_iota(jnp.int32, (length, length), 1)
    for turn in range(count // STEP):
        first = (1 - core if other else core) * half + begin + turn * STEP
        decay = decays_at(decay_ref, core, first)
        across = sums_over(decay, lambda u, s: u <= s)
        down = across.T
        down_ref[turn] = jnp.exp(down)
        columns = [heads_at(first, head, dim) for head in range(STEP)]
        scores = [dot(queries_ref[0, :, c], keys_ref[0, :, c], NT) for c in columns]
        weights = []
        for head in range(STEP):
            gap = down[:, head : head + 1] - across[head : head + 1, :]
            weight = scores[head] * jnp.exp(jnp.where(causal, gap, -jnp.inf))
            weights.append(weight.astype(jnp.bfloat16))
        for head, c in enumerate(columns):
            at = (turn * STEP + head) * dim
            inside_ref[:, at : at + dim] = dot(weights[head], values_ref[0, :, c], NN)
    done_ref[...] = jnp.zeros_like(done_ref)


def gather_states(part, slots, stacked_ref):
    parts = len(slots)
    for slot, slot_ref in enumerate(slots):
        for block in range(2):
            stacked_ref[block * parts + (part ^ slot)] = slot_ref[block]


def total_kernel(dim, owned, parts, me_ref, *refs):
    total_ref, stacked_ref = refs[-2:]
    gather_states(me_ref[0], refs[:parts], stacked_ref)
    count = 2 * parts
    extra = [stacked_ref[at, owned * dim :, :] for at in range(count)]
    sums = []
    for head in range(owned):
        span = slice(head * dim, (head + 1) * dim)
        after = jnp.zeros((1, dim), jnp.float32)
        total = stacked_ref[count - 1, span, :].astype(jnp.float32)
        for at in range(count - 2, -1, -1):
            after += join(extra[at + 1], head)
            total += jnp.exp(after) * stacked_ref[at, span, :].astype(jnp.float32)
        total_ref[span, :] = total.astype(jnp.bfloat16)
        sums.append(after + join(extra[0], head))
    total_ref[owned * dim :, :] = decay_rows(sums)


def widen_kernel(dim, owned, step, me_ref, mine_ref, other_ref, *refs):
    out_ref = refs[-1]
    later = (me_ref[2] >> step) % 2 == 1
    extra = mine_ref[owned * dim :, :], other_ref[owned * dim :, :]
    sums = []
    for head in range(owned):
        span = slice(head * dim, (head + 1) * dim)
        mine, other = join(extra[0], head), join(extra[1], head)
        total = jnp.where(later, 1.0, jnp.exp(other)) * mine_ref[span, :].astype(jnp.float32)
        total += jnp.where(later, jnp.exp(mine), 1.0) * other_ref[span, :].astype(jnp.float32)
        out_ref[span, :] = total.astype(jnp.bfloat16)
        sums.append(mine + other)
    out_ref[owned * dim :, :] = decay_rows(sums)


def prefix_kernel(dim, owned, parts, stretches, me_ref, gain_ref, *refs):
    stacked_ref, prefix_ref = refs[-2:]
    slots, totals = refs[:parts], refs[parts : parts + stretches]
    count = 2 * parts
    results = refs[-2 - parts : -2]
    gather_states(me_ref[0], slots, stacked_ref)
    extra = [stacked_ref[at, owned * dim :, :] for at in range(count)]
    more = [total_ref[owned * dim :, :] for total_ref in totals]
    earlier = [
        ((me_ref[2] >> step) % 2).astype(jnp.float32) for step in range(len(totals))
    ]
    for head in range(owned):
        span = slice(head * dim, (head + 1) * dim)
        prefix = jnp.zeros((dim, dim), jnp.float32)
        after = jnp.zeros((1, dim), jnp.float32)
        for turn, total_ref in enumerate(totals):
            factor = earlier[turn] * jnp.exp(after)
            prefix += factor * total_ref[span, :].astype(jnp.float32)
            after += earlier[turn] * join(more[turn], head)
        for at in range(count):
            prefix_ref[at, span, :] = prefix.astype(jnp.bfloat16)
            if at < count - 1:
                prefix = jnp.exp(join(extra[at], head)) * prefix
                prefix += stacked_ref[at, span, :].astype(jnp.float32)
    size = owned * dim
    for slot, result_ref in enumerate(results):
        for block in range(2):
            result_ref[block * size : (block + 1) * size, :] = prefix_ref[
                block * parts + (me_ref[0] ^ slot)
            ]
        if result_ref.shape[0] > 2 * size:
            result_ref[2 * size :, :] = gain_ref[...]


def merge_kernel(parts, me_ref, *refs):
    slots, gain_ref, prefix_ref = refs[:parts], refs[-2], refs[-1]
    others = refs[-4:-2]
    size = prefix_ref.shape[1]
    local = gain_ref.shape[0] // parts
    block = 1 - me_ref[1]
    for slot, slot_ref in enumerate(slots):
        owner = me_ref[0] ^ slot
        prefix_ref[owner] = slot_ref[pl.ds(pl.multiple_of(block * size, size), size), :]
        if slot_ref.shape[0] > 2 * size:
            rows = pl.ds(pl.multiple_of(owner * local, local), local)
            gain_ref[rows, :] = slot_ref[2 * size :, :].astype(jnp.float32)
    if slots[0].shape[0] == 2 * size:
        gain_ref[...] = jnp.zeros_like(gain_ref)
    each = parts // len(others)
    for turn, other_ref in enumerate(others):
        other_ref[...] = prefix_ref[turn * each : (turn + 1) * each]


def output_kernel(
    dim, owned, half, begin, masks, other, me_ref,
    queries_ref, inside_ref, down_ref, gate_ref, gains, *refs,
):
    out_ref, done_ref, prefix_ref, result_ref, sent = refs[-5:]
    part, core = me_ref[0], me_ref[1]
    size = owned * dim
    if other:
        turns, prefixes = [0, 1], [refs[0], refs[1]]
    else:
        turns = [(part >> 1) ^ mask for mask in masks]
        prefixes = [prefix_ref.at[turn] for turn in range(len(masks))]
        rows = pl.ds(pl.multiple_of(core * size, size), size)
        for turn in range(len(masks)):
            for at in range(2):
                prefix_ref[turn, (part & 1) ^ at] = refs[2 * turn + at][rows, :]
    blocks = [lax.broadcasted_iota(jnp.int32, (2 * dim, 2 * dim), axis) // dim for axis in (0, 1)]
    average = jnp.where(blocks[0] == blocks[1], 1.0 / dim, 0.0).astype(jnp.bfloat16)
    moves = []
    for at, turn in enumerate(turns):
        first = (1 - core if other else core) * half + begin + turn * STEP
        gain = gains[pl.ds(pl.multiple_of(first, STEP), STEP), :]
        down = down_ref[turn]
        columns = [heads_at(first, head, dim) for head in range(STEP)]
        here = [heads_at(turn * STEP, head, dim) for head in range(STEP)]
        carried = []
        for head, c in enumerate(columns):
            owner, spot = divmod(head, owned)
            prefix = prefixes[at][owner, spot * dim : (spot + 1) * dim, :]
            carried.append(dot(queries_ref[0, :, c], prefix, NN))
        mixed, means = [], []
        for head in range(STEP):
            mixed.append(inside_ref[:, here[head]] + carried[head] * down[:, head : head + 1])
        for head in range(0, STEP, 2):
            squares = [(value * value).astype(jnp.bfloat16) for value in mixed[head : head + 2]]
            both = dot(jnp.concatenate(squares, axis=1), average, NN)
            means += [both[:, :dim], both[:, dim:]]
        for head in range(STEP):
            factor = gain[head : head + 1, :] * gate_ref[:, here[head]]
            normed = mixed[head] * lax.rsqrt(means[head] + 1e-06) * factor
            result_ref[at, :, head * dim : (head + 1) * dim] = normed.astype(jnp.bfloat16)
            if head % 2 == 1:
                start = pl.multiple_of((first + head - 1) * dim, 2 * dim)
                moves.append(
                    pltpu.make_async_copy(
                        result_ref.at[at, :, (head - 1) * dim : (head + 1) * dim],
                        out_ref.at[0, :, pl.ds(start, 2 * dim)],
                        sent.at[at, head // 2],
                    )
                )
                moves[-1].start()
    done_ref[...] = jnp.zeros_like(done_ref)
    for move in moves:
        move.wait()


def kernel_call(body, name, in_specs, out_specs, out_shape, scratch=(), aliases={}, cost=0):
    return pl.pallas_call(
        body,
        grid_spec=pltpu.PrefetchScalarGridSpec(
            num_scalar_prefetch=1,
            grid=(),
            in_specs=in_specs,
            out_specs=out_specs,
            scratch_shapes=scratch,
        ),
        out_shape=out_shape,
        input_output_aliases=aliases,
        compiler_params=pltpu.CompilerParams(vmem_limit_bytes=VMEM_LIMIT),
        cost_estimate=pl.CostEstimate(
            flops=int(1e9 * cost) + 1, transcendentals=0, bytes_accessed=1
        ),
        name=name,
    )


def on_device(parts, planes, queries, keys, values, gate, log_decay, norm_gain):
    _, length, width = queries.shape
    local = log_decay.shape[1]
    dim = width // (local * parts)
    count = 2 * parts
    half = local * parts // 2
    owned = half // (GROUPS * parts)
    rows = owned * dim + EXTRA
    me = jnp.stack([lax.axis_index(axis) for axis in ("head", "core", "z")]).astype(jnp.int32)
    swap = [(0, 1), (1, 0)]

    values_other = lax.ppermute(values, "core", swap)
    keys_other = lax.ppermute(keys, "core", swap)
    packed = pl.pallas_call(
        functools.partial(pack_kernel, parts),
        out_shape=jax.ShapeDtypeStruct((count, local, length), jnp.float32),
        name="pack",
    )(log_decay)
    decay = lax.all_to_all(packed, ("core", "head"), 0, 0, tiled=True)
    gain = norm_gain.reshape(local, dim)

    vmem = pl.BlockSpec(memory_space=pltpu.VMEM)
    hbm = pl.BlockSpec(memory_space=pl.ANY)

    def in_vmem(array):
        return pltpu.with_memory_space_constraint(array, pltpu.VMEM)

    def in_hbm(array):
        return pltpu.with_memory_space_constraint(array, pltpu.HBM)

    own = in_hbm(keys), in_hbm(values)
    share = half // GROUPS
    keys, values, queries = (in_vmem(array) for array in (keys, values, queries))

    def exchange(slots):
        arrived = list(slots)
        for slot in sorted(range(1, parts), key=lambda s: -bin(s).count("1")):
            pairs = [(at, at ^ slot) for at in range(parts)]
            arrived[slot] = lax.ppermute(slots[slot], "head", pairs)
        return arrived

    before = ()
    held = []
    state_type = jax.ShapeDtypeStruct((2, rows, dim), jnp.bfloat16)
    token = jax.ShapeDtypeStruct((8, 128), jnp.float32)
    inside = {}

    def inside_part(before, cost=0):
        group, other = divmod(len(inside), 2)
        *inside[group, other], made = kernel_call(
            functools.partial(inside_kernel, dim, half, group * share, share, other),
            f"inside{group}_{other}",
            [vmem] * 4 + [hbm] * len(before),
            [vmem] * 3,
            [
                pltpu.VMEM((length, share * dim), jnp.float32),
                jax.ShapeDtypeStruct((share // STEP, length, STEP), jnp.float32),
                token,
            ],
            cost=cost,
        )(me, queries, keys, values, decay, *before)
        return (made,)

    gate_type = jax.ShapeDtypeStruct((length, share * dim), jnp.float32)
    gates = {}

    def gates_of(group, before):
        gates[group, 0], gates[group, 1], made = kernel_call(
            functools.partial(gate_kernel, half, group * share, share, dim),
            f"gates{group}",
            [hbm] * (1 + len(before)),
            [hbm, hbm, vmem],
            [pltpu.HBM(gate_type.shape, gate_type.dtype)] * 2 + [token],
            [
                pltpu.VMEM((2, length, share * dim), jnp.bfloat16),
                pltpu.VMEM((2,) + gate_type.shape, jnp.float32),
                pltpu.SemaphoreType.DMA((4,)),
            ],
        )(me, in_hbm(gate), *before)
        return (made,)

    first_slices = kernel_call(
        functools.partial(load_kernel, half, 0, share, dim),
        "load",
        [hbm] * 3,
        [vmem] * 2,
        [jax.ShapeDtypeStruct((length, share * dim), jnp.bfloat16)] * 2,
        [pltpu.SemaphoreType.DMA((2,))],
    )(me, *own, packed)
    for group in range(GROUPS):
        slots = {}
        for masks in ((1, 0),):
            loaded = group == 0
            state = kernel_call(
                functools.partial(state_kernel, dim, owned, half, group * share, masks, loaded),
                f"state{group}",
                [vmem] + [vmem if loaded else hbm] * 2 + [hbm] * (2 + len(before)),
                [vmem] * (2 * len(masks)),
                [state_type] * (2 * len(masks)),
                [
                    pltpu.VMEM((len(masks), 2) + state_type.shape, jnp.bfloat16),
                    pltpu.VMEM((len(masks), 4, length, STEP * dim), jnp.bfloat16),
                    pltpu.SemaphoreType.DMA((len(masks), 4)),
                ],
            )(me, decay, *(first_slices if loaded else own), keys_other, values_other, *before)
            before = tuple(state[:1])
            for at, array in enumerate(state):
                slots[2 * masks[at // 2] + at % 2] = array
        held.append(exchange([slots[slot] for slot in range(parts)]))
    before = inside_part(inside_part(before))

    arrived = []
    stacked = pltpu.VMEM((count, rows, dim), jnp.bfloat16)
    total_type = jax.ShapeDtypeStruct((rows, dim), jnp.bfloat16)

    def with_plane(total, step):
        pairs = [(at, at ^ (1 << step)) for at in range(planes)]
        return lax.ppermute(total, "z", pairs)

    def widen(group, step, total, other, before):
        return kernel_call(
            functools.partial(widen_kernel, dim, owned, step),
            f"widen{group}_{step}",
            [vmem] * 2 + [hbm] * len(before),
            vmem,
            total_type,
        )(me, total, other, *before)

    def prefix_of(group, before):
        stretches = arrived[group]
        return kernel_call(
            functools.partial(prefix_kernel, dim, owned, parts, len(stretches)),
            f"prefix{group}",
            [vmem] * (1 + parts + len(stretches)) + [hbm] * len(before),
            [vmem] * parts,
            [prefix_type] * parts,
            [stacked, pltpu.VMEM((count, size, dim), jnp.bfloat16)],
        )(me, gain, *held[group], *stretches, *before)

    size = owned * dim
    prefix_type = jax.ShapeDtypeStruct((2 * size + local, dim), jnp.bfloat16)
    prefixes = []
    for group in range(GROUPS):
        total = kernel_call(
            functools.partial(total_kernel, dim, owned, parts),
            f"total{group}",
            [vmem] * parts + [hbm],
            vmem,
            total_type,
            [stacked],
        )(me, *held[group], *before)
        before = (total,)
        stretches = [with_plane(total, 0)]
        arrived.append(stretches)
        if group > 0:
            prefix = prefix_of(group - 1, before)
            before = tuple(prefix[:1])
            prefixes.append(exchange(prefix))
        if group < GROUPS - 1:
            before = inside_part(before)
        for step in range(1, planes.bit_length() - 1):
            total = widen(group, step - 1, total, stretches[-1], before)
            before = (total,)
            stretches.append(with_plane(total, step))
        while group == GROUPS - 1 and len(inside) < 2 * GROUPS:
            before = inside_part(before, 2)
        before = gates_of(group, before)
    prefix = prefix_of(GROUPS - 1, before)
    before = tuple(prefix[:1])
    prefixes.append(exchange(prefix))

    part_type = jax.ShapeDtypeStruct((parts, size, dim), jnp.bfloat16)
    half_type = jax.ShapeDtypeStruct((parts // 2, size, dim), jnp.bfloat16)
    gain_type = jax.ShapeDtypeStruct((parts * local, dim), jnp.float32)

    def merge(group, before, cost):
        return kernel_call(
            functools.partial(merge_kernel, parts),
            f"merge{group}",
            [vmem] * parts + [hbm] * len(before),
            [vmem] * 3,
            [half_type, half_type, gain_type],
            [pltpu.VMEM(part_type.shape, part_type.dtype)],
            cost=cost,
        )(me, *prefixes[group], *before)

    def output(group, other, masks, received, out, before, cost=0):
        *out, made = kernel_call(
            functools.partial(output_kernel, dim, owned, half, group * share, masks, other),
            f"output{group}_{other}_{masks[0]}",
            [vmem] * (5 + len(received)) + [hbm] * (len(out) + len(before)),
            [hbm, vmem],
            [pltpu.HBM((1, length, width), jnp.bfloat16), token],
            [
                pltpu.VMEM((len(masks), 2, size, dim), jnp.bfloat16),
                pltpu.VMEM((len(masks), length, STEP * dim), jnp.bfloat16),
                pltpu.SemaphoreType.DMA((len(masks), STEP // 2)),
            ],
            aliases={6 + len(received): 0} if out else {},
            cost=cost,
        )(
            me, queries, in_vmem(inside[group, other][0]), inside[group, other][1],
            in_vmem(gates[group, other]), gains, *received, *out, *before,
        )
        return out, (made,)

    out = ()
    for group in range(GROUPS):
        last = group == GROUPS - 1
        slots = prefixes[group]
        if last:
            out, before = output(group, 0, (0,), slots[:2], out, before)
        *others, came = merge(group, before, 0)
        if group == 0:
            gains = came
        others = [lax.ppermute(other, "core", swap) for other in others]
        before = (came,)
        if last:
            out, before = output(group, 0, (1,), slots[2:], out, before, cost=20)
        else:
            out, before = output(group, 0, (0, 1), slots, out, before)
        out, before = output(group, 1, (0, 1), others, out, before)
    return out[0]


def solution(mesh):
    parts, blocks = mesh.shape["head"], mesh.shape["ctx"]
    names = mesh.axis_names
    at = names.index("ctx")
    shape = mesh.devices.shape[:at] + (blocks // 2, 2) + mesh.devices.shape[at + 1 :]
    finer = Mesh(mesh.devices.reshape(shape), names[:at] + ("z", "core") + names[at + 1 :])
    tokens = P(("z", "core"), "head", None)
    return jax.shard_map(
        functools.partial(on_device, parts, blocks // 2),
        mesh=finer,
        in_specs=(tokens,) * 5 + (P("head"),),
        out_specs=tokens,
        check_vma=False,
    )
```

```python
import functools

import jax
import jax.numpy as jnp
from jax import lax
from jax.experimental import pallas as pl
from jax.experimental.pallas import tpu as pltpu
from jax.sharding import Mesh
from jax.sharding import PartitionSpec as P

GROUPS = 2
STEP = 8
EXTRA = 16
VMEM_LIMIT = 8 * 1024 * 1024
NN = (((1,), (0,)), ((), ()))
NT = (((1,), (1,)), ((), ()))
TN = (((0,), (0,)), ((), ()))


def dot(a, b, dims, precision=None):
    return lax.dot_general(a, b, dims, precision=precision, preferred_element_type=jnp.float32)


def split(value):
    first = value.astype(jnp.bfloat16)
    left = value - first.astype(jnp.float32)
    second = left.astype(jnp.bfloat16)
    return first, second, (left - second.astype(jnp.float32)).astype(jnp.bfloat16)


def sums_over(decay, keep):
    heads, length = decay.shape
    rows = lax.broadcasted_iota(jnp.int32, (length, length), 0)
    columns = lax.broadcasted_iota(jnp.int32, (length, length), 1)
    chosen = jnp.where(keep(rows, columns), 1.0, 0.0).astype(jnp.bfloat16)
    parts = [part.astype(jnp.float32) for part in split(decay)]
    both = dot(jnp.concatenate(parts, axis=0).astype(jnp.bfloat16), chosen, NN)
    return both[:heads] + (both[heads : 2 * heads] + both[2 * heads :])


def join(rows, head):
    wide = rows.astype(jnp.float32)
    return wide[3 * head : 3 * head + 1] + (
        wide[3 * head + 1 : 3 * head + 2] + wide[3 * head + 2 : 3 * head + 3]
    )


def decay_rows(totals):
    parts = [part for total in totals for part in split(total)]
    blank = jnp.zeros((EXTRA - len(parts), totals[0].shape[1]), jnp.bfloat16)
    return jnp.concatenate(parts + [blank], axis=0)


def pack_kernel(parts, decay_ref, packed_ref):
    length = packed_ref.shape[2]
    for place in range(packed_ref.shape[0]):
        start = place % parts * length
        packed_ref[place] = decay_ref[0, :, start : start + length]


def heads_at(first, head, dim):
    return pl.ds(pl.multiple_of((first + head) * dim, dim), dim)


def decays_at(decay_ref, block, first):
    local = decay_ref.shape[1]
    parts = decay_ref.shape[0] // 2
    rows = pl.ds(pl.multiple_of(first % local, STEP), STEP)
    return decay_ref[block * parts + first // local, rows, :]


def load_kernel(half, begin, count, dim, me_ref, *refs):
    sources, copies, done = refs[:2], refs[-3:-1], refs[-1]
    width = count * dim
    columns = pl.ds(pl.multiple_of((me_ref[1] * half + begin) * dim, width), width)
    moves = [
        pltpu.make_async_copy(source.at[0, :, columns], copy, done.at[at])
        for at, (source, copy) in enumerate(zip(sources, copies))
    ]
    for move in moves:
        move.start()
    for move in moves:
        move.wait()


def state_kernel(dim, owned, half, begin, masks, loaded, me_ref, decay_ref, *refs):
    arrays = refs[:4]
    stacked_ref, copy_ref, done = refs[-3:]
    slots = refs[-3 - 2 * len(masks) : -3]
    part, core = me_ref[0], me_ref[1]
    turns = [(part >> 1) ^ mask for mask in masks]
    firsts = [core * half + begin + turn * STEP for turn in turns]
    width = STEP * dim
    moves = {}
    for at in range(2 if loaded else 0, 4):
        for turn, first in enumerate(firsts):
            columns = pl.ds(pl.multiple_of(first * dim, width), width)
            moves[at, turn] = pltpu.make_async_copy(
                arrays[at].at[0, :, columns], copy_ref.at[turn, at], done.at[turn, at]
            )
            moves[at, turn].start()

    def piece(turn, at, head):
        if loaded and at < 2:
            return arrays[at][:, heads_at(turns[turn] * STEP, head, dim)]
        return copy_ref[turn, at, :, head * dim : (head + 1) * dim]

    for source in range(2):
        block = core if source == 0 else 1 - core
        for turn, first in enumerate(firsts):
            decay = decays_at(decay_ref, block, first)
            weight = jnp.exp(sums_over(decay, lambda u, s: u > s))
            whole = jnp.broadcast_to(jnp.sum(decay, axis=1, keepdims=True), (STEP, dim))
            for at in (2 * source, 2 * source + 1):
                if (at, turn) in moves:
                    moves[at, turn].wait()
            states = []
            for head in range(STEP):
                decayed = piece(turn, 2 * source, head).T.astype(jnp.float32)
                decayed = (decayed * weight[head : head + 1, :]).astype(jnp.bfloat16)
                states.append(dot(decayed, piece(turn, 2 * source + 1, head), NN))
            for head in range(STEP):
                owner, spot = divmod(head, owned)
                span = slice(spot * dim, (spot + 1) * dim)
                stacked_ref[turn, owner, block, span, :] = states[head].astype(jnp.bfloat16)
            for at in range(2):
                stacked_ref[turn, at, block, owned * dim :, :] = decay_rows(
                    [whole[head : head + 1] for head in range(at * owned, (at + 1) * owned)]
                )
    for turn in range(len(masks)):
        for at in range(2):
            slots[2 * turn + at][...] = stacked_ref[turn, (part & 1) ^ at]


def inside_kernel(
    dim, half, begin, count, other, me_ref,
    queries_ref, keys_ref, values_ref, gate_ref, decay_ref, *rest,
):
    inside_ref, down_ref, sigmoid_ref, done_ref = rest[-4:]
    core = me_ref[1]
    length = decay_ref.shape[2]
    rows = lax.broadcasted_iota(jnp.int32, (length, length), 0)
    causal = rows >= lax.broadcasted_iota(jnp.int32, (length, length), 1)
    for turn in range(count // STEP):
        first = (1 - core if other else core) * half + begin + turn * STEP
        decay = decays_at(decay_ref, core, first)
        across = sums_over(decay, lambda u, s: u <= s)
        down = across.T
        down_ref[turn] = jnp.exp(down)
        columns = [heads_at(first, head, dim) for head in range(STEP)]
        scores = [dot(queries_ref[0, :, c], keys_ref[0, :, c], NT) for c in columns]
        weights = []
        for head in range(STEP):
            gap = down[:, head : head + 1] - across[head : head + 1, :]
            weight = scores[head] * jnp.exp(jnp.where(causal, gap, -jnp.inf))
            weights.append(weight.astype(jnp.bfloat16))
        for head, c in enumerate(columns):
            at = (turn * STEP + head) * dim
            inside_ref[:, at : at + dim] = dot(weights[head], values_ref[0, :, c], NN)
            turned = jnp.tanh(0.5 * gate_ref[0, :, c].astype(jnp.float32))
            sigmoid_ref[:, at : at + dim] = 0.5 + 0.5 * turned
    done_ref[...] = jnp.zeros_like(done_ref)


def gather_states(part, slots, stacked_ref):
    parts = len(slots)
    for slot, slot_ref in enumerate(slots):
        for block in range(2):
            stacked_ref[block * parts + (part ^ slot)] = slot_ref[block]


def total_kernel(dim, owned, parts, me_ref, *refs):
    total_ref, stacked_ref = refs[-2:]
    gather_states(me_ref[0], refs[:parts], stacked_ref)
    count = 2 * parts
    extra = [stacked_ref[at, owned * dim :, :] for at in range(count)]
    sums = []
    for head in range(owned):
        span = slice(head * dim, (head + 1) * dim)
        after = jnp.zeros((1, dim), jnp.float32)
        total = stacked_ref[count - 1, span, :].astype(jnp.float32)
        for at in range(count - 2, -1, -1):
            after += join(extra[at + 1], head)
            total += jnp.exp(after) * stacked_ref[at, span, :].astype(jnp.float32)
        total_ref[span, :] = total.astype(jnp.bfloat16)
        sums.append(after + join(extra[0], head))
    total_ref[owned * dim :, :] = decay_rows(sums)


def widen_kernel(dim, owned, step, me_ref, mine_ref, other_ref, *refs):
    out_ref = refs[-1]
    later = (me_ref[2] >> step) % 2 == 1
    extra = mine_ref[owned * dim :, :], other_ref[owned * dim :, :]
    sums = []
    for head in range(owned):
        span = slice(head * dim, (head + 1) * dim)
        mine, other = join(extra[0], head), join(extra[1], head)
        total = jnp.where(later, 1.0, jnp.exp(other)) * mine_ref[span, :].astype(jnp.float32)
        total += jnp.where(later, jnp.exp(mine), 1.0) * other_ref[span, :].astype(jnp.float32)
        out_ref[span, :] = total.astype(jnp.bfloat16)
        sums.append(mine + other)
    out_ref[owned * dim :, :] = decay_rows(sums)


def prefix_kernel(dim, owned, parts, stretches, me_ref, gain_ref, *refs):
    stacked_ref, prefix_ref = refs[-2:]
    slots, totals = refs[:parts], refs[parts : parts + stretches]
    count = 2 * parts
    results = refs[-2 - parts : -2]
    gather_states(me_ref[0], slots, stacked_ref)
    extra = [stacked_ref[at, owned * dim :, :] for at in range(count)]
    more = [total_ref[owned * dim :, :] for total_ref in totals]
    earlier = [
        ((me_ref[2] >> step) % 2).astype(jnp.float32) for step in range(len(totals))
    ]
    for head in range(owned):
        span = slice(head * dim, (head + 1) * dim)
        prefix = jnp.zeros((dim, dim), jnp.float32)
        after = jnp.zeros((1, dim), jnp.float32)
        for turn, total_ref in enumerate(totals):
            factor = earlier[turn] * jnp.exp(after)
            prefix += factor * total_ref[span, :].astype(jnp.float32)
            after += earlier[turn] * join(more[turn], head)
        for at in range(count):
            prefix_ref[at, span, :] = prefix.astype(jnp.bfloat16)
            if at < count - 1:
                prefix = jnp.exp(join(extra[at], head)) * prefix
                prefix += stacked_ref[at, span, :].astype(jnp.float32)
    size = owned * dim
    for slot, result_ref in enumerate(results):
        for block in range(2):
            result_ref[block * size : (block + 1) * size, :] = prefix_ref[
                block * parts + (me_ref[0] ^ slot)
            ]
        if result_ref.shape[0] > 2 * size:
            result_ref[2 * size :, :] = gain_ref[...]


def merge_kernel(parts, me_ref, *refs):
    slots, gain_ref, prefix_ref = refs[:parts], refs[-2], refs[-1]
    others = refs[-4:-2]
    size = prefix_ref.shape[1]
    local = gain_ref.shape[0] // parts
    block = 1 - me_ref[1]
    for slot, slot_ref in enumerate(slots):
        owner = me_ref[0] ^ slot
        prefix_ref[owner] = slot_ref[pl.ds(pl.multiple_of(block * size, size), size), :]
        if slot_ref.shape[0] > 2 * size:
            rows = pl.ds(pl.multiple_of(owner * local, local), local)
            gain_ref[rows, :] = slot_ref[2 * size :, :].astype(jnp.float32)
    if slots[0].shape[0] == 2 * size:
        gain_ref[...] = jnp.zeros_like(gain_ref)
    each = parts // len(others)
    for turn, other_ref in enumerate(others):
        other_ref[...] = prefix_ref[turn * each : (turn + 1) * each]


def output_kernel(
    dim, owned, half, begin, masks, other, me_ref,
    queries_ref, inside_ref, down_ref, gate_ref, gains, *refs,
):
    out_ref, done_ref, prefix_ref, result_ref, sent = refs[-5:]
    part, core = me_ref[0], me_ref[1]
    size = owned * dim
    if other:
        turns, prefixes = [0, 1], [refs[0], refs[1]]
    else:
        turns = [(part >> 1) ^ mask for mask in masks]
        prefixes = [prefix_ref.at[turn] for turn in range(len(masks))]
        rows = pl.ds(pl.multiple_of(core * size, size), size)
        for turn in range(len(masks)):
            for at in range(2):
                prefix_ref[turn, (part & 1) ^ at] = refs[2 * turn + at][rows, :]
    blocks = [lax.broadcasted_iota(jnp.int32, (2 * dim, 2 * dim), axis) // dim for axis in (0, 1)]
    average = jnp.where(blocks[0] == blocks[1], 1.0 / dim, 0.0).astype(jnp.bfloat16)
    moves = []
    for at, turn in enumerate(turns):
        first = (1 - core if other else core) * half + begin + turn * STEP
        gain = gains[pl.ds(pl.multiple_of(first, STEP), STEP), :]
        down = down_ref[turn]
        columns = [heads_at(first, head, dim) for head in range(STEP)]
        here = [heads_at(turn * STEP, head, dim) for head in range(STEP)]
        carried = []
        for head, c in enumerate(columns):
            owner, spot = divmod(head, owned)
            prefix = prefixes[at][owner, spot * dim : (spot + 1) * dim, :]
            carried.append(dot(queries_ref[0, :, c], prefix, NN))
        mixed, means = [], []
        for head in range(STEP):
            mixed.append(inside_ref[:, here[head]] + carried[head] * down[:, head : head + 1])
        for head in range(0, STEP, 2):
            squares = [(value * value).astype(jnp.bfloat16) for value in mixed[head : head + 2]]
            both = dot(jnp.concatenate(squares, axis=1), average, NN)
            means += [both[:, :dim], both[:, dim:]]
        for head in range(STEP):
            factor = gain[head : head + 1, :] * gate_ref[:, here[head]]
            normed = mixed[head] * lax.rsqrt(means[head] + 1e-06) * factor
            result_ref[at, :, head * dim : (head + 1) * dim] = normed.astype(jnp.bfloat16)
            if head % 2 == 1:
                start = pl.multiple_of((first + head - 1) * dim, 2 * dim)
                moves.append(
                    pltpu.make_async_copy(
                        result_ref.at[at, :, (head - 1) * dim : (head + 1) * dim],
                        out_ref.at[0, :, pl.ds(start, 2 * dim)],
                        sent.at[at, head // 2],
                    )
                )
                moves[-1].start()
    done_ref[...] = jnp.zeros_like(done_ref)
    for move in moves:
        move.wait()


def kernel_call(body, name, in_specs, out_specs, out_shape, scratch=(), aliases={}, cost=0):
    return pl.pallas_call(
        body,
        grid_spec=pltpu.PrefetchScalarGridSpec(
            num_scalar_prefetch=1,
            grid=(),
            in_specs=in_specs,
            out_specs=out_specs,
            scratch_shapes=scratch,
        ),
        out_shape=out_shape,
        input_output_aliases=aliases,
        compiler_params=pltpu.CompilerParams(vmem_limit_bytes=VMEM_LIMIT),
        cost_estimate=pl.CostEstimate(
            flops=int(1e9 * cost) + 1, transcendentals=0, bytes_accessed=1
        ),
        name=name,
    )


def on_device(parts, planes, queries, keys, values, gate, log_decay, norm_gain):
    _, length, width = queries.shape
    local = log_decay.shape[1]
    dim = width // (local * parts)
    count = 2 * parts
    half = local * parts // 2
    owned = half // (GROUPS * parts)
    rows = owned * dim + EXTRA
    me = jnp.stack([lax.axis_index(axis) for axis in ("head", "core", "z")]).astype(jnp.int32)
    swap = [(0, 1), (1, 0)]

    values_other = lax.ppermute(values, "core", swap)
    keys_other = lax.ppermute(keys, "core", swap)
    packed = pl.pallas_call(
        functools.partial(pack_kernel, parts),
        out_shape=jax.ShapeDtypeStruct((count, local, length), jnp.float32),
        name="pack",
    )(log_decay)
    decay = lax.all_to_all(packed, ("core", "head"), 0, 0, tiled=True)
    gain = norm_gain.reshape(local, dim)

    vmem = pl.BlockSpec(memory_space=pltpu.VMEM)
    hbm = pl.BlockSpec(memory_space=pl.ANY)

    def in_vmem(array):
        return pltpu.with_memory_space_constraint(array, pltpu.VMEM)

    def in_hbm(array):
        return pltpu.with_memory_space_constraint(array, pltpu.HBM)

    own = in_hbm(keys), in_hbm(values)
    share = half // GROUPS
    keys, values, queries, gate = (in_vmem(array) for array in (keys, values, queries, gate))

    def exchange(slots):
        arrived = list(slots)
        for slot in sorted(range(1, parts), key=lambda s: -bin(s).count("1")):
            pairs = [(at, at ^ slot) for at in range(parts)]
            arrived[slot] = lax.ppermute(slots[slot], "head", pairs)
        return arrived

    before = ()
    held = []
    state_type = jax.ShapeDtypeStruct((2, rows, dim), jnp.bfloat16)
    token = jax.ShapeDtypeStruct((8, 128), jnp.float32)
    inside = {}

    def inside_part(before, cost=0):
        group, other = divmod(len(inside), 2)
        *inside[group, other], made = kernel_call(
            functools.partial(inside_kernel, dim, half, group * share, share, other),
            f"inside{group}_{other}",
            [vmem] * 5 + [hbm] * len(before),
            [vmem] * 4,
            [
                pltpu.VMEM((length, share * dim), jnp.float32),
                jax.ShapeDtypeStruct((share // STEP, length, STEP), jnp.float32),
                pltpu.VMEM((length, share * dim), jnp.float32),
                token,
            ],
            cost=cost,
        )(me, queries, keys, values, gate, decay, *before)
        return (made,)

    first_slices = kernel_call(
        functools.partial(load_kernel, half, 0, share, dim),
        "load",
        [hbm] * 3,
        [vmem] * 2,
        [jax.ShapeDtypeStruct((length, share * dim), jnp.bfloat16)] * 2,
        [pltpu.SemaphoreType.DMA((2,))],
    )(me, *own, packed)
    for group in range(GROUPS):
        slots = {}
        for masks in ((1, 0),):
            loaded = group == 0
            state = kernel_call(
                functools.partial(state_kernel, dim, owned, half, group * share, masks, loaded),
                f"state{group}",
                [vmem] + [vmem if loaded else hbm] * 2 + [hbm] * (2 + len(before)),
                [vmem] * (2 * len(masks)),
                [state_type] * (2 * len(masks)),
                [
                    pltpu.VMEM((len(masks), 2) + state_type.shape, jnp.bfloat16),
                    pltpu.VMEM((len(masks), 4, length, STEP * dim), jnp.bfloat16),
                    pltpu.SemaphoreType.DMA((len(masks), 4)),
                ],
            )(me, decay, *(first_slices if loaded else own), keys_other, values_other, *before)
            before = tuple(state[:1])
            for at, array in enumerate(state):
                slots[2 * masks[at // 2] + at % 2] = array
        held.append(exchange([slots[slot] for slot in range(parts)]))
    before = inside_part(inside_part(before))

    arrived = []
    stacked = pltpu.VMEM((count, rows, dim), jnp.bfloat16)
    total_type = jax.ShapeDtypeStruct((rows, dim), jnp.bfloat16)

    def with_plane(total, step):
        pairs = [(at, at ^ (1 << step)) for at in range(planes)]
        return lax.ppermute(total, "z", pairs)

    def widen(group, step, total, other, before):
        return kernel_call(
            functools.partial(widen_kernel, dim, owned, step),
            f"widen{group}_{step}",
            [vmem] * 2 + [hbm] * len(before),
            vmem,
            total_type,
        )(me, total, other, *before)

    def prefix_of(group, before):
        stretches = arrived[group]
        return kernel_call(
            functools.partial(prefix_kernel, dim, owned, parts, len(stretches)),
            f"prefix{group}",
            [vmem] * (1 + parts + len(stretches)) + [hbm] * len(before),
            [vmem] * parts,
            [prefix_type] * parts,
            [stacked, pltpu.VMEM((count, size, dim), jnp.bfloat16)],
        )(me, gain, *held[group], *stretches, *before)

    size = owned * dim
    prefix_type = jax.ShapeDtypeStruct((2 * size + local, dim), jnp.bfloat16)
    prefixes = []
    for group in range(GROUPS):
        total = kernel_call(
            functools.partial(total_kernel, dim, owned, parts),
            f"total{group}",
            [vmem] * parts + [hbm],
            vmem,
            total_type,
            [stacked],
        )(me, *held[group], *before)
        before = (total,)
        stretches = [with_plane(total, 0)]
        arrived.append(stretches)
        if group > 0:
            prefix = prefix_of(group - 1, before)
            before = tuple(prefix[:1])
            prefixes.append(exchange(prefix))
        if group < GROUPS - 1:
            before = inside_part(before)
        for step in range(1, planes.bit_length() - 1):
            total = widen(group, step - 1, total, stretches[-1], before)
            before = (total,)
            stretches.append(with_plane(total, step))
        while group == GROUPS - 1 and len(inside) < 2 * GROUPS:
            before = inside_part(before, 2)
    prefix = prefix_of(GROUPS - 1, before)
    before = tuple(prefix[:1])
    prefixes.append(exchange(prefix))

    part_type = jax.ShapeDtypeStruct((parts, size, dim), jnp.bfloat16)
    half_type = jax.ShapeDtypeStruct((parts // 2, size, dim), jnp.bfloat16)
    gain_type = jax.ShapeDtypeStruct((parts * local, dim), jnp.float32)

    def merge(group, before, cost):
        return kernel_call(
            functools.partial(merge_kernel, parts),
            f"merge{group}",
            [vmem] * parts + [hbm] * len(before),
            [vmem] * 3,
            [half_type, half_type, gain_type],
            [pltpu.VMEM(part_type.shape, part_type.dtype)],
            cost=cost,
        )(me, *prefixes[group], *before)

    def output(group, other, masks, received, out, before, cost=0):
        *out, made = kernel_call(
            functools.partial(output_kernel, dim, owned, half, group * share, masks, other),
            f"output{group}_{other}_{masks[0]}",
            [vmem] * (5 + len(received)) + [hbm] * (len(out) + len(before)),
            [hbm, vmem],
            [pltpu.HBM((1, length, width), jnp.bfloat16), token],
            [
                pltpu.VMEM((len(masks), 2, size, dim), jnp.bfloat16),
                pltpu.VMEM((len(masks), length, STEP * dim), jnp.bfloat16),
                pltpu.SemaphoreType.DMA((len(masks), STEP // 2)),
            ],
            aliases={6 + len(received): 0} if out else {},
            cost=cost,
        )(
            me, queries, in_vmem(inside[group, other][0]), inside[group, other][1],
            in_vmem(inside[group, other][2]), gains, *received, *out, *before,
        )
        return out, (made,)

    out = ()
    for group in range(GROUPS):
        last = group == GROUPS - 1
        slots = prefixes[group]
        if last:
            out, before = output(group, 0, (0,), slots[:2], out, before)
        *others, came = merge(group, before, 0)
        if group == 0:
            gains = came
        others = [lax.ppermute(other, "core", swap) for other in others]
        before = (came,)
        if last:
            out, before = output(group, 0, (1,), slots[2:], out, before, cost=20)
        else:
            out, before = output(group, 0, (0, 1), slots, out, before)
        out, before = output(group, 1, (0, 1), others, out, before)
    return out[0]


def solution(mesh):
    parts, blocks = mesh.shape["head"], mesh.shape["ctx"]
    names = mesh.axis_names
    at = names.index("ctx")
    shape = mesh.devices.shape[:at] + (blocks // 2, 2) + mesh.devices.shape[at + 1 :]
    finer = Mesh(mesh.devices.reshape(shape), names[:at] + ("z", "core") + names[at + 1 :])
    tokens = P(("z", "core"), "head", None)
    return jax.shard_map(
        functools.partial(on_device, parts, blocks // 2),
        mesh=finer,
        in_specs=(tokens,) * 5 + (P("head"),),
        out_specs=tokens,
        check_vma=False,
    )
```

```python
import functools

import jax
import jax.numpy as jnp
from jax import lax
from jax.experimental import pallas as pl
from jax.experimental.pallas import tpu as pltpu
from jax.sharding import Mesh
from jax.sharding import PartitionSpec as P

GROUPS = 2
STEP = 8
EXTRA = 16
VMEM_LIMIT = 8 * 1024 * 1024
NN = (((1,), (0,)), ((), ()))
NT = (((1,), (1,)), ((), ()))
TN = (((0,), (0,)), ((), ()))


def dot(a, b, dims, precision=None):
    return lax.dot_general(a, b, dims, precision=precision, preferred_element_type=jnp.float32)


def split(value):
    first = value.astype(jnp.bfloat16)
    left = value - first.astype(jnp.float32)
    second = left.astype(jnp.bfloat16)
    return first, second, (left - second.astype(jnp.float32)).astype(jnp.bfloat16)


def sums_over(decay, keep):
    heads, length = decay.shape
    rows = lax.broadcasted_iota(jnp.int32, (length, length), 0)
    columns = lax.broadcasted_iota(jnp.int32, (length, length), 1)
    chosen = jnp.where(keep(rows, columns), 1.0, 0.0).astype(jnp.bfloat16)
    parts = [part.astype(jnp.float32) for part in split(decay)]
    both = dot(jnp.concatenate(parts, axis=0).astype(jnp.bfloat16), chosen, NN)
    return both[:heads] + (both[heads : 2 * heads] + both[2 * heads :])


def join(rows, head):
    wide = rows.astype(jnp.float32)
    return wide[3 * head : 3 * head + 1] + (
        wide[3 * head + 1 : 3 * head + 2] + wide[3 * head + 2 : 3 * head + 3]
    )


def decay_rows(totals):
    parts = [part for total in totals for part in split(total)]
    blank = jnp.zeros((EXTRA - len(parts), totals[0].shape[1]), jnp.bfloat16)
    return jnp.concatenate(parts + [blank], axis=0)


def pack_kernel(parts, decay_ref, packed_ref):
    length = packed_ref.shape[2]
    for place in range(packed_ref.shape[0]):
        start = place % parts * length
        packed_ref[place] = decay_ref[0, :, start : start + length]


def heads_at(first, head, dim):
    return pl.ds(pl.multiple_of((first + head) * dim, dim), dim)


def decays_at(decay_ref, block, first):
    local = decay_ref.shape[1]
    parts = decay_ref.shape[0] // 2
    rows = pl.ds(pl.multiple_of(first % local, STEP), STEP)
    return decay_ref[block * parts + first // local, rows, :]


def load_kernel(half, begin, count, dim, me_ref, *refs):
    sources, copies, done = refs[:2], refs[-3:-1], refs[-1]
    width = count * dim
    columns = pl.ds(pl.multiple_of((me_ref[1] * half + begin) * dim, width), width)
    moves = [
        pltpu.make_async_copy(source.at[0, :, columns], copy, done.at[at])
        for at, (source, copy) in enumerate(zip(sources, copies))
    ]
    for move in moves:
        move.start()
    for move in moves:
        move.wait()


def state_kernel(dim, owned, half, begin, masks, loaded, me_ref, decay_ref, *refs):
    arrays = refs[:4]
    stacked_ref, copy_ref, done = refs[-3:]
    slots = refs[-3 - 2 * len(masks) : -3]
    part, core = me_ref[0], me_ref[1]
    turns = [(part >> 1) ^ mask for mask in masks]
    firsts = [core * half + begin + turn * STEP for turn in turns]
    width = STEP * dim
    moves = {}
    for at in range(2 if loaded else 0, 4):
        for turn, first in enumerate(firsts):
            columns = pl.ds(pl.multiple_of(first * dim, width), width)
            moves[at, turn] = pltpu.make_async_copy(
                arrays[at].at[0, :, columns], copy_ref.at[turn, at], done.at[turn, at]
            )
            moves[at, turn].start()

    def piece(turn, at, head):
        if loaded and at < 2:
            return arrays[at][:, heads_at(turns[turn] * STEP, head, dim)]
        return copy_ref[turn, at, :, head * dim : (head + 1) * dim]

    for source in range(2):
        block = core if source == 0 else 1 - core
        for turn, first in enumerate(firsts):
            decay = decays_at(decay_ref, block, first)
            weight = jnp.exp(sums_over(decay, lambda u, s: u > s))
            whole = jnp.broadcast_to(jnp.sum(decay, axis=1, keepdims=True), (STEP, dim))
            for at in (2 * source, 2 * source + 1):
                if (at, turn) in moves:
                    moves[at, turn].wait()
            states = []
            for head in range(STEP):
                decayed = piece(turn, 2 * source, head).T.astype(jnp.float32)
                decayed = (decayed * weight[head : head + 1, :]).astype(jnp.bfloat16)
                states.append(dot(decayed, piece(turn, 2 * source + 1, head), NN))
            for head in range(STEP):
                owner, spot = divmod(head, owned)
                span = slice(spot * dim, (spot + 1) * dim)
                stacked_ref[turn, owner, block, span, :] = states[head].astype(jnp.bfloat16)
            for at in range(2):
                stacked_ref[turn, at, block, owned * dim :, :] = decay_rows(
                    [whole[head : head + 1] for head in range(at * owned, (at + 1) * owned)]
                )
    for turn in range(len(masks)):
        for at in range(2):
            slots[2 * turn + at][...] = stacked_ref[turn, (part & 1) ^ at]


def inside_kernel(
    dim, half, begin, count, other, me_ref,
    queries_ref, keys_ref, values_ref, gate_ref, decay_ref, *rest,
):
    inside_ref, down_ref, sigmoid_ref, done_ref = rest[-4:]
    core = me_ref[1]
    length = decay_ref.shape[2]
    rows = lax.broadcasted_iota(jnp.int32, (length, length), 0)
    causal = rows >= lax.broadcasted_iota(jnp.int32, (length, length), 1)
    for turn in range(count // STEP):
        first = (1 - core if other else core) * half + begin + turn * STEP
        decay = decays_at(decay_ref, core, first)
        across = sums_over(decay, lambda u, s: u <= s)
        down = across.T
        down_ref[turn] = jnp.exp(down)
        columns = [heads_at(first, head, dim) for head in range(STEP)]
        scores = [dot(queries_ref[0, :, c], keys_ref[0, :, c], NT) for c in columns]
        weights = []
        for head in range(STEP):
            gap = down[:, head : head + 1] - across[head : head + 1, :]
            weight = scores[head] * jnp.exp(jnp.where(causal, gap, -jnp.inf))
            weights.append(weight.astype(jnp.bfloat16))
        for head, c in enumerate(columns):
            at = (turn * STEP + head) * dim
            inside_ref[:, at : at + dim] = dot(weights[head], values_ref[0, :, c], NN)
            turned = jnp.tanh(0.5 * gate_ref[0, :, c].astype(jnp.float32))
            sigmoid_ref[:, at : at + dim] = 0.5 + 0.5 * turned
    done_ref[...] = jnp.zeros_like(done_ref)


def gather_states(part, slots, stacked_ref):
    parts = len(slots)
    for slot, slot_ref in enumerate(slots):
        for block in range(2):
            stacked_ref[block * parts + (part ^ slot)] = slot_ref[block]


def total_kernel(dim, owned, parts, me_ref, *refs):
    total_ref, stacked_ref = refs[-2:]
    gather_states(me_ref[0], refs[:parts], stacked_ref)
    count = 2 * parts
    extra = [stacked_ref[at, owned * dim :, :] for at in range(count)]
    sums = []
    for head in range(owned):
        span = slice(head * dim, (head + 1) * dim)
        after = jnp.zeros((1, dim), jnp.float32)
        total = stacked_ref[count - 1, span, :].astype(jnp.float32)
        for at in range(count - 2, -1, -1):
            after += join(extra[at + 1], head)
            total += jnp.exp(after) * stacked_ref[at, span, :].astype(jnp.float32)
        total_ref[span, :] = total.astype(jnp.bfloat16)
        sums.append(after + join(extra[0], head))
    total_ref[owned * dim :, :] = decay_rows(sums)


def widen_kernel(dim, owned, step, me_ref, mine_ref, other_ref, *refs):
    out_ref = refs[-1]
    later = (me_ref[2] >> step) % 2 == 1
    extra = mine_ref[owned * dim :, :], other_ref[owned * dim :, :]
    sums = []
    for head in range(owned):
        span = slice(head * dim, (head + 1) * dim)
        mine, other = join(extra[0], head), join(extra[1], head)
        total = jnp.where(later, 1.0, jnp.exp(other)) * mine_ref[span, :].astype(jnp.float32)
        total += jnp.where(later, jnp.exp(mine), 1.0) * other_ref[span, :].astype(jnp.float32)
        out_ref[span, :] = total.astype(jnp.bfloat16)
        sums.append(mine + other)
    out_ref[owned * dim :, :] = decay_rows(sums)


def prefix_kernel(dim, owned, parts, stretches, me_ref, gain_ref, *refs):
    stacked_ref, prefix_ref = refs[-2:]
    slots, totals = refs[:parts], refs[parts : parts + stretches]
    count = 2 * parts
    results = refs[-2 - parts : -2]
    gather_states(me_ref[0], slots, stacked_ref)
    extra = [stacked_ref[at, owned * dim :, :] for at in range(count)]
    more = [total_ref[owned * dim :, :] for total_ref in totals]
    earlier = [
        ((me_ref[2] >> step) % 2).astype(jnp.float32) for step in range(len(totals))
    ]
    for head in range(owned):
        span = slice(head * dim, (head + 1) * dim)
        prefix = jnp.zeros((dim, dim), jnp.float32)
        after = jnp.zeros((1, dim), jnp.float32)
        for turn, total_ref in enumerate(totals):
            factor = earlier[turn] * jnp.exp(after)
            prefix += factor * total_ref[span, :].astype(jnp.float32)
            after += earlier[turn] * join(more[turn], head)
        for at in range(count):
            prefix_ref[at, span, :] = prefix.astype(jnp.bfloat16)
            if at < count - 1:
                prefix = jnp.exp(join(extra[at], head)) * prefix
                prefix += stacked_ref[at, span, :].astype(jnp.float32)
    size = owned * dim
    for slot, result_ref in enumerate(results):
        for block in range(2):
            result_ref[block * size : (block + 1) * size, :] = prefix_ref[
                block * parts + (me_ref[0] ^ slot)
            ]
        if result_ref.shape[0] > 2 * size:
            result_ref[2 * size :, :] = gain_ref[...]


def merge_kernel(parts, order, me_ref, *refs):
    slots, gain_ref, prefix_ref = refs[:parts], refs[-2], refs[-1]
    others = refs[-4:-2]
    size = prefix_ref.shape[1]
    local = gain_ref.shape[0] // parts
    block = 1 - me_ref[1]
    for slot, slot_ref in zip(order, slots):
        owner = me_ref[0] ^ slot
        prefix_ref[owner] = slot_ref[pl.ds(pl.multiple_of(block * size, size), size), :]
        if slot_ref.shape[0] > 2 * size:
            rows = pl.ds(pl.multiple_of(owner * local, local), local)
            gain_ref[rows, :] = slot_ref[2 * size :, :].astype(jnp.float32)
    if slots[0].shape[0] == 2 * size:
        gain_ref[...] = jnp.zeros_like(gain_ref)
    each = parts // len(others)
    for turn, other_ref in enumerate(others):
        other_ref[...] = prefix_ref[turn * each : (turn + 1) * each]


def output_kernel(
    dim, owned, half, begin, masks, other, me_ref,
    queries_ref, inside_ref, down_ref, gate_ref, gains, *refs,
):
    out_ref, done_ref, prefix_ref, result_ref, sent = refs[-5:]
    part, core = me_ref[0], me_ref[1]
    size = owned * dim
    if other:
        turns, prefixes = [0, 1], [refs[0], refs[1]]
    else:
        turns = [(part >> 1) ^ mask for mask in masks]
        prefixes = [prefix_ref.at[turn] for turn in range(len(masks))]
        rows = pl.ds(pl.multiple_of(core * size, size), size)
        for turn in range(len(masks)):
            for at in range(2):
                prefix_ref[turn, (part & 1) ^ at] = refs[2 * turn + at][rows, :]
    blocks = [lax.broadcasted_iota(jnp.int32, (2 * dim, 2 * dim), axis) // dim for axis in (0, 1)]
    average = jnp.where(blocks[0] == blocks[1], 1.0 / dim, 0.0).astype(jnp.bfloat16)
    moves = []
    for at, turn in enumerate(turns):
        first = (1 - core if other else core) * half + begin + turn * STEP
        gain = gains[pl.ds(pl.multiple_of(first, STEP), STEP), :]
        down = down_ref[turn]
        columns = [heads_at(first, head, dim) for head in range(STEP)]
        here = [heads_at(turn * STEP, head, dim) for head in range(STEP)]
        carried = []
        for head, c in enumerate(columns):
            owner, spot = divmod(head, owned)
            prefix = prefixes[at][owner, spot * dim : (spot + 1) * dim, :]
            carried.append(dot(queries_ref[0, :, c], prefix, NN))
        mixed, means = [], []
        for head in range(STEP):
            mixed.append(inside_ref[:, here[head]] + carried[head] * down[:, head : head + 1])
        for head in range(0, STEP, 2):
            squares = [(value * value).astype(jnp.bfloat16) for value in mixed[head : head + 2]]
            both = dot(jnp.concatenate(squares, axis=1), average, NN)
            means += [both[:, :dim], both[:, dim:]]
        for head in range(STEP):
            factor = gain[head : head + 1, :] * gate_ref[:, here[head]]
            normed = mixed[head] * lax.rsqrt(means[head] + 1e-06) * factor
            result_ref[at, :, head * dim : (head + 1) * dim] = normed.astype(jnp.bfloat16)
            if head % 2 == 1:
                start = pl.multiple_of((first + head - 1) * dim, 2 * dim)
                moves.append(
                    pltpu.make_async_copy(
                        result_ref.at[at, :, (head - 1) * dim : (head + 1) * dim],
                        out_ref.at[0, :, pl.ds(start, 2 * dim)],
                        sent.at[at, head // 2],
                    )
                )
                moves[-1].start()
    done_ref[...] = jnp.zeros_like(done_ref)
    for move in moves:
        move.wait()


def kernel_call(body, name, in_specs, out_specs, out_shape, scratch=(), aliases={}, cost=0):
    return pl.pallas_call(
        body,
        grid_spec=pltpu.PrefetchScalarGridSpec(
            num_scalar_prefetch=1,
            grid=(),
            in_specs=in_specs,
            out_specs=out_specs,
            scratch_shapes=scratch,
        ),
        out_shape=out_shape,
        input_output_aliases=aliases,
        compiler_params=pltpu.CompilerParams(vmem_limit_bytes=VMEM_LIMIT),
        cost_estimate=pl.CostEstimate(
            flops=int(1e9 * cost) + 1, transcendentals=0, bytes_accessed=1
        ),
        name=name,
    )


def on_device(parts, planes, queries, keys, values, gate, log_decay, norm_gain):
    _, length, width = queries.shape
    local = log_decay.shape[1]
    dim = width // (local * parts)
    count = 2 * parts
    half = local * parts // 2
    owned = half // (GROUPS * parts)
    rows = owned * dim + EXTRA
    me = jnp.stack([lax.axis_index(axis) for axis in ("head", "core", "z")]).astype(jnp.int32)
    swap = [(0, 1), (1, 0)]

    values_other = lax.ppermute(values, "core", swap)
    keys_other = lax.ppermute(keys, "core", swap)
    packed = pl.pallas_call(
        functools.partial(pack_kernel, parts),
        out_shape=jax.ShapeDtypeStruct((count, local, length), jnp.float32),
        name="pack",
    )(log_decay)
    decay = lax.all_to_all(packed, ("core", "head"), 0, 0, tiled=True)
    gain = norm_gain.reshape(local, dim)

    vmem = pl.BlockSpec(memory_space=pltpu.VMEM)
    hbm = pl.BlockSpec(memory_space=pl.ANY)

    def in_vmem(array):
        return pltpu.with_memory_space_constraint(array, pltpu.VMEM)

    def in_hbm(array):
        return pltpu.with_memory_space_constraint(array, pltpu.HBM)

    own = in_hbm(keys), in_hbm(values)
    share = half // GROUPS
    keys, values, queries, gate = (in_vmem(array) for array in (keys, values, queries, gate))

    def exchange(slots):
        arrived = list(slots)
        for slot in sorted(range(1, parts), key=lambda s: -bin(s).count("1")):
            pairs = [(at, at ^ slot) for at in range(parts)]
            arrived[slot] = lax.ppermute(slots[slot], "head", pairs)
        return arrived

    before = ()
    held = []
    state_type = jax.ShapeDtypeStruct((2, rows, dim), jnp.bfloat16)
    token = jax.ShapeDtypeStruct((8, 128), jnp.float32)
    inside = {}

    def inside_part(before, cost=0):
        group, other = divmod(len(inside), 2)
        *inside[group, other], made = kernel_call(
            functools.partial(inside_kernel, dim, half, group * share, share, other),
            f"inside{group}_{other}",
            [vmem] * 5 + [hbm] * len(before),
            [vmem] * 4,
            [
                pltpu.VMEM((length, share * dim), jnp.float32),
                jax.ShapeDtypeStruct((share // STEP, length, STEP), jnp.float32),
                pltpu.VMEM((length, share * dim), jnp.float32),
                token,
            ],
            cost=cost,
        )(me, queries, keys, values, gate, decay, *before)
        return (made,)

    first_slices = kernel_call(
        functools.partial(load_kernel, half, 0, share, dim),
        "load",
        [hbm] * 3,
        [vmem] * 2,
        [jax.ShapeDtypeStruct((length, share * dim), jnp.bfloat16)] * 2,
        [pltpu.SemaphoreType.DMA((2,))],
    )(me, *own, packed)
    for group in range(GROUPS):
        slots = {}
        for masks in ((1, 0),):
            loaded = group == 0
            state = kernel_call(
                functools.partial(state_kernel, dim, owned, half, group * share, masks, loaded),
                f"state{group}",
                [vmem] + [vmem if loaded else hbm] * 2 + [hbm] * (2 + len(before)),
                [vmem] * (2 * len(masks)),
                [state_type] * (2 * len(masks)),
                [
                    pltpu.VMEM((len(masks), 2) + state_type.shape, jnp.bfloat16),
                    pltpu.VMEM((len(masks), 4, length, STEP * dim), jnp.bfloat16),
                    pltpu.SemaphoreType.DMA((len(masks), 4)),
                ],
            )(me, decay, *(first_slices if loaded else own), keys_other, values_other, *before)
            before = tuple(state[:1])
            for at, array in enumerate(state):
                slots[2 * masks[at // 2] + at % 2] = array
        held.append(exchange([slots[slot] for slot in range(parts)]))
    before = inside_part(inside_part(before))

    arrived = []
    stacked = pltpu.VMEM((count, rows, dim), jnp.bfloat16)
    total_type = jax.ShapeDtypeStruct((rows, dim), jnp.bfloat16)

    def with_plane(total, step):
        pairs = [(at, at ^ (1 << step)) for at in range(planes)]
        return lax.ppermute(total, "z", pairs)

    def widen(group, step, total, other, before):
        return kernel_call(
            functools.partial(widen_kernel, dim, owned, step),
            f"widen{group}_{step}",
            [vmem] * 2 + [hbm] * len(before),
            vmem,
            total_type,
        )(me, total, other, *before)

    def prefix_of(group, before):
        stretches = arrived[group]
        return kernel_call(
            functools.partial(prefix_kernel, dim, owned, parts, len(stretches)),
            f"prefix{group}",
            [vmem] * (1 + parts + len(stretches)) + [hbm] * len(before),
            [vmem] * parts,
            [prefix_type] * parts,
            [stacked, pltpu.VMEM((count, size, dim), jnp.bfloat16)],
        )(me, gain, *held[group], *stretches, *before)

    size = owned * dim
    prefix_type = jax.ShapeDtypeStruct((2 * size + local, dim), jnp.bfloat16)
    prefixes = []
    for group in range(GROUPS):
        total = kernel_call(
            functools.partial(total_kernel, dim, owned, parts),
            f"total{group}",
            [vmem] * parts + [hbm],
            vmem,
            total_type,
            [stacked],
        )(me, *held[group], *before)
        before = (total,)
        stretches = [with_plane(total, 0)]
        arrived.append(stretches)
        if group > 0:
            prefix = prefix_of(group - 1, before)
            before = tuple(prefix[:1])
            prefixes.append(exchange(prefix))
        if group < GROUPS - 1:
            before = inside_part(before)
        for step in range(1, planes.bit_length() - 1):
            total = widen(group, step - 1, total, stretches[-1], before)
            before = (total,)
            stretches.append(with_plane(total, step))
        while group == GROUPS - 1 and len(inside) < 2 * GROUPS:
            before = inside_part(before, 2)
    prefix = prefix_of(GROUPS - 1, before)
    before = tuple(prefix[:1])
    prefixes.append(exchange(prefix))

    part_type = jax.ShapeDtypeStruct((parts, size, dim), jnp.bfloat16)
    half_type = jax.ShapeDtypeStruct((parts // 2, size, dim), jnp.bfloat16)
    gain_type = jax.ShapeDtypeStruct((parts * local, dim), jnp.float32)

    def merge(group, before, cost):
        order = list(range(parts))
        if group == GROUPS - 1:
            order = [0] + order[2:] + [1]
        return kernel_call(
            functools.partial(merge_kernel, parts, order),
            f"merge{group}",
            [vmem] * parts + [hbm] * len(before),
            [vmem] * 3,
            [half_type, half_type, gain_type],
            [pltpu.VMEM(part_type.shape, part_type.dtype)],
            cost=cost,
        )(me, *(prefixes[group][slot] for slot in order), *before)

    def output(group, other, masks, received, out, before, cost=0):
        *out, made = kernel_call(
            functools.partial(output_kernel, dim, owned, half, group * share, masks, other),
            f"output{group}_{other}_{masks[0]}",
            [vmem] * (5 + len(received)) + [hbm] * (len(out) + len(before)),
            [hbm, vmem],
            [pltpu.HBM((1, length, width), jnp.bfloat16), token],
            [
                pltpu.VMEM((len(masks), 2, size, dim), jnp.bfloat16),
                pltpu.VMEM((len(masks), length, STEP * dim), jnp.bfloat16),
                pltpu.SemaphoreType.DMA((len(masks), STEP // 2)),
            ],
            aliases={6 + len(received): 0} if out else {},
            cost=cost,
        )(
            me, queries, in_vmem(inside[group, other][0]), inside[group, other][1],
            in_vmem(inside[group, other][2]), gains, *received, *out, *before,
        )
        return out, (made,)

    out = ()
    for group in range(GROUPS):
        last = group == GROUPS - 1
        slots = prefixes[group]
        *others, came = merge(group, before, 0)
        if group == 0:
            gains = came
        others = [lax.ppermute(other, "core", swap) for other in others]
        before = (came,)
        out, before = output(group, 0, (0, 1), slots, out, before, cost=20 if last else 0)
        out, before = output(group, 1, (0, 1), others, out, before)
    return out[0]


def solution(mesh):
    parts, blocks = mesh.shape["head"], mesh.shape["ctx"]
    names = mesh.axis_names
    at = names.index("ctx")
    shape = mesh.devices.shape[:at] + (blocks // 2, 2) + mesh.devices.shape[at + 1 :]
    finer = Mesh(mesh.devices.reshape(shape), names[:at] + ("z", "core") + names[at + 1 :])
    tokens = P(("z", "core"), "head", None)
    return jax.shard_map(
        functools.partial(on_device, parts, blocks // 2),
        mesh=finer,
        in_specs=(tokens,) * 5 + (P("head"),),
        out_specs=tokens,
        check_vma=False,
    )
```
